32 devices in a mesh: section: 2 (over x), ctx: 16 (over z, y, core).
Axes of the slice: x: 2, y: 2, z: 4, core: 2. Of those that a mesh axis runs over, the one named last changes fastest.
Arguments:
- activations: bfloat16 [2, 24, 8192], P('section'), may hold values from -6 to 6
- act_frames: int32 [2, 24], replicated, may hold values from 0 to 191
- fresh_batch: bfloat16 [24, 8192], replicated, may hold values from -6 to 6
- fresh_frames: int32 [24], replicated, may hold values from 0 to 191
- norm_gain: float32 [2, 8192], P('section'), may hold values from 0.1 to 1.9
- cached_keys: bfloat16 [2, 12288, 1024], P('section', 'ctx'), may hold values from -64 to 64
- cached_values: bfloat16 [2, 12288, 1024], P('section', 'ctx'), may hold values from -6 to 6
- key_frames: int32 [12288], P('ctx'), may hold values from 0 to 191, never falling along the last dimension, each value on 1 to 128 neighbouring positions
Outputs:
- result: bfloat16 [2, 24, 8192], P('section')
The draws below stay inside these ranges and needn't reach their ends.
Inputs may be any that keep to these rules, and one draw needn't show every extreme that they name: `key_frames`: frame indices never fall along the clip, and every frame of 0 to 191 holds at least one token.
All inputs are finite; a program needn't handle non-finite values.
Results may differ from the reference program's by a relative error of at most 0.019.
Values may be sent and summed in bfloat16 or wider, within the bound.
No kernel may reach another device: no remote copies, remote signals or barrier semaphores. Data moves between devices by JAX's collectives and lax.ppermute only.
A program may use at most 64 MiB of HBM per device.

```python
import math
import jax
import jax.numpy as jnp
import numpy as np
from jax import lax

HEADS = 64
KVH = 8
HD = 128
D = 8192
Q_TOK = 24
CTX_DEV = 768
SECTIONS = 2
CTXTOK = 12288
FRAMES = 192
N_CTX = 16


def draw_cached_keys(key, part):
    key_one = jax.random.fold_in(key, 0)
    full_shape = (SECTIONS, CTXTOK, KVH * HD)
    return jnp.clip(jax.random.normal(key_one, full_shape, jnp.float32), -6.0, 6.0).astype(jnp.bfloat16)


def set_ends(entries, own_key, smallest, top_value):
    index_at = [jax.random.randint(jax.random.fold_in(own_key, axis), (), 0, length) for axis, length in enumerate(entries.shape)]
    widest = entries.shape.index(max(entries.shape))
    beside = index_at[:widest] + [(index_at[widest] + 1) % entries.shape[widest]] + index_at[widest + 1:]
    return entries.at[tuple(index_at)].set(smallest).at[tuple(beside)].set(top_value)


def steps_of(key, dims, pieces, least, largest):
    level, own = 1.0, jax.random.fold_in(key, 6)
    for dim, parts in pieces:
        heights = jnp.exp(jax.random.uniform(jax.random.fold_in(own, dim), (parts,), jnp.float32, least / len(pieces), largest / len(pieces)))
        level = level * jnp.repeat(heights, dims[dim] // parts).reshape([-1 if axis == dim else 1 for axis in range(len(dims))])
    return level


def split_up(count, total, most, lean):
    loads = [(1 << 20) // math.isqrt(rank ** lean) + 1 for rank in range(2, count + 1)]
    surplus, holding = total - most - (count - 1), [1] * (count - 1)
    while surplus > 0:
        movable = [i for i in range(count - 1) if holding[i] < most]
        whole, left = sum([loads[i] for i in movable]), surplus
        for i in movable:
            addition = min(most - holding[i], max(1, left * loads[i] // whole), surplus)
            holding[i] = holding[i] + addition
            surplus = surplus - addition
    return np.array([most] + holding)


def ragged_sizes(stream_key, count, total, reach, skew):
    if count == 2:
        one = jax.random.randint(stream_key, (), max(1, total - reach), min(reach, total - 1) + 1)
        return jnp.stack([one, total - one])
    sizes = jnp.asarray(split_up(count, total, reach, skew), jnp.int32)
    twos = (count - 1) // 2
    donor, sink = sizes[1:1 + 2 * twos:2], sizes[2:2 + 2 * twos:2]
    margin = jnp.minimum(donor - 1, reach - sink)
    passed = jax.random.randint(jax.random.fold_in(stream_key, 1), (twos,), 0, 1 << 20) % (margin + 1)
    sizes = sizes.at[1:1 + 2 * twos:2].set(donor - passed).at[2:2 + 2 * twos:2].set(sink + passed)
    return sizes[jax.random.permutation(jax.random.fold_in(stream_key, 2), count)]


def bell_draw(own_key, extent, width, reach, cuts=(), kind=jnp.bfloat16):
    factor_of = steps_of(own_key, extent, cuts, -0.22, 0.18) if cuts else 1.0
    array = jax.random.normal(own_key, extent, jnp.float32) * width * factor_of
    return jnp.minimum(jnp.maximum(array, -reach), reach).astype(kind)


def setup_inputs(seed: int = 0) -> dict:
    arg_keys = jax.random.split(jax.random.key(seed), 9)
    return {
        "activations": bell_draw(arg_keys[0], (SECTIONS, Q_TOK, D), 1.0, 6.0, ((0, 2),)),
        "act_frames": set_ends(jax.random.randint(arg_keys[1], (SECTIONS, Q_TOK), 0, FRAMES), jax.random.fold_in(arg_keys[1], 1), 0, FRAMES - 1).astype(jnp.int32),
        "fresh_batch": bell_draw(arg_keys[2], (Q_TOK, D), 1.0, 6.0),
        "fresh_frames": set_ends(jax.random.randint(arg_keys[3], (Q_TOK,), 0, FRAMES), jax.random.fold_in(arg_keys[3], 1), 0, FRAMES - 1).astype(jnp.int32),
        "norm_gain": jnp.clip(1.0 + 0.18 * jax.random.normal(arg_keys[4], (SECTIONS, D), jnp.float32), 0.1, 1.9),
        "cached_keys": draw_cached_keys(jax.random.fold_in(arg_keys[8], 71), 0),
        "cached_values": bell_draw(arg_keys[6], (SECTIONS, CTXTOK, KVH * HD), 1.0, 6.0, ((0, 2), (1, 16))),
        "key_frames": jnp.searchsorted(jnp.cumsum(ragged_sizes(arg_keys[7], FRAMES, CTXTOK, min(128, CTXTOK), 0)), jnp.arange(CTXTOK), side="right").astype(jnp.int32),
    }


epsilon = 1e-05
masked_score = -1e+30

def block_terms(grouped, frames, key_block, value_block, frame_block):
    scores = jnp.einsum('tkgd,jkd->tkgj', grouped.astype(jnp.float32), key_block.astype(jnp.float32)) * HD ** (-0.5)
    visible = frame_block[None, None, None, :] <= frames[:, None, None, None]
    scores = jnp.where(visible, scores, masked_score)
    block_max = lax.optimization_barrier(jnp.max(scores, axis=-1))
    probabilities = jnp.where(visible, jnp.exp(scores - block_max[..., None]), 0.0).astype(jnp.bfloat16)
    totals = lax.optimization_barrier(jnp.sum(probabilities.astype(jnp.float32), axis=-1))
    weighted = jnp.einsum('tkgj,jkd->tkgd', probabilities.astype(jnp.float32), value_block.astype(jnp.float32))
    return (block_max, totals, weighted)

def layer(hidden, frames, norm_scale, key_cache, value_cache, key_frames):
    widened = hidden.astype(jnp.float32)
    per_head = widened.reshape(Q_TOK, HEADS, HD)
    scale_heads = norm_scale.reshape(HEADS, HD)
    queries = (per_head * lax.rsqrt(lax.optimization_barrier(jnp.mean(per_head * per_head, axis=-1, keepdims=True)) + epsilon) * scale_heads[None]).astype(jnp.bfloat16)
    grouped = queries.reshape(Q_TOK, KVH, HEADS // KVH, HD)
    key_blocks = key_cache.reshape(N_CTX, CTX_DEV, KVH, HD)
    value_blocks = value_cache.reshape(N_CTX, CTX_DEV, KVH, HD)
    frame_blocks = key_frames.reshape(N_CTX, CTX_DEV)

    def one_block(blocks):
        return block_terms(grouped, frames, blocks[0], blocks[1], blocks[2])
    maxima, totals, weighted = lax.map(one_block, (key_blocks, value_blocks, frame_blocks))
    overall = lax.optimization_barrier(jnp.max(maxima, axis=0))
    factors = jnp.exp(maxima - overall[None])
    numerator = lax.optimization_barrier(jnp.sum(factors[..., None] * weighted, axis=0))
    denominator = lax.optimization_barrier(jnp.sum(factors * totals, axis=0))
    attended = (numerator / denominator[..., None]).reshape(Q_TOK, HEADS * HD)
    return (widened + attended).astype(jnp.bfloat16)

def reference(activations, act_frames, fresh_batch, fresh_frames, norm_gain, cached_keys, cached_values, key_frames):

    def first_tick(section_index):
        return layer(activations[section_index], act_frames[section_index], norm_gain[section_index], cached_keys[section_index], cached_values[section_index], key_frames)
    handed = lax.map(first_tick, jnp.arange(SECTIONS, dtype=jnp.int32))
    incoming = jnp.concatenate([fresh_batch[None], handed[:-1]], axis=0)
    frames_in = jnp.concatenate([fresh_frames[None], act_frames[:-1]], axis=0)

    def second_tick(section_index):
        return layer(incoming[section_index], frames_in[section_index], norm_gain[section_index], cached_keys[section_index], cached_values[section_index], key_frames)
    return lax.map(second_tick, jnp.arange(SECTIONS, dtype=jnp.int32))
```

```python
import jax
import jax.numpy as jnp
from jax import lax
from jax.sharding import PartitionSpec as P

HEADS = 64
HD = 128


epsilon = 1e-05
masked_score = -1e30


def passed_along(block, axis, distance):
    devices = range(lax.axis_size(axis))
    route = [(i - distance, i) for i in devices if i - distance in devices]
    return lax.ppermute(block, axis, route)


def partial_terms(
    hidden, frames, norm_scale, key_cache, value_cache, key_frames, head_count, head_size
):
    token_count = hidden.shape[0]
    kv_heads = key_cache.shape[1] // head_size
    widened = hidden.astype(jnp.float32)
    per_head = widened.reshape(token_count, head_count, head_size)
    scale_heads = norm_scale.reshape(head_count, head_size)
    queries = (
        per_head
        * lax.rsqrt(jnp.mean(per_head * per_head, axis=-1, keepdims=True) + epsilon)
        * scale_heads[None]
    ).astype(jnp.bfloat16)
    grouped = queries.reshape(token_count, kv_heads, head_count // kv_heads, head_size)
    key_rows = key_cache.reshape(-1, kv_heads, head_size)
    value_rows = value_cache.reshape(-1, kv_heads, head_size)
    scores = jnp.einsum(
        "tkgd,jkd->tkgj", grouped, key_rows, preferred_element_type=jnp.float32
    ) * head_size ** (-0.5)
    visible = key_frames[None, None, None, :] <= frames[:, None, None, None]
    scores = jnp.where(visible, scores, masked_score)
    block_max = jnp.max(scores, axis=-1)
    probabilities = jnp.where(visible, jnp.exp(scores - block_max[..., None]), 0.0).astype(
        jnp.bfloat16
    )
    totals = jnp.sum(probabilities.astype(jnp.float32), axis=-1)
    weighted = jnp.einsum(
        "tkgj,jkd->tkgd", probabilities, value_rows, preferred_element_type=jnp.float32
    )
    return (
        block_max.reshape(token_count, head_count),
        totals.reshape(token_count, head_count),
        weighted.reshape(token_count, head_count, head_size),
    )


def layer_chunk(hidden, own, frames, norm_scale, key_cache, value_cache, key_frames):
    shares = lax.axis_size("ctx")
    tokens = hidden.shape[0]
    held = HEADS // shares
    maxima, totals, weighted = partial_terms(
        hidden, frames, norm_scale, key_cache, value_cache, key_frames, HEADS, HD
    )
    sent = weighted.astype(jnp.bfloat16).reshape(tokens, shares, held, HD).transpose(1, 0, 2, 3)
    stats = jnp.stack([maxima, totals]).reshape(2, tokens, shares, held).transpose(2, 0, 1, 3)
    sent = lax.all_to_all(sent, "ctx", 0, 0, tiled=True).astype(jnp.float32)
    stats = lax.all_to_all(stats, "ctx", 0, 0, tiled=True)
    overall = jnp.max(stats[:, 0], axis=0)
    factors = jnp.exp(stats[:, 0] - overall[None])
    denominator = jnp.sum(factors * stats[:, 1], axis=0)
    numerator = jnp.sum(factors[..., None] * sent, axis=0)
    attended = (numerator / denominator[..., None]).reshape(tokens, held * HD)
    return (own.astype(jnp.float32) + attended).astype(jnp.bfloat16)


def spread(chunk):
    shares = lax.axis_size("ctx")
    gathered = lax.all_gather(chunk, "ctx", axis=0)
    return gathered.transpose(1, 0, 2).reshape(chunk.shape[0], shares * chunk.shape[1])


def body(
    activations,
    act_frames,
    fresh_batch,
    fresh_frames,
    norm_gain,
    cached_keys,
    cached_values,
    key_frames,
):
    section_index = lax.axis_index("section")
    width = fresh_batch.shape[1] // lax.axis_size("ctx")
    start = lax.axis_index("ctx") * width

    def share_of(batch):
        return lax.dynamic_slice_in_dim(batch, start, width, 1)

    own_frames = lax.dynamic_index_in_dim(act_frames, section_index, 0, keepdims=False)
    rest = (norm_gain[0], cached_keys[0], cached_values[0], key_frames)
    first = layer_chunk(activations[0], share_of(activations[0]), own_frames, *rest)
    handed = passed_along(first, "section", 1)
    prior_frames = lax.dynamic_index_in_dim(
        act_frames, jnp.maximum(section_index - 1, 0), 0, keepdims=False
    )
    own = jnp.where(section_index == 0, share_of(fresh_batch), handed)
    frames_in = jnp.where(section_index == 0, fresh_frames, prior_frames)
    incoming = spread(own)
    second = layer_chunk(incoming, own, frames_in, *rest)
    return spread(second)[None]


def solution(mesh):
    placed = (
        P("section", None, None),
        P(),
        P(),
        P(),
        P("section", None),
        P("section", "ctx", None),
        P("section", "ctx", None),
        P("ctx"),
    )
    return jax.shard_map(
        body, mesh=mesh, in_specs=placed, out_specs=P("section", None, None), check_vma=False
    )
```

```python
import functools
import math

import jax
import jax.numpy as jnp
from jax import lax
from jax.experimental import pallas as pl
from jax.experimental.pallas import tpu as pltpu
from jax.sharding import PartitionSpec as P

HEADS = 64
HD = 128
PAIR = 2
STAT_ROWS = 16
HIDDEN = -(2.0**100)
SCALE = HD**-0.5 * math.log2(math.e)

epsilon = 1e-05


def passed_along(block, axis, distance):
    devices = range(lax.axis_size(axis))
    route = [(i - distance, i) for i in devices if i - distance in devices]
    return lax.ppermute(block, axis, route)


def swapped(block):
    return lax.ppermute(block, "ctx", [(i, i ^ 1) for i in range(lax.axis_size("ctx"))])


def exchanged(chunks):
    size = lax.axis_size("ctx")
    groups = [list(range(place, size, PAIR)) for place in range(PAIR)]
    return lax.all_to_all(chunks, "ctx", 0, 0, axis_index_groups=groups, tiled=True)


def head_rows(block):
    return jnp.concatenate(
        [block[:, at : at + HD] for at in range(0, block.shape[1], HD)], axis=0
    )


def on_diagonal(rows):
    shape = (rows, HD)
    return lax.broadcasted_iota(jnp.int32, shape, 0) == lax.broadcasted_iota(jnp.int32, shape, 1)


def partial_kernel(
    place_ref, x_ref, gain_ref, frames_ref, own_frames_ref, got_frames_ref,
    own_keys_ref, own_values_ref, got_keys_ref, got_values_ref, out_ref,
):
    keys = own_keys_ref.shape[0]
    if len(x_ref.shape) == 3:
        x = jnp.concatenate([x_ref[i] for i in range(x_ref.shape[0])], axis=1)
    else:
        x = x_ref[...]
    x = x.astype(jnp.float32)
    tokens = x.shape[0]
    rows = head_rows(x)
    gain = head_rows(jnp.broadcast_to(gain_ref[...], x.shape))
    norm = lax.rsqrt(jnp.mean(rows * rows, axis=-1, keepdims=True) + epsilon)
    queries = (rows * norm * gain).astype(jnp.bfloat16)
    count = queries.shape[0]
    frames = frames_ref[...]

    def scores(key_block, key_frames):
        raw = lax.dot_general(
            queries, key_block, (((1,), (1,)), ((), ())), preferred_element_type=jnp.float32
        )
        bias = jnp.where(key_frames <= frames, 0.0, HIDDEN)
        raw = raw.reshape(count // tokens, tokens, keys) * SCALE + bias[None]
        return raw.reshape(count, keys)

    got_frames = got_frames_ref[0:1, :keys].astype(jnp.float32)
    first = scores(own_keys_ref[...], own_frames_ref[...])
    second = scores(got_keys_ref[:keys], got_frames)
    top = jnp.maximum(
        jnp.max(first, axis=-1, keepdims=True), jnp.max(second, axis=-1, keepdims=True)
    )
    top = top.astype(jnp.bfloat16).astype(jnp.float32)
    ones = jnp.ones((keys, HD), jnp.bfloat16)

    def weigh(raw, value_block):
        probs = jnp.exp2(raw - top).astype(jnp.bfloat16)
        return jnp.dot(
            probs, jnp.concatenate([value_block, ones], axis=1),
            preferred_element_type=jnp.float32,
        )

    both = weigh(first, own_values_ref[...]) + weigh(second, got_values_ref[:keys])
    weighted, totals = both[:, :HD], both[:, HD:]
    tops = jnp.broadcast_to(top, weighted.shape)

    chunks = out_ref.shape[0]
    held = count // chunks
    diagonal = on_diagonal(held)
    line = lax.broadcasted_iota(jnp.int32, (STAT_ROWS, HD), 0)
    for c in range(chunks):
        part = slice(c * held, (c + 1) * held)
        top_row = jnp.sum(jnp.where(diagonal, tops[part], 0.0), axis=0, keepdims=True)
        total_row = jnp.sum(jnp.where(diagonal, totals[part], 0.0), axis=0, keepdims=True)
        high = total_row.astype(jnp.bfloat16).astype(jnp.float32)
        stats = jnp.where(
            line == 0, top_row,
            jnp.where(line == 1, high, jnp.where(line == 2, total_row - high, 0.0)),
        )
        out_ref[c, :held] = weighted[part].astype(jnp.bfloat16)
        out_ref[c, held:] = stats.astype(jnp.bfloat16)


def partials(place, x, gain, frames, own_frames, keys, values, got, pairs):
    tokens = frames.shape[0]
    length, width = keys.shape
    kv_here = width // HD // PAIR
    group = HEADS // (width // HD)
    chunks = pairs // kv_here
    held = HEADS // PAIR // pairs * tokens
    if x.ndim == 3:
        x_spec = pl.BlockSpec((chunks, tokens, x.shape[2]), lambda g, place: (g, 0, 0))
    else:
        x_spec = pl.BlockSpec((tokens, group * HD), lambda g, place: (0, place[0] * kv_here + g))
    mine = lambda g, place: (0, place[0] * kv_here + g)
    grid_spec = pltpu.PrefetchScalarGridSpec(
        num_scalar_prefetch=1,
        grid=(kv_here,),
        in_specs=[
            x_spec,
            pl.BlockSpec((1, group * HD), mine),
            pl.BlockSpec((tokens, 1), lambda g, place: (0, 0)),
            pl.BlockSpec((1, length), lambda g, place: (0, 0)),
            pl.BlockSpec((STAT_ROWS, width), lambda g, place: (length // STAT_ROWS, 0)),
            pl.BlockSpec((length, HD), mine),
            pl.BlockSpec((length, HD), mine),
            pl.BlockSpec((length, HD), lambda g, place: (0, g)),
            pl.BlockSpec((length, HD), lambda g, place: (0, kv_here + g)),
        ],
        out_specs=pl.BlockSpec((chunks, held + STAT_ROWS, HD), lambda g, place: (g, 0, 0)),
    )
    queries = HEADS // PAIR * tokens
    return pl.pallas_call(
        partial_kernel,
        grid_spec=grid_spec,
        out_shape=jax.ShapeDtypeStruct((pairs, held + STAT_ROWS, HD), jnp.bfloat16),
        cost_estimate=pl.CostEstimate(
            flops=2 * queries * PAIR * length * 3 * HD,
            bytes_accessed=4 * length * width,
            transcendentals=queries * PAIR * length,
        ),
        name="partials",
    )(place, x, gain, frames, own_frames, got, keys, values, got, got)


def combine_kernel(block_ref, parts_ref, own_ref, out_ref):
    pairs = parts_ref.shape[0]
    tokens = own_ref.shape[0]
    held = parts_ref.shape[1] - STAT_ROWS
    stats = [parts_ref[p, held:].astype(jnp.float32) for p in range(pairs)]
    tops = [s[0:1] for s in stats]
    overall = functools.reduce(jnp.maximum, tops)
    factors = [jnp.exp2(top - overall) for top in tops]
    denominator = sum(f * (s[1:2] + s[2:3]) for f, s in zip(factors, stats))
    inverse = 1.0 / denominator
    diagonal = on_diagonal(held)
    total = head_rows(own_ref[...].astype(jnp.float32))
    for p in range(pairs):
        weight = jnp.sum(
            jnp.where(diagonal, factors[p] * inverse, 0.0), axis=1, keepdims=True
        )
        total = total + weight * parts_ref[p, :held].astype(jnp.float32)
    for h in range(held // tokens):
        piece = total[h * tokens : (h + 1) * tokens].astype(jnp.bfloat16)
        if len(out_ref.shape) == 3:
            for p in range(out_ref.shape[0]):
                out_ref[p, :, h * HD : (h + 1) * HD] = piece
        else:
            out_ref[:, h * HD : (h + 1) * HD] = piece


def combine(block, parts, own, copies):
    pairs, rows, _ = parts.shape
    tokens = own.shape[0]
    width = (rows - STAT_ROWS) // tokens * HD
    shape = (copies, tokens, width) if copies else (tokens, width)
    grid_spec = pltpu.PrefetchScalarGridSpec(
        num_scalar_prefetch=1,
        grid=(1,),
        in_specs=[
            pl.BlockSpec(parts.shape, lambda i, block: (0, 0, 0)),
            pl.BlockSpec((tokens, width), lambda i, block: (0, block[0])),
        ],
        out_specs=pl.BlockSpec(shape, lambda i, block: (0,) * len(shape)),
    )
    return pl.pallas_call(
        combine_kernel,
        grid_spec=grid_spec,
        out_shape=jax.ShapeDtypeStruct(shape, jnp.bfloat16),
        name="combine",
    )(block, parts, own)


def assemble_kernel(place_ref, mine_ref, other_ref, out_ref):
    pairs, _, width = mine_ref.shape
    half = pairs * width
    place = place_ref[0]
    for p in range(pairs):
        at = pl.multiple_of(place * half + p * width, width)
        out_ref[:, pl.ds(at, width)] = mine_ref[p]
        at = pl.multiple_of((1 - place) * half + p * width, width)
        out_ref[:, pl.ds(at, width)] = other_ref[p]


def assemble(place, mine, other):
    pairs, tokens, width = mine.shape
    return pl.pallas_call(
        assemble_kernel,
        in_specs=[
            pl.BlockSpec(memory_space=pltpu.SMEM),
            pl.BlockSpec(memory_space=pltpu.VMEM),
            pl.BlockSpec(memory_space=pltpu.VMEM),
        ],
        out_specs=pl.BlockSpec(memory_space=pltpu.VMEM),
        out_shape=jax.ShapeDtypeStruct((tokens, PAIR * pairs * width), jnp.bfloat16),
        name="assemble",
    )(place, mine, other)


def body(
    activations,
    act_frames,
    fresh_batch,
    fresh_frames,
    norm_gain,
    cached_keys,
    cached_values,
    key_frames,
):
    section_index = lax.axis_index("section")
    ctx_index = lax.axis_index("ctx")
    pairs = lax.axis_size("ctx") // PAIR
    keys, values = cached_keys[0], cached_values[0]
    length, width = keys.shape
    tokens, model = fresh_batch.shape
    share = model // lax.axis_size("ctx")
    place = (ctx_index % PAIR).astype(jnp.int32)
    block = place * pairs + ctx_index // PAIR
    places, blocks = place[None], block[None]

    half = width // PAIR
    away = (1 - place) * half
    frame_row = jnp.pad(key_frames.astype(jnp.bfloat16)[None], ((0, STAT_ROWS - 1), (0, width - length)))
    given = jnp.concatenate(
        [
            jnp.concatenate(
                [lax.dynamic_slice_in_dim(keys, away, half, 1), lax.dynamic_slice_in_dim(values, away, half, 1)],
                axis=1,
            ),
            frame_row,
        ],
        axis=0,
    )
    got = swapped(given)

    own_key_frames = key_frames.astype(jnp.float32)[None]

    def column(frames):
        return frames.astype(jnp.float32)[:, None]

    own_frames = lax.dynamic_index_in_dim(act_frames, section_index, 0, keepdims=False)
    prior_frames = lax.dynamic_index_in_dim(
        act_frames, jnp.maximum(section_index - 1, 0), 0, keepdims=False
    )
    frames_in = jnp.where(section_index == 0, fresh_frames, prior_frames)

    def run(x, frames):
        chunks = partials(
            places, x, norm_gain, column(frames), own_key_frames, keys, values, got, pairs
        )
        return exchanged(chunks)

    first = combine(blocks, run(activations[0], own_frames), activations[0], 0)
    handed = passed_along(first, "section", 1)
    fresh_share = lax.dynamic_slice_in_dim(fresh_batch, block * share, share, 1)
    own = jnp.where(section_index == 0, fresh_share, handed)
    incoming = exchanged(jnp.broadcast_to(own[None], (pairs, tokens, share)))
    second = combine(jnp.zeros_like(blocks), run(incoming, frames_in), own, pairs)
    mine = exchanged(second)
    return assemble(places, mine, swapped(mine))[None]


def solution(mesh):
    placed = (
        P("section", None, None),
        P(),
        P(),
        P(),
        P("section", None),
        P("section", "ctx", None),
        P("section", "ctx", None),
        P("ctx"),
    )
    return jax.shard_map(
        body, mesh=mesh, in_specs=placed, out_specs=P("section", None, None), check_vma=False
    )
```

```python
import functools
import math

import jax
import jax.numpy as jnp
from jax import lax
from jax.experimental import pallas as pl
from jax.experimental.pallas import tpu as pltpu
from jax.sharding import PartitionSpec as P

HEADS = 64
HD = 128
PAIR = 2
STAT_ROWS = 16
HIDDEN = -(2.0**100)
SCALE = HD**-0.5 * math.log2(math.e)

epsilon = 1e-05


def swapped(block):
    return lax.ppermute(block, "ctx", [(i, i ^ 1) for i in range(lax.axis_size("ctx"))])


def exchanged(chunks):
    size = lax.axis_size("ctx")
    groups = [list(range(place, size, PAIR)) for place in range(PAIR)]
    return lax.all_to_all(chunks, "ctx", 0, 0, axis_index_groups=groups, tiled=True)


def head_rows(block):
    return jnp.concatenate(
        [block[:, at : at + HD] for at in range(0, block.shape[1], HD)], axis=0
    )


def on_diagonal(rows):
    shape = (rows, HD)
    return lax.broadcasted_iota(jnp.int32, shape, 0) == lax.broadcasted_iota(jnp.int32, shape, 1)


def taken(place, ref, at, width):
    half = ref.shape[1] // PAIR
    return ref[:, pl.ds(pl.multiple_of(place * half + at, HD), width)]


def partial_kernel(
    where_ref, batch_ref, gain_ref, frames_ref, own_frames_ref, own_ref, got_ref, *rest
):
    *handed_refs, out_ref, x_ref = rest
    place, pair, first_section = where_ref[0], where_ref[1], where_ref[2]
    pairs, tokens, share = x_ref.shape
    keys, width = own_ref.shape
    kv_here = width // HD // 2
    chunks = pairs // kv_here
    held = out_ref.shape[1] - STAT_ROWS
    count = chunks * held

    for p in range(pairs):
        x_ref[p] = taken(place, batch_ref, p * share, share)
    if handed_refs:

        @pl.when(first_section == 0)
        def _():
            for step, handed_ref in enumerate(handed_refs):
                x_ref[(pair + pairs - step) % pairs] = handed_ref[...]

    frames = frames_ref[...]
    got_frames = got_ref[keys : keys + STAT_ROWS, :keys].astype(jnp.float32)[0:1]
    own_bias = jnp.where(own_frames_ref[...] <= frames, 0.0, HIDDEN)[None]
    got_bias = jnp.where(got_frames <= frames, 0.0, HIDDEN)[None]
    ones = jnp.ones((keys, HD), jnp.bfloat16)
    diagonal = on_diagonal(held)
    line = lax.broadcasted_iota(jnp.int32, (STAT_ROWS, HD), 0)

    for g in range(kv_here):
        x = jnp.concatenate([x_ref[g * chunks + c] for c in range(chunks)], axis=1)
        rows = head_rows(x.astype(jnp.float32))
        gain = taken(place, gain_ref, g * x.shape[1], x.shape[1])
        gain = head_rows(jnp.broadcast_to(gain, x.shape))
        norm = lax.rsqrt(jnp.mean(rows * rows, axis=-1, keepdims=True) + epsilon)
        queries = (rows * norm * gain).astype(jnp.bfloat16)

        def scores(ref, bias):
            raw = lax.dot_general(
                queries, ref[:keys, g * HD : (g + 1) * HD], (((1,), (1,)), ((), ())),
                preferred_element_type=jnp.float32,
            )
            raw = raw.reshape(count // tokens, tokens, keys) * SCALE + bias
            return raw.reshape(count, keys)

        first, second = scores(own_ref, own_bias), scores(got_ref, got_bias)
        top = jnp.maximum(
            jnp.max(first, axis=-1, keepdims=True), jnp.max(second, axis=-1, keepdims=True)
        )
        top = top.astype(jnp.bfloat16).astype(jnp.float32)

        def weigh(raw, ref):
            probs = jnp.exp2(raw - top).astype(jnp.bfloat16)
            block = ref[:keys, (kv_here + g) * HD : (kv_here + g + 1) * HD]
            return jnp.dot(
                probs, jnp.concatenate([block, ones], axis=1),
                preferred_element_type=jnp.float32,
            )

        both = weigh(first, own_ref) + weigh(second, got_ref)
        weighted, totals = both[:, :HD], both[:, HD:]
        tops = jnp.broadcast_to(top, weighted.shape)
        for c in range(chunks):
            part = slice(c * held, (c + 1) * held)
            top_row = jnp.sum(jnp.where(diagonal, tops[part], 0.0), axis=0, keepdims=True)
            total_row = jnp.sum(jnp.where(diagonal, totals[part], 0.0), axis=0, keepdims=True)
            high = total_row.astype(jnp.bfloat16).astype(jnp.float32)
            stats = jnp.where(
                line == 0, top_row,
                jnp.where(line == 1, high, jnp.where(line == 2, total_row - high, 0.0)),
            )
            out_ref[g * chunks + c, :held] = weighted[part].astype(jnp.bfloat16)
            out_ref[g * chunks + c, held:] = stats.astype(jnp.bfloat16)


SCALARS = pl.BlockSpec(memory_space=pltpu.SMEM)
WHOLE = pl.BlockSpec(memory_space=pltpu.VMEM)


def partials(where, batch, handed, gain, frames, own_frames, own, got, pairs):
    tokens = frames.shape[0]
    length, width = own.shape
    share = batch.shape[1] // (PAIR * pairs)
    held = share // HD * tokens
    queries = HEADS // PAIR * tokens
    return pl.pallas_call(
        partial_kernel,
        in_specs=[SCALARS] + [WHOLE] * (6 + len(handed)),
        out_specs=WHOLE,
        out_shape=jax.ShapeDtypeStruct((pairs, held + STAT_ROWS, HD), jnp.bfloat16),
        scratch_shapes=[pltpu.VMEM((pairs, tokens, share), jnp.bfloat16)],
        cost_estimate=pl.CostEstimate(
            flops=2 * queries * PAIR * length * 3 * HD,
            bytes_accessed=4 * length * width,
            transcendentals=queries * PAIR * length,
        ),
        compiler_params=pltpu.CompilerParams(vmem_limit_bytes=16 << 20),
        name="partials",
    )(where, batch, gain, frames, own_frames, own, got, *handed)


def combine_kernel(where_ref, parts_ref, batch_ref, *rest):
    *handed_refs, out_ref = rest
    place, pair, first_section = where_ref[0], where_ref[1], where_ref[2]
    pairs, rows, _ = parts_ref.shape
    tokens, share = out_ref.shape[-2:]
    held = rows - STAT_ROWS
    at = pl.multiple_of((place * pairs + pair) * share, share)
    own = batch_ref[:, pl.ds(at, share)].astype(jnp.float32)
    if handed_refs:
        own = jnp.where(first_section == 1, own, handed_refs[0][...].astype(jnp.float32))
    stats = [parts_ref[p, held:].astype(jnp.float32) for p in range(pairs)]
    tops = [s[0:1] for s in stats]
    overall = functools.reduce(jnp.maximum, tops)
    factors = [jnp.exp2(top - overall) for top in tops]
    denominator = sum(f * (s[1:2] + s[2:3]) for f, s in zip(factors, stats))
    inverse = 1.0 / denominator
    diagonal = on_diagonal(held)
    total = head_rows(own)
    for p in range(pairs):
        weight = jnp.where(diagonal, factors[p] * inverse, 0.0)
        high = weight.astype(jnp.bfloat16)
        low = (weight - high.astype(jnp.float32)).astype(jnp.bfloat16)
        for term in (high, low):
            total = total + jnp.dot(
                term[:, :rows], parts_ref[p], preferred_element_type=jnp.float32
            )
    for h in range(held // tokens):
        piece = total[h * tokens : (h + 1) * tokens].astype(jnp.bfloat16)
        if len(out_ref.shape) == 3:
            for p in range(out_ref.shape[0]):
                out_ref[p, :, h * HD : (h + 1) * HD] = piece
        else:
            out_ref[:, h * HD : (h + 1) * HD] = piece


def combine(where, parts, batch, handed, copies):
    pairs, rows, _ = parts.shape
    tokens = batch.shape[0]
    width = (rows - STAT_ROWS) // tokens * HD
    shape = (copies, tokens, width) if copies else (tokens, width)
    return pl.pallas_call(
        combine_kernel,
        in_specs=[SCALARS] + [WHOLE] * (2 + len(handed)),
        out_specs=WHOLE,
        out_shape=jax.ShapeDtypeStruct(shape, jnp.bfloat16),
        compiler_params=pltpu.CompilerParams(vmem_limit_bytes=8 << 20),
        name="combine",
    )(where, parts, batch, *handed)


def assemble_kernel(where_ref, mine_ref, other_ref, out_ref):
    pairs, _, width = mine_ref.shape
    half = pairs * width
    place = where_ref[0]
    for p in range(pairs):
        at = pl.multiple_of(place * half + p * width, width)
        out_ref[:, pl.ds(at, width)] = mine_ref[p]
        at = pl.multiple_of((1 - place) * half + p * width, width)
        out_ref[:, pl.ds(at, width)] = other_ref[p]


def assemble(where, mine, other):
    pairs, tokens, width = mine.shape
    return pl.pallas_call(
        assemble_kernel,
        in_specs=[SCALARS, WHOLE, WHOLE],
        out_specs=WHOLE,
        out_shape=jax.ShapeDtypeStruct((tokens, PAIR * pairs * width), jnp.bfloat16),
        compiler_params=pltpu.CompilerParams(vmem_limit_bytes=8 << 20),
        name="assemble",
    )(where, mine, other)


def handed_on(chunk):
    sections, size = lax.axis_size("section"), lax.axis_size("ctx")
    got = []
    for step in range(size // PAIR):
        route = [
            (s * size + i, (s + 1) * size + (i + PAIR * step) % size)
            for s in range(sections - 1)
            for i in range(size)
        ]
        got.append(lax.ppermute(chunk, ("section", "ctx"), route))
    return got


def body(
    activations,
    act_frames,
    fresh_batch,
    fresh_frames,
    norm_gain,
    cached_keys,
    cached_values,
    key_frames,
):
    section_index = lax.axis_index("section")
    ctx_index = lax.axis_index("ctx")
    pairs = lax.axis_size("ctx") // PAIR
    keys, values = cached_keys[0], cached_values[0]
    length, width = keys.shape
    place = ctx_index % PAIR
    where = jnp.stack([place, ctx_index // PAIR, section_index == 0]).astype(jnp.int32)

    half = width // PAIR

    def halves(at):
        return [lax.dynamic_slice_in_dim(a, at * half, half, 1) for a in (keys, values)]

    frame_row = jnp.pad(
        key_frames.astype(jnp.bfloat16)[None], ((0, STAT_ROWS - 1), (0, width - length))
    )
    got = swapped(
        jnp.concatenate([jnp.concatenate(halves(1 - place), axis=1), frame_row], axis=0)
    )
    own = jnp.concatenate(halves(place), axis=1)
    own_key_frames = key_frames.astype(jnp.float32)[None]

    def column(frames):
        return frames.astype(jnp.float32)[:, None]

    own_frames = lax.dynamic_index_in_dim(act_frames, section_index, 0, keepdims=False)
    prior_frames = lax.dynamic_index_in_dim(
        act_frames, jnp.maximum(section_index - 1, 0), 0, keepdims=False
    )
    frames_in = jnp.where(section_index == 0, fresh_frames, prior_frames)

    def layer(batch, handed, frames, copies):
        chunks = partials(
            where, batch, handed, norm_gain, column(frames), own_key_frames, own, got, pairs
        )
        return combine(where, exchanged(chunks), batch, handed[:1], copies)

    first = layer(activations[0], [], own_frames, 0)
    second = layer(fresh_batch, handed_on(first), frames_in, pairs)
    mine = exchanged(second)
    return assemble(where, mine, swapped(mine))[None]


def solution(mesh):
    placed = (
        P("section", None, None),
        P(),
        P(),
        P(),
        P("section", None),
        P("section", "ctx", None),
        P("section", "ctx", None),
        P("ctx"),
    )
    return jax.shard_map(
        body, mesh=mesh, in_specs=placed, out_specs=P("section", None, None), check_vma=False
    )
```

```python
import functools
import math

import jax
import jax.numpy as jnp
from jax import lax
from jax.experimental import pallas as pl
from jax.experimental.pallas import tpu as pltpu
from jax.sharding import PartitionSpec as P

HEADS = 64
HD = 128
PAIR = 2
INNER = 2
STAT_ROWS = 16
HIDDEN = -(2.0**100)
SCALE = HD**-0.5 * math.log2(math.e)

epsilon = 1e-05


def swapped(block):
    return lax.ppermute(block, "ctx", [(i, i ^ 1) for i in range(lax.axis_size("ctx"))])


def exchanged(chunks):
    size = lax.axis_size("ctx")
    groups = [list(range(place, size, PAIR)) for place in range(PAIR)]
    return lax.all_to_all(chunks, "ctx", 0, 0, axis_index_groups=groups, tiled=True)


def head_rows(block):
    return jnp.concatenate(
        [block[:, at : at + HD] for at in range(0, block.shape[1], HD)], axis=0
    )


def on_diagonal(rows):
    shape = (rows, HD)
    return lax.broadcasted_iota(jnp.int32, shape, 0) == lax.broadcasted_iota(jnp.int32, shape, 1)


SCALARS = pl.BlockSpec(memory_space=pltpu.SMEM)
WHOLE = pl.BlockSpec(memory_space=pltpu.VMEM)
IN_HBM = pl.BlockSpec(memory_space=pltpu.HBM)
MIB = 1 << 20


def queries_of(x, gain):
    rows = head_rows(x.astype(jnp.float32))
    gain = head_rows(jnp.broadcast_to(gain, x.shape))
    norm = lax.rsqrt(jnp.mean(rows * rows, axis=-1, keepdims=True) + epsilon)
    return (rows * norm * gain).astype(jnp.bfloat16)


def gain_of(place, gain_ref, g, width):
    half = gain_ref.shape[1] // PAIR
    return gain_ref[:, pl.ds(pl.multiple_of(place * half + g * width, HD), width)]


def bias_of(key_frames, frames):
    return jnp.where(key_frames.astype(jnp.float32) <= frames, 0.0, HIDDEN)[None]


def scores(queries, key_block, bias):
    count, keys, tokens = queries.shape[0], key_block.shape[0], bias.shape[1]
    raw = lax.dot_general(
        queries, key_block, (((1,), (1,)), ((), ())), preferred_element_type=jnp.float32
    )
    raw = raw.reshape(count // tokens, tokens, keys) * SCALE + bias
    return raw.reshape(count, keys)


def top_of(raw):
    top = jnp.max(raw, axis=-1, keepdims=True)
    return top.astype(jnp.bfloat16).astype(jnp.float32)


def weigh(raw, top, value_block):
    probs = jnp.exp2(raw - top).astype(jnp.bfloat16)
    ones = jnp.ones((value_block.shape[0], HD), jnp.bfloat16)
    return jnp.dot(
        probs, jnp.concatenate([value_block, ones], axis=1), preferred_element_type=jnp.float32
    )


def own_copies(place, keys_ref, values_ref, own_ref, sems):
    half = keys_ref.shape[1] // PAIR
    copies = []
    for g in range(half // HD):
        both = []
        for n, ref in enumerate((keys_ref, values_ref)):
            source = ref.at[:, pl.ds(pl.multiple_of(place * half + g * HD, HD), HD)]
            target = own_ref.at[:, pl.ds(n * half + g * HD, HD)]
            both.append(pltpu.make_async_copy(source, target, sems.at[n, g]))
        copies.append(both)
    return copies


def write_chunks(out_ref, g, tops, both):
    held = out_ref.shape[1] - STAT_ROWS
    chunks = both.shape[0] // held
    diagonal = on_diagonal(held)
    line = lax.broadcasted_iota(jnp.int32, (STAT_ROWS, HD), 0)
    for c in range(chunks):
        part = both[c * held : (c + 1) * held]
        top = tops[c * held : (c + 1) * held]
        top_row = jnp.sum(jnp.where(diagonal, top, 0.0), axis=0, keepdims=True)
        total_row = jnp.sum(jnp.where(diagonal, part[:, HD:], 0.0), axis=0, keepdims=True)
        high = total_row.astype(jnp.bfloat16).astype(jnp.float32)
        stats = jnp.where(
            line == 0, top_row,
            jnp.where(line == 1, high, jnp.where(line == 2, total_row - high, 0.0)),
        )
        out_ref[g * chunks + c, :held] = part[:, :HD].astype(jnp.bfloat16)
        out_ref[g * chunks + c, held:] = stats.astype(jnp.bfloat16)


def got_frames_of(got_ref, keys):
    return got_ref[keys : keys + STAT_ROWS, :keys].astype(jnp.float32)[0:1]


def begin_kernel(
    where_ref, gain_ref, frames_ref, key_frames_ref, batch_in, fresh_in, keys_ref, values_ref,
    queries_ref, tops_ref, sums_ref, batch_ref, fresh_ref, own_ref, sems, batch_sems,
):
    place = where_ref[0]
    half = batch_ref.shape[1]
    kv_here = own_ref.shape[1] // HD // 2
    count, width = queries_ref.shape[0] // kv_here, half // kv_here
    batches = [
        pltpu.make_async_copy(
            ref.at[:, pl.ds(pl.multiple_of(place * half, half), half)], target, batch_sems.at[n]
        )
        for n, (ref, target) in enumerate(((batch_in, batch_ref), (fresh_in, fresh_ref)))
    ]
    copies = own_copies(place, keys_ref, values_ref, own_ref, sems)
    batches[0].start()
    for both in copies:
        for copy in both:
            copy.start()
    batches[1].start()
    bias = bias_of(key_frames_ref[...], frames_ref[...])
    batches[0].wait()
    for g in range(kv_here):
        rows = slice(g * count, (g + 1) * count)
        x = batch_ref[:, g * width : (g + 1) * width]
        queries = queries_of(x, gain_of(place, gain_ref, g, width))
        queries_ref[rows] = queries
        copies[g][0].wait()
        raw = scores(queries, own_ref[:, g * HD : (g + 1) * HD], bias)
        top = top_of(raw)
        tops_ref[rows] = jnp.broadcast_to(top, (count, HD))
        copies[g][1].wait()
        sums_ref[rows] = weigh(raw, top, own_ref[:, (kv_here + g) * HD : (kv_here + g + 1) * HD])
    batches[1].wait()


def begin(where, gain, frames, key_frames, batch, fresh, keys, values):
    length, width = keys.shape
    tokens, model = batch.shape
    queries = HEADS // PAIR * tokens
    kv_here = width // HD // PAIR
    half = jax.ShapeDtypeStruct((tokens, model // PAIR), batch.dtype)
    return pl.pallas_call(
        begin_kernel,
        in_specs=[SCALARS] + [WHOLE] * 3 + [IN_HBM] * 4,
        out_specs=[WHOLE] * 5,
        out_shape=[
            jax.ShapeDtypeStruct((queries, HD), jnp.bfloat16),
            jax.ShapeDtypeStruct((queries, HD), jnp.float32),
            jax.ShapeDtypeStruct((queries, 2 * HD), jnp.float32),
            half,
            half,
        ],
        scratch_shapes=[
            pltpu.VMEM((length, width), keys.dtype),
            pltpu.SemaphoreType.DMA((2, kv_here)),
            pltpu.SemaphoreType.DMA((2,)),
        ],
        cost_estimate=pl.CostEstimate(
            flops=2 * queries * length * 3 * HD,
            bytes_accessed=2 * length * width,
            transcendentals=queries * length,
        ),
        compiler_params=pltpu.CompilerParams(vmem_limit_bytes=51 * MIB),
        name="begin",
    )(where, gain, frames, key_frames, batch, fresh, keys, values)


def finish_kernel(frames_ref, queries_ref, tops_ref, sums_ref, got_ref, out_ref):
    kv_here = got_ref.shape[1] // HD // 2
    keys = got_ref.shape[0] - STAT_ROWS
    count = queries_ref.shape[0] // kv_here
    bias = bias_of(got_frames_of(got_ref, keys), frames_ref[...])
    for g in range(kv_here):
        rows = slice(g * count, (g + 1) * count)
        raw = scores(queries_ref[rows], got_ref[:keys, g * HD : (g + 1) * HD], bias)
        before = tops_ref[rows]
        tops = jnp.maximum(before, top_of(raw))
        factor = jnp.exp2(before - tops)
        sums = weigh(
            raw, tops[:, :1], got_ref[:keys, (kv_here + g) * HD : (kv_here + g + 1) * HD]
        )
        sums = sums + sums_ref[rows] * jnp.concatenate([factor, factor], axis=1)
        write_chunks(out_ref, g, tops, sums)


def finish(frames, queries, tops, sums, got, pairs):
    count = queries.shape[0]
    length, width = got.shape
    return pl.pallas_call(
        finish_kernel,
        in_specs=[WHOLE] * 5,
        out_specs=WHOLE,
        out_shape=jax.ShapeDtypeStruct((pairs, count // pairs + STAT_ROWS, HD), jnp.bfloat16),
        cost_estimate=pl.CostEstimate(
            flops=2 * count * length * 3 * HD,
            bytes_accessed=2 * length * width,
            transcendentals=count * length,
        ),
        compiler_params=pltpu.CompilerParams(vmem_limit_bytes=16 * MIB),
        name="finish",
    )(frames, queries, tops, sums, got)


def partials_kernel(
    where_ref, gain_ref, frames_ref, key_frames_ref, batch_ref, got_ref, keys_ref, values_ref,
    *rest,
):
    *handed_refs, out_ref, x_ref, own_ref, sems = rest
    place, pair, first_section = where_ref[0], where_ref[1], where_ref[2]
    copies = own_copies(place, keys_ref, values_ref, own_ref, sems)
    for both in copies:
        for copy in both:
            copy.start()
    pairs, outer = out_ref.shape[0], len(handed_refs)
    keys, width = own_ref.shape
    kv_here = width // HD // 2
    share = x_ref.shape[1] // pairs
    columns = x_ref.shape[1] // kv_here

    x_ref[...] = batch_ref[...]

    @pl.when(first_section == 0)
    def _():
        for step, handed_ref in enumerate(handed_refs):
            base = (pair // INNER + outer - step) % outer * INNER
            for e in range(INNER):
                at = pl.multiple_of((base + (pair + e) % INNER) * share, share)
                x_ref[:, pl.ds(at, share)] = handed_ref[e]

    own_bias = bias_of(key_frames_ref[...], frames_ref[...])
    got_bias = bias_of(got_frames_of(got_ref, keys), frames_ref[...])
    for g in range(kv_here):
        queries = queries_of(
            x_ref[:, g * columns : (g + 1) * columns], gain_of(place, gain_ref, g, columns)
        )
        of_keys = slice(g * HD, (g + 1) * HD)
        of_values = slice((kv_here + g) * HD, (kv_here + g + 1) * HD)
        got_raw = scores(queries, got_ref[:keys, of_keys], got_bias)
        copies[g][0].wait()
        own_raw = scores(queries, own_ref[:, of_keys], own_bias)
        top = jnp.maximum(top_of(got_raw), top_of(own_raw))
        sums = weigh(got_raw, top, got_ref[:keys, of_values])
        copies[g][1].wait()
        sums = sums + weigh(own_raw, top, own_ref[:, of_values])
        write_chunks(out_ref, g, jnp.broadcast_to(top, (sums.shape[0], HD)), sums)


def partials(where, gain, frames, key_frames, batch, got, keys, values, handed, pairs):
    length, width = keys.shape
    tokens, half = batch.shape
    queries = HEADS // PAIR * tokens
    kv_here = width // HD // PAIR
    return pl.pallas_call(
        partials_kernel,
        in_specs=[SCALARS] + [WHOLE] * 5 + [IN_HBM] * 2 + [WHOLE] * len(handed),
        out_specs=WHOLE,
        out_shape=jax.ShapeDtypeStruct((pairs, queries // pairs + STAT_ROWS, HD), jnp.bfloat16),
        scratch_shapes=[
            pltpu.VMEM((tokens, half), batch.dtype),
            pltpu.VMEM((length, width), keys.dtype),
            pltpu.SemaphoreType.DMA((2, kv_here)),
        ],
        cost_estimate=pl.CostEstimate(
            flops=2 * queries * PAIR * length * 3 * HD,
            bytes_accessed=4 * length * width,
            transcendentals=queries * PAIR * length,
        ),
        compiler_params=pltpu.CompilerParams(vmem_limit_bytes=51 * MIB),
        name="partials",
    )(where, gain, frames, key_frames, batch, got, keys, values, *handed)


def combine_kernel(where_ref, parts_ref, batch_ref, *rest):
    *handed_refs, out_ref = rest
    pair, first_section = where_ref[1], where_ref[2]
    pairs, rows, _ = parts_ref.shape
    tokens, share = out_ref.shape[-2:]
    held = rows - STAT_ROWS
    own = batch_ref[:, pl.ds(pl.multiple_of(pair * share, share), share)].astype(jnp.float32)
    if handed_refs:
        own = jnp.where(first_section == 1, own, handed_refs[0][0].astype(jnp.float32))
    stats = [parts_ref[p, held:].astype(jnp.float32) for p in range(pairs)]
    tops = [s[0:1] for s in stats]
    overall = functools.reduce(jnp.maximum, tops)
    factors = [jnp.exp2(top - overall) for top in tops]
    denominator = sum(f * (s[1:2] + s[2:3]) for f, s in zip(factors, stats))
    inverse = 1.0 / denominator
    diagonal = on_diagonal(held)
    total = head_rows(own)
    for p in range(pairs):
        weight = jnp.where(diagonal, factors[p] * inverse, 0.0)
        high = weight.astype(jnp.bfloat16)
        low = (weight - high.astype(jnp.float32)).astype(jnp.bfloat16)
        for term in (high, low):
            total = total + jnp.dot(
                term[:, :rows], parts_ref[p], preferred_element_type=jnp.float32
            )
    for h in range(held // tokens):
        piece = total[h * tokens : (h + 1) * tokens].astype(jnp.bfloat16)
        if len(out_ref.shape) == 3:
            for p in range(out_ref.shape[0]):
                out_ref[p, :, h * HD : (h + 1) * HD] = piece
        else:
            out_ref[:, h * HD : (h + 1) * HD] = piece


def combine(where, parts, batch, handed, copies):
    pairs, rows, _ = parts.shape
    tokens = batch.shape[0]
    width = (rows - STAT_ROWS) // tokens * HD
    shape = (copies, tokens, width) if copies else (tokens, width)
    return pl.pallas_call(
        combine_kernel,
        in_specs=[SCALARS] + [WHOLE] * (2 + len(handed)),
        out_specs=WHOLE,
        out_shape=jax.ShapeDtypeStruct(shape, jnp.bfloat16),
        compiler_params=pltpu.CompilerParams(vmem_limit_bytes=8 * MIB),
        name="combine",
    )(where, parts, batch, *handed)


def assemble_kernel(where_ref, mine_ref, other_ref, out_ref):
    pairs, _, width = mine_ref.shape
    half = pairs * width
    place = where_ref[0]
    for p in range(pairs):
        at = pl.multiple_of(place * half + p * width, width)
        out_ref[:, pl.ds(at, width)] = mine_ref[p]
        at = pl.multiple_of((1 - place) * half + p * width, width)
        out_ref[:, pl.ds(at, width)] = other_ref[p]


def assemble(where, mine, other):
    pairs, tokens, width = mine.shape
    return pl.pallas_call(
        assemble_kernel,
        in_specs=[SCALARS, WHOLE, WHOLE],
        out_specs=WHOLE,
        out_shape=jax.ShapeDtypeStruct((tokens, PAIR * pairs * width), jnp.bfloat16),
        compiler_params=pltpu.CompilerParams(vmem_limit_bytes=8 * MIB),
        name="assemble",
    )(where, mine, other)


def handed_on(chunk):
    sections, size = lax.axis_size("section"), lax.axis_size("ctx")
    block = INNER * PAIR
    near = []
    for e in range(INNER):
        route = [
            (s * size + i, (s + 1) * size + i // block * block + (i + PAIR * e) % block)
            for s in range(sections - 1)
            for i in range(size)
        ]
        near.append(lax.ppermute(chunk, ("section", "ctx"), route))
    near = jnp.stack(near)
    far = [
        lax.ppermute(near, "ctx", [(i, (i + block * step) % size) for i in range(size)])
        for step in range(1, size // block)
    ]
    return [near] + far


def halves_copied(at, sources, target_ref, sems):
    copies = []
    for n, ref in enumerate(sources):
        length, half = ref.shape[0], ref.shape[1] // PAIR
        copies.append(
            pltpu.make_async_copy(
                ref.at[:, pl.ds(pl.multiple_of(at * half, half), half)],
                target_ref.at[pl.ds(0, length), pl.ds(n * half, half)],
                sems.at[n],
            )
        )
    for copy in copies:
        copy.start()
    return copies


def give_kernel(where_ref, frames_ref, keys_ref, values_ref, out_ref, sems):
    copies = halves_copied(1 - where_ref[0], (keys_ref, values_ref), out_ref, sems)
    length = keys_ref.shape[0]
    shape = (STAT_ROWS, length)
    frames = jnp.broadcast_to(frames_ref[...].astype(jnp.float32), shape)
    line = lax.broadcasted_iota(jnp.int32, shape, 0)
    tail = jnp.where(line == 0, frames, 0.0).astype(jnp.bfloat16)
    out_ref[length : length + STAT_ROWS, :length] = tail
    out_ref[length : length + STAT_ROWS, length:] = jnp.zeros(
        (STAT_ROWS, out_ref.shape[1] - length), jnp.bfloat16
    )
    for copy in copies:
        copy.wait()


def give(where, frames, keys, values):
    length, width = keys.shape
    return pl.pallas_call(
        give_kernel,
        in_specs=[SCALARS, WHOLE, IN_HBM, IN_HBM],
        out_specs=WHOLE,
        out_shape=jax.ShapeDtypeStruct((length + STAT_ROWS, width), keys.dtype),
        scratch_shapes=[pltpu.SemaphoreType.DMA((2,))],
        cost_estimate=pl.CostEstimate(
            flops=0, bytes_accessed=2 * length * width * 2, transcendentals=0
        ),
        compiler_params=pltpu.CompilerParams(vmem_limit_bytes=62 * MIB),
        name="give",
    )(where, frames, keys, values)


def body(
    activations,
    act_frames,
    fresh_batch,
    fresh_frames,
    norm_gain,
    cached_keys,
    cached_values,
    key_frames,
):
    section_index = lax.axis_index("section")
    ctx_index = lax.axis_index("ctx")
    pairs = lax.axis_size("ctx") // PAIR
    keys, values = cached_keys[0], cached_values[0]
    place = ctx_index % PAIR
    where = jnp.stack([place, ctx_index // PAIR, section_index == 0]).astype(jnp.int32)
    key_frames = key_frames[None]

    got = swapped(give(where, key_frames, keys, values))

    def column(frames):
        return frames.astype(jnp.float32)[:, None]

    own_frames = lax.dynamic_index_in_dim(act_frames, section_index, 0, keepdims=False)
    prior_frames = lax.dynamic_index_in_dim(
        act_frames, jnp.maximum(section_index - 1, 0), 0, keepdims=False
    )
    frames_in = jnp.where(section_index == 0, fresh_frames, prior_frames)

    frames, frames_in = column(own_frames), column(frames_in)
    *terms, batch, fresh = begin(
        where, norm_gain, frames, key_frames, activations[0], fresh_batch, keys, values
    )
    chunks = exchanged(finish(frames, *terms, got, pairs))
    handed = handed_on(combine(where, chunks, batch, [], 0))
    chunks = exchanged(
        partials(where, norm_gain, frames_in, key_frames, fresh, got, keys, values, handed, pairs)
    )
    mine = exchanged(combine(where, chunks, fresh, handed[:1], pairs))
    return assemble(where, mine, swapped(mine))[None]


def solution(mesh):
    placed = (
        P("section", None, None),
        P(),
        P(),
        P(),
        P("section", None),
        P("section", "ctx", None),
        P("section", "ctx", None),
        P("ctx"),
    )
    return jax.shard_map(
        body, mesh=mesh, in_specs=placed, out_specs=P("section", None, None), check_vma=False
    )
```

```python
import functools
import math

import jax
import jax.numpy as jnp
from jax import lax
from jax.experimental import pallas as pl
from jax.experimental.pallas import tpu as pltpu
from jax.sharding import PartitionSpec as P

HEADS = 64
HD = 128
PAIR = 2
INNER = 2
STAT_ROWS = 16
HIDDEN = -(2.0**100)
SCALE = HD**-0.5 * math.log2(math.e)

epsilon = 1e-05


def swapped(block):
    return lax.ppermute(block, "ctx", [(i, i ^ 1) for i in range(lax.axis_size("ctx"))])


def exchanged(chunks):
    size = lax.axis_size("ctx")
    groups = [list(range(place, size, PAIR)) for place in range(PAIR)]
    return lax.all_to_all(chunks, "ctx", 0, 0, axis_index_groups=groups, tiled=True)


def head_rows(block):
    return jnp.concatenate(
        [block[:, at : at + HD] for at in range(0, block.shape[1], HD)], axis=0
    )


def on_diagonal(rows):
    shape = (rows, HD)
    return lax.broadcasted_iota(jnp.int32, shape, 0) == lax.broadcasted_iota(jnp.int32, shape, 1)


SCALARS = pl.BlockSpec(memory_space=pltpu.SMEM)
WHOLE = pl.BlockSpec(memory_space=pltpu.VMEM)
IN_HBM = pl.BlockSpec(memory_space=pltpu.HBM)
MIB = 1 << 20
LOAD_VMEM = 16 * MIB
BLOCKS = 4


def in_hbm(*arrays):
    return [pltpu.with_memory_space_constraint(a, pltpu.HBM) for a in arrays]


def in_vmem(*arrays):
    return [pltpu.with_memory_space_constraint(a, pltpu.VMEM) for a in arrays]


def queries_of(x, gain):
    rows = head_rows(x.astype(jnp.float32))
    gain = head_rows(jnp.broadcast_to(gain, x.shape))
    norm = lax.rsqrt(jnp.mean(rows * rows, axis=-1, keepdims=True) + epsilon)
    return (rows * norm * gain).astype(jnp.bfloat16)


def gain_of(place, gain_ref, g, width):
    half = gain_ref.shape[1] // PAIR
    return gain_ref[:, pl.ds(pl.multiple_of(place * half + g * width, HD), width)]


def bias_of(key_frames, frames):
    return jnp.where(key_frames.astype(jnp.float32) <= frames, 0.0, HIDDEN)[None]


def scores(queries, key_block, bias):
    count, keys, tokens = queries.shape[0], key_block.shape[0], bias.shape[1]
    raw = lax.dot_general(
        queries, key_block, (((1,), (1,)), ((), ())), preferred_element_type=jnp.float32
    )
    raw = raw.reshape(count // tokens, tokens, keys) * SCALE + bias
    return raw.reshape(count, keys)


def top_of(raw):
    top = jnp.max(raw, axis=-1, keepdims=True)
    return top.astype(jnp.bfloat16).astype(jnp.float32)


def weigh(raw, top, value_block):
    probs = jnp.exp2(raw - top).astype(jnp.bfloat16)
    ones = jnp.ones((value_block.shape[0], HD), jnp.bfloat16)
    return jnp.dot(
        probs, jnp.concatenate([value_block, ones], axis=1), preferred_element_type=jnp.float32
    )


def own_block(place, ref, g):
    half = ref.shape[1] // PAIR
    return ref[:, pl.ds(pl.multiple_of(place * half + g * HD, HD), HD)]


def write_chunks(out_ref, g, tops, both):
    held = out_ref.shape[1] - STAT_ROWS
    chunks = both.shape[0] // held
    diagonal = on_diagonal(held)
    line = lax.broadcasted_iota(jnp.int32, (STAT_ROWS, HD), 0)
    for c in range(chunks):
        part = both[c * held : (c + 1) * held]
        top = tops[c * held : (c + 1) * held]
        top_row = jnp.sum(jnp.where(diagonal, top, 0.0), axis=0, keepdims=True)
        total_row = jnp.sum(jnp.where(diagonal, part[:, HD:], 0.0), axis=0, keepdims=True)
        high = total_row.astype(jnp.bfloat16).astype(jnp.float32)
        stats = jnp.where(
            line == 0, top_row,
            jnp.where(line == 1, high, jnp.where(line == 2, total_row - high, 0.0)),
        )
        out_ref[g * chunks + c, :held] = part[:, :HD].astype(jnp.bfloat16)
        out_ref[g * chunks + c, held:] = stats.astype(jnp.bfloat16)


def row_of(ref):
    return jnp.concatenate([ref[i : i + 1] for i in range(ref.shape[0])], axis=1)


def got_frames_of(got_ref, keys):
    return got_ref[keys : keys + STAT_ROWS, :keys].astype(jnp.float32)[0:1]


def begin_kernel(
    where_ref, gain_ref, frames_ref, key_frames_ref, batches_ref, held_ref,
    queries_ref, tops_ref, sums_ref,
):
    place = where_ref[0]
    batch_ref = batches_ref.at[0]
    kv_here = held_ref.shape[2] // HD // PAIR
    count, width = queries_ref.shape[0] // kv_here, batch_ref.shape[1] // kv_here
    bias = bias_of(row_of(key_frames_ref), frames_ref[...])
    for g in range(kv_here):
        rows = slice(g * count, (g + 1) * count)
        x = batch_ref[:, g * width : (g + 1) * width]
        queries = queries_of(x, gain_of(place, gain_ref, g, width))
        queries_ref[rows] = queries
        raw = scores(queries, own_block(place, held_ref.at[0], g), bias)
        top = top_of(raw)
        tops_ref[rows] = jnp.broadcast_to(top, (count, HD))
        sums_ref[rows] = weigh(raw, top, own_block(place, held_ref.at[1], g))


def begin(where, gain, frames, key_frames, batches, held):
    _, length, width = held.shape
    queries = HEADS // PAIR * frames.shape[0]
    return pl.pallas_call(
        begin_kernel,
        in_specs=[SCALARS] + [WHOLE] * 5,
        out_specs=[WHOLE] * 3,
        out_shape=[
            jax.ShapeDtypeStruct((queries, HD), jnp.bfloat16),
            jax.ShapeDtypeStruct((queries, HD), jnp.float32),
            jax.ShapeDtypeStruct((queries, 2 * HD), jnp.float32),
        ],
        cost_estimate=pl.CostEstimate(
            flops=2 * queries * length * 3 * HD,
            bytes_accessed=2 * length * width,
            transcendentals=queries * length,
        ),
        compiler_params=pltpu.CompilerParams(vmem_limit_bytes=16 * MIB),
        name="begin",
    )(where, gain, frames, key_frames, *in_vmem(batches, held))


def finish_kernel(frames_ref, queries_ref, tops_ref, sums_ref, got_ref, out_ref):
    kv_here = got_ref.shape[1] // HD // 2
    keys = got_ref.shape[0] - STAT_ROWS
    count = queries_ref.shape[0] // kv_here
    bias = bias_of(got_frames_of(got_ref, keys), frames_ref[...])
    for g in range(kv_here):
        rows = slice(g * count, (g + 1) * count)
        raw = scores(queries_ref[rows], got_ref[:keys, g * HD : (g + 1) * HD], bias)
        before = tops_ref[rows]
        tops = jnp.maximum(before, top_of(raw))
        factor = jnp.exp2(before - tops)
        sums = weigh(
            raw, tops[:, :1], got_ref[:keys, (kv_here + g) * HD : (kv_here + g + 1) * HD]
        )
        sums = sums + sums_ref[rows] * jnp.concatenate([factor, factor], axis=1)
        write_chunks(out_ref, g, tops, sums)


def finish(frames, queries, tops, sums, got, pairs):
    count = queries.shape[0]
    length, width = got.shape
    return pl.pallas_call(
        finish_kernel,
        in_specs=[WHOLE] * 5,
        out_specs=WHOLE,
        out_shape=jax.ShapeDtypeStruct((pairs, count // pairs + STAT_ROWS, HD), jnp.bfloat16),
        cost_estimate=pl.CostEstimate(
            flops=2 * count * length * 3 * HD,
            bytes_accessed=2 * length * width,
            transcendentals=count * length,
        ),
        compiler_params=pltpu.CompilerParams(vmem_limit_bytes=16 * MIB),
        name="finish",
    )(frames, queries, tops, sums, *in_vmem(got))


def partials_kernel(
    where_ref, gain_ref, frames_ref, key_frames_ref, batches_ref, got_ref, held_ref, *rest
):
    *handed_refs, out_ref, x_ref = rest
    place, pair, first_section = where_ref[0], where_ref[1], where_ref[2]
    pairs, outer = out_ref.shape[0], len(handed_refs)
    _, keys, width = held_ref.shape
    kv_here = width // HD // PAIR
    share = x_ref.shape[1] // pairs
    columns = x_ref.shape[1] // kv_here

    x_ref[...] = batches_ref[1]

    @pl.when(first_section == 0)
    def _():
        for step, handed_ref in enumerate(handed_refs):
            base = (pair // INNER + outer - step) % outer * INNER
            for e in range(INNER):
                at = pl.multiple_of((base + (pair + e) % INNER) * share, share)
                x_ref[:, pl.ds(at, share)] = handed_ref[e]

    own_bias = bias_of(row_of(key_frames_ref), frames_ref[...])
    got_bias = bias_of(got_frames_of(got_ref, keys), frames_ref[...])
    for g in range(kv_here):
        queries = queries_of(
            x_ref[:, g * columns : (g + 1) * columns], gain_of(place, gain_ref, g, columns)
        )
        of_keys = slice(g * HD, (g + 1) * HD)
        of_values = slice((kv_here + g) * HD, (kv_here + g + 1) * HD)
        got_raw = scores(queries, got_ref[:keys, of_keys], got_bias)
        own_raw = scores(queries, own_block(place, held_ref.at[0], g), own_bias)
        top = jnp.maximum(top_of(got_raw), top_of(own_raw))
        sums = weigh(got_raw, top, got_ref[:keys, of_values])
        sums = sums + weigh(own_raw, top, own_block(place, held_ref.at[1], g))
        write_chunks(out_ref, g, jnp.broadcast_to(top, (sums.shape[0], HD)), sums)


def partials(where, gain, frames, key_frames, batches, got, held, handed, pairs):
    _, length, width = held.shape
    _, tokens, half = batches.shape
    queries = HEADS // PAIR * tokens
    return pl.pallas_call(
        partials_kernel,
        in_specs=[SCALARS] + [WHOLE] * (6 + len(handed)),
        out_specs=WHOLE,
        out_shape=jax.ShapeDtypeStruct((pairs, queries // pairs + STAT_ROWS, HD), jnp.bfloat16),
        scratch_shapes=[pltpu.VMEM((tokens, half), batches.dtype)],
        cost_estimate=pl.CostEstimate(
            flops=2 * queries * PAIR * length * 3 * HD,
            bytes_accessed=4 * length * width,
            transcendentals=queries * PAIR * length,
        ),
        compiler_params=pltpu.CompilerParams(vmem_limit_bytes=16 * MIB),
        name="partials",
    )(where, gain, frames, key_frames, *in_vmem(batches, got, held), *handed)


def combine_kernel(where_ref, parts_ref, batches_ref, *rest):
    *handed_refs, out_ref = rest
    pair, first_section = where_ref[1], where_ref[2]
    pairs, rows, _ = parts_ref.shape
    tokens, share = out_ref.shape[-2:]
    held = rows - STAT_ROWS
    tick = 1 if handed_refs else 0
    columns = pl.ds(pl.multiple_of(pair * share, share), share)
    own = batches_ref[tick, :, columns].astype(jnp.float32)
    if handed_refs:
        own = jnp.where(first_section == 1, own, handed_refs[0][0].astype(jnp.float32))
    stats = [parts_ref[p, held:].astype(jnp.float32) for p in range(pairs)]
    tops = [s[0:1] for s in stats]
    overall = functools.reduce(jnp.maximum, tops)
    factors = [jnp.exp2(top - overall) for top in tops]
    denominator = sum(f * (s[1:2] + s[2:3]) for f, s in zip(factors, stats))
    inverse = 1.0 / denominator
    diagonal = on_diagonal(held)
    total = head_rows(own)
    for p in range(pairs):
        weight = jnp.where(diagonal, factors[p] * inverse, 0.0)
        high = weight.astype(jnp.bfloat16)
        low = (weight - high.astype(jnp.float32)).astype(jnp.bfloat16)
        for term in (high, low):
            total = total + jnp.dot(
                term[:, :rows], parts_ref[p], preferred_element_type=jnp.float32
            )
    for h in range(held // tokens):
        piece = total[h * tokens : (h + 1) * tokens].astype(jnp.bfloat16)
        if len(out_ref.shape) == 3:
            for p in range(out_ref.shape[0]):
                out_ref[p, :, h * HD : (h + 1) * HD] = piece
        else:
            out_ref[:, h * HD : (h + 1) * HD] = piece


def combine(where, parts, batches, handed, copies):
    pairs, rows, _ = parts.shape
    tokens = batches.shape[1]
    width = (rows - STAT_ROWS) // tokens * HD
    shape = (copies, tokens, width) if copies else (tokens, width)
    return pl.pallas_call(
        combine_kernel,
        in_specs=[SCALARS] + [WHOLE] * (2 + len(handed)),
        out_specs=WHOLE,
        out_shape=jax.ShapeDtypeStruct(shape, jnp.bfloat16),
        compiler_params=pltpu.CompilerParams(vmem_limit_bytes=8 * MIB),
        name="combine",
    )(where, parts, batches, *handed)


def assemble_kernel(where_ref, mine_ref, other_ref, out_ref):
    pairs, _, width = mine_ref.shape
    half = pairs * width
    place = where_ref[0]
    for p in range(pairs):
        at = pl.multiple_of(place * half + p * width, width)
        out_ref[:, pl.ds(at, width)] = mine_ref[p]
        at = pl.multiple_of((1 - place) * half + p * width, width)
        out_ref[:, pl.ds(at, width)] = other_ref[p]


def assemble(where, mine, other):
    pairs, tokens, width = mine.shape
    return pl.pallas_call(
        assemble_kernel,
        in_specs=[SCALARS, WHOLE, WHOLE],
        out_specs=WHOLE,
        out_shape=jax.ShapeDtypeStruct((tokens, PAIR * pairs * width), jnp.bfloat16),
        compiler_params=pltpu.CompilerParams(vmem_limit_bytes=8 * MIB),
        name="assemble",
    )(where, mine, other)


def handed_on(chunk):
    sections, size = lax.axis_size("section"), lax.axis_size("ctx")
    block = INNER * PAIR
    near = []
    for e in range(INNER):
        route = [
            (s * size + i, (s + 1) * size + i // block * block + (i + PAIR * e) % block)
            for s in range(sections - 1)
            for i in range(size)
        ]
        near.append(lax.ppermute(chunk, ("section", "ctx"), route))
    near = jnp.stack(near)
    far = [
        lax.ppermute(near, "ctx", [(i, (i + block * step) % size) for i in range(size)])
        for step in range(1, size // block)
    ]
    return [near] + far


def load_kernel(
    where_ref, frames_ref, keys_in, values_in, batch_in, fresh_in,
    held_ref, given_ref, batches_ref, sems, batch_sems,
):
    place = where_ref[0]
    _, length, width = held_ref.shape
    half = width // PAIR
    step = length // BLOCKS
    copies = []
    for b in range(BLOCKS):
        rows = pl.ds(b * step, step)
        for n, source in enumerate((keys_in, values_in)):
            target = held_ref.at[n, rows]
            copies.append((b, n, pltpu.make_async_copy(source.at[rows], target, sems.at[n, b])))
    for *_, copy in copies:
        copy.start()
    part = batches_ref.shape[2]
    batches = [
        pltpu.make_async_copy(
            source.at[:, pl.ds(pl.multiple_of(place * part, part), part)],
            batches_ref.at[n],
            batch_sems.at[n],
        )
        for n, source in enumerate((batch_in, fresh_in))
    ]
    for copy in batches:
        copy.start()

    shape = (STAT_ROWS, length)
    frames = jnp.broadcast_to(row_of(frames_ref).astype(jnp.float32), shape)
    line = lax.broadcasted_iota(jnp.int32, shape, 0)
    tail = jnp.where(line == 0, frames, 0.0).astype(jnp.bfloat16)
    given_ref[length : length + STAT_ROWS, :length] = tail
    given_ref[length : length + STAT_ROWS, length:] = jnp.zeros(
        (STAT_ROWS, width - length), jnp.bfloat16
    )
    away = pl.multiple_of((1 - place) * half, half)
    for b, n, copy in copies:
        copy.wait()
        rows = slice(b * step, (b + 1) * step)
        given_ref[rows, n * half : (n + 1) * half] = held_ref[n, rows, pl.ds(away, half)]
    for copy in batches:
        copy.wait()


def load(where, key_frames, keys, values, batch, fresh):
    length, width = keys.shape
    tokens, model = batch.shape
    return pl.pallas_call(
        load_kernel,
        in_specs=[SCALARS, WHOLE] + [IN_HBM] * 4,
        out_specs=[WHOLE] * 3,
        out_shape=[
            pltpu.VMEM((2, length, width), keys.dtype),
            pltpu.VMEM((length + STAT_ROWS, width), keys.dtype),
            pltpu.VMEM((2, tokens, model // PAIR), batch.dtype),
        ],
        scratch_shapes=[pltpu.SemaphoreType.DMA((2, BLOCKS)), pltpu.SemaphoreType.DMA((2,))],
        cost_estimate=pl.CostEstimate(
            flops=0, bytes_accessed=4 * length * width, transcendentals=0
        ),
        compiler_params=pltpu.CompilerParams(vmem_limit_bytes=LOAD_VMEM),
        name="load",
    )(where, key_frames, *in_hbm(keys, values, batch, fresh))


def body(
    activations,
    act_frames,
    fresh_batch,
    fresh_frames,
    norm_gain,
    cached_keys,
    cached_values,
    key_frames,
):
    section_index = lax.axis_index("section")
    ctx_index = lax.axis_index("ctx")
    pairs = lax.axis_size("ctx") // PAIR
    keys, values = cached_keys[0], cached_values[0]
    place = ctx_index % PAIR
    where = jnp.stack([place, ctx_index // PAIR, section_index == 0]).astype(jnp.int32)
    key_frames = key_frames.reshape(-1, HD)

    held, given, batches = load(where, key_frames, keys, values, activations[0], fresh_batch)
    got = swapped(given)

    def column(frames):
        return frames.astype(jnp.float32)[:, None]

    own_frames = lax.dynamic_index_in_dim(act_frames, section_index, 0, keepdims=False)
    prior_frames = lax.dynamic_index_in_dim(
        act_frames, jnp.maximum(section_index - 1, 0), 0, keepdims=False
    )
    frames_in = jnp.where(section_index == 0, fresh_frames, prior_frames)

    frames, frames_in = column(own_frames), column(frames_in)
    terms = begin(where, norm_gain, frames, key_frames, batches, held)
    chunks = exchanged(finish(frames, *terms, got, pairs))
    handed = handed_on(combine(where, chunks, batches, [], 0))
    chunks = exchanged(
        partials(where, norm_gain, frames_in, key_frames, batches, got, held, handed, pairs)
    )
    mine = exchanged(combine(where, chunks, batches, handed[:1], pairs))
    return assemble(where, mine, swapped(mine))[None]


def solution(mesh):
    placed = (
        P("section", None, None),
        P(),
        P(),
        P(),
        P("section", None),
        P("section", "ctx", None),
        P("section", "ctx", None),
        P("ctx"),
    )
    return jax.shard_map(
        body, mesh=mesh, in_specs=placed, out_specs=P("section", None, None), check_vma=False
    )
```

```python
import functools
import math

import jax
import jax.numpy as jnp
from jax import lax
from jax.experimental import pallas as pl
from jax.experimental.pallas import tpu as pltpu
from jax.sharding import PartitionSpec as P

HEADS = 64
HD = 128
PAIR = 2
INNER = 2
STAT_ROWS = 16
HIDDEN = -(2.0**100)
SCALE = HD**-0.5 * math.log2(math.e)

epsilon = 1e-05


def swapped(block):
    return lax.ppermute(block, "ctx", [(i, i ^ 1) for i in range(lax.axis_size("ctx"))])


def exchanged(chunks):
    size = lax.axis_size("ctx")
    groups = [list(range(place, size, PAIR)) for place in range(PAIR)]
    return lax.all_to_all(chunks, "ctx", 0, 0, axis_index_groups=groups, tiled=True)


def head_rows(block):
    return jnp.concatenate(
        [block[:, at : at + HD] for at in range(0, block.shape[1], HD)], axis=0
    )


def on_diagonal(rows):
    shape = (rows, HD)
    return lax.broadcasted_iota(jnp.int32, shape, 0) == lax.broadcasted_iota(jnp.int32, shape, 1)


SCALARS = pl.BlockSpec(memory_space=pltpu.SMEM)
WHOLE = pl.BlockSpec(memory_space=pltpu.VMEM)
IN_HBM = pl.BlockSpec(memory_space=pltpu.HBM)
MIB = 1 << 20
BLOCKS = 4


def in_hbm(*arrays):
    return [pltpu.with_memory_space_constraint(a, pltpu.HBM) for a in arrays]


def in_vmem(*arrays):
    return [pltpu.with_memory_space_constraint(a, pltpu.VMEM) for a in arrays]


def queries_of(x, gain):
    rows = head_rows(x.astype(jnp.float32))
    gain = head_rows(jnp.broadcast_to(gain, x.shape))
    norm = lax.rsqrt(jnp.mean(rows * rows, axis=-1, keepdims=True) + epsilon)
    return (rows * norm * gain).astype(jnp.bfloat16)


def bias_of(key_frames, frames):
    return jnp.where(key_frames.astype(jnp.float32) <= frames, 0.0, HIDDEN)[None]


def scores(queries, key_block, bias):
    count, keys, tokens = queries.shape[0], key_block.shape[0], bias.shape[1]
    raw = lax.dot_general(
        queries, key_block, (((1,), (1,)), ((), ())), preferred_element_type=jnp.float32
    )
    raw = raw.reshape(count // tokens, tokens, keys) * SCALE + bias
    return raw.reshape(count, keys)


def top_of(raw):
    top = jnp.max(raw, axis=-1, keepdims=True)
    return top.astype(jnp.bfloat16).astype(jnp.float32)


def weigh(raw, top, value_block):
    probs = jnp.exp2(raw - top).astype(jnp.bfloat16)
    ones = jnp.ones((value_block.shape[0], HD), jnp.bfloat16)
    return jnp.dot(
        probs, jnp.concatenate([value_block, ones], axis=1), preferred_element_type=jnp.float32
    )


def write_chunks(out_ref, g, tops, both):
    held = out_ref.shape[1] - STAT_ROWS
    chunks = both.shape[0] // held
    diagonal = on_diagonal(held)
    line = lax.broadcasted_iota(jnp.int32, (STAT_ROWS, HD), 0)
    for c in range(chunks):
        part = both[c * held : (c + 1) * held]
        top = tops[c * held : (c + 1) * held]
        top_row = jnp.sum(jnp.where(diagonal, top, 0.0), axis=0, keepdims=True)
        total_row = jnp.sum(jnp.where(diagonal, part[:, HD:], 0.0), axis=0, keepdims=True)
        high = total_row.astype(jnp.bfloat16).astype(jnp.float32)
        stats = jnp.where(
            line == 0, top_row,
            jnp.where(line == 1, high, jnp.where(line == 2, total_row - high, 0.0)),
        )
        out_ref[g * chunks + c, :held] = part[:, :HD].astype(jnp.bfloat16)
        out_ref[g * chunks + c, held:] = stats.astype(jnp.bfloat16)


def row_of(ref):
    return jnp.concatenate([ref[i : i + 1] for i in range(ref.shape[0])], axis=1)


def kv_block(ref, g, values):
    at = (values * ref.shape[1] // HD // 2 + g) * HD
    return ref[: ref.shape[0] - STAT_ROWS, at : at + HD]


def key_frames_of(ref):
    length = ref.shape[0] - STAT_ROWS
    return ref[length:, :length].astype(jnp.float32)[0:1]


def begin_kernel(gain_ref, frames_ref, batches_ref, own_ref, queries_ref, sums_ref, stats_ref):
    kv_here = own_ref.shape[1] // HD // 2
    count, width = queries_ref.shape[0] // kv_here, gain_ref.shape[1] // kv_here
    bias = bias_of(key_frames_of(own_ref), frames_ref[0, :, :1])
    for g in range(kv_here):
        rows, columns = slice(g * count, (g + 1) * count), slice(g * width, (g + 1) * width)
        queries = queries_of(batches_ref[0, :, columns], gain_ref[:, columns])
        queries_ref[rows] = queries
        raw = scores(queries, kv_block(own_ref, g, 0), bias)
        top = top_of(raw)
        both = weigh(raw, top, kv_block(own_ref, g, 1))
        sums_ref[rows] = both[:, :HD]
        lane = lax.broadcasted_iota(jnp.int32, (count, HD), 1)
        stats_ref[rows] = jnp.where(lane < HD // 2, top, both[:, HD:])


def begin(gain, frames, batches, own):
    length, width = own.shape
    queries = HEADS // PAIR * frames.shape[1]
    return pl.pallas_call(
        begin_kernel,
        in_specs=[WHOLE] * 4,
        out_specs=[WHOLE] * 3,
        out_shape=[
            jax.ShapeDtypeStruct((queries, HD), jnp.bfloat16),
            jax.ShapeDtypeStruct((queries, HD), jnp.float32),
            jax.ShapeDtypeStruct((queries, HD), jnp.float32),
        ],
        cost_estimate=pl.CostEstimate(
            flops=2 * queries * length * 3 * HD,
            bytes_accessed=2 * length * width,
            transcendentals=queries * length,
        ),
        compiler_params=pltpu.CompilerParams(vmem_limit_bytes=16 * MIB),
        name="begin",
    )(*in_vmem(gain, frames, batches, own))


def finish_kernel(frames_ref, queries_ref, sums_ref, stats_ref, got_ref, out_ref):
    kv_here = got_ref.shape[1] // HD // 2
    count = queries_ref.shape[0] // kv_here
    bias = bias_of(key_frames_of(got_ref), frames_ref[0, :, :1])
    for g in range(kv_here):
        rows = slice(g * count, (g + 1) * count)
        raw = scores(queries_ref[rows], kv_block(got_ref, g, 0), bias)
        before, totals = stats_ref[rows, :1], stats_ref[rows, HD // 2 : HD // 2 + 1]
        top = jnp.maximum(before, top_of(raw))
        factor = jnp.exp2(before - top)
        both = weigh(raw, top, kv_block(got_ref, g, 1))
        earlier = [sums_ref[rows] * factor, jnp.broadcast_to(totals * factor, (count, HD))]
        write_chunks(
            out_ref, g, jnp.broadcast_to(top, (count, HD)), both + jnp.concatenate(earlier, axis=1)
        )


def finish(frames, queries, sums, stats, got, pairs):
    count = queries.shape[0]
    length, width = got.shape
    return pl.pallas_call(
        finish_kernel,
        in_specs=[WHOLE] * 5,
        out_specs=WHOLE,
        out_shape=jax.ShapeDtypeStruct((pairs, count // pairs + STAT_ROWS, HD), jnp.bfloat16),
        cost_estimate=pl.CostEstimate(
            flops=2 * count * length * 3 * HD,
            bytes_accessed=2 * length * width,
            transcendentals=count * length,
        ),
        compiler_params=pltpu.CompilerParams(vmem_limit_bytes=16 * MIB),
        name="finish",
    )(*in_vmem(frames, queries, sums, stats, got))


def partials_kernel(where_ref, gain_ref, frames_ref, batches_ref, got_ref, own_ref, *rest):
    *handed_refs, out_ref, x_ref = rest
    pair, first_section = where_ref[1], where_ref[2]
    pairs, outer = out_ref.shape[0], len(handed_refs)
    kv_here = own_ref.shape[1] // HD // 2
    share = x_ref.shape[1] // pairs
    width = x_ref.shape[1] // kv_here

    x_ref[...] = batches_ref[1]

    @pl.when(first_section == 0)
    def _():
        for step, handed_ref in enumerate(handed_refs):
            base = (pair // INNER + outer - step) % outer * INNER
            for e in range(INNER):
                at = pl.multiple_of((base + (pair + e) % INNER) * share, share)
                x_ref[:, pl.ds(at, share)] = handed_ref[e]

    frames = frames_ref[1, :, :1]
    refs = (own_ref, got_ref)
    biases = [bias_of(key_frames_of(ref), frames) for ref in refs]
    for g in range(kv_here):
        columns = slice(g * width, (g + 1) * width)
        queries = queries_of(x_ref[:, columns], gain_ref[:, columns])
        raws = [scores(queries, kv_block(ref, g, 0), bias) for ref, bias in zip(refs, biases)]
        top = functools.reduce(jnp.maximum, [top_of(raw) for raw in raws])
        both = sum(weigh(raw, top, kv_block(ref, g, 1)) for ref, raw in zip(refs, raws))
        write_chunks(out_ref, g, jnp.broadcast_to(top, (both.shape[0], HD)), both)


def partials(where, gain, frames, batches, got, own, handed, pairs):
    length, width = own.shape
    _, tokens, half = batches.shape
    queries = HEADS // PAIR * tokens
    return pl.pallas_call(
        partials_kernel,
        in_specs=[SCALARS] + [WHOLE] * (5 + len(handed)),
        out_specs=WHOLE,
        out_shape=jax.ShapeDtypeStruct((pairs, queries // pairs + STAT_ROWS, HD), jnp.bfloat16),
        scratch_shapes=[pltpu.VMEM((tokens, half), batches.dtype)],
        cost_estimate=pl.CostEstimate(
            flops=2 * queries * PAIR * length * 3 * HD,
            bytes_accessed=4 * length * width,
            transcendentals=queries * PAIR * length,
        ),
        compiler_params=pltpu.CompilerParams(vmem_limit_bytes=16 * MIB),
        name="partials",
    )(where, *in_vmem(gain, frames, batches, got, own, *handed))


def combine_kernel(where_ref, parts_ref, batches_ref, *rest):
    *handed_refs, out_ref = rest
    pair, first_section = where_ref[1], where_ref[2]
    pairs, rows, _ = parts_ref.shape
    tokens, share = out_ref.shape[-2:]
    held = rows - STAT_ROWS
    tick = 1 if handed_refs else 0
    columns = pl.ds(pl.multiple_of(pair * share, share), share)
    own = batches_ref[tick, :, columns].astype(jnp.float32)
    if handed_refs:
        own = jnp.where(first_section == 1, own, handed_refs[0][0].astype(jnp.float32))
    stats = [parts_ref[p, held:].astype(jnp.float32) for p in range(pairs)]
    tops = [s[0:1] for s in stats]
    overall = functools.reduce(jnp.maximum, tops)
    factors = [jnp.exp2(top - overall) for top in tops]
    denominator = sum(f * (s[1:2] + s[2:3]) for f, s in zip(factors, stats))
    inverse = 1.0 / denominator
    diagonal = on_diagonal(held)
    total = head_rows(own)
    for p in range(pairs):
        weight = jnp.where(diagonal, factors[p] * inverse, 0.0)
        high = weight.astype(jnp.bfloat16)
        low = (weight - high.astype(jnp.float32)).astype(jnp.bfloat16)
        for term in (high, low):
            total = total + jnp.dot(
                term[:, :rows], parts_ref[p], preferred_element_type=jnp.float32
            )
    for h in range(held // tokens):
        piece = total[h * tokens : (h + 1) * tokens].astype(jnp.bfloat16)
        if len(out_ref.shape) == 3:
            for p in range(out_ref.shape[0]):
                out_ref[p, :, h * HD : (h + 1) * HD] = piece
        else:
            out_ref[:, h * HD : (h + 1) * HD] = piece


def combine(where, parts, batches, handed, copies):
    pairs, rows, _ = parts.shape
    tokens = batches.shape[1]
    width = (rows - STAT_ROWS) // tokens * HD
    shape = (copies, tokens, width) if copies else (tokens, width)
    return pl.pallas_call(
        combine_kernel,
        in_specs=[SCALARS] + [WHOLE] * (2 + len(handed)),
        out_specs=WHOLE,
        out_shape=jax.ShapeDtypeStruct(shape, jnp.bfloat16),
        compiler_params=pltpu.CompilerParams(vmem_limit_bytes=8 * MIB),
        name="combine",
    )(where, *in_vmem(parts, batches, *handed))


def assemble_kernel(where_ref, mine_ref, other_ref, out_ref):
    pairs, _, width = mine_ref.shape
    half = pairs * width
    place = where_ref[0]
    for p in range(pairs):
        at = pl.multiple_of(place * half + p * width, width)
        out_ref[:, pl.ds(at, width)] = mine_ref[p]
        at = pl.multiple_of((1 - place) * half + p * width, width)
        out_ref[:, pl.ds(at, width)] = other_ref[p]


def assemble(where, mine, other):
    pairs, tokens, width = mine.shape
    return pl.pallas_call(
        assemble_kernel,
        in_specs=[SCALARS, WHOLE, WHOLE],
        out_specs=WHOLE,
        out_shape=jax.ShapeDtypeStruct((tokens, PAIR * pairs * width), jnp.bfloat16),
        compiler_params=pltpu.CompilerParams(vmem_limit_bytes=8 * MIB),
        name="assemble",
    )(where, *in_vmem(mine, other))


def handed_on(chunk):
    sections, size = lax.axis_size("section"), lax.axis_size("ctx")
    block = INNER * PAIR
    near = []
    for e in range(INNER):
        route = [
            (s * size + i, (s + 1) * size + i // block * block + (i + PAIR * e) % block)
            for s in range(sections - 1)
            for i in range(size)
        ]
        near.append(lax.ppermute(chunk, ("section", "ctx"), route))
    near = jnp.stack(near)
    far = [
        lax.ppermute(near, "ctx", [(i, (i + block * step) % size) for i in range(size)])
        for step in range(1, size // block)
    ]
    return [near] + far


def columns_of(place, ref, width):
    return ref.at[:, pl.ds(pl.multiple_of(place * width, HD), width)]


def load_kernel(
    where_ref, act_frames_in, fresh_frames_in, key_frames_in, keys_in, values_in, batch_in,
    fresh_in, gain_in, own_ref, given_ref, batches_ref, gain_ref, frames_ref, staged_ref,
    tail_ref, act_frames_ref, fresh_frames_ref, key_frames_ref, sems, given_sems, small_sems,
):
    place, first_section, section = where_ref[0], where_ref[2], where_ref[3]
    _, length, width = staged_ref.shape
    half = width // PAIR
    step = length // BLOCKS
    part = gain_ref.shape[1]
    small = [
        (key_frames_in, key_frames_ref),
        (act_frames_in, act_frames_ref),
        (fresh_frames_in, fresh_frames_ref),
        (columns_of(place, batch_in, part), batches_ref.at[0]),
        (columns_of(place, gain_in, part), gain_ref),
        (columns_of(place, fresh_in, part), batches_ref.at[1]),
    ]
    small = [pltpu.make_async_copy(a, b, small_sems.at[n]) for n, (a, b) in enumerate(small)]
    for copy in small[:3]:
        copy.start()
    copies = []
    for b in range(BLOCKS):
        rows = pl.ds(b * step, step)
        for n, source in enumerate((keys_in, values_in)):
            target = staged_ref.at[n, rows]
            copies.append((b, n, pltpu.make_async_copy(source.at[rows], target, sems.at[n, b])))
    for *_, copy in copies:
        copy.start()
    for copy in small[3:]:
        copy.start()
    for copy in small[:3]:
        copy.wait()

    tokens = frames_ref.shape[1]
    own_row = act_frames_ref[pl.ds(section, 1), :].astype(jnp.float32)
    prior_row = act_frames_ref[pl.ds(jnp.maximum(section - 1, 0), 1), :].astype(jnp.float32)
    next_row = jnp.where(first_section == 1, fresh_frames_ref[...].astype(jnp.float32), prior_row)
    shape = (tokens, tokens)
    diagonal = lax.broadcasted_iota(jnp.int32, shape, 0) == lax.broadcasted_iota(jnp.int32, shape, 1)
    for tick, row in enumerate((own_row, next_row)):
        column = jnp.sum(jnp.where(diagonal, row, 0.0), axis=1, keepdims=True)
        frames_ref[tick] = jnp.broadcast_to(column, (tokens, HD))

    shape = (STAT_ROWS, length)
    frames = jnp.broadcast_to(row_of(key_frames_ref).astype(jnp.float32), shape)
    line = lax.broadcasted_iota(jnp.int32, shape, 0)
    tail = jnp.where(line == 0, frames, 0.0).astype(jnp.bfloat16)
    tail = jnp.concatenate([tail, jnp.zeros((STAT_ROWS, width - length), jnp.bfloat16)], axis=1)
    tail_ref[...] = tail
    own_ref[length:] = tail
    gifts = [
        pltpu.make_async_copy(tail_ref, given_ref.at[pl.ds(length, STAT_ROWS)], small_sems.at[len(small)])
    ]
    gifts[0].start()
    for b, n, copy in copies:
        copy.wait()
        rows, columns = pl.ds(b * step, step), pl.ds(n * half, half)
        gift = pltpu.make_async_copy(
            columns_of(1 - place, staged_ref.at[n, rows], half),
            given_ref.at[rows, columns],
            given_sems.at[n, b],
        )
        gift.start()
        gifts.append(gift)
        own_ref[rows, columns] = columns_of(place, staged_ref.at[n, rows], half)[...]
    for copy in small[3:] + gifts:
        copy.wait()


def load(where, act_frames, fresh_frames, key_frames, keys, values, batch, fresh, gain):
    length, width = keys.shape
    tokens, model = batch.shape
    half = model // PAIR
    return pl.pallas_call(
        load_kernel,
        in_specs=[SCALARS] + [IN_HBM] * 8,
        out_specs=[WHOLE, IN_HBM] + [WHOLE] * 3,
        out_shape=[
            pltpu.VMEM((length + STAT_ROWS, width), keys.dtype),
            pltpu.HBM((length + STAT_ROWS, width), keys.dtype),
            pltpu.VMEM((2, tokens, half), batch.dtype),
            pltpu.VMEM((1, half), gain.dtype),
            pltpu.VMEM((2, tokens, HD), jnp.float32),
        ],
        scratch_shapes=[
            pltpu.VMEM((2, length, width), keys.dtype),
            pltpu.VMEM((STAT_ROWS, width), keys.dtype),
            pltpu.VMEM(act_frames.shape, act_frames.dtype),
            pltpu.VMEM(fresh_frames.shape, fresh_frames.dtype),
            pltpu.VMEM(key_frames.shape, key_frames.dtype),
            pltpu.SemaphoreType.DMA((2, BLOCKS)),
            pltpu.SemaphoreType.DMA((2, BLOCKS)),
            pltpu.SemaphoreType.DMA((7,)),
        ],
        cost_estimate=pl.CostEstimate(
            flops=0, bytes_accessed=4 * length * width, transcendentals=0
        ),
        compiler_params=pltpu.CompilerParams(vmem_limit_bytes=16 * MIB),
        name="load",
    )(
        where,
        *in_hbm(act_frames, fresh_frames, key_frames, keys, values, batch, fresh, gain),
    )


def body(
    activations,
    act_frames,
    fresh_batch,
    fresh_frames,
    norm_gain,
    cached_keys,
    cached_values,
    key_frames,
):
    section_index = lax.axis_index("section")
    ctx_index = lax.axis_index("ctx")
    pairs = lax.axis_size("ctx") // PAIR
    place, pair = ctx_index % PAIR, ctx_index // PAIR
    where = jnp.stack([place, pair, section_index == 0, section_index]).astype(jnp.int32)

    own, given, batches, gain, frames = load(
        where, act_frames, fresh_frames[None], key_frames.reshape(-1, HD), cached_keys[0],
        cached_values[0], activations[0], fresh_batch, norm_gain,
    )
    got = swapped(given)
    terms = begin(gain, frames, batches, own)
    chunks = exchanged(finish(frames, *terms, got, pairs))
    handed = handed_on(combine(where, chunks, batches, [], 0))
    chunks = exchanged(partials(where, gain, frames, batches, got, own, handed, pairs))
    mine = exchanged(combine(where, chunks, batches, handed[:1], pairs))
    return assemble(where, mine, swapped(mine))[None]


def solution(mesh):
    placed = (
        P("section", None, None),
        P(),
        P(),
        P(),
        P("section", None),
        P("section", "ctx", None),
        P("section", "ctx", None),
        P("ctx"),
    )
    return jax.shard_map(
        body, mesh=mesh, in_specs=placed, out_specs=P("section", None, None), check_vma=False
    )
```

```python
import functools
import math

import jax
import jax.numpy as jnp
from jax import lax
from jax.experimental import pallas as pl
from jax.experimental.pallas import tpu as pltpu
from jax.sharding import PartitionSpec as P

HEADS = 64
HD = 128
PAIR = 2
STAT_ROWS = 16
HIDDEN = -(2.0**100)
SCALE = HD**-0.5 * math.log2(math.e)

epsilon = 1e-05


def swapped(block):
    return lax.ppermute(block, "ctx", [(i, i ^ 1) for i in range(lax.axis_size("ctx"))])


def exchanged(chunks):
    size = lax.axis_size("ctx")
    groups = [list(range(place, size, PAIR)) for place in range(PAIR)]
    return lax.all_to_all(chunks, "ctx", 0, 0, axis_index_groups=groups, tiled=True)


def head_rows(block):
    return jnp.concatenate(
        [block[:, at : at + HD] for at in range(0, block.shape[1], HD)], axis=0
    )


def on_diagonal(rows):
    shape = (rows, HD)
    return lax.broadcasted_iota(jnp.int32, shape, 0) == lax.broadcasted_iota(jnp.int32, shape, 1)


SCALARS = pl.BlockSpec(memory_space=pltpu.SMEM)
WHOLE = pl.BlockSpec(memory_space=pltpu.VMEM)
IN_HBM = pl.BlockSpec(memory_space=pltpu.HBM)
MIB = 1 << 20
BLOCKS = 4


def in_hbm(*arrays):
    return [pltpu.with_memory_space_constraint(a, pltpu.HBM) for a in arrays]


def in_vmem(*arrays):
    return [pltpu.with_memory_space_constraint(a, pltpu.VMEM) for a in arrays]


def queries_of(x, gain):
    rows = head_rows(x.astype(jnp.float32))
    gain = head_rows(jnp.broadcast_to(gain, x.shape))
    norm = lax.rsqrt(jnp.mean(rows * rows, axis=-1, keepdims=True) + epsilon)
    return (rows * norm * gain).astype(jnp.bfloat16)


def bias_of(key_frames, frames):
    return jnp.where(key_frames.astype(jnp.float32) <= frames, 0.0, HIDDEN)[None]


def scores(queries, key_block, bias):
    count, keys, tokens = queries.shape[0], key_block.shape[0], bias.shape[1]
    raw = lax.dot_general(
        queries, key_block, (((1,), (1,)), ((), ())), preferred_element_type=jnp.float32
    )
    raw = raw.reshape(count // tokens, tokens, keys) * SCALE + bias
    return raw.reshape(count, keys)


def top_of(raw):
    top = jnp.max(raw, axis=-1, keepdims=True)
    return top.astype(jnp.bfloat16).astype(jnp.float32)


def weigh(raw, top, value_block):
    probs = jnp.exp2(raw - top).astype(jnp.bfloat16)
    ones = jnp.ones((value_block.shape[0], HD), jnp.bfloat16)
    return jnp.dot(
        probs, jnp.concatenate([value_block, ones], axis=1), preferred_element_type=jnp.float32
    )


def write_chunks(out_ref, g, tops, both):
    held = out_ref.shape[1] - STAT_ROWS
    chunks = both.shape[0] // held
    diagonal = on_diagonal(held)
    line = lax.broadcasted_iota(jnp.int32, (STAT_ROWS, HD), 0)
    for c in range(chunks):
        part = both[c * held : (c + 1) * held]
        top = tops[c * held : (c + 1) * held]
        top_row = jnp.sum(jnp.where(diagonal, top, 0.0), axis=0, keepdims=True)
        total_row = jnp.sum(jnp.where(diagonal, part[:, HD:], 0.0), axis=0, keepdims=True)
        high = total_row.astype(jnp.bfloat16).astype(jnp.float32)
        stats = jnp.where(
            line == 0, top_row,
            jnp.where(line == 1, high, jnp.where(line == 2, total_row - high, 0.0)),
        )
        out_ref[g * chunks + c, :held] = part[:, :HD].astype(jnp.bfloat16)
        out_ref[g * chunks + c, held:] = stats.astype(jnp.bfloat16)


def row_of(ref):
    return jnp.concatenate([ref[i : i + 1] for i in range(ref.shape[0])], axis=1)


def kv_block(ref, g, values):
    at = (values * ref.shape[1] // HD // 2 + g) * HD
    return ref[: ref.shape[0] - STAT_ROWS, at : at + HD]


def key_frames_of(ref):
    length = ref.shape[0] - STAT_ROWS
    return ref[length:, :length].astype(jnp.float32)[0:1]


def begin_kernel(gain_ref, frames_ref, batches_ref, own_ref, queries_ref, sums_ref, stats_ref):
    kv_here = own_ref.shape[1] // HD // 2
    count, width = queries_ref.shape[0] // kv_here, gain_ref.shape[1] // kv_here
    bias = bias_of(key_frames_of(own_ref), frames_ref[0, :, :1])
    for g in range(kv_here):
        rows, columns = slice(g * count, (g + 1) * count), slice(g * width, (g + 1) * width)
        queries = queries_of(batches_ref[0, :, columns], gain_ref[:, columns])
        queries_ref[rows] = queries
        raw = scores(queries, kv_block(own_ref, g, 0), bias)
        top = top_of(raw)
        both = weigh(raw, top, kv_block(own_ref, g, 1))
        sums_ref[rows] = both[:, :HD]
        lane = lax.broadcasted_iota(jnp.int32, (count, HD), 1)
        stats_ref[rows] = jnp.where(lane < HD // 2, top, both[:, HD:])


def begin(gain, frames, batches, own):
    length, width = own.shape
    queries = HEADS // PAIR * frames.shape[1]
    return pl.pallas_call(
        begin_kernel,
        in_specs=[WHOLE] * 4,
        out_specs=[WHOLE] * 3,
        out_shape=[
            jax.ShapeDtypeStruct((queries, HD), jnp.bfloat16),
            jax.ShapeDtypeStruct((queries, HD), jnp.float32),
            jax.ShapeDtypeStruct((queries, HD), jnp.float32),
        ],
        cost_estimate=pl.CostEstimate(
            flops=2 * queries * length * 3 * HD,
            bytes_accessed=2 * length * width,
            transcendentals=queries * length,
        ),
        compiler_params=pltpu.CompilerParams(vmem_limit_bytes=16 * MIB),
        name="begin",
    )(*in_vmem(gain, frames, batches, own))


def finish_kernel(
    where_ref, frames_ref, batches_ref, queries_ref, sums_ref, stats_ref, got_ref, *rest
):
    *out_refs, chunks_ref = rest
    pair, pairs = where_ref[1], len(out_refs)
    kv_here = got_ref.shape[1] // HD // 2
    count = queries_ref.shape[0] // kv_here
    bias = bias_of(key_frames_of(got_ref), frames_ref[0, :, :1])
    for g in range(kv_here):
        rows = slice(g * count, (g + 1) * count)
        raw = scores(queries_ref[rows], kv_block(got_ref, g, 0), bias)
        before, totals = stats_ref[rows, :1], stats_ref[rows, HD // 2 : HD // 2 + 1]
        top = jnp.maximum(before, top_of(raw))
        factor = jnp.exp2(before - top)
        both = weigh(raw, top, kv_block(got_ref, g, 1))
        earlier = [sums_ref[rows] * factor, jnp.broadcast_to(totals * factor, (count, HD))]
        write_chunks(
            chunks_ref, g, jnp.broadcast_to(top, (count, HD)),
            both + jnp.concatenate(earlier, axis=1),
        )
    size, share = chunks_ref.shape[1], batches_ref.shape[2] // pairs
    for step, out_ref in enumerate(out_refs):
        out_ref[:size] = chunks_ref[(pair + step) % pairs]
    own = batches_ref[0, :, pl.ds(pl.multiple_of(pair * share, share), share)]
    out_refs[0][size:] = head_rows(own.astype(jnp.float32)).astype(jnp.bfloat16)


def finish(where, frames, batches, queries, sums, stats, got, pairs):
    count = queries.shape[0]
    length, width = got.shape
    held = count // pairs
    size = held + STAT_ROWS
    return pl.pallas_call(
        finish_kernel,
        in_specs=[SCALARS] + [WHOLE] * 6,
        out_specs=[WHOLE] * pairs,
        out_shape=[
            jax.ShapeDtypeStruct((size + (0 if step else held), HD), jnp.bfloat16)
            for step in range(pairs)
        ],
        scratch_shapes=[pltpu.VMEM((pairs, size, HD), jnp.bfloat16)],
        cost_estimate=pl.CostEstimate(
            flops=2 * count * length * 3 * HD,
            bytes_accessed=2 * length * width,
            transcendentals=count * length,
        ),
        compiler_params=pltpu.CompilerParams(vmem_limit_bytes=16 * MIB),
        name="finish",
    )(where, *in_vmem(frames, batches, queries, sums, stats, got))


def partials_kernel(
    where_ref, gain_ref, frames_ref, batches_ref, got_ref, own_ref, handed_ref, out_ref, x_ref
):
    first_section, pairs = where_ref[2], out_ref.shape[0]
    kv_here = own_ref.shape[1] // HD // 2
    share = x_ref.shape[1] // pairs
    width = x_ref.shape[1] // kv_here

    x_ref[...] = batches_ref[1]

    @pl.when(first_section == 0)
    def _():
        for p in range(pairs):
            x_ref[:, p * share : (p + 1) * share] = handed_ref[p]

    frames = frames_ref[1, :, :1]
    refs = (own_ref, got_ref)
    biases = [bias_of(key_frames_of(ref), frames) for ref in refs]
    for g in range(kv_here):
        columns = slice(g * width, (g + 1) * width)
        queries = queries_of(x_ref[:, columns], gain_ref[:, columns])
        raws = [scores(queries, kv_block(ref, g, 0), bias) for ref, bias in zip(refs, biases)]
        top = functools.reduce(jnp.maximum, [top_of(raw) for raw in raws])
        both = sum(weigh(raw, top, kv_block(ref, g, 1)) for ref, raw in zip(refs, raws))
        write_chunks(out_ref, g, jnp.broadcast_to(top, (both.shape[0], HD)), both)


def partials(where, gain, frames, batches, got, own, handed, pairs):
    length, width = own.shape
    _, tokens, half = batches.shape
    queries = HEADS // PAIR * tokens
    return pl.pallas_call(
        partials_kernel,
        in_specs=[SCALARS] + [WHOLE] * 6,
        out_specs=WHOLE,
        out_shape=jax.ShapeDtypeStruct((pairs, queries // pairs + STAT_ROWS, HD), jnp.bfloat16),
        scratch_shapes=[pltpu.VMEM((tokens, half), batches.dtype)],
        cost_estimate=pl.CostEstimate(
            flops=2 * queries * PAIR * length * 3 * HD,
            bytes_accessed=4 * length * width,
            transcendentals=queries * PAIR * length,
        ),
        compiler_params=pltpu.CompilerParams(vmem_limit_bytes=16 * MIB),
        name="partials",
    )(where, *in_vmem(gain, frames, batches, got, own, handed))


def combined(own, parts, rows):
    held = rows - STAT_ROWS
    stats = [part[held:rows].astype(jnp.float32) for part in parts]
    tops = [s[0:1] for s in stats]
    overall = functools.reduce(jnp.maximum, tops)
    factors = [jnp.exp2(top - overall) for top in tops]
    denominator = sum(f * (s[1:2] + s[2:3]) for f, s in zip(factors, stats))
    inverse = 1.0 / denominator
    diagonal = on_diagonal(held)
    total = own
    for factor, part in zip(factors, parts):
        weight = jnp.where(diagonal, factor * inverse, 0.0)
        high = weight.astype(jnp.bfloat16)
        low = (weight - high.astype(jnp.float32)).astype(jnp.bfloat16)
        for term in (high, low):
            total = total + jnp.dot(
                term[:, :rows], part[:rows], preferred_element_type=jnp.float32
            )
    return total


def write_copies(total, out_ref):
    copies, tokens, _ = out_ref.shape
    for h in range(total.shape[0] // tokens):
        piece = total[h * tokens : (h + 1) * tokens].astype(jnp.bfloat16)
        for p in range(copies):
            out_ref[p, :, h * HD : (h + 1) * HD] = piece


def combine_kernel(*refs):
    *parts, out_ref = refs
    rows = parts[-1].shape[0]
    own = parts[0][rows:].astype(jnp.float32)
    write_copies(combined(own, parts, rows), out_ref)


def combine_last_kernel(where_ref, parts_ref, batches_ref, handed_ref, out_ref):
    pair, first_section = where_ref[1], where_ref[2]
    pairs, rows, _ = parts_ref.shape
    share = out_ref.shape[2]
    columns = pl.ds(pl.multiple_of(pair * share, share), share)
    own = batches_ref[1, :, columns].astype(jnp.float32)
    own = jnp.where(first_section == 1, own, handed_ref[pair].astype(jnp.float32))
    parts = [parts_ref.at[p] for p in range(pairs)]
    write_copies(combined(head_rows(own), parts, rows), out_ref)


def combine(kernel, operands, copies, tokens, width):
    scalars = 1 if operands[0].ndim == 1 else 0
    return pl.pallas_call(
        kernel,
        in_specs=[SCALARS] * scalars + [WHOLE] * (len(operands) - scalars),
        out_specs=WHOLE,
        out_shape=jax.ShapeDtypeStruct((copies, tokens, width), jnp.bfloat16),
        compiler_params=pltpu.CompilerParams(vmem_limit_bytes=8 * MIB),
        name="combine",
    )(*operands[:scalars], *in_vmem(*operands[scalars:]))


def assemble_kernel(where_ref, mine_ref, other_ref, out_ref):
    pairs, _, width = mine_ref.shape
    half = pairs * width
    place = where_ref[0]
    for p in range(pairs):
        at = pl.multiple_of(place * half + p * width, width)
        out_ref[:, pl.ds(at, width)] = mine_ref[p]
        at = pl.multiple_of((1 - place) * half + p * width, width)
        out_ref[:, pl.ds(at, width)] = other_ref[p]


def assemble(where, mine, other):
    pairs, tokens, width = mine.shape
    return pl.pallas_call(
        assemble_kernel,
        in_specs=[SCALARS, WHOLE, WHOLE],
        out_specs=WHOLE,
        out_shape=jax.ShapeDtypeStruct((tokens, PAIR * pairs * width), jnp.bfloat16),
        compiler_params=pltpu.CompilerParams(vmem_limit_bytes=8 * MIB),
        name="assemble",
    )(where, *in_vmem(mine, other))


def handed_on(chunks):
    sections, size = lax.axis_size("section"), lax.axis_size("ctx")
    got = []
    for step, chunk in enumerate(chunks):
        route = [
            (s * size + i, (s + 1) * size + (i + PAIR * step) % size)
            for s in range(sections - 1)
            for i in range(size)
        ]
        got.append(lax.ppermute(chunk, ("section", "ctx"), route))
    return got


def columns_of(place, ref, width):
    return ref.at[:, pl.ds(pl.multiple_of(place * width, HD), width)]


def load_kernel(
    where_ref, act_frames_in, fresh_frames_in, key_frames_in, keys_in, values_in, batch_in,
    fresh_in, gain_in, own_ref, given_ref, batches_ref, gain_ref, frames_ref, staged_ref,
    gift_ref, act_frames_ref, fresh_frames_ref, key_frames_ref, sems, given_sems, small_sems,
):
    place, first_section, section = where_ref[0], where_ref[2], where_ref[3]
    _, length, width = staged_ref.shape
    half = width // PAIR
    step = length // BLOCKS
    part = gain_ref.shape[1]
    small = [
        (key_frames_in, key_frames_ref),
        (act_frames_in, act_frames_ref),
        (fresh_frames_in, fresh_frames_ref),
        (columns_of(place, batch_in, part), batches_ref.at[0]),
        (columns_of(place, gain_in, part), gain_ref),
        (columns_of(place, fresh_in, part), batches_ref.at[1]),
    ]
    small = [pltpu.make_async_copy(a, b, small_sems.at[n]) for n, (a, b) in enumerate(small)]
    for copy in small[:3]:
        copy.start()
    copies = []
    for b in range(BLOCKS):
        rows = pl.ds(b * step, step)
        for n, source in enumerate((keys_in, values_in)):
            target = staged_ref.at[n, rows]
            copies.append((b, n, pltpu.make_async_copy(source.at[rows], target, sems.at[n, b])))
    for *_, copy in copies:
        copy.start()
    for copy in small[3:]:
        copy.start()
    for copy in small[:3]:
        copy.wait()

    tokens = frames_ref.shape[1]
    own_row = act_frames_ref[pl.ds(section, 1), :].astype(jnp.float32)
    prior_row = act_frames_ref[pl.ds(jnp.maximum(section - 1, 0), 1), :].astype(jnp.float32)
    next_row = jnp.where(first_section == 1, fresh_frames_ref[...].astype(jnp.float32), prior_row)
    shape = (tokens, tokens)
    diagonal = lax.broadcasted_iota(jnp.int32, shape, 0) == lax.broadcasted_iota(jnp.int32, shape, 1)
    for tick, row in enumerate((own_row, next_row)):
        column = jnp.sum(jnp.where(diagonal, row, 0.0), axis=1, keepdims=True)
        frames_ref[tick] = jnp.broadcast_to(column, (tokens, HD))

    shape = (STAT_ROWS, length)
    frames = jnp.broadcast_to(row_of(key_frames_ref).astype(jnp.float32), shape)
    line = lax.broadcasted_iota(jnp.int32, shape, 0)
    tail = jnp.where(line == 0, frames, 0.0).astype(jnp.bfloat16)
    tail = jnp.concatenate([tail, jnp.zeros((STAT_ROWS, width - length), jnp.bfloat16)], axis=1)
    gift_ref[length:] = tail
    own_ref[length:] = tail
    gifts = []
    for b, n, copy in copies:
        copy.wait()
        rows, columns = pl.ds(b * step, step), pl.ds(n * half, half)
        gift_ref[rows, columns] = columns_of(1 - place, staged_ref.at[n, rows], half)[...]
        own_ref[rows, columns] = columns_of(place, staged_ref.at[n, rows], half)[...]
        if n == 1:
            rows = pl.ds(b * step, step + (STAT_ROWS if b == BLOCKS - 1 else 0))
            gifts.append(
                pltpu.make_async_copy(gift_ref.at[rows], given_ref.at[rows], given_sems.at[b])
            )
            gifts[-1].start()
    for copy in small[3:] + gifts:
        copy.wait()


def load(where, act_frames, fresh_frames, key_frames, keys, values, batch, fresh, gain):
    length, width = keys.shape
    tokens, model = batch.shape
    half = model // PAIR
    return pl.pallas_call(
        load_kernel,
        in_specs=[SCALARS] + [IN_HBM] * 8,
        out_specs=[WHOLE, IN_HBM] + [WHOLE] * 3,
        out_shape=[
            pltpu.VMEM((length + STAT_ROWS, width), keys.dtype),
            pltpu.HBM((length + STAT_ROWS, width), keys.dtype),
            pltpu.VMEM((2, tokens, half), batch.dtype),
            pltpu.VMEM((1, half), gain.dtype),
            pltpu.VMEM((2, tokens, HD), jnp.float32),
        ],
        scratch_shapes=[
            pltpu.VMEM((2, length, width), keys.dtype),
            pltpu.VMEM((length + STAT_ROWS, width), keys.dtype),
            pltpu.VMEM(act_frames.shape, act_frames.dtype),
            pltpu.VMEM(fresh_frames.shape, fresh_frames.dtype),
            pltpu.VMEM(key_frames.shape, key_frames.dtype),
            pltpu.SemaphoreType.DMA((2, BLOCKS)),
            pltpu.SemaphoreType.DMA((BLOCKS,)),
            pltpu.SemaphoreType.DMA((6,)),
        ],
        cost_estimate=pl.CostEstimate(
            flops=0, bytes_accessed=4 * length * width, transcendentals=0
        ),
        compiler_params=pltpu.CompilerParams(vmem_limit_bytes=16 * MIB),
        name="load",
    )(
        where,
        *in_hbm(act_frames, fresh_frames, key_frames, keys, values, batch, fresh, gain),
    )


def body(
    activations,
    act_frames,
    fresh_batch,
    fresh_frames,
    norm_gain,
    cached_keys,
    cached_values,
    key_frames,
):
    section_index = lax.axis_index("section")
    ctx_index = lax.axis_index("ctx")
    pairs = lax.axis_size("ctx") // PAIR
    place, pair = ctx_index % PAIR, ctx_index // PAIR
    where = jnp.stack([place, pair, section_index == 0, section_index]).astype(jnp.int32)

    own, given, batches, gain, frames = load(
        where, act_frames, fresh_frames[None], key_frames.reshape(-1, HD), cached_keys[0],
        cached_values[0], activations[0], fresh_batch, norm_gain,
    )
    got = swapped(given)
    terms = begin(gain, frames, batches, own)
    _, tokens, half = batches.shape
    share = half // pairs
    chunks = handed_on(finish(where, frames, batches, *terms, got, pairs))
    handed = exchanged(combine(combine_kernel, chunks, pairs, tokens, share))
    chunks = exchanged(partials(where, gain, frames, batches, got, own, handed, pairs))
    operands = (where, chunks, batches, handed)
    mine = exchanged(combine(combine_last_kernel, operands, pairs, tokens, share))
    return assemble(where, mine, swapped(mine))[None]


def solution(mesh):
    placed = (
        P("section", None, None),
        P(),
        P(),
        P(),
        P("section", None),
        P("section", "ctx", None),
        P("section", "ctx", None),
        P("ctx"),
    )
    return jax.shard_map(
        body, mesh=mesh, in_specs=placed, out_specs=P("section", None, None), check_vma=False
    )
```

```python
import functools
import math

import jax
import jax.numpy as jnp
from jax import lax
from jax.experimental import pallas as pl
from jax.experimental.pallas import tpu as pltpu
from jax.sharding import PartitionSpec as P

HEADS = 64
HD = 128
PAIR = 2
INNER = 2
BLOCKS = 4
STAT_ROWS = 16
HIDDEN = -(2.0**100)
SCALE = HD**-0.5 * math.log2(math.e)
MIB = 1 << 20

epsilon = 1e-05

WHOLE = pl.BlockSpec(memory_space=pltpu.VMEM)
IN_HBM = pl.BlockSpec(memory_space=pltpu.HBM)


def in_hbm(*arrays):
    return [pltpu.with_memory_space_constraint(a, pltpu.HBM) for a in arrays]


def in_vmem(*arrays):
    return [pltpu.with_memory_space_constraint(a, pltpu.VMEM) for a in arrays]


def place_here():
    return lax.axis_index("ctx") % PAIR


def inner_here():
    return lax.axis_index("ctx") // PAIR % INNER


def outer_here():
    return lax.axis_index("ctx") // (PAIR * INNER)


def in_first_section():
    return lax.axis_index("section") == 0


def swapped(block):
    return lax.ppermute(block, "ctx", [(i, i ^ 1) for i in range(lax.axis_size("ctx"))])


def beside(i, step):
    block = INNER * PAIR
    return i // block * block + (i + PAIR * step) % block


def from_inner(block):
    return lax.ppermute(block, "ctx", [(i, beside(i, 1)) for i in range(lax.axis_size("ctx"))])


def from_outer(blocks):
    size = lax.axis_size("ctx")
    return [
        lax.ppermute(block, "ctx", [(i, (i + INNER * PAIR * (d + 1)) % size) for i in range(size)])
        for d, block in enumerate(blocks)
    ]


def from_section_before(block, step):
    sections, size = lax.axis_size("section"), lax.axis_size("ctx")
    route = [
        (s * size + i, (s + 1) * size + beside(i, step))
        for s in range(sections - 1)
        for i in range(size)
    ]
    return lax.ppermute(block, ("section", "ctx"), route)


def head_rows(block):
    return jnp.concatenate(
        [block[:, at : at + HD] for at in range(0, block.shape[1], HD)], axis=0
    )


def row_of(ref):
    return jnp.concatenate([ref[i : i + 1] for i in range(ref.shape[0])], axis=1)


def columns_of(index, ref, width):
    return ref.at[:, pl.ds(pl.multiple_of(index * width, HD), width)]


def on_diagonal(rows):
    shape = (rows, HD)
    return lax.broadcasted_iota(jnp.int32, shape, 0) == lax.broadcasted_iota(jnp.int32, shape, 1)


def queries_of(x, gain):
    rows = head_rows(x.astype(jnp.float32))
    gain = head_rows(jnp.broadcast_to(gain, x.shape))
    norm = lax.rsqrt(jnp.mean(rows * rows, axis=-1, keepdims=True) + epsilon)
    return (rows * norm * gain).astype(jnp.bfloat16)


def bias_of(keys_ref, frames):
    length = keys_ref.shape[0] - STAT_ROWS
    width = keys_ref.shape[1]
    rows = -(-length // width)
    tail = keys_ref[length:].astype(jnp.float32)
    key_frames = jnp.concatenate([tail[i : i + 1] for i in range(rows)], axis=1)[:, :length]
    return jnp.where(key_frames <= frames, 0.0, HIDDEN)[None]


def scores(queries, key_block, bias):
    count, keys, tokens = queries.shape[0], key_block.shape[0], bias.shape[1]
    raw = lax.dot_general(
        queries, key_block, (((1,), (1,)), ((), ())), preferred_element_type=jnp.float32
    )
    raw = raw.reshape(count // tokens, tokens, keys) * SCALE + bias
    return raw.reshape(count, keys)


def top_of(raw):
    top = jnp.max(raw, axis=-1, keepdims=True)
    return top.astype(jnp.bfloat16).astype(jnp.float32)


def weigh(raw, top, value_block):
    probs = jnp.exp2(raw - top).astype(jnp.bfloat16)
    ones = jnp.ones((value_block.shape[0], HD), jnp.bfloat16)
    return jnp.dot(
        probs, jnp.concatenate([value_block, ones], axis=1), preferred_element_type=jnp.float32
    )


def groups_of(count):
    groups = -(-count // HD)
    held = count // groups
    return [slice(c * held, (c + 1) * held) for c in range(groups)]


def write_chunk(out_ref, weighted, tops, totals):
    count = weighted.shape[0]
    line = lax.broadcasted_iota(jnp.int32, (STAT_ROWS, HD), 0)
    stats = jnp.zeros((STAT_ROWS, HD), jnp.float32)
    for c, (top, total) in enumerate(zip(tops, totals)):
        high = total.astype(jnp.bfloat16).astype(jnp.float32)
        for n, row in enumerate((top, high, total - high)):
            stats = jnp.where(line == 3 * c + n, row, stats)
    out_ref[:count] = weighted.astype(jnp.bfloat16)
    out_ref[count:] = stats.astype(jnp.bfloat16)


def write_sums(out_ref, weighted, top, total):
    groups = groups_of(weighted.shape[0])
    diagonal = on_diagonal(groups[0].stop)

    def rows(column):
        column = jnp.broadcast_to(column, weighted.shape)
        return [
            jnp.sum(jnp.where(diagonal, column[group], 0.0), axis=0, keepdims=True)
            for group in groups
        ]

    write_chunk(out_ref, weighted, rows(top), rows(total))


def joined(parts, normed):
    count = parts[0].shape[0] - STAT_ROWS
    groups = groups_of(count)
    diagonal = on_diagonal(groups[0].stop)
    stats = [part[count:].astype(jnp.float32) for part in parts]
    values, tops, totals = [], [], []
    for c, group in enumerate(groups):
        points = [s[3 * c : 3 * c + 1] for s in stats]
        top = functools.reduce(jnp.maximum, points)
        factors = [jnp.exp2(point - top) for point in points]
        total = sum(
            f * (s[3 * c + 1 : 3 * c + 2] + s[3 * c + 2 : 3 * c + 3])
            for f, s in zip(factors, stats)
        )
        if normed:
            inverse = 1.0 / total
            factors = [f * inverse for f in factors]
        value = 0.0
        for factor, part in zip(factors, parts):
            weight = jnp.where(diagonal, factor, 0.0)[:, : group.stop - group.start]
            high = weight.astype(jnp.bfloat16)
            low = (weight - high.astype(jnp.float32)).astype(jnp.bfloat16)
            for term in (high, low):
                value = value + jnp.dot(term, part[group], preferred_element_type=jnp.float32)
        values.append(value)
        tops.append(top)
        totals.append(total)
    return jnp.concatenate(values, axis=0), tops, totals


def stage(sources, own_ref, given_ref, staged_ref, gift_ref, sems, gift_sems, tail):
    length, width = staged_ref.shape
    half, step = width // PAIR, length // BLOCKS
    copies = []
    for b in range(BLOCKS):
        rows = pl.ds(b * step, step)
        copies.append(pltpu.make_async_copy(sources.at[rows], staged_ref.at[rows], sems.at[b]))
        copies[-1].start()
    yield
    if tail is not None:
        gift_ref[length:] = tail()
        own_ref[length:] = tail()
    place = place_here()
    gifts = []
    for b, copy in enumerate(copies):
        copy.wait()
        rows = pl.ds(b * step, step)
        gift_ref[rows] = columns_of(1 - place, staged_ref.at[rows], half)[...]
        own_ref[rows] = columns_of(place, staged_ref.at[rows], half)[...]
        if b == BLOCKS - 1:
            rows = pl.ds(b * step, gift_ref.shape[0] - b * step)
        gifts.append(pltpu.make_async_copy(gift_ref.at[rows], given_ref.at[rows], gift_sems.at[b]))
        gifts[-1].start()
    yield
    for gift in gifts:
        gift.wait()
    yield


def load_keys_kernel(
    key_frames_in, keys_in, own_ref, given_ref,
    key_frames_ref, staged_ref, gift_ref, sems, gift_sems, small_sem,
):
    length, half = staged_ref.shape[0], own_ref.shape[1]
    small = pltpu.make_async_copy(key_frames_in, key_frames_ref, small_sem)
    small.start()

    def tail():
        row = row_of(key_frames_ref).astype(jnp.float32)
        lines = -(-length // half)
        row = jnp.concatenate([row, jnp.zeros((1, lines * half - length), jnp.float32)], axis=1)
        line = lax.broadcasted_iota(jnp.int32, (STAT_ROWS, half), 0)
        lower = jnp.zeros((STAT_ROWS, half), jnp.float32)
        for n in range(lines):
            lower = jnp.where(line == n, row[:, n * half : (n + 1) * half], lower)
        return lower.astype(jnp.bfloat16)

    steps = stage(keys_in, own_ref, given_ref, staged_ref, gift_ref, sems, gift_sems, tail)
    next(steps)
    small.wait()
    next(steps)
    next(steps)


def load_keys(key_frames, keys):
    length, width = keys.shape
    shape = (length + STAT_ROWS, width // PAIR)
    return pl.pallas_call(
        load_keys_kernel,
        in_specs=[IN_HBM] * 2,
        out_specs=[WHOLE, IN_HBM],
        out_shape=[pltpu.VMEM(shape, keys.dtype), pltpu.HBM(shape, keys.dtype)],
        scratch_shapes=[
            pltpu.VMEM(key_frames.shape, key_frames.dtype),
            pltpu.VMEM((length, width), keys.dtype),
            pltpu.VMEM(shape, keys.dtype),
            pltpu.SemaphoreType.DMA((BLOCKS,)),
            pltpu.SemaphoreType.DMA((BLOCKS,)),
            pltpu.SemaphoreType.DMA,
        ],
        cost_estimate=pl.CostEstimate(
            flops=0, bytes_accessed=2 * length * width, transcendentals=0
        ),
        compiler_params=pltpu.CompilerParams(vmem_limit_bytes=16 * MIB),
        name="load_keys",
    )(*in_hbm(key_frames, keys))


def load_values_kernel(
    act_frames_in, fresh_frames_in, values_in, batch_in, fresh_in, gain_in,
    own_ref, given_ref, batches_ref, gain_ref, frames_ref,
    act_frames_ref, fresh_frames_ref, staged_ref, gift_ref, sems, gift_sems, small_sems,
):
    place, half = place_here(), gain_ref.shape[1]
    small = [
        (act_frames_in, act_frames_ref),
        (fresh_frames_in, fresh_frames_ref),
        (columns_of(place, batch_in, half), batches_ref.at[0]),
        (columns_of(place, gain_in, half), gain_ref),
        (columns_of(place, fresh_in, half), batches_ref.at[1]),
    ]
    small = [pltpu.make_async_copy(a, b, small_sems.at[n]) for n, (a, b) in enumerate(small)]
    for copy in small[:2]:
        copy.start()
    steps = stage(values_in, own_ref, given_ref, staged_ref, gift_ref, sems, gift_sems, None)
    next(steps)
    for copy in small[2:]:
        copy.start()
    for copy in small[:2]:
        copy.wait()

    tokens = frames_ref.shape[1]
    section = lax.axis_index("section")
    own_row = act_frames_ref[pl.ds(section, 1), :].astype(jnp.float32)
    prior_row = act_frames_ref[pl.ds(jnp.maximum(section - 1, 0), 1), :].astype(jnp.float32)
    fresh_row = fresh_frames_ref[...].astype(jnp.float32)
    next_row = jnp.where(in_first_section(), fresh_row, prior_row)
    shape = (tokens, tokens)
    diagonal = lax.broadcasted_iota(jnp.int32, shape, 0) == lax.broadcasted_iota(jnp.int32, shape, 1)
    for tick, row in enumerate((own_row, next_row)):
        column = jnp.sum(jnp.where(diagonal, row, 0.0), axis=1, keepdims=True)
        frames_ref[tick] = jnp.broadcast_to(column, (tokens, HD))

    next(steps)
    for copy in small[2:]:
        copy.wait()
    next(steps)


def load_values(act_frames, fresh_frames, values, batch, fresh, gain):
    length, width = values.shape
    tokens, model = batch.shape
    half = model // PAIR
    shape = (length, width // PAIR)
    return pl.pallas_call(
        load_values_kernel,
        in_specs=[IN_HBM] * 6,
        out_specs=[WHOLE, IN_HBM] + [WHOLE] * 3,
        out_shape=[
            pltpu.VMEM(shape, values.dtype),
            pltpu.HBM(shape, values.dtype),
            pltpu.VMEM((2, tokens, half), batch.dtype),
            pltpu.VMEM((1, half), gain.dtype),
            pltpu.VMEM((2, tokens, HD), jnp.float32),
        ],
        scratch_shapes=[
            pltpu.VMEM(act_frames.shape, act_frames.dtype),
            pltpu.VMEM(fresh_frames.shape, fresh_frames.dtype),
            pltpu.VMEM((length, width), values.dtype),
            pltpu.VMEM(shape, values.dtype),
            pltpu.SemaphoreType.DMA((BLOCKS,)),
            pltpu.SemaphoreType.DMA((BLOCKS,)),
            pltpu.SemaphoreType.DMA((5,)),
        ],
        cost_estimate=pl.CostEstimate(
            flops=0, bytes_accessed=2 * length * width, transcendentals=0
        ),
        compiler_params=pltpu.CompilerParams(vmem_limit_bytes=16 * MIB),
        name="load_values",
    )(*in_hbm(act_frames, fresh_frames, values, batch, fresh, gain))


def begin_kernel(
    gain_ref, frames_ref, batches_ref, keys_ref, values_ref,
    queries_ref, sums_ref, stats_ref, share_ref,
):
    length = values_ref.shape[0]
    kv_here = values_ref.shape[1] // HD
    count, width = queries_ref.shape[0] // kv_here, gain_ref.shape[1] // kv_here
    bias = bias_of(keys_ref, frames_ref[0, :, :1])
    share_ref[...] = columns_of(outer_here(), batches_ref.at[0], share_ref.shape[1])[...]
    for g in range(kv_here):
        rows, columns = slice(g * count, (g + 1) * count), slice(g * width, (g + 1) * width)
        block = slice(g * HD, (g + 1) * HD)
        queries = queries_of(batches_ref[0, :, columns], gain_ref[:, columns])
        queries_ref[rows] = queries
        raw = scores(queries, keys_ref[:length, block], bias)
        top = top_of(raw)
        both = weigh(raw, top, values_ref[:, block])
        sums_ref[rows] = both[:, :HD]
        lane = lax.broadcasted_iota(jnp.int32, (count, HD), 1)
        stats_ref[rows] = jnp.where(lane < HD // 2, top, both[:, HD:])


def begin(gain, frames, batches, keys, values):
    length, width = values.shape
    _, tokens, half = batches.shape
    queries = HEADS // PAIR * tokens
    return pl.pallas_call(
        begin_kernel,
        in_specs=[WHOLE] * 5,
        out_specs=[WHOLE] * 4,
        out_shape=[
            jax.ShapeDtypeStruct((queries, HD), jnp.bfloat16),
            jax.ShapeDtypeStruct((queries, HD), jnp.float32),
            jax.ShapeDtypeStruct((queries, HD), jnp.float32),
            jax.ShapeDtypeStruct((tokens, half * HD // width), batches.dtype),
        ],
        cost_estimate=pl.CostEstimate(
            flops=2 * queries * length * 3 * HD,
            bytes_accessed=4 * length * width,
            transcendentals=queries * length,
        ),
        compiler_params=pltpu.CompilerParams(vmem_limit_bytes=16 * MIB),
        name="begin",
    )(*in_vmem(gain, frames, batches, keys, values))


def chunk_shapes(count):
    shape = jax.ShapeDtypeStruct((count + STAT_ROWS, HD), jnp.bfloat16)
    return shape


def finish_kernel(
    frames_ref, queries_ref, sums_ref, stats_ref, keys_ref, values_ref, *out_refs
):
    length = values_ref.shape[0]
    kv_here, outer = len(out_refs), outer_here()
    count = queries_ref.shape[0] // kv_here
    bias = bias_of(keys_ref, frames_ref[0, :, :1])
    for d, out_ref in enumerate(out_refs):
        g = (outer + d) % kv_here
        rows = pl.ds(pl.multiple_of(g * count, count), count)
        raw = scores(queries_ref[rows], columns_of(g, keys_ref.at[:length], HD)[...], bias)
        stats = stats_ref[rows]
        before, totals = stats[:, :1], stats[:, HD // 2 : HD // 2 + 1]
        top = jnp.maximum(before, top_of(raw))
        factor = jnp.exp2(before - top)
        both = weigh(raw, top, columns_of(g, values_ref, HD)[...])
        weighted = both[:, :HD] + sums_ref[rows] * factor
        write_sums(out_ref, weighted, top, both[:, HD:] + totals * factor)


def finish(frames, queries, sums, stats, keys, values):
    length, width = values.shape
    count, kv_here = queries.shape[0], width // HD
    return pl.pallas_call(
        finish_kernel,
        in_specs=[WHOLE] * 6,
        out_specs=[WHOLE] * kv_here,
        out_shape=[chunk_shapes(count // kv_here)] * kv_here,
        cost_estimate=pl.CostEstimate(
            flops=2 * count * length * 3 * HD,
            bytes_accessed=4 * length * width,
            transcendentals=count * length,
        ),
        compiler_params=pltpu.CompilerParams(vmem_limit_bytes=16 * MIB),
        name="finish",
    )(*in_vmem(frames, queries, sums, stats, keys, values))


def partials_kernel(gain_ref, frames_ref, batches_ref, *refs):
    kv_refs, refs = (refs[0:2], refs[2:4]), refs[4:]
    kv_here = len(refs) // 2
    handed_refs, out_refs = refs[:kv_here], refs[kv_here:]
    length, outer, first = kv_refs[0][1].shape[0], outer_here(), in_first_section()
    width = gain_ref.shape[1] // kv_here
    frames = frames_ref[1, :, :1]
    biases = [bias_of(keys_ref, frames) for keys_ref, _ in kv_refs]
    for d, out_ref in enumerate(out_refs):
        g = (outer + d) % kv_here
        fresh = columns_of(g, batches_ref.at[1], width)[...].astype(jnp.float32)
        handed = handed_refs[(kv_here - d) % kv_here][...].astype(jnp.float32)
        x = jnp.where(first, fresh, handed)
        queries = queries_of(x, columns_of(g, gain_ref, width)[...])
        raws = [
            scores(queries, columns_of(g, keys_ref.at[:length], HD)[...], bias)
            for (keys_ref, _), bias in zip(kv_refs, biases)
        ]
        top = functools.reduce(jnp.maximum, [top_of(raw) for raw in raws])
        both = sum(
            weigh(raw, top, columns_of(g, values_ref, HD)[...])
            for raw, (_, values_ref) in zip(raws, kv_refs)
        )
        write_sums(out_ref, both[:, :HD], top, both[:, HD:])


def partials(gain, frames, batches, own, got, handed):
    length, width = own[1].shape
    _, tokens, half = batches.shape
    queries = HEADS // PAIR * tokens
    kv_here = width // HD
    return pl.pallas_call(
        partials_kernel,
        in_specs=[WHOLE] * (7 + kv_here),
        out_specs=[WHOLE] * kv_here,
        out_shape=[chunk_shapes(queries // kv_here)] * kv_here,
        cost_estimate=pl.CostEstimate(
            flops=2 * queries * PAIR * length * 3 * HD,
            bytes_accessed=8 * length * width,
            transcendentals=queries * PAIR * length,
        ),
        compiler_params=pltpu.CompilerParams(vmem_limit_bytes=16 * MIB),
        name="partials",
    )(*in_vmem(gain, frames, batches, *own, *got, *handed))


def merge_kernel(*refs):
    *parts, out_ref = refs
    write_chunk(out_ref, *joined(parts, False))


def merge(parts):
    return pl.pallas_call(
        merge_kernel,
        in_specs=[WHOLE] * len(parts),
        out_specs=WHOLE,
        out_shape=jax.ShapeDtypeStruct(parts[0].shape, parts[0].dtype),
        compiler_params=pltpu.CompilerParams(vmem_limit_bytes=8 * MIB),
        name="merge",
    )(*in_vmem(*parts))


def combined(one_ref, two_ref, x, out_ref):
    one, two = one_ref[...].astype(jnp.float32), two_ref[...].astype(jnp.float32)
    here = inner_here() == 0
    parts = [jnp.where(here, one, two), jnp.where(here, two, one)]
    attended, _, _ = joined([part.astype(jnp.bfloat16) for part in parts], True)
    total = head_rows(x.astype(jnp.float32)) + attended
    tokens = out_ref.shape[0]
    for h in range(total.shape[0] // tokens):
        piece = total[h * tokens : (h + 1) * tokens]
        out_ref[:, h * HD : (h + 1) * HD] = piece.astype(jnp.bfloat16)


def combine_kernel(one_ref, two_ref, share_ref, out_ref):
    combined(one_ref, two_ref, share_ref[...], out_ref)


def combine_last_kernel(one_ref, two_ref, batches_ref, handed_ref, out_ref):
    fresh = columns_of(outer_here(), batches_ref.at[1], out_ref.shape[1])[...]
    x = jnp.where(
        in_first_section(), fresh.astype(jnp.float32), handed_ref[...].astype(jnp.float32)
    )
    combined(one_ref, two_ref, x, out_ref)


def combine(kernel, one, two, *rest):
    return pl.pallas_call(
        kernel,
        in_specs=[WHOLE] * (2 + len(rest)),
        out_specs=WHOLE,
        out_shape=jax.ShapeDtypeStruct(rest[-1].shape, jnp.bfloat16),
        compiler_params=pltpu.CompilerParams(vmem_limit_bytes=8 * MIB),
        name="combine",
    )(*in_vmem(one, two, *rest))


def assemble_kernel(*refs):
    *pieces, out_ref = refs
    outers = len(pieces) // PAIR
    width = pieces[0].shape[1]
    for n, refs in enumerate((pieces[:outers], pieces[outers:])):
        place = (place_here() + n) % PAIR
        for d, ref in enumerate(refs):
            index = place * outers + (outer_here() + outers - d) % outers
            columns_of(index, out_ref, width)[...] = ref[...]


def assemble(mine, others):
    tokens, width = mine[0].shape
    pieces = [*mine, *others]
    return pl.pallas_call(
        assemble_kernel,
        in_specs=[WHOLE] * len(pieces),
        out_specs=WHOLE,
        out_shape=jax.ShapeDtypeStruct((tokens, len(pieces) * width), jnp.bfloat16),
        compiler_params=pltpu.CompilerParams(vmem_limit_bytes=8 * MIB),
        name="assemble",
    )(*in_vmem(*pieces))


def body(
    activations,
    act_frames,
    fresh_batch,
    fresh_frames,
    norm_gain,
    cached_keys,
    cached_values,
    key_frames,
):
    own_keys, given_keys = load_keys(key_frames.reshape(-1, HD), cached_keys[0])
    got_keys = swapped(given_keys)
    own_values, given_values, batches, gain, frames = load_values(
        act_frames, fresh_frames[None], cached_values[0], activations[0], fresh_batch, norm_gain
    )
    got_values = swapped(given_values)
    own, got = (own_keys, own_values), (got_keys, got_values)

    *terms, share = begin(gain, frames, batches, *own)
    share = from_section_before(share, 0)
    chunk, *others = finish(frames, *terms, *got)
    chunk = merge([chunk, *from_outer(others)])
    one, two = [from_section_before(chunk, step) for step in range(INNER)]
    handed = combine(combine_kernel, one, two, share)
    handed = [handed, *from_outer([handed] * (lax.axis_size("ctx") // (INNER * PAIR) - 1))]

    chunk, *others = partials(gain, frames, batches, own, got, handed)
    chunk = merge([chunk, *from_outer(others)])
    share = combine(combine_last_kernel, chunk, from_inner(chunk), batches, handed[0])
    mine = [share, *from_outer([share] * len(others))]
    return assemble(mine, [swapped(piece) for piece in mine])[None]


def solution(mesh):
    placed = (
        P("section", None, None),
        P(),
        P(),
        P(),
        P("section", None),
        P("section", "ctx", None),
        P("section", "ctx", None),
        P("ctx"),
    )
    return jax.shard_map(
        body, mesh=mesh, in_specs=placed, out_specs=P("section", None, None), check_vma=False
    )
```

```python
import functools
import math

import jax
import jax.numpy as jnp
from jax import lax
from jax.experimental import pallas as pl
from jax.experimental.pallas import tpu as pltpu
from jax.sharding import PartitionSpec as P

HEADS = 64
HD = 128
PAIR = 2
INNER = 2
BLOCKS = 4
STAT_ROWS = 16
HIDDEN = -(2.0**100)
SCALE = HD**-0.5 * math.log2(math.e)
MIB = 1 << 20

epsilon = 1e-05

WHOLE = pl.BlockSpec(memory_space=pltpu.VMEM)
IN_HBM = pl.BlockSpec(memory_space=pltpu.HBM)


def in_hbm(*arrays):
    return [pltpu.with_memory_space_constraint(a, pltpu.HBM) for a in arrays]


def in_vmem(*arrays):
    return [pltpu.with_memory_space_constraint(a, pltpu.VMEM) for a in arrays]


def place_here():
    return lax.axis_index("ctx") % PAIR


def inner_here():
    return lax.axis_index("ctx") // PAIR % INNER


def outer_here():
    return lax.axis_index("ctx") // (PAIR * INNER)


def in_first_section():
    return lax.axis_index("section") == 0


def swapped(block):
    return lax.ppermute(block, "ctx", [(i, i ^ 1) for i in range(lax.axis_size("ctx"))])


def beside(i, step):
    block = INNER * PAIR
    return i // block * block + (i + PAIR * step) % block


def from_inner(block):
    return lax.ppermute(block, "ctx", [(i, beside(i, 1)) for i in range(lax.axis_size("ctx"))])


def from_outer(blocks):
    size, block_size = lax.axis_size("ctx"), INNER * PAIR
    got = []
    for d, block in enumerate(blocks, 1):
        route = [(i, (i // block_size ^ d) * block_size + i % block_size) for i in range(size)]
        got.append(lax.ppermute(block, "ctx", route))
    return got


def from_section_before(block, step):
    sections, size = lax.axis_size("section"), lax.axis_size("ctx")
    route = [
        (s * size + i, (s + 1) * size + beside(i, step))
        for s in range(sections - 1)
        for i in range(size)
    ]
    return lax.ppermute(block, ("section", "ctx"), route)


def head_rows(block):
    return jnp.concatenate(
        [block[:, at : at + HD] for at in range(0, block.shape[1], HD)], axis=0
    )


def row_of(ref):
    return jnp.concatenate([ref[i : i + 1] for i in range(ref.shape[0])], axis=1)


def columns_of(index, ref, width):
    return ref.at[:, pl.ds(pl.multiple_of(index * width, HD), width)]


def on_diagonal(rows):
    shape = (rows, HD)
    return lax.broadcasted_iota(jnp.int32, shape, 0) == lax.broadcasted_iota(jnp.int32, shape, 1)


def queries_of(x, gain):
    rows = head_rows(x.astype(jnp.float32))
    gain = head_rows(jnp.broadcast_to(gain, x.shape))
    norm = lax.rsqrt(jnp.mean(rows * rows, axis=-1, keepdims=True) + epsilon)
    return (rows * norm * gain).astype(jnp.bfloat16)


def bias_of(keys_ref, frames):
    length = keys_ref.shape[0] - STAT_ROWS
    width = keys_ref.shape[1]
    rows = -(-length // width)
    tail = keys_ref[length:].astype(jnp.float32)
    key_frames = jnp.concatenate([tail[i : i + 1] for i in range(rows)], axis=1)[:, :length]
    return jnp.where(key_frames <= frames, 0.0, HIDDEN)[None]


def scores(queries, key_block, bias):
    count, keys, tokens = queries.shape[0], key_block.shape[0], bias.shape[1]
    raw = lax.dot_general(
        queries, key_block, (((1,), (1,)), ((), ())), preferred_element_type=jnp.float32
    )
    raw = raw.reshape(count // tokens, tokens, keys) * SCALE + bias
    return raw.reshape(count, keys)


def top_of(raw):
    top = jnp.max(raw, axis=-1, keepdims=True)
    return top.astype(jnp.bfloat16).astype(jnp.float32)


def weigh(raw, top, value_block):
    probs = jnp.exp2(raw - top).astype(jnp.bfloat16)
    ones = jnp.ones((value_block.shape[0], HD), jnp.bfloat16)
    return jnp.dot(
        probs, jnp.concatenate([value_block, ones], axis=1), preferred_element_type=jnp.float32
    )


def groups_of(count):
    groups = -(-count // HD)
    held = count // groups
    return [slice(c * held, (c + 1) * held) for c in range(groups)]


def write_chunk(out_ref, weighted, tops, totals):
    count = weighted.shape[0]
    line = lax.broadcasted_iota(jnp.int32, (STAT_ROWS, HD), 0)
    stats = jnp.zeros((STAT_ROWS, HD), jnp.float32)
    for c, (top, total) in enumerate(zip(tops, totals)):
        high = total.astype(jnp.bfloat16).astype(jnp.float32)
        for n, row in enumerate((top, high, total - high)):
            stats = jnp.where(line == 3 * c + n, row, stats)
    out_ref[:count] = weighted.astype(jnp.bfloat16)
    out_ref[count:] = stats.astype(jnp.bfloat16)


def write_sums(out_ref, weighted, top, total):
    groups = groups_of(weighted.shape[0])
    diagonal = on_diagonal(groups[0].stop)

    def rows(column):
        column = jnp.broadcast_to(column, weighted.shape)
        return [
            jnp.sum(jnp.where(diagonal, column[group], 0.0), axis=0, keepdims=True)
            for group in groups
        ]

    write_chunk(out_ref, weighted, rows(top), rows(total))


def joined(parts, normed, x=None):
    count = parts[0].shape[0] - STAT_ROWS
    groups = groups_of(count)
    diagonal = on_diagonal(groups[0].stop)
    stats = [part[count:].astype(jnp.float32) for part in parts]
    values, tops, totals = [], [], []
    for c, group in enumerate(groups):
        points = [s[3 * c : 3 * c + 1] for s in stats]
        top = functools.reduce(jnp.maximum, points)
        factors = [jnp.exp2(point - top) for point in points]
        total = sum(
            f * (s[3 * c + 1 : 3 * c + 2] + s[3 * c + 2 : 3 * c + 3])
            for f, s in zip(factors, stats)
        )
        if normed:
            inverse = 1.0 / total
            factors = [f * inverse for f in factors]
        terms = list(zip(factors, parts)) + ([] if x is None else [(total, x)])
        value = 0.0
        for factor, part in terms:
            weight = jnp.where(diagonal, factor, 0.0)[:, : group.stop - group.start]
            high = weight.astype(jnp.bfloat16)
            low = (weight - high.astype(jnp.float32)).astype(jnp.bfloat16)
            for term in (high, low):
                value = value + jnp.dot(term, part[group], preferred_element_type=jnp.float32)
        values.append(value)
        tops.append(top)
        totals.append(total)
    return jnp.concatenate(values, axis=0), tops, totals


def halve(staged_ref, copies, own_ref, given_ref, gift_ref, gift_sems, tail):
    length, width = staged_ref.shape
    half, step = width // PAIR, length // BLOCKS
    if tail is not None:
        gift_ref[length:] = tail()
        own_ref[length:] = tail()
    place = place_here()
    gifts = []
    for b in range(BLOCKS):
        if copies:
            copies[b].wait()
        rows = pl.ds(b * step, step)
        gift_ref[rows] = columns_of(1 - place, staged_ref.at[rows], half)[...]
        own_ref[rows] = columns_of(place, staged_ref.at[rows], half)[...]
        if b == BLOCKS - 1:
            rows = pl.ds(b * step, gift_ref.shape[0] - b * step)
        gifts.append(pltpu.make_async_copy(gift_ref.at[rows], given_ref.at[rows], gift_sems.at[b]))
        gifts[-1].start()
    return gifts


def load_keys_kernel(
    key_frames_in, keys_in, own_ref, given_ref,
    key_frames_ref, staged_ref, gift_ref, sems, gift_sems, small_sem,
):
    length, half = staged_ref.shape[0], own_ref.shape[1]
    small = pltpu.make_async_copy(key_frames_in, key_frames_ref, small_sem)
    small.start()

    def tail():
        row = row_of(key_frames_ref).astype(jnp.float32)
        lines = -(-length // half)
        row = jnp.concatenate([row, jnp.zeros((1, lines * half - length), jnp.float32)], axis=1)
        line = lax.broadcasted_iota(jnp.int32, (STAT_ROWS, half), 0)
        lower = jnp.zeros((STAT_ROWS, half), jnp.float32)
        for n in range(lines):
            lower = jnp.where(line == n, row[:, n * half : (n + 1) * half], lower)
        return lower.astype(jnp.bfloat16)

    copies, step = [], length // BLOCKS
    for b in range(BLOCKS):
        rows = pl.ds(b * step, step)
        copies.append(pltpu.make_async_copy(keys_in.at[rows], staged_ref.at[rows], sems.at[b]))
        copies[-1].start()
    small.wait()
    for gift in halve(staged_ref, copies, own_ref, given_ref, gift_ref, gift_sems, tail):
        gift.wait()


def load_keys(key_frames, keys):
    length, width = keys.shape
    shape = (length + STAT_ROWS, width // PAIR)
    return pl.pallas_call(
        load_keys_kernel,
        in_specs=[IN_HBM] * 2,
        out_specs=[WHOLE, IN_HBM],
        out_shape=[pltpu.VMEM(shape, keys.dtype), pltpu.HBM(shape, keys.dtype)],
        scratch_shapes=[
            pltpu.VMEM(key_frames.shape, key_frames.dtype),
            pltpu.VMEM((length, width), keys.dtype),
            pltpu.VMEM(shape, keys.dtype),
            pltpu.SemaphoreType.DMA((BLOCKS,)),
            pltpu.SemaphoreType.DMA((BLOCKS,)),
            pltpu.SemaphoreType.DMA,
        ],
        cost_estimate=pl.CostEstimate(
            flops=0, bytes_accessed=2 * length * width, transcendentals=0
        ),
        compiler_params=pltpu.CompilerParams(vmem_limit_bytes=16 * MIB),
        name="load_keys",
    )(*in_hbm(key_frames, keys))


def load_values_kernel(
    values_ref, act_frames_in, fresh_frames_in, batch_in, fresh_in, gain_in,
    own_ref, given_ref, batches_ref, gain_ref, frames_ref,
    act_frames_ref, fresh_frames_ref, gift_ref, gift_sems, small_sems,
):
    place, half = place_here(), gain_ref.shape[1]
    small = [
        (act_frames_in, act_frames_ref),
        (fresh_frames_in, fresh_frames_ref),
        (columns_of(place, batch_in, half), batches_ref.at[0]),
        (columns_of(place, gain_in, half), gain_ref),
        (columns_of(place, fresh_in, half), batches_ref.at[1]),
    ]
    small = [pltpu.make_async_copy(a, b, small_sems.at[n]) for n, (a, b) in enumerate(small)]
    for copy in small:
        copy.start()
    gifts = halve(values_ref, [], own_ref, given_ref, gift_ref, gift_sems, None)
    for copy in small[:2]:
        copy.wait()

    tokens = frames_ref.shape[1]
    section = lax.axis_index("section")
    own_row = act_frames_ref[pl.ds(section, 1), :].astype(jnp.float32)
    prior_row = act_frames_ref[pl.ds(jnp.maximum(section - 1, 0), 1), :].astype(jnp.float32)
    fresh_row = fresh_frames_ref[...].astype(jnp.float32)
    next_row = jnp.where(in_first_section(), fresh_row, prior_row)
    shape = (tokens, tokens)
    diagonal = lax.broadcasted_iota(jnp.int32, shape, 0) == lax.broadcasted_iota(jnp.int32, shape, 1)
    for tick, row in enumerate((own_row, next_row)):
        column = jnp.sum(jnp.where(diagonal, row, 0.0), axis=1, keepdims=True)
        frames_ref[tick] = jnp.broadcast_to(column, (tokens, HD))

    for copy in small[2:] + gifts:
        copy.wait()


def load_values(act_frames, fresh_frames, values, batch, fresh, gain):
    length, width = values.shape
    tokens, model = batch.shape
    half = model // PAIR
    shape = (length, width // PAIR)
    return pl.pallas_call(
        load_values_kernel,
        in_specs=[WHOLE] + [IN_HBM] * 5,
        out_specs=[WHOLE, IN_HBM] + [WHOLE] * 3,
        out_shape=[
            pltpu.VMEM(shape, values.dtype),
            pltpu.HBM(shape, values.dtype),
            pltpu.VMEM((2, tokens, half), batch.dtype),
            pltpu.VMEM((1, half), gain.dtype),
            pltpu.VMEM((2, tokens, HD), jnp.float32),
        ],
        scratch_shapes=[
            pltpu.VMEM(act_frames.shape, act_frames.dtype),
            pltpu.VMEM(fresh_frames.shape, fresh_frames.dtype),
            pltpu.VMEM(shape, values.dtype),
            pltpu.SemaphoreType.DMA((BLOCKS,)),
            pltpu.SemaphoreType.DMA((5,)),
        ],
        cost_estimate=pl.CostEstimate(
            flops=0, bytes_accessed=2 * length * width, transcendentals=0
        ),
        compiler_params=pltpu.CompilerParams(vmem_limit_bytes=16 * MIB),
        name="load_values",
    )(*in_vmem(values), *in_hbm(act_frames, fresh_frames, batch, fresh, gain))


def begin_kernel(
    gain_ref, frames_ref, batches_ref, keys_ref, values_ref,
    queries_ref, sums_ref, stats_ref, share_ref,
):
    length = values_ref.shape[0]
    kv_here = values_ref.shape[1] // HD
    count, width = queries_ref.shape[0] // kv_here, gain_ref.shape[1] // kv_here
    bias = bias_of(keys_ref, frames_ref[0, :, :1])
    share_ref[...] = columns_of(outer_here(), batches_ref.at[0], share_ref.shape[1])[...]
    for g in range(kv_here):
        rows, columns = slice(g * count, (g + 1) * count), slice(g * width, (g + 1) * width)
        block = slice(g * HD, (g + 1) * HD)
        queries = queries_of(batches_ref[0, :, columns], gain_ref[:, columns])
        queries_ref[rows] = queries
        raw = scores(queries, keys_ref[:length, block], bias)
        top = top_of(raw)
        both = weigh(raw, top, values_ref[:, block])
        sums_ref[rows] = both[:, :HD]
        lane = lax.broadcasted_iota(jnp.int32, (count, HD), 1)
        stats_ref[rows] = jnp.where(lane < HD // 2, top, both[:, HD:])


def begin(gain, frames, batches, keys, values):
    length, width = values.shape
    _, tokens, half = batches.shape
    queries = HEADS // PAIR * tokens
    return pl.pallas_call(
        begin_kernel,
        in_specs=[WHOLE] * 5,
        out_specs=[WHOLE] * 4,
        out_shape=[
            jax.ShapeDtypeStruct((queries, HD), jnp.bfloat16),
            jax.ShapeDtypeStruct((queries, HD), jnp.float32),
            jax.ShapeDtypeStruct((queries, HD), jnp.float32),
            jax.ShapeDtypeStruct((tokens, half * HD // width), batches.dtype),
        ],
        cost_estimate=pl.CostEstimate(
            flops=2 * queries * length * 3 * HD,
            bytes_accessed=4 * length * width,
            transcendentals=queries * length,
        ),
        compiler_params=pltpu.CompilerParams(vmem_limit_bytes=16 * MIB),
        name="begin",
    )(*in_vmem(gain, frames, batches, keys, values))


def chunk_shapes(count):
    shape = jax.ShapeDtypeStruct((count + STAT_ROWS, HD), jnp.bfloat16)
    return shape


def finish_kernel(
    frames_ref, queries_ref, sums_ref, stats_ref, keys_ref, values_ref, *out_refs
):
    length = values_ref.shape[0]
    kv_here, outer = len(out_refs), outer_here()
    count = queries_ref.shape[0] // kv_here
    bias = bias_of(keys_ref, frames_ref[0, :, :1])
    for d, out_ref in enumerate(out_refs):
        g = outer ^ d
        rows = pl.ds(pl.multiple_of(g * count, count), count)
        raw = scores(queries_ref[rows], columns_of(g, keys_ref.at[:length], HD)[...], bias)
        stats = stats_ref[rows]
        before, totals = stats[:, :1], stats[:, HD // 2 : HD // 2 + 1]
        top = jnp.maximum(before, top_of(raw))
        factor = jnp.exp2(before - top)
        both = weigh(raw, top, columns_of(g, values_ref, HD)[...])
        weighted = both[:, :HD] + sums_ref[rows] * factor
        write_sums(out_ref, weighted, top, both[:, HD:] + totals * factor)


def finish(frames, queries, sums, stats, keys, values):
    length, width = values.shape
    count, kv_here = queries.shape[0], width // HD
    return pl.pallas_call(
        finish_kernel,
        in_specs=[WHOLE] * 6,
        out_specs=[WHOLE] * kv_here,
        out_shape=[chunk_shapes(count // kv_here)] * kv_here,
        cost_estimate=pl.CostEstimate(
            flops=2 * count * length * 3 * HD,
            bytes_accessed=4 * length * width,
            transcendentals=count * length,
        ),
        compiler_params=pltpu.CompilerParams(vmem_limit_bytes=16 * MIB),
        name="finish",
    )(*in_vmem(frames, queries, sums, stats, keys, values))


def partials_kernel(gain_ref, frames_ref, batches_ref, *refs):
    kv_refs, refs = (refs[0:2], refs[2:4]), refs[4:]
    kv_here = len(refs) // 2
    handed_refs, out_refs = refs[:kv_here], refs[kv_here:]
    length, outer, first = kv_refs[0][1].shape[0], outer_here(), in_first_section()
    width = gain_ref.shape[1] // kv_here
    frames = frames_ref[1, :, :1]
    biases = [bias_of(keys_ref, frames) for keys_ref, _ in kv_refs]
    for d, out_ref in enumerate(out_refs):
        g = outer ^ d
        fresh = columns_of(g, batches_ref.at[1], width)[...].astype(jnp.float32)
        handed = handed_refs[d][...].astype(jnp.float32)
        x = jnp.where(first, fresh, handed)
        queries = queries_of(x, columns_of(g, gain_ref, width)[...])
        raws = [
            scores(queries, columns_of(g, keys_ref.at[:length], HD)[...], bias)
            for (keys_ref, _), bias in zip(kv_refs, biases)
        ]
        top = functools.reduce(jnp.maximum, [top_of(raw) for raw in raws])
        both = sum(
            weigh(raw, top, columns_of(g, values_ref, HD)[...])
            for raw, (_, values_ref) in zip(raws, kv_refs)
        )
        write_sums(out_ref, both[:, :HD], top, both[:, HD:])


def partials(gain, frames, batches, own, got, handed):
    length, width = own[1].shape
    _, tokens, half = batches.shape
    queries = HEADS // PAIR * tokens
    kv_here = width // HD
    return pl.pallas_call(
        partials_kernel,
        in_specs=[WHOLE] * (7 + kv_here),
        out_specs=[WHOLE] * kv_here,
        out_shape=[chunk_shapes(queries // kv_here)] * kv_here,
        cost_estimate=pl.CostEstimate(
            flops=2 * queries * PAIR * length * 3 * HD,
            bytes_accessed=8 * length * width,
            transcendentals=queries * PAIR * length,
        ),
        compiler_params=pltpu.CompilerParams(vmem_limit_bytes=16 * MIB),
        name="partials",
    )(*in_vmem(gain, frames, batches, *own, *got, *handed))


def merge_kernel(*refs):
    *parts, out_ref = refs
    write_chunk(out_ref, *joined(parts, False))


def merge_first_kernel(*refs):
    *parts, share_ref, out_ref = refs
    x = head_rows(share_ref[...].astype(jnp.float32)).astype(jnp.bfloat16)
    write_chunk(out_ref, *joined(parts, False, x))


def merge(kernel, *parts):
    return pl.pallas_call(
        kernel,
        in_specs=[WHOLE] * len(parts),
        out_specs=WHOLE,
        out_shape=jax.ShapeDtypeStruct(parts[0].shape, parts[0].dtype),
        compiler_params=pltpu.CompilerParams(vmem_limit_bytes=8 * MIB),
        name="merge",
    )(*in_vmem(*parts))


def combined(one_ref, two_ref, x, out_ref):
    one, two = one_ref[...].astype(jnp.float32), two_ref[...].astype(jnp.float32)
    here = inner_here() == 0
    parts = [jnp.where(here, one, two), jnp.where(here, two, one)]
    total, _, _ = joined([part.astype(jnp.bfloat16) for part in parts], True)
    if x is not None:
        total = head_rows(x) + total
    tokens = out_ref.shape[0]
    for h in range(total.shape[0] // tokens):
        piece = total[h * tokens : (h + 1) * tokens]
        out_ref[:, h * HD : (h + 1) * HD] = piece.astype(jnp.bfloat16)


def combine_kernel(one_ref, two_ref, out_ref):
    combined(one_ref, two_ref, None, out_ref)


def combine_last_kernel(one_ref, two_ref, batches_ref, handed_ref, out_ref):
    fresh = columns_of(outer_here(), batches_ref.at[1], out_ref.shape[1])[...]
    x = jnp.where(
        in_first_section(), fresh.astype(jnp.float32), handed_ref[...].astype(jnp.float32)
    )
    combined(one_ref, two_ref, x, out_ref)


def combine(kernel, tokens, one, two, *rest):
    width = (one.shape[0] - STAT_ROWS) // tokens * HD
    return pl.pallas_call(
        kernel,
        in_specs=[WHOLE] * (2 + len(rest)),
        out_specs=WHOLE,
        out_shape=jax.ShapeDtypeStruct((tokens, width), jnp.bfloat16),
        compiler_params=pltpu.CompilerParams(vmem_limit_bytes=8 * MIB),
        name="combine",
    )(*in_vmem(one, two, *rest))


def assemble_kernel(mine_ref, others_ref, out_ref):
    outers, _, width = mine_ref.shape
    for n, ref in enumerate((mine_ref, others_ref)):
        place = (place_here() + n) % PAIR
        for d in range(outers):
            columns_of(place * outers + (outer_here() ^ d), out_ref, width)[...] = ref[d]


def assemble(mine, others):
    outers, tokens, width = mine.shape
    return pl.pallas_call(
        assemble_kernel,
        in_specs=[WHOLE] * 2,
        out_specs=WHOLE,
        out_shape=jax.ShapeDtypeStruct((tokens, PAIR * outers * width), jnp.bfloat16),
        compiler_params=pltpu.CompilerParams(vmem_limit_bytes=8 * MIB),
        name="assemble",
    )(*in_vmem(mine, others))


def body(
    activations,
    act_frames,
    fresh_batch,
    fresh_frames,
    norm_gain,
    cached_keys,
    cached_values,
    key_frames,
):
    own_keys, given_keys = load_keys(key_frames.reshape(-1, HD), cached_keys[0])
    got_keys = swapped(given_keys)
    own_values, given_values, batches, gain, frames = load_values(
        act_frames, fresh_frames[None], cached_values[0], activations[0], fresh_batch, norm_gain
    )
    got_values = swapped(given_values)
    own, got = (own_keys, own_values), (got_keys, got_values)

    tokens = fresh_batch.shape[0]
    *terms, share = begin(gain, frames, batches, *own)
    chunk, *others = finish(frames, *terms, *got)
    chunk = merge(merge_first_kernel, chunk, *from_outer(others), share)
    one, two = [from_section_before(chunk, step) for step in range(INNER)]
    handed = combine(combine_kernel, tokens, one, two)
    handed = [handed, *from_outer([handed] * len(others))]

    chunk, *others = partials(gain, frames, batches, own, got, handed)
    chunk = merge(merge_kernel, chunk, *from_outer(others))
    share = combine(combine_last_kernel, tokens, chunk, from_inner(chunk), batches, handed[0])
    mine = jnp.stack([share, *from_outer([share] * len(others))])
    return assemble(mine, swapped(mine))[None]


def solution(mesh):
    placed = (
        P("section", None, None),
        P(),
        P(),
        P(),
        P("section", None),
        P("section", "ctx", None),
        P("section", "ctx", None),
        P("ctx"),
    )
    return jax.shard_map(
        body, mesh=mesh, in_specs=placed, out_specs=P("section", None, None), check_vma=False
    )
```

```python
import functools
import math

import jax
import jax.numpy as jnp
from jax import lax
from jax.experimental import pallas as pl
from jax.experimental.pallas import tpu as pltpu
from jax.sharding import PartitionSpec as P

HEADS = 64
HD = 128
PAIR = 2
INNER = 2
BLOCKS = 4
STAT_ROWS = 16
HIDDEN = -(2.0**100)
SCALE = HD**-0.5 * math.log2(math.e)
MIB = 1 << 20

epsilon = 1e-05

WHOLE = pl.BlockSpec(memory_space=pltpu.VMEM)
IN_HBM = pl.BlockSpec(memory_space=pltpu.HBM)


def in_hbm(*arrays):
    return [pltpu.with_memory_space_constraint(a, pltpu.HBM) for a in arrays]


def in_vmem(*arrays):
    return [pltpu.with_memory_space_constraint(a, pltpu.VMEM) for a in arrays]


def place_here():
    return lax.axis_index("ctx") % PAIR


def inner_here():
    return lax.axis_index("ctx") // PAIR % INNER


def outer_here():
    return lax.axis_index("ctx") // (PAIR * INNER)


def in_first_section():
    return lax.axis_index("section") == 0


def swapped(block):
    return lax.ppermute(block, "ctx", [(i, i ^ 1) for i in range(lax.axis_size("ctx"))])


def from_inner(block):
    return lax.ppermute(block, "ctx", [(i, i ^ PAIR) for i in range(lax.axis_size("ctx"))])


def across(i, d):
    return i ^ (INNER * PAIR * d)


def from_outer(blocks):
    size = lax.axis_size("ctx")
    return [
        lax.ppermute(block, "ctx", [(i, across(i, d)) for i in range(size)])
        for d, block in enumerate(blocks, 1)
    ]


def from_section_before(blocks):
    sections, size = lax.axis_size("section"), lax.axis_size("ctx")
    got = []
    for d, block in enumerate(blocks):
        route = [
            (s * size + i, (s + 1) * size + across(i, d))
            for s in range(sections - 1)
            for i in range(size)
        ]
        got.append(lax.ppermute(block, ("section", "ctx"), route))
    return got


def head_rows(block):
    return jnp.concatenate(
        [block[:, at : at + HD] for at in range(0, block.shape[1], HD)], axis=0
    )


def row_of(ref):
    return jnp.concatenate([ref[i : i + 1] for i in range(ref.shape[0])], axis=1)


def columns_of(index, ref, width):
    return ref.at[:, pl.ds(pl.multiple_of(index * width, HD), width)]


def on_diagonal(rows):
    shape = (rows, HD)
    return lax.broadcasted_iota(jnp.int32, shape, 0) == lax.broadcasted_iota(jnp.int32, shape, 1)


def queries_of(x, gain):
    rows = head_rows(x.astype(jnp.float32))
    gain = head_rows(jnp.broadcast_to(gain, x.shape))
    norm = lax.rsqrt(jnp.mean(rows * rows, axis=-1, keepdims=True) + epsilon)
    return (rows * norm * gain).astype(jnp.bfloat16)


def bias_of(key_frames, frames):
    return jnp.where(key_frames <= frames, 0.0, HIDDEN)[None]


def column_of(row):
    shape = (row.shape[1], row.shape[1])
    diagonal = lax.broadcasted_iota(jnp.int32, shape, 0) == lax.broadcasted_iota(jnp.int32, shape, 1)
    return jnp.sum(jnp.where(diagonal, row, 0.0), axis=1, keepdims=True)


def scores(queries, key_block, bias):
    count, keys, tokens = queries.shape[0], key_block.shape[0], bias.shape[1]
    raw = lax.dot_general(
        queries, key_block, (((1,), (1,)), ((), ())), preferred_element_type=jnp.float32
    )
    raw = raw.reshape(count // tokens, tokens, keys) * SCALE + bias
    return raw.reshape(count, keys)


def top_of(raw):
    top = jnp.max(raw, axis=-1, keepdims=True)
    return top.astype(jnp.bfloat16).astype(jnp.float32)


def probs_of(raw, top):
    return jnp.exp2(raw - top).astype(jnp.bfloat16)


def weigh(probs, value_block):
    ones = jnp.ones((value_block.shape[0], HD), jnp.bfloat16)
    return jnp.dot(
        probs, jnp.concatenate([value_block, ones], axis=1), preferred_element_type=jnp.float32
    )


def groups_of(count):
    groups = -(-count // HD)
    held = count // groups
    return [slice(c * held, (c + 1) * held) for c in range(groups)]


def write_chunk(out_ref, weighted, tops, totals):
    count = weighted.shape[0]
    line = lax.broadcasted_iota(jnp.int32, (STAT_ROWS, HD), 0)
    stats = jnp.zeros((STAT_ROWS, HD), jnp.float32)
    for c, (top, total) in enumerate(zip(tops, totals)):
        high = total.astype(jnp.bfloat16).astype(jnp.float32)
        for n, row in enumerate((top, high, total - high)):
            stats = jnp.where(line == 3 * c + n, row, stats)
    out_ref[:count] = weighted.astype(jnp.bfloat16)
    out_ref[count:] = stats.astype(jnp.bfloat16)


def write_sums(out_ref, weighted, top, total):
    groups = groups_of(weighted.shape[0])
    diagonal = on_diagonal(groups[0].stop)

    def rows(column):
        column = jnp.broadcast_to(column, weighted.shape)
        return [
            jnp.sum(jnp.where(diagonal, column[group], 0.0), axis=0, keepdims=True)
            for group in groups
        ]

    write_chunk(out_ref, weighted, rows(top), rows(total))


def joined(parts, normed, x=None):
    count = parts[0].shape[0] - STAT_ROWS
    groups = groups_of(count)
    diagonal = on_diagonal(groups[0].stop)
    stats = [part[count:].astype(jnp.float32) for part in parts]
    values, tops, totals = [], [], []
    for c, group in enumerate(groups):
        points = [s[3 * c : 3 * c + 1] for s in stats]
        top = functools.reduce(jnp.maximum, points)
        factors = [jnp.exp2(point - top) for point in points]
        total = sum(
            f * (s[3 * c + 1 : 3 * c + 2] + s[3 * c + 2 : 3 * c + 3])
            for f, s in zip(factors, stats)
        )
        if normed:
            inverse = 1.0 / total
            factors = [f * inverse for f in factors]
        terms = list(zip(factors, parts)) + ([] if x is None else [(total, x)])
        value = 0.0
        for factor, part in terms:
            weight = jnp.where(diagonal, factor, 0.0)[:, : group.stop - group.start]
            high = weight.astype(jnp.bfloat16)
            low = (weight - high.astype(jnp.float32)).astype(jnp.bfloat16)
            for term in (high, low):
                value = value + jnp.dot(term, part[group], preferred_element_type=jnp.float32)
        values.append(value)
        tops.append(top)
        totals.append(total)
    return jnp.concatenate(values, axis=0), tops, totals


def row_copies(source, target, sems):
    rows = source.shape[0]
    step = rows // BLOCKS // STAT_ROWS * STAT_ROWS
    blocks = [pl.ds(b * step, step if b < BLOCKS - 1 else rows - b * step) for b in range(BLOCKS)]
    return [
        pltpu.make_async_copy(source.at[rows], target.at[rows], sems.at[b])
        for b, rows in enumerate(blocks)
    ]


def first_kernel(
    act_frames_in, fresh_frames_in, key_frames_in, batch_in, gain_in, fresh_in, keys_in, values_in,
    mine_ref, theirs_ref, half_ref, own_ref, given_ref, fresh_ref, gain_half_ref, frames_ref,
    act_frames_ref, fresh_frames_ref, key_frames_ref, batch_ref, gain_ref, keys_ref, values_ref,
    gift_ref, small_sems, key_sems, value_sems, gift_sems,
):
    place, kv_here, model_half = place_here(), mine_ref.shape[0], half_ref.shape[1]
    length, width = keys_ref.shape
    small = [
        (act_frames_in, act_frames_ref),
        (fresh_frames_in, fresh_frames_ref),
        (key_frames_in, key_frames_ref),
        (batch_in, batch_ref),
        (gain_in, gain_ref),
        (columns_of(place, fresh_in, model_half), fresh_ref),
    ]
    small = [pltpu.make_async_copy(a, b, small_sems.at[n]) for n, (a, b) in enumerate(small)]
    key_copies = row_copies(keys_in, keys_ref, key_sems)
    value_copies = row_copies(values_in, values_ref, value_sems)
    for copy in small[:-1] + key_copies + value_copies + small[-1:]:
        copy.start()
    for copy in small[:-1]:
        copy.wait()

    half_ref[...] = columns_of(place, batch_ref, model_half)[...]
    gain_half_ref[...] = columns_of(place, gain_ref, model_half)[...]
    section = lax.axis_index("section")
    prior = act_frames_ref[pl.ds(jnp.maximum(section - 1, 0), 1), :].astype(jnp.float32)
    row = jnp.where(in_first_section(), fresh_frames_ref[...].astype(jnp.float32), prior)
    frames_ref[...] = jnp.broadcast_to(column_of(row), frames_ref.shape)
    row = act_frames_ref[pl.ds(section, 1), :].astype(jnp.float32)
    key_frames = row_of(key_frames_ref).astype(jnp.float32)
    bias = bias_of(key_frames, column_of(row))
    line = lax.broadcasted_iota(jnp.int32, (STAT_ROWS, length), 0)
    tail = jnp.where(line == 0, jnp.broadcast_to(key_frames, line.shape), 0.0)
    tail = jnp.concatenate(
        [tail.astype(jnp.bfloat16), jnp.zeros((STAT_ROWS, width - length), jnp.bfloat16)], axis=1
    )
    for ref in (gift_ref, own_ref):
        ref[length:] = tail

    def halve(n, ref):
        part = width // PAIR
        columns = slice(n * part, (n + 1) * part)
        gift_ref[:length, columns] = columns_of(1 - place, ref, part)[...]
        own_ref[:length, columns] = columns_of(place, ref, part)[...]

    order = [
        ((place + 1 + n) % PAIR * kv_here + g, out, g)
        for n, out in enumerate((theirs_ref, mine_ref))
        for g in range(kv_here)
    ]
    columns = model_half // kv_here

    def scored(h):
        x, gain = columns_of(h, batch_ref, columns)[...], columns_of(h, gain_ref, columns)[...]
        raw = scores(queries_of(x, gain), columns_of(h, keys_ref, HD)[...], bias)
        top = top_of(raw)
        return top, probs_of(raw, top)

    def summed(h, out, g, top, probs):
        both = weigh(probs, columns_of(h, values_ref, HD)[...])
        write_sums(out.at[g], both[:, :HD], top, both[:, HD:])

    for copy in key_copies:
        copy.wait()
    halve(0, keys_ref)
    early = [scored(h) for h, _, _ in order[:kv_here]]
    for copy in value_copies:
        copy.wait()
    halve(1, values_ref)
    gifts = row_copies(gift_ref, given_ref, gift_sems)
    for gift in gifts:
        gift.start()
    for (h, out, g), terms in zip(order, early):
        summed(h, out, g, *terms)
    for h, out, g in order[kv_here:]:
        summed(h, out, g, *scored(h))
    for copy in small[-1:] + gifts:
        copy.wait()


def first(act_frames, fresh_frames, key_frames, batch, gain, fresh, keys, values):
    length, width = keys.shape
    tokens, model = batch.shape
    kv_here = width // HD // PAIR
    queries = HEADS // PAIR * tokens
    sums = pltpu.VMEM((kv_here, queries // kv_here + STAT_ROWS, HD), jnp.bfloat16)
    shape = (length + STAT_ROWS, width)
    small = (act_frames, fresh_frames, key_frames, batch, gain)
    return pl.pallas_call(
        first_kernel,
        in_specs=[IN_HBM] * 8,
        out_specs=[WHOLE] * 4 + [IN_HBM] + [WHOLE] * 3,
        out_shape=[
            sums,
            sums,
            pltpu.VMEM((tokens, model // PAIR), batch.dtype),
            pltpu.VMEM(shape, keys.dtype),
            pltpu.HBM(shape, keys.dtype),
            pltpu.VMEM((tokens, model // PAIR), fresh.dtype),
            pltpu.VMEM((1, model // PAIR), gain.dtype),
            pltpu.VMEM((tokens, HD), jnp.float32),
        ],
        scratch_shapes=[
            *(pltpu.VMEM(a.shape, a.dtype) for a in small),
            pltpu.VMEM((length, width), keys.dtype),
            pltpu.VMEM((length, width), values.dtype),
            pltpu.VMEM(shape, keys.dtype),
            pltpu.SemaphoreType.DMA((6,)),
            pltpu.SemaphoreType.DMA((BLOCKS,)),
            pltpu.SemaphoreType.DMA((BLOCKS,)),
            pltpu.SemaphoreType.DMA((BLOCKS,)),
        ],
        cost_estimate=pl.CostEstimate(
            flops=2 * queries * PAIR * length * 3 * HD,
            bytes_accessed=8 * length * width,
            transcendentals=queries * PAIR * length,
        ),
        compiler_params=pltpu.CompilerParams(vmem_limit_bytes=24 * MIB),
        name="first",
    )(*in_hbm(*small, fresh, keys, values))


def merge_first_kernel(mine_ref, got_ref, half_ref, *out_refs):
    width = half_ref.shape[1] // mine_ref.shape[0]
    for d, out_ref in enumerate(out_refs):
        g = outer_here() ^ d
        x = columns_of(g, half_ref, width)[...].astype(jnp.float32)
        x = head_rows(x).astype(jnp.bfloat16)
        write_chunk(out_ref, *joined([mine_ref.at[g], got_ref.at[g]], False, x))


def merge_first(mine, got, half):
    kv_here, rows, _ = mine.shape
    return pl.pallas_call(
        merge_first_kernel,
        in_specs=[WHOLE] * 3,
        out_specs=[WHOLE] * kv_here,
        out_shape=[jax.ShapeDtypeStruct((rows, HD), mine.dtype)] * kv_here,
        compiler_params=pltpu.CompilerParams(vmem_limit_bytes=8 * MIB),
        name="merge_first",
    )(*in_vmem(mine, got, half))


def kv_block(ref, g, values):
    index = values * (ref.shape[1] // HD // 2) + g
    return columns_of(index, ref.at[: ref.shape[0] - STAT_ROWS], HD)[...]


def key_frames_of(ref):
    length = ref.shape[0] - STAT_ROWS
    return ref[length:, :length].astype(jnp.float32)[0:1]


def partials_kernel(gain_ref, frames_ref, fresh_ref, own_ref, got_ref, *refs):
    kv_here = len(refs) // 2
    handed_refs, out_refs = refs[:kv_here], refs[kv_here:]
    outer, first = outer_here(), in_first_section()
    width = gain_ref.shape[1] // kv_here
    kv_refs = (own_ref, got_ref)
    biases = [bias_of(key_frames_of(ref), frames_ref[:, :1]) for ref in kv_refs]
    for d, out_ref in enumerate(out_refs):
        g = outer ^ d
        fresh = columns_of(g, fresh_ref, width)[...].astype(jnp.float32)
        x = jnp.where(first, fresh, handed_refs[d][...].astype(jnp.float32))
        queries = queries_of(x, columns_of(g, gain_ref, width)[...])
        raws = [scores(queries, kv_block(ref, g, 0), bias) for ref, bias in zip(kv_refs, biases)]
        top = functools.reduce(jnp.maximum, [top_of(raw) for raw in raws])
        both = sum(
            weigh(probs_of(raw, top), kv_block(ref, g, 1)) for ref, raw in zip(kv_refs, raws)
        )
        write_sums(out_ref, both[:, :HD], top, both[:, HD:])


def partials(gain, frames, fresh, own, got, handed):
    length, width = own.shape
    tokens, half = fresh.shape
    queries = HEADS // PAIR * tokens
    kv_here = width // HD // 2
    chunk = jax.ShapeDtypeStruct((queries // kv_here + STAT_ROWS, HD), jnp.bfloat16)
    return pl.pallas_call(
        partials_kernel,
        in_specs=[WHOLE] * (5 + kv_here),
        out_specs=[WHOLE] * kv_here,
        out_shape=[chunk] * kv_here,
        cost_estimate=pl.CostEstimate(
            flops=2 * queries * PAIR * length * 3 * HD,
            bytes_accessed=4 * length * width,
            transcendentals=queries * PAIR * length,
        ),
        compiler_params=pltpu.CompilerParams(vmem_limit_bytes=16 * MIB),
        name="partials",
    )(*in_vmem(gain, frames, fresh, own, got, *handed))


def merge_kernel(*refs):
    *parts, out_ref = refs
    write_chunk(out_ref, *joined(parts, False))


def merge(parts):
    return pl.pallas_call(
        merge_kernel,
        in_specs=[WHOLE] * len(parts),
        out_specs=WHOLE,
        out_shape=jax.ShapeDtypeStruct(parts[0].shape, parts[0].dtype),
        compiler_params=pltpu.CompilerParams(vmem_limit_bytes=8 * MIB),
        name="merge",
    )(*in_vmem(*parts))


def combined(one_ref, two_ref, x, out_ref):
    one, two = one_ref[...].astype(jnp.float32), two_ref[...].astype(jnp.float32)
    here = inner_here() == 0
    parts = [jnp.where(here, one, two), jnp.where(here, two, one)]
    total, _, _ = joined([part.astype(jnp.bfloat16) for part in parts], True)
    if x is not None:
        total = head_rows(x) + total
    tokens = out_ref.shape[0]
    for h in range(total.shape[0] // tokens):
        piece = total[h * tokens : (h + 1) * tokens]
        out_ref[:, h * HD : (h + 1) * HD] = piece.astype(jnp.bfloat16)


def combine_kernel(one_ref, two_ref, out_ref):
    combined(one_ref, two_ref, None, out_ref)


def combine_last_kernel(one_ref, two_ref, fresh_ref, handed_ref, out_ref):
    fresh = columns_of(outer_here(), fresh_ref, out_ref.shape[1])[...]
    x = jnp.where(
        in_first_section(), fresh.astype(jnp.float32), handed_ref[...].astype(jnp.float32)
    )
    combined(one_ref, two_ref, x, out_ref)


def combine(kernel, tokens, one, two, *rest):
    width = (one.shape[0] - STAT_ROWS) // tokens * HD
    return pl.pallas_call(
        kernel,
        in_specs=[WHOLE] * (2 + len(rest)),
        out_specs=WHOLE,
        out_shape=jax.ShapeDtypeStruct((tokens, width), jnp.bfloat16),
        compiler_params=pltpu.CompilerParams(vmem_limit_bytes=8 * MIB),
        name="combine",
    )(*in_vmem(one, two, *rest))


def assemble_kernel(mine_ref, others_ref, out_ref):
    outers, _, width = mine_ref.shape
    for n, ref in enumerate((mine_ref, others_ref)):
        place = (place_here() + n) % PAIR
        for d in range(outers):
            columns_of(place * outers + (outer_here() ^ d), out_ref, width)[...] = ref[d]


def assemble(mine, others):
    outers, tokens, width = mine.shape
    return pl.pallas_call(
        assemble_kernel,
        in_specs=[WHOLE] * 2,
        out_specs=WHOLE,
        out_shape=jax.ShapeDtypeStruct((tokens, PAIR * outers * width), jnp.bfloat16),
        compiler_params=pltpu.CompilerParams(vmem_limit_bytes=8 * MIB),
        name="assemble",
    )(*in_vmem(mine, others))


def body(
    activations,
    act_frames,
    fresh_batch,
    fresh_frames,
    norm_gain,
    cached_keys,
    cached_values,
    key_frames,
):
    tokens = fresh_batch.shape[0]

    mine, theirs, half, own, given, fresh, gain, frames = first(
        act_frames, fresh_frames[None], key_frames.reshape(-1, HD), activations[0], norm_gain,
        fresh_batch, cached_keys[0], cached_values[0],
    )
    chunks = merge_first(mine, swapped(theirs), half)
    given, *chunks = lax.optimization_barrier((given, *chunks))
    got = swapped(given)
    chunk = merge(from_section_before(chunks))
    handed = combine(combine_kernel, tokens, chunk, from_inner(chunk))
    handed = [handed, *from_outer([handed] * (len(chunks) - 1))]

    chunk, *others = partials(gain, frames, fresh, own, got, handed)
    chunk = merge([chunk, *from_outer(others)])
    share = combine(combine_last_kernel, tokens, chunk, from_inner(chunk), fresh, handed[0])
    mine = jnp.stack([share, *from_outer([share] * len(others))])
    return assemble(mine, swapped(mine))[None]


def solution(mesh):
    placed = (
        P("section", None, None),
        P(),
        P(),
        P(),
        P("section", None),
        P("section", "ctx", None),
        P("section", "ctx", None),
        P("ctx"),
    )
    return jax.shard_map(
        body, mesh=mesh, in_specs=placed, out_specs=P("section", None, None), check_vma=False
    )
```

```python
import functools
import math

import jax
import jax.numpy as jnp
from jax import lax
from jax.experimental import pallas as pl
from jax.experimental.pallas import tpu as pltpu
from jax.sharding import PartitionSpec as P

HEADS = 64
HD = 128
PAIR = 2
INNER = 2
BLOCKS = 4
STAT_ROWS = 16
HIDDEN = -(2.0**100)
SCALE = HD**-0.5 * math.log2(math.e)
MIB = 1 << 20

epsilon = 1e-05

WHOLE = pl.BlockSpec(memory_space=pltpu.VMEM)
IN_HBM = pl.BlockSpec(memory_space=pltpu.HBM)


def in_hbm(*arrays):
    return [pltpu.with_memory_space_constraint(a, pltpu.HBM) for a in arrays]


def in_vmem(*arrays):
    return [pltpu.with_memory_space_constraint(a, pltpu.VMEM) for a in arrays]


def place_here():
    return lax.axis_index("ctx") % PAIR


def inner_here():
    return lax.axis_index("ctx") // PAIR % INNER


def outer_here():
    return lax.axis_index("ctx") // (PAIR * INNER)


def in_first_section():
    return lax.axis_index("section") == 0


def swapped(block):
    return lax.ppermute(block, "ctx", [(i, i ^ 1) for i in range(lax.axis_size("ctx"))])


def from_inner(block):
    size = lax.axis_size("ctx")
    return lax.ppermute(block, "ctx", [(i, i ^ PAIR ^ 1) for i in range(size)])


def from_outer(blocks, other_place=1):
    size = lax.axis_size("ctx")
    got = [
        lax.ppermute(
            block, "ctx", [(i, i ^ (INNER * PAIR * d) ^ other_place) for i in range(size)]
        )
        for d, block in reversed(list(enumerate(blocks, 1)))
    ]
    return got[::-1]


def from_section_before(block, step):
    sections, size = lax.axis_size("section"), lax.axis_size("ctx")
    route = [
        (s * size + i, (s + 1) * size + (i ^ (PAIR * step) ^ 1))
        for s in range(sections - 1)
        for i in range(size)
    ]
    return lax.ppermute(block, ("section", "ctx"), route)


def head_rows(block):
    return jnp.concatenate(
        [block[:, at : at + HD] for at in range(0, block.shape[1], HD)], axis=0
    )


def row_of(ref):
    return jnp.concatenate([ref[i : i + 1] for i in range(ref.shape[0])], axis=1)


def columns_of(index, ref, width):
    return ref.at[:, pl.ds(pl.multiple_of(index * width, HD), width)]


def on_diagonal(rows):
    shape = (rows, HD)
    return lax.broadcasted_iota(jnp.int32, shape, 0) == lax.broadcasted_iota(jnp.int32, shape, 1)


def queries_of(x, gain):
    rows = head_rows(x.astype(jnp.float32))
    gain = head_rows(jnp.broadcast_to(gain, x.shape))
    norm = lax.rsqrt(jnp.mean(rows * rows, axis=-1, keepdims=True) + epsilon)
    return (rows * norm * gain).astype(jnp.bfloat16)


def bias_of(keys_ref, frames):
    length = keys_ref.shape[0] - STAT_ROWS
    width = keys_ref.shape[1]
    rows = -(-length // width)
    tail = keys_ref[length:].astype(jnp.float32)
    key_frames = jnp.concatenate([tail[i : i + 1] for i in range(rows)], axis=1)[:, :length]
    return jnp.where(key_frames <= frames, 0.0, HIDDEN)[None]


def scores(queries, key_block, bias):
    count, keys, tokens = queries.shape[0], key_block.shape[0], bias.shape[1]
    raw = lax.dot_general(
        queries, key_block, (((1,), (1,)), ((), ())), preferred_element_type=jnp.float32
    )
    raw = raw.reshape(count // tokens, tokens, keys) * SCALE + bias
    return raw.reshape(count, keys)


def top_of(raw):
    top = jnp.max(raw, axis=-1, keepdims=True)
    return top.astype(jnp.bfloat16).astype(jnp.float32)


def weigh(raw, top, value_block):
    probs = jnp.exp2(raw - top).astype(jnp.bfloat16)
    ones = jnp.ones((value_block.shape[0], HD), jnp.bfloat16)
    return jnp.dot(
        probs, jnp.concatenate([value_block, ones], axis=1), preferred_element_type=jnp.float32
    )


def groups_of(count):
    groups = -(-count // HD)
    held = count // groups
    return [slice(c * held, (c + 1) * held) for c in range(groups)]


def write_chunk(out_ref, weighted, tops, totals):
    count = weighted.shape[0]
    line = lax.broadcasted_iota(jnp.int32, (STAT_ROWS, HD), 0)
    stats = jnp.zeros((STAT_ROWS, HD), jnp.float32)
    for c, (top, total) in enumerate(zip(tops, totals)):
        high = total.astype(jnp.bfloat16).astype(jnp.float32)
        for n, row in enumerate((top, high, total - high)):
            stats = jnp.where(line == 3 * c + n, row, stats)
    out_ref[:count] = weighted.astype(jnp.bfloat16)
    out_ref[count:] = stats.astype(jnp.bfloat16)


def write_sums(out_ref, weighted, top, total):
    groups = groups_of(weighted.shape[0])
    diagonal = on_diagonal(groups[0].stop)

    def rows(column):
        column = jnp.broadcast_to(column, weighted.shape)
        return [
            jnp.sum(jnp.where(diagonal, column[group], 0.0), axis=0, keepdims=True)
            for group in groups
        ]

    write_chunk(out_ref, weighted, rows(top), rows(total))


def joined(parts, normed, x=None):
    count = parts[0].shape[0] - STAT_ROWS
    groups = groups_of(count)
    diagonal = on_diagonal(groups[0].stop)
    stats = [part[count:].astype(jnp.float32) for part in parts]
    values, tops, totals = [], [], []
    for c, group in enumerate(groups):
        points = [s[3 * c : 3 * c + 1] for s in stats]
        top = functools.reduce(jnp.maximum, points)
        factors = [jnp.exp2(point - top) for point in points]
        total = sum(
            f * (s[3 * c + 1 : 3 * c + 2] + s[3 * c + 2 : 3 * c + 3])
            for f, s in zip(factors, stats)
        )
        if normed:
            inverse = 1.0 / total
            factors = [f * inverse for f in factors]
        terms = list(zip(factors, parts)) + ([] if x is None else [(total, x)])
        value = 0.0
        for factor, part in terms:
            weight = jnp.where(diagonal, factor, 0.0)[:, : group.stop - group.start]
            high = weight.astype(jnp.bfloat16)
            low = (weight - high.astype(jnp.float32)).astype(jnp.bfloat16)
            for term in (high, low):
                value = value + jnp.dot(term, part[group], preferred_element_type=jnp.float32)
        values.append(value)
        tops.append(top)
        totals.append(total)
    return jnp.concatenate(values, axis=0), tops, totals


def halve(staged_ref, copies, own_ref, given_ref, gift_ref, gift_sems, tail):
    length, width = staged_ref.shape
    half, step = width // PAIR, length // BLOCKS
    if tail is not None:
        gift_ref[length:] = tail()
        own_ref[length:] = tail()
    place = place_here()
    gifts = []
    for b in range(BLOCKS):
        if copies:
            copies[b].wait()
        rows = pl.ds(b * step, step)
        gift_ref[rows] = columns_of(1 - place, staged_ref.at[rows], half)[...]
        own_ref[rows] = columns_of(place, staged_ref.at[rows], half)[...]
        if b == BLOCKS - 1:
            rows = pl.ds(b * step, gift_ref.shape[0] - b * step)
        gifts.append(pltpu.make_async_copy(gift_ref.at[rows], given_ref.at[rows], gift_sems.at[b]))
        gifts[-1].start()
    return gifts


def load_keys_kernel(
    key_frames_in, keys_in, own_ref, given_ref,
    key_frames_ref, staged_ref, gift_ref, sems, gift_sems, small_sem,
):
    length, half = staged_ref.shape[0], own_ref.shape[1]
    small = pltpu.make_async_copy(key_frames_in, key_frames_ref, small_sem)
    small.start()

    def tail():
        row = row_of(key_frames_ref).astype(jnp.float32)
        lines = -(-length // half)
        row = jnp.concatenate([row, jnp.zeros((1, lines * half - length), jnp.float32)], axis=1)
        line = lax.broadcasted_iota(jnp.int32, (STAT_ROWS, half), 0)
        lower = jnp.zeros((STAT_ROWS, half), jnp.float32)
        for n in range(lines):
            lower = jnp.where(line == n, row[:, n * half : (n + 1) * half], lower)
        return lower.astype(jnp.bfloat16)

    copies, step = [], length // BLOCKS
    for b in range(BLOCKS):
        rows = pl.ds(b * step, step)
        copies.append(pltpu.make_async_copy(keys_in.at[rows], staged_ref.at[rows], sems.at[b]))
        copies[-1].start()
    small.wait()
    for gift in halve(staged_ref, copies, own_ref, given_ref, gift_ref, gift_sems, tail):
        gift.wait()


def load_keys(key_frames, keys):
    length, width = keys.shape
    shape = (length + STAT_ROWS, width // PAIR)
    return pl.pallas_call(
        load_keys_kernel,
        in_specs=[IN_HBM] * 2,
        out_specs=[WHOLE, IN_HBM],
        out_shape=[pltpu.VMEM(shape, keys.dtype), pltpu.HBM(shape, keys.dtype)],
        scratch_shapes=[
            pltpu.VMEM(key_frames.shape, key_frames.dtype),
            pltpu.VMEM((length, width), keys.dtype),
            pltpu.VMEM(shape, keys.dtype),
            pltpu.SemaphoreType.DMA((BLOCKS,)),
            pltpu.SemaphoreType.DMA((BLOCKS,)),
            pltpu.SemaphoreType.DMA,
        ],
        cost_estimate=pl.CostEstimate(
            flops=0, bytes_accessed=2 * length * width, transcendentals=0
        ),
        compiler_params=pltpu.CompilerParams(vmem_limit_bytes=16 * MIB),
        name="load_keys",
    )(*in_hbm(key_frames, keys))


def load_values_kernel(
    values_ref, act_frames_in, fresh_frames_in, batch_in, fresh_in, gain_in,
    own_ref, given_ref, batches_ref, gain_ref, frames_ref,
    act_frames_ref, fresh_frames_ref, gift_ref, gift_sems, small_sems,
):
    place, half = place_here(), gain_ref.shape[1]
    small = [
        (act_frames_in, act_frames_ref),
        (fresh_frames_in, fresh_frames_ref),
        (columns_of(place, batch_in, half), batches_ref.at[0]),
        (columns_of(place, gain_in, half), gain_ref),
        (columns_of(place, fresh_in, half), batches_ref.at[1]),
    ]
    small = [pltpu.make_async_copy(a, b, small_sems.at[n]) for n, (a, b) in enumerate(small)]
    for copy in small:
        copy.start()
    gifts = halve(values_ref, [], own_ref, given_ref, gift_ref, gift_sems, None)
    for copy in small[:2]:
        copy.wait()

    tokens = frames_ref.shape[1]
    section = lax.axis_index("section")
    own_row = act_frames_ref[pl.ds(section, 1), :].astype(jnp.float32)
    prior_row = act_frames_ref[pl.ds(jnp.maximum(section - 1, 0), 1), :].astype(jnp.float32)
    fresh_row = fresh_frames_ref[...].astype(jnp.float32)
    next_row = jnp.where(in_first_section(), fresh_row, prior_row)
    shape = (tokens, tokens)
    diagonal = lax.broadcasted_iota(jnp.int32, shape, 0) == lax.broadcasted_iota(jnp.int32, shape, 1)
    for tick, row in enumerate((own_row, next_row)):
        column = jnp.sum(jnp.where(diagonal, row, 0.0), axis=1, keepdims=True)
        frames_ref[tick] = jnp.broadcast_to(column, (tokens, HD))

    for copy in small[2:] + gifts:
        copy.wait()


def load_values(act_frames, fresh_frames, values, batch, fresh, gain):
    length, width = values.shape
    tokens, model = batch.shape
    half = model // PAIR
    shape = (length, width // PAIR)
    return pl.pallas_call(
        load_values_kernel,
        in_specs=[WHOLE] + [IN_HBM] * 5,
        out_specs=[WHOLE, IN_HBM] + [WHOLE] * 3,
        out_shape=[
            pltpu.VMEM(shape, values.dtype),
            pltpu.HBM(shape, values.dtype),
            pltpu.VMEM((2, tokens, half), batch.dtype),
            pltpu.VMEM((1, half), gain.dtype),
            pltpu.VMEM((2, tokens, HD), jnp.float32),
        ],
        scratch_shapes=[
            pltpu.VMEM(act_frames.shape, act_frames.dtype),
            pltpu.VMEM(fresh_frames.shape, fresh_frames.dtype),
            pltpu.VMEM(shape, values.dtype),
            pltpu.SemaphoreType.DMA((BLOCKS,)),
            pltpu.SemaphoreType.DMA((5,)),
        ],
        cost_estimate=pl.CostEstimate(
            flops=0, bytes_accessed=2 * length * width, transcendentals=0
        ),
        compiler_params=pltpu.CompilerParams(vmem_limit_bytes=16 * MIB),
        name="load_values",
    )(*in_vmem(values), *in_hbm(act_frames, fresh_frames, batch, fresh, gain))


def begin_kernel(
    gain_ref, frames_ref, batches_ref, keys_ref, values_ref,
    queries_ref, sums_ref, stats_ref, share_ref,
):
    length = values_ref.shape[0]
    kv_here = values_ref.shape[1] // HD
    count, width = queries_ref.shape[0] // kv_here, gain_ref.shape[1] // kv_here
    bias = bias_of(keys_ref, frames_ref[0, :, :1])
    share_ref[...] = columns_of(outer_here(), batches_ref.at[0], share_ref.shape[1])[...]
    for g in range(kv_here):
        rows, columns = slice(g * count, (g + 1) * count), slice(g * width, (g + 1) * width)
        block = slice(g * HD, (g + 1) * HD)
        queries = queries_of(batches_ref[0, :, columns], gain_ref[:, columns])
        queries_ref[rows] = queries
        raw = scores(queries, keys_ref[:length, block], bias)
        top = top_of(raw)
        both = weigh(raw, top, values_ref[:, block])
        sums_ref[rows] = both[:, :HD]
        lane = lax.broadcasted_iota(jnp.int32, (count, HD), 1)
        stats_ref[rows] = jnp.where(lane < HD // 2, top, both[:, HD:])


def begin(gain, frames, batches, keys, values):
    length, width = values.shape
    _, tokens, half = batches.shape
    queries = HEADS // PAIR * tokens
    return pl.pallas_call(
        begin_kernel,
        in_specs=[WHOLE] * 5,
        out_specs=[WHOLE] * 4,
        out_shape=[
            jax.ShapeDtypeStruct((queries, HD), jnp.bfloat16),
            jax.ShapeDtypeStruct((queries, HD), jnp.float32),
            jax.ShapeDtypeStruct((queries, HD), jnp.float32),
            jax.ShapeDtypeStruct((tokens, half * HD // width), batches.dtype),
        ],
        cost_estimate=pl.CostEstimate(
            flops=2 * queries * length * 3 * HD,
            bytes_accessed=4 * length * width,
            transcendentals=queries * length,
        ),
        compiler_params=pltpu.CompilerParams(vmem_limit_bytes=16 * MIB),
        name="begin",
    )(*in_vmem(gain, frames, batches, keys, values))


def chunk_shapes(count):
    shape = jax.ShapeDtypeStruct((count + STAT_ROWS, HD), jnp.bfloat16)
    return shape


def finish_kernel(
    frames_ref, queries_ref, sums_ref, stats_ref, keys_ref, values_ref, *out_refs
):
    length = values_ref.shape[0]
    kv_here, outer = len(out_refs), outer_here()
    count = queries_ref.shape[0] // kv_here
    bias = bias_of(keys_ref, frames_ref[0, :, :1])
    for d, out_ref in enumerate(out_refs):
        g = outer ^ d
        rows = pl.ds(pl.multiple_of(g * count, count), count)
        raw = scores(queries_ref[rows], columns_of(g, keys_ref.at[:length], HD)[...], bias)
        stats = stats_ref[rows]
        before, totals = stats[:, :1], stats[:, HD // 2 : HD // 2 + 1]
        top = jnp.maximum(before, top_of(raw))
        factor = jnp.exp2(before - top)
        both = weigh(raw, top, columns_of(g, values_ref, HD)[...])
        weighted = both[:, :HD] + sums_ref[rows] * factor
        write_sums(out_ref, weighted, top, both[:, HD:] + totals * factor)


def finish(frames, queries, sums, stats, keys, values):
    length, width = values.shape
    count, kv_here = queries.shape[0], width // HD
    return pl.pallas_call(
        finish_kernel,
        in_specs=[WHOLE] * 6,
        out_specs=[WHOLE] * kv_here,
        out_shape=[chunk_shapes(count // kv_here)] * kv_here,
        cost_estimate=pl.CostEstimate(
            flops=2 * count * length * 3 * HD,
            bytes_accessed=4 * length * width,
            transcendentals=count * length,
        ),
        compiler_params=pltpu.CompilerParams(vmem_limit_bytes=16 * MIB),
        name="finish",
    )(*in_vmem(frames, queries, sums, stats, keys, values))


def partials_kernel(gain_ref, frames_ref, batches_ref, *refs):
    kv_refs, refs = (refs[0:2], refs[2:4]), refs[4:]
    kv_here = len(refs) // 2
    handed_refs, out_refs = refs[:kv_here], refs[kv_here:]
    length, outer, first = kv_refs[0][1].shape[0], outer_here(), in_first_section()
    width = gain_ref.shape[1] // kv_here
    frames = frames_ref[1, :, :1]
    biases = [bias_of(keys_ref, frames) for keys_ref, _ in kv_refs]
    for d, out_ref in enumerate(out_refs):
        g = outer ^ d
        fresh = columns_of(g, batches_ref.at[1], width)[...].astype(jnp.float32)
        handed = handed_refs[d][...].astype(jnp.float32)
        x = jnp.where(first, fresh, handed)
        queries = queries_of(x, columns_of(g, gain_ref, width)[...])
        raws = [
            scores(queries, columns_of(g, keys_ref.at[:length], HD)[...], bias)
            for (keys_ref, _), bias in zip(kv_refs, biases)
        ]
        top = functools.reduce(jnp.maximum, [top_of(raw) for raw in raws])
        both = sum(
            weigh(raw, top, columns_of(g, values_ref, HD)[...])
            for raw, (_, values_ref) in zip(raws, kv_refs)
        )
        write_sums(out_ref, both[:, :HD], top, both[:, HD:])


def partials(gain, frames, batches, own, got, handed):
    length, width = own[1].shape
    _, tokens, half = batches.shape
    queries = HEADS // PAIR * tokens
    kv_here = width // HD
    return pl.pallas_call(
        partials_kernel,
        in_specs=[WHOLE] * (7 + kv_here),
        out_specs=[WHOLE] * kv_here,
        out_shape=[chunk_shapes(queries // kv_here)] * kv_here,
        cost_estimate=pl.CostEstimate(
            flops=2 * queries * PAIR * length * 3 * HD,
            bytes_accessed=8 * length * width,
            transcendentals=queries * PAIR * length,
        ),
        compiler_params=pltpu.CompilerParams(vmem_limit_bytes=16 * MIB),
        name="partials",
    )(*in_vmem(gain, frames, batches, *own, *got, *handed))


def merge_kernel(*refs):
    *parts, out_ref = refs
    write_chunk(out_ref, *joined(parts, False))


def merge_first_kernel(*refs):
    *parts, share_ref, out_ref = refs
    x = head_rows(share_ref[...].astype(jnp.float32)).astype(jnp.bfloat16)
    write_chunk(out_ref, *joined(parts, False, x))


def merge(kernel, *parts):
    return pl.pallas_call(
        kernel,
        in_specs=[WHOLE] * len(parts),
        out_specs=WHOLE,
        out_shape=jax.ShapeDtypeStruct(parts[0].shape, parts[0].dtype),
        compiler_params=pltpu.CompilerParams(vmem_limit_bytes=8 * MIB),
        name="merge",
    )(*in_vmem(*parts))


def combined(one_ref, two_ref, x, out_ref):
    one, two = one_ref[...].astype(jnp.float32), two_ref[...].astype(jnp.float32)
    here = inner_here() == 0
    parts = [jnp.where(here, one, two), jnp.where(here, two, one)]
    total, _, _ = joined([part.astype(jnp.bfloat16) for part in parts], True)
    if x is not None:
        total = head_rows(x) + total
    tokens = out_ref.shape[0]
    for h in range(total.shape[0] // tokens):
        piece = total[h * tokens : (h + 1) * tokens]
        out_ref[:, h * HD : (h + 1) * HD] = piece.astype(jnp.bfloat16)


def combine_kernel(one_ref, two_ref, out_ref):
    combined(one_ref, two_ref, None, out_ref)


def combine_last_kernel(one_ref, two_ref, batches_ref, handed_ref, out_ref):
    fresh = columns_of(outer_here(), batches_ref.at[1], out_ref.shape[1])[...]
    x = jnp.where(
        in_first_section(), fresh.astype(jnp.float32), handed_ref[...].astype(jnp.float32)
    )
    combined(one_ref, two_ref, x, out_ref)


def combine(kernel, tokens, one, two, *rest):
    width = (one.shape[0] - STAT_ROWS) // tokens * HD
    return pl.pallas_call(
        kernel,
        in_specs=[WHOLE] * (2 + len(rest)),
        out_specs=WHOLE,
        out_shape=jax.ShapeDtypeStruct((tokens, width), jnp.bfloat16),
        compiler_params=pltpu.CompilerParams(vmem_limit_bytes=8 * MIB),
        name="combine",
    )(*in_vmem(one, two, *rest))


def assemble_kernel(mine_ref, others_ref, out_ref):
    outers, _, width = mine_ref.shape
    for n, ref in enumerate((mine_ref, others_ref)):
        place = (place_here() + n) % PAIR
        for d in range(outers):
            columns_of(place * outers + (outer_here() ^ d), out_ref, width)[...] = ref[d]


def assemble(mine, others):
    outers, tokens, width = mine.shape
    return pl.pallas_call(
        assemble_kernel,
        in_specs=[WHOLE] * 2,
        out_specs=WHOLE,
        out_shape=jax.ShapeDtypeStruct((tokens, PAIR * outers * width), jnp.bfloat16),
        compiler_params=pltpu.CompilerParams(vmem_limit_bytes=8 * MIB),
        name="assemble",
    )(*in_vmem(mine, others))


def body(
    activations,
    act_frames,
    fresh_batch,
    fresh_frames,
    norm_gain,
    cached_keys,
    cached_values,
    key_frames,
):
    own_keys, given_keys = load_keys(key_frames.reshape(-1, HD), cached_keys[0])
    got_keys = swapped(given_keys)
    own_values, given_values, batches, gain, frames = load_values(
        act_frames, fresh_frames[None], cached_values[0], activations[0], fresh_batch, norm_gain
    )
    got_values = swapped(given_values)
    own, got = (own_keys, own_values), (got_keys, got_values)

    tokens = fresh_batch.shape[0]
    *terms, share = begin(gain, frames, batches, *own)
    chunk, *others = finish(frames, *terms, *got)
    chunk = merge(merge_first_kernel, *from_outer(others, 0)[::-1], chunk, share)
    one, two = [from_section_before(chunk, step) for step in range(INNER)]
    handed = combine(combine_kernel, tokens, one, two)
    handed = [swapped(handed), *from_outer([handed] * len(others))]

    chunk, *others = partials(gain, frames, batches, own, got, handed)
    chunk = merge(merge_kernel, *from_outer(others)[::-1], swapped(chunk))
    one, two = swapped(chunk), from_inner(chunk)
    share = combine(combine_last_kernel, tokens, one, two, batches, handed[0])
    theirs = jnp.stack([swapped(share), *from_outer([share] * len(others))])
    return assemble(swapped(theirs), theirs)[None]


def solution(mesh):
    placed = (
        P("section", None, None),
        P(),
        P(),
        P(),
        P("section", None),
        P("section", "ctx", None),
        P("section", "ctx", None),
        P("ctx"),
    )
    return jax.shard_map(
        body, mesh=mesh, in_specs=placed, out_specs=P("section", None, None), check_vma=False
    )
```

```python
import functools
import math

import jax
import jax.numpy as jnp
from jax import lax
from jax.experimental import pallas as pl
from jax.experimental.pallas import tpu as pltpu
from jax.sharding import PartitionSpec as P

HEADS = 64
HD = 128
PAIR = 2
INNER = 2
BLOCKS = 4
STAT_ROWS = 16
HIDDEN = -(2.0**100)
SCALE = HD**-0.5 * math.log2(math.e)
MIB = 1 << 20

epsilon = 1e-05

WHOLE = pl.BlockSpec(memory_space=pltpu.VMEM)
IN_HBM = pl.BlockSpec(memory_space=pltpu.HBM)


def in_hbm(*arrays):
    return [pltpu.with_memory_space_constraint(a, pltpu.HBM) for a in arrays]


def in_vmem(*arrays):
    return [pltpu.with_memory_space_constraint(a, pltpu.VMEM) for a in arrays]


def place_here():
    return lax.axis_index("ctx") % PAIR


def inner_here():
    return lax.axis_index("ctx") // PAIR % INNER


def outer_here():
    return lax.axis_index("ctx") // (PAIR * INNER)


def in_first_section():
    return lax.axis_index("section") == 0


def swapped(block):
    return lax.ppermute(block, "ctx", [(i, i ^ 1) for i in range(lax.axis_size("ctx"))])


def from_inner(block):
    size = lax.axis_size("ctx")
    return lax.ppermute(block, "ctx", [(i, i ^ PAIR ^ 1) for i in range(size)])


def from_outer(blocks, other_place=1):
    size = lax.axis_size("ctx")
    got = [
        lax.ppermute(
            block, "ctx", [(i, i ^ (INNER * PAIR * d) ^ other_place) for i in range(size)]
        )
        for d, block in reversed(list(enumerate(blocks, 1)))
    ]
    return got[::-1]


def from_section_before(block, step):
    sections, size = lax.axis_size("section"), lax.axis_size("ctx")
    route = [
        (s * size + i, (s + 1) * size + (i ^ (PAIR * step) ^ 1))
        for s in range(sections - 1)
        for i in range(size)
    ]
    return lax.ppermute(block, ("section", "ctx"), route)


def head_rows(block):
    return jnp.concatenate(
        [block[:, at : at + HD] for at in range(0, block.shape[1], HD)], axis=0
    )


def row_of(ref):
    return jnp.concatenate([ref[i : i + 1] for i in range(ref.shape[0])], axis=1)


def columns_of(index, ref, width):
    return ref.at[:, pl.ds(pl.multiple_of(index * width, HD), width)]


def on_diagonal(rows):
    shape = (rows, HD)
    return lax.broadcasted_iota(jnp.int32, shape, 0) == lax.broadcasted_iota(jnp.int32, shape, 1)


def queries_of(x, gain):
    rows = head_rows(x.astype(jnp.float32))
    gain = head_rows(jnp.broadcast_to(gain, x.shape))
    norm = lax.rsqrt(jnp.mean(rows * rows, axis=-1, keepdims=True) + epsilon)
    return (rows * norm * gain).astype(jnp.bfloat16)


def bias_of(keys_ref, frames):
    length = keys_ref.shape[0] - STAT_ROWS
    width = keys_ref.shape[1]
    rows = -(-length // width)
    tail = keys_ref[length:].astype(jnp.float32)
    key_frames = jnp.concatenate([tail[i : i + 1] for i in range(rows)], axis=1)[:, :length]
    return jnp.where(key_frames <= frames, 0.0, HIDDEN)[None]


def scores(queries, key_block, bias):
    count, keys, tokens = queries.shape[0], key_block.shape[0], bias.shape[1]
    raw = lax.dot_general(
        queries, key_block, (((1,), (1,)), ((), ())), preferred_element_type=jnp.float32
    )
    raw = raw.reshape(count // tokens, tokens, keys) * SCALE + bias
    return raw.reshape(count, keys)


def top_of(raw):
    top = jnp.max(raw, axis=-1, keepdims=True)
    return top.astype(jnp.bfloat16).astype(jnp.float32)


def weigh(raw, top, value_block):
    probs = jnp.exp2(raw - top).astype(jnp.bfloat16)
    ones = jnp.ones((value_block.shape[0], HD), jnp.bfloat16)
    return jnp.dot(
        probs, jnp.concatenate([value_block, ones], axis=1), preferred_element_type=jnp.float32
    )


def groups_of(count):
    groups = -(-count // HD)
    held = count // groups
    return [slice(c * held, (c + 1) * held) for c in range(groups)]


def write_chunk(out_ref, weighted, tops, totals):
    count = weighted.shape[0]
    line = lax.broadcasted_iota(jnp.int32, (STAT_ROWS, HD), 0)
    stats = jnp.zeros((STAT_ROWS, HD), jnp.float32)
    for c, (top, total) in enumerate(zip(tops, totals)):
        high = total.astype(jnp.bfloat16).astype(jnp.float32)
        for n, row in enumerate((top, high, total - high)):
            stats = jnp.where(line == 3 * c + n, row, stats)
    out_ref[:count] = weighted.astype(jnp.bfloat16)
    out_ref[count:] = stats.astype(jnp.bfloat16)


def write_sums(out_ref, weighted, top, total):
    groups = groups_of(weighted.shape[0])
    diagonal = on_diagonal(groups[0].stop)

    def rows(column):
        column = jnp.broadcast_to(column, weighted.shape)
        return [
            jnp.sum(jnp.where(diagonal, column[group], 0.0), axis=0, keepdims=True)
            for group in groups
        ]

    write_chunk(out_ref, weighted, rows(top), rows(total))


def joined(parts, normed, x=None):
    count = parts[0].shape[0] - STAT_ROWS
    groups = groups_of(count)
    diagonal = on_diagonal(groups[0].stop)
    stats = [part[count:].astype(jnp.float32) for part in parts]
    values, tops, totals = [], [], []
    for c, group in enumerate(groups):
        points = [s[3 * c : 3 * c + 1] for s in stats]
        top = functools.reduce(jnp.maximum, points)
        factors = [jnp.exp2(point - top) for point in points]
        total = sum(
            f * (s[3 * c + 1 : 3 * c + 2] + s[3 * c + 2 : 3 * c + 3])
            for f, s in zip(factors, stats)
        )
        if normed:
            inverse = 1.0 / total
            factors = [f * inverse for f in factors]
        terms = list(zip(factors, parts)) + ([] if x is None else [(total, x)])
        value = 0.0
        for factor, part in terms:
            weight = jnp.where(diagonal, factor, 0.0)[:, : group.stop - group.start]
            high = weight.astype(jnp.bfloat16)
            low = (weight - high.astype(jnp.float32)).astype(jnp.bfloat16)
            for term in (high, low):
                value = value + jnp.dot(term, part[group], preferred_element_type=jnp.float32)
        values.append(value)
        tops.append(top)
        totals.append(total)
    return jnp.concatenate(values, axis=0), tops, totals


def halve(staged_ref, copies, own_ref, given_ref, gift_ref, gift_sems, tail):
    length, width = staged_ref.shape
    half, step = width // PAIR, length // BLOCKS
    if tail is not None:
        gift_ref[length:] = tail()
        own_ref[length:] = tail()
    place = place_here()
    gifts = []
    for b in range(BLOCKS):
        if copies:
            copies[b].wait()
        rows = pl.ds(b * step, step)
        gift_ref[rows] = columns_of(1 - place, staged_ref.at[rows], half)[...]
        own_ref[rows] = columns_of(place, staged_ref.at[rows], half)[...]
        if b == BLOCKS - 1:
            rows = pl.ds(b * step, gift_ref.shape[0] - b * step)
        gifts.append(pltpu.make_async_copy(gift_ref.at[rows], given_ref.at[rows], gift_sems.at[b]))
        gifts[-1].start()
    return gifts


def load_keys_kernel(
    key_frames_in, keys_in, own_ref, given_ref,
    key_frames_ref, staged_ref, gift_ref, sems, gift_sems, small_sem,
):
    length, half = staged_ref.shape[0], own_ref.shape[1]
    small = pltpu.make_async_copy(key_frames_in, key_frames_ref, small_sem)
    small.start()

    def tail():
        row = row_of(key_frames_ref).astype(jnp.float32)
        lines = -(-length // half)
        row = jnp.concatenate([row, jnp.zeros((1, lines * half - length), jnp.float32)], axis=1)
        line = lax.broadcasted_iota(jnp.int32, (STAT_ROWS, half), 0)
        lower = jnp.zeros((STAT_ROWS, half), jnp.float32)
        for n in range(lines):
            lower = jnp.where(line == n, row[:, n * half : (n + 1) * half], lower)
        return lower.astype(jnp.bfloat16)

    copies, step = [], length // BLOCKS
    for b in range(BLOCKS):
        rows = pl.ds(b * step, step)
        copies.append(pltpu.make_async_copy(keys_in.at[rows], staged_ref.at[rows], sems.at[b]))
        copies[-1].start()
    small.wait()
    for gift in halve(staged_ref, copies, own_ref, given_ref, gift_ref, gift_sems, tail):
        gift.wait()


def load_keys(key_frames, keys):
    length, width = keys.shape
    shape = (length + STAT_ROWS, width // PAIR)
    return pl.pallas_call(
        load_keys_kernel,
        in_specs=[IN_HBM] * 2,
        out_specs=[WHOLE, IN_HBM],
        out_shape=[pltpu.VMEM(shape, keys.dtype), pltpu.HBM(shape, keys.dtype)],
        scratch_shapes=[
            pltpu.VMEM(key_frames.shape, key_frames.dtype),
            pltpu.VMEM((length, width), keys.dtype),
            pltpu.VMEM(shape, keys.dtype),
            pltpu.SemaphoreType.DMA((BLOCKS,)),
            pltpu.SemaphoreType.DMA((BLOCKS,)),
            pltpu.SemaphoreType.DMA,
        ],
        cost_estimate=pl.CostEstimate(
            flops=0, bytes_accessed=2 * length * width, transcendentals=0
        ),
        compiler_params=pltpu.CompilerParams(vmem_limit_bytes=16 * MIB),
        name="load_keys",
    )(*in_hbm(key_frames, keys))


def load_values_kernel(
    values_ref, act_frames_in, fresh_frames_in, batch_in, fresh_in, gain_in,
    own_ref, given_ref, batches_ref, gain_ref, frames_ref,
    act_frames_ref, fresh_frames_ref, gift_ref, gift_sems, small_sems,
):
    place, half = place_here(), gain_ref.shape[1]
    small = [
        (act_frames_in, act_frames_ref),
        (fresh_frames_in, fresh_frames_ref),
        (columns_of(place, batch_in, half), batches_ref.at[0]),
        (columns_of(place, gain_in, half), gain_ref),
        (columns_of(place, fresh_in, half), batches_ref.at[1]),
    ]
    small = [pltpu.make_async_copy(a, b, small_sems.at[n]) for n, (a, b) in enumerate(small)]
    for copy in small:
        copy.start()
    gifts = halve(values_ref, [], own_ref, given_ref, gift_ref, gift_sems, None)
    for copy in small[:2]:
        copy.wait()

    tokens = frames_ref.shape[1]
    section = lax.axis_index("section")
    own_row = act_frames_ref[pl.ds(section, 1), :].astype(jnp.float32)
    prior_row = act_frames_ref[pl.ds(jnp.maximum(section - 1, 0), 1), :].astype(jnp.float32)
    fresh_row = fresh_frames_ref[...].astype(jnp.float32)
    next_row = jnp.where(in_first_section(), fresh_row, prior_row)
    shape = (tokens, tokens)
    diagonal = lax.broadcasted_iota(jnp.int32, shape, 0) == lax.broadcasted_iota(jnp.int32, shape, 1)
    for tick, row in enumerate((own_row, next_row)):
        column = jnp.sum(jnp.where(diagonal, row, 0.0), axis=1, keepdims=True)
        frames_ref[tick] = jnp.broadcast_to(column, (tokens, HD))

    for copy in small[2:] + gifts:
        copy.wait()


def load_values(act_frames, fresh_frames, values, batch, fresh, gain):
    length, width = values.shape
    tokens, model = batch.shape
    half = model // PAIR
    shape = (length, width // PAIR)
    return pl.pallas_call(
        load_values_kernel,
        in_specs=[WHOLE] + [IN_HBM] * 5,
        out_specs=[WHOLE, IN_HBM] + [WHOLE] * 3,
        out_shape=[
            pltpu.VMEM(shape, values.dtype),
            pltpu.HBM(shape, values.dtype),
            pltpu.VMEM((2, tokens, half), batch.dtype),
            pltpu.VMEM((1, half), gain.dtype),
            pltpu.VMEM((2, tokens, HD), jnp.float32),
        ],
        scratch_shapes=[
            pltpu.VMEM(act_frames.shape, act_frames.dtype),
            pltpu.VMEM(fresh_frames.shape, fresh_frames.dtype),
            pltpu.VMEM(shape, values.dtype),
            pltpu.SemaphoreType.DMA((BLOCKS,)),
            pltpu.SemaphoreType.DMA((5,)),
        ],
        cost_estimate=pl.CostEstimate(
            flops=0, bytes_accessed=2 * length * width, transcendentals=0
        ),
        compiler_params=pltpu.CompilerParams(vmem_limit_bytes=16 * MIB),
        name="load_values",
    )(*in_vmem(values), *in_hbm(act_frames, fresh_frames, batch, fresh, gain))


def begin_kernel(
    gain_ref, frames_ref, batches_ref, keys_ref, values_ref,
    queries_ref, sums_ref, stats_ref, share_ref,
):
    length = values_ref.shape[0]
    kv_here = values_ref.shape[1] // HD
    count, width = queries_ref.shape[0] // kv_here, gain_ref.shape[1] // kv_here
    bias = bias_of(keys_ref, frames_ref[0, :, :1])
    share_ref[...] = columns_of(outer_here(), batches_ref.at[0], share_ref.shape[1])[...]
    for g in range(kv_here):
        rows, columns = slice(g * count, (g + 1) * count), slice(g * width, (g + 1) * width)
        block = slice(g * HD, (g + 1) * HD)
        queries = queries_of(batches_ref[0, :, columns], gain_ref[:, columns])
        queries_ref[rows] = queries
        raw = scores(queries, keys_ref[:length, block], bias)
        top = top_of(raw)
        both = weigh(raw, top, values_ref[:, block])
        sums_ref[rows] = both[:, :HD]
        lane = lax.broadcasted_iota(jnp.int32, (count, HD), 1)
        stats_ref[rows] = jnp.where(lane < HD // 2, top, both[:, HD:])


def begin(gain, frames, batches, keys, values):
    length, width = values.shape
    _, tokens, half = batches.shape
    queries = HEADS // PAIR * tokens
    return pl.pallas_call(
        begin_kernel,
        in_specs=[WHOLE] * 5,
        out_specs=[WHOLE] * 4,
        out_shape=[
            jax.ShapeDtypeStruct((queries, HD), jnp.bfloat16),
            jax.ShapeDtypeStruct((queries, HD), jnp.float32),
            jax.ShapeDtypeStruct((queries, HD), jnp.float32),
            jax.ShapeDtypeStruct((tokens, half * HD // width), batches.dtype),
        ],
        cost_estimate=pl.CostEstimate(
            flops=2 * queries * length * 3 * HD,
            bytes_accessed=4 * length * width,
            transcendentals=queries * length,
        ),
        compiler_params=pltpu.CompilerParams(vmem_limit_bytes=16 * MIB),
        name="begin",
    )(*in_vmem(gain, frames, batches, keys, values))


def finish_kernel(
    d, kv_here, frames_ref, queries_ref, sums_ref, stats_ref, keys_ref, values_ref, out_ref
):
    length, count = values_ref.shape[0], queries_ref.shape[0] // kv_here
    g = outer_here() ^ d
    bias = bias_of(keys_ref, frames_ref[0, :, :1])
    rows = pl.ds(pl.multiple_of(g * count, count), count)
    raw = scores(queries_ref[rows], columns_of(g, keys_ref.at[:length], HD)[...], bias)
    stats = stats_ref[rows]
    before, totals = stats[:, :1], stats[:, HD // 2 : HD // 2 + 1]
    top = jnp.maximum(before, top_of(raw))
    factor = jnp.exp2(before - top)
    both = weigh(raw, top, columns_of(g, values_ref, HD)[...])
    weighted = both[:, :HD] + sums_ref[rows] * factor
    write_sums(out_ref, weighted, top, both[:, HD:] + totals * factor)


def chunk_call(kernel, name, d, kv_here, count, length, operands):
    return pl.pallas_call(
        functools.partial(kernel, d, kv_here),
        in_specs=[WHOLE] * len(operands),
        out_specs=WHOLE,
        out_shape=jax.ShapeDtypeStruct((count + STAT_ROWS, HD), jnp.bfloat16),
        cost_estimate=pl.CostEstimate(
            flops=2 * count * length * 3 * HD,
            bytes_accessed=4 * length * HD,
            transcendentals=count * length,
        ),
        compiler_params=pltpu.CompilerParams(vmem_limit_bytes=16 * MIB),
        name=name,
    )(*in_vmem(*operands))


def finish(d, frames, queries, sums, stats, keys, values):
    length, width = values.shape
    kv_here = width // HD
    operands = (frames, queries, sums, stats, keys, values)
    count = queries.shape[0] // kv_here
    return chunk_call(finish_kernel, "finish", d, kv_here, count, length, operands)


def partials_kernel(d, kv_here, gain_ref, frames_ref, batches_ref, *refs):
    kv_refs, (handed_ref, out_ref) = (refs[0:2], refs[2:4]), refs[4:]
    length, width = kv_refs[0][1].shape[0], handed_ref.shape[1]
    g = outer_here() ^ d
    fresh = columns_of(g, batches_ref.at[1], width)[...].astype(jnp.float32)
    x = jnp.where(in_first_section(), fresh, handed_ref[...].astype(jnp.float32))
    queries = queries_of(x, columns_of(g, gain_ref, width)[...])
    raws = [
        scores(
            queries,
            columns_of(g, keys_ref.at[:length], HD)[...],
            bias_of(keys_ref, frames_ref[1, :, :1]),
        )
        for keys_ref, _ in kv_refs
    ]
    top = functools.reduce(jnp.maximum, [top_of(raw) for raw in raws])
    both = sum(
        weigh(raw, top, columns_of(g, values_ref, HD)[...])
        for raw, (_, values_ref) in zip(raws, kv_refs)
    )
    write_sums(out_ref, both[:, :HD], top, both[:, HD:])


def partials(d, gain, frames, batches, own, got, handed):
    length, width = own[1].shape
    tokens = batches.shape[1]
    count = handed.shape[1] // HD * tokens
    operands = (gain, frames, batches, *own, *got, handed)
    return chunk_call(
        partials_kernel, "partials", d, width // HD, count, PAIR * length, operands
    )


def merge_kernel(*refs):
    *parts, out_ref = refs
    write_chunk(out_ref, *joined(parts, False))


def merge_first_kernel(*refs):
    *parts, share_ref, out_ref = refs
    x = head_rows(share_ref[...].astype(jnp.float32)).astype(jnp.bfloat16)
    write_chunk(out_ref, *joined(parts, False, x))


def merge(kernel, *parts):
    return pl.pallas_call(
        kernel,
        in_specs=[WHOLE] * len(parts),
        out_specs=WHOLE,
        out_shape=jax.ShapeDtypeStruct(parts[0].shape, parts[0].dtype),
        compiler_params=pltpu.CompilerParams(vmem_limit_bytes=8 * MIB),
        name="merge",
    )(*in_vmem(*parts))


def combined(one_ref, two_ref, x, out_ref):
    one, two = one_ref[...].astype(jnp.float32), two_ref[...].astype(jnp.float32)
    here = inner_here() == 0
    parts = [jnp.where(here, one, two), jnp.where(here, two, one)]
    total, _, _ = joined([part.astype(jnp.bfloat16) for part in parts], True)
    if x is not None:
        total = head_rows(x) + total
    tokens = out_ref.shape[0]
    for h in range(total.shape[0] // tokens):
        piece = total[h * tokens : (h + 1) * tokens]
        out_ref[:, h * HD : (h + 1) * HD] = piece.astype(jnp.bfloat16)


def combine_kernel(one_ref, two_ref, out_ref):
    combined(one_ref, two_ref, None, out_ref)


def combine_last_kernel(one_ref, two_ref, batches_ref, handed_ref, out_ref):
    fresh = columns_of(outer_here(), batches_ref.at[1], out_ref.shape[1])[...]
    x = jnp.where(
        in_first_section(), fresh.astype(jnp.float32), handed_ref[...].astype(jnp.float32)
    )
    combined(one_ref, two_ref, x, out_ref)


def combine(kernel, tokens, one, two, *rest):
    width = (one.shape[0] - STAT_ROWS) // tokens * HD
    return pl.pallas_call(
        kernel,
        in_specs=[WHOLE] * (2 + len(rest)),
        out_specs=WHOLE,
        out_shape=jax.ShapeDtypeStruct((tokens, width), jnp.bfloat16),
        compiler_params=pltpu.CompilerParams(vmem_limit_bytes=8 * MIB),
        name="combine",
    )(*in_vmem(one, two, *rest))


def assemble_kernel(*refs):
    *pieces, out_ref = refs
    outers, width = len(pieces) // PAIR, pieces[0].shape[1]
    for n, refs in enumerate((pieces[:outers], pieces[outers:])):
        place = (place_here() + n) % PAIR
        for d, ref in enumerate(refs):
            columns_of(place * outers + (outer_here() ^ d), out_ref, width)[...] = ref[...]


def assemble(mine, others):
    tokens, width = mine[0].shape
    pieces = [*mine, *others]
    return pl.pallas_call(
        assemble_kernel,
        in_specs=[WHOLE] * len(pieces),
        out_specs=WHOLE,
        out_shape=jax.ShapeDtypeStruct((tokens, len(pieces) * width), jnp.bfloat16),
        compiler_params=pltpu.CompilerParams(vmem_limit_bytes=8 * MIB),
        name="assemble",
    )(*in_vmem(*pieces))


def body(
    activations,
    act_frames,
    fresh_batch,
    fresh_frames,
    norm_gain,
    cached_keys,
    cached_values,
    key_frames,
):
    own_keys, given_keys = load_keys(key_frames.reshape(-1, HD), cached_keys[0])
    got_keys = swapped(given_keys)
    own_values, given_values, batches, gain, frames = load_values(
        act_frames, fresh_frames[None], cached_values[0], activations[0], fresh_batch, norm_gain
    )
    got_values = swapped(given_values)
    own, got = (own_keys, own_values), (got_keys, got_values)

    tokens = fresh_batch.shape[0]
    outers = lax.axis_size("ctx") // (INNER * PAIR)
    *terms, share = begin(gain, frames, batches, *own)
    chunk, *others = [finish(d, frames, *terms, *got) for d in range(outers)]
    chunk = merge(merge_first_kernel, *from_outer(others, 0)[::-1], chunk, share)
    one, two = [from_section_before(chunk, step) for step in range(INNER)]
    handed = combine(combine_kernel, tokens, one, two)
    handed = [swapped(handed), *from_outer([handed] * len(others))]

    chunk, *others = [
        partials(d, gain, frames, batches, own, got, piece) for d, piece in enumerate(handed)
    ]
    chunk = merge(merge_kernel, *from_outer(others)[::-1], swapped(chunk))
    one, two = swapped(chunk), from_inner(chunk)
    share = combine(combine_last_kernel, tokens, one, two, batches, handed[0])
    theirs = [swapped(share), *from_outer([share] * len(others))]
    return assemble([share, *(swapped(piece) for piece in theirs[1:])], theirs)[None]


def solution(mesh):
    placed = (
        P("section", None, None),
        P(),
        P(),
        P(),
        P("section", None),
        P("section", "ctx", None),
        P("section", "ctx", None),
        P("ctx"),
    )
    return jax.shard_map(
        body, mesh=mesh, in_specs=placed, out_specs=P("section", None, None), check_vma=False
    )
```

```python
import functools
import math

import jax
import jax.numpy as jnp
from jax import lax
from jax.experimental import pallas as pl
from jax.experimental.pallas import tpu as pltpu
from jax.sharding import PartitionSpec as P

HEADS = 64
HD = 128
PAIR = 2
INNER = 2
BLOCKS = 4
STAT_ROWS = 16
HIDDEN = -(2.0**100)
SCALE = HD**-0.5 * math.log2(math.e)
MIB = 1 << 20

epsilon = 1e-05

WHOLE = pl.BlockSpec(memory_space=pltpu.VMEM)
IN_HBM = pl.BlockSpec(memory_space=pltpu.HBM)


def in_hbm(*arrays):
    return [pltpu.with_memory_space_constraint(a, pltpu.HBM) for a in arrays]


def in_vmem(*arrays):
    return [pltpu.with_memory_space_constraint(a, pltpu.VMEM) for a in arrays]


def place_here():
    return lax.axis_index("ctx") % PAIR


def inner_here():
    return lax.axis_index("ctx") // PAIR % INNER


def outer_here():
    return lax.axis_index("ctx") // (PAIR * INNER)


def in_first_section():
    return lax.axis_index("section") == 0


def swapped(block):
    return lax.ppermute(block, "ctx", [(i, i ^ 1) for i in range(lax.axis_size("ctx"))])


def from_inner(block):
    size = lax.axis_size("ctx")
    return lax.ppermute(block, "ctx", [(i, i ^ PAIR ^ 1) for i in range(size)])


def from_outer(blocks, other_place=1):
    size = lax.axis_size("ctx")
    got = [
        lax.ppermute(
            block, "ctx", [(i, i ^ (INNER * PAIR * d) ^ other_place) for i in range(size)]
        )
        for d, block in reversed(list(enumerate(blocks, 1)))
    ]
    return got[::-1]


def from_section_before(block, step):
    sections, size = lax.axis_size("section"), lax.axis_size("ctx")
    route = [
        (s * size + i, (s + 1) * size + (i ^ (PAIR * step) ^ 1))
        for s in range(sections - 1)
        for i in range(size)
    ]
    return lax.ppermute(block, ("section", "ctx"), route)


def head_rows(block):
    return jnp.concatenate(
        [block[:, at : at + HD] for at in range(0, block.shape[1], HD)], axis=0
    )


def row_of(ref):
    return jnp.concatenate([ref[i : i + 1] for i in range(ref.shape[0])], axis=1)


def columns_of(index, ref, width):
    return ref.at[:, pl.ds(pl.multiple_of(index * width, HD), width)]


def on_diagonal(rows):
    shape = (rows, HD)
    return lax.broadcasted_iota(jnp.int32, shape, 0) == lax.broadcasted_iota(jnp.int32, shape, 1)


def queries_of(x, gain):
    rows = head_rows(x.astype(jnp.float32))
    gain = head_rows(jnp.broadcast_to(gain, x.shape))
    norm = lax.rsqrt(jnp.mean(rows * rows, axis=-1, keepdims=True) + epsilon)
    return (rows * norm * gain).astype(jnp.bfloat16)


def bias_of(keys_ref, frames):
    length = keys_ref.shape[0] - STAT_ROWS
    width = keys_ref.shape[1]
    rows = -(-length // width)
    tail = keys_ref[length:].astype(jnp.float32)
    key_frames = jnp.concatenate([tail[i : i + 1] for i in range(rows)], axis=1)[:, :length]
    return jnp.where(key_frames <= frames, 0.0, HIDDEN)[None]


def scores(queries, key_block, bias):
    count, keys, tokens = queries.shape[0], key_block.shape[0], bias.shape[1]
    raw = lax.dot_general(
        queries, key_block, (((1,), (1,)), ((), ())), preferred_element_type=jnp.float32
    )
    raw = raw.reshape(count // tokens, tokens, keys) * SCALE + bias
    return raw.reshape(count, keys)


def top_of(raw):
    top = jnp.max(raw, axis=-1, keepdims=True)
    return top.astype(jnp.bfloat16).astype(jnp.float32)


def weigh(raw, top, value_block):
    probs = jnp.exp2(raw - top).astype(jnp.bfloat16)
    ones = jnp.ones((value_block.shape[0], HD), jnp.bfloat16)
    return jnp.dot(
        probs, jnp.concatenate([value_block, ones], axis=1), preferred_element_type=jnp.float32
    )


def groups_of(count):
    groups = -(-count // HD)
    held = count // groups
    return [slice(c * held, (c + 1) * held) for c in range(groups)]


def write_chunk(out_ref, weighted, tops, totals):
    count = weighted.shape[0]
    line = lax.broadcasted_iota(jnp.int32, (STAT_ROWS, HD), 0)
    stats = jnp.zeros((STAT_ROWS, HD), jnp.float32)
    for c, (top, total) in enumerate(zip(tops, totals)):
        high = total.astype(jnp.bfloat16).astype(jnp.float32)
        for n, row in enumerate((top, high, total - high)):
            stats = jnp.where(line == 3 * c + n, row, stats)
    out_ref[:count] = weighted.astype(jnp.bfloat16)
    out_ref[count:] = stats.astype(jnp.bfloat16)


def write_sums(out_ref, weighted, top, total):
    groups = groups_of(weighted.shape[0])
    diagonal = on_diagonal(groups[0].stop)

    def rows(column):
        column = jnp.broadcast_to(column, weighted.shape)
        return [
            jnp.sum(jnp.where(diagonal, column[group], 0.0), axis=0, keepdims=True)
            for group in groups
        ]

    write_chunk(out_ref, weighted, rows(top), rows(total))


def joined(parts, normed, x=None):
    count = parts[0].shape[0] - STAT_ROWS
    groups = groups_of(count)
    diagonal = on_diagonal(groups[0].stop)
    stats = [part[count:].astype(jnp.float32) for part in parts]
    values, tops, totals = [], [], []
    for c, group in enumerate(groups):
        points = [s[3 * c : 3 * c + 1] for s in stats]
        top = functools.reduce(jnp.maximum, points)
        factors = [jnp.exp2(point - top) for point in points]
        total = sum(
            f * (s[3 * c + 1 : 3 * c + 2] + s[3 * c + 2 : 3 * c + 3])
            for f, s in zip(factors, stats)
        )
        if normed:
            inverse = 1.0 / total
            factors = [f * inverse for f in factors]
        terms = list(zip(factors, parts)) + ([] if x is None else [(total, x)])
        value = 0.0
        for factor, part in terms:
            weight = jnp.where(diagonal, factor, 0.0)[:, : group.stop - group.start]
            high = weight.astype(jnp.bfloat16)
            low = (weight - high.astype(jnp.float32)).astype(jnp.bfloat16)
            for term in (high, low):
                value = value + jnp.dot(term, part[group], preferred_element_type=jnp.float32)
        values.append(value)
        tops.append(top)
        totals.append(total)
    return jnp.concatenate(values, axis=0), tops, totals


def halve(staged_ref, copies, own_ref, given_ref, tail):
    length, width = staged_ref.shape
    half, step = width // PAIR, length // BLOCKS
    if tail is not None:
        given_ref[length:] = tail()
        own_ref[length:] = tail()
    place = place_here()
    for b in range(BLOCKS):
        if copies:
            copies[b].wait()
        rows = pl.ds(b * step, step)
        given_ref[rows] = columns_of(1 - place, staged_ref.at[rows], half)[...]
        own_ref[rows] = columns_of(place, staged_ref.at[rows], half)[...]


def load_keys_kernel(
    key_frames_in, keys_in, own_ref, given_ref,
    key_frames_ref, staged_ref, sems, small_sem,
):
    length, half = staged_ref.shape[0], own_ref.shape[1]
    small = pltpu.make_async_copy(key_frames_in, key_frames_ref, small_sem)
    small.start()

    def tail():
        row = row_of(key_frames_ref).astype(jnp.float32)
        lines = -(-length // half)
        row = jnp.concatenate([row, jnp.zeros((1, lines * half - length), jnp.float32)], axis=1)
        line = lax.broadcasted_iota(jnp.int32, (STAT_ROWS, half), 0)
        lower = jnp.zeros((STAT_ROWS, half), jnp.float32)
        for n in range(lines):
            lower = jnp.where(line == n, row[:, n * half : (n + 1) * half], lower)
        return lower.astype(jnp.bfloat16)

    copies, step = [], length // BLOCKS
    for b in range(BLOCKS):
        rows = pl.ds(b * step, step)
        copies.append(pltpu.make_async_copy(keys_in.at[rows], staged_ref.at[rows], sems.at[b]))
        copies[-1].start()
    small.wait()
    halve(staged_ref, copies, own_ref, given_ref, tail)


def load_keys(key_frames, keys):
    length, width = keys.shape
    shape = (length + STAT_ROWS, width // PAIR)
    return pl.pallas_call(
        load_keys_kernel,
        in_specs=[IN_HBM] * 2,
        out_specs=[WHOLE] * 2,
        out_shape=[pltpu.VMEM(shape, keys.dtype)] * 2,
        scratch_shapes=[
            pltpu.VMEM(key_frames.shape, key_frames.dtype),
            pltpu.VMEM((length, width), keys.dtype),
            pltpu.SemaphoreType.DMA((BLOCKS,)),
            pltpu.SemaphoreType.DMA,
        ],
        cost_estimate=pl.CostEstimate(
            flops=0, bytes_accessed=2 * length * width, transcendentals=0
        ),
        compiler_params=pltpu.CompilerParams(vmem_limit_bytes=16 * MIB),
        name="load_keys",
    )(*in_hbm(key_frames, keys))


def load_values_kernel(
    values_ref, act_frames_in, fresh_frames_in, batch_in, fresh_in, gain_in,
    own_ref, given_ref, batch_ref, gain_ref, fresh_ref, fresh_gain_ref, frames_ref,
    act_frames_ref, fresh_frames_ref, small_sems,
):
    place, half, width = place_here(), gain_ref.shape[1], fresh_ref.shape[1]
    share = (1 - place) * (half // width) + outer_here()
    small = [
        (act_frames_in, act_frames_ref),
        (fresh_frames_in, fresh_frames_ref),
        (columns_of(place, batch_in, half), batch_ref),
        (columns_of(place, gain_in, half), gain_ref),
        (columns_of(share, fresh_in, width), fresh_ref),
        (columns_of(share, gain_in, width), fresh_gain_ref),
    ]
    small = [pltpu.make_async_copy(a, b, small_sems.at[n]) for n, (a, b) in enumerate(small)]
    for copy in small:
        copy.start()
    halve(values_ref, [], own_ref, given_ref, None)
    for copy in small[:2]:
        copy.wait()

    tokens = frames_ref.shape[1]
    section = lax.axis_index("section")
    own_row = act_frames_ref[pl.ds(section, 1), :].astype(jnp.float32)
    prior_row = act_frames_ref[pl.ds(jnp.maximum(section - 1, 0), 1), :].astype(jnp.float32)
    fresh_row = fresh_frames_ref[...].astype(jnp.float32)
    next_row = jnp.where(in_first_section(), fresh_row, prior_row)
    shape = (tokens, tokens)
    diagonal = lax.broadcasted_iota(jnp.int32, shape, 0) == lax.broadcasted_iota(jnp.int32, shape, 1)
    for tick, row in enumerate((own_row, next_row)):
        column = jnp.sum(jnp.where(diagonal, row, 0.0), axis=1, keepdims=True)
        frames_ref[tick] = jnp.broadcast_to(column, (tokens, HD))

    for copy in small[2:]:
        copy.wait()


def load_values(act_frames, fresh_frames, values, batch, fresh, gain):
    length, width = values.shape
    tokens, model = batch.shape
    half = model // PAIR
    share = half * INNER * PAIR // lax.axis_size("ctx")
    shape = (length, width // PAIR)
    return pl.pallas_call(
        load_values_kernel,
        in_specs=[WHOLE] + [IN_HBM] * 5,
        out_specs=[WHOLE] * 7,
        out_shape=[
            pltpu.VMEM(shape, values.dtype),
            pltpu.VMEM(shape, values.dtype),
            pltpu.VMEM((tokens, half), batch.dtype),
            pltpu.VMEM((1, half), gain.dtype),
            pltpu.VMEM((tokens, share), fresh.dtype),
            pltpu.VMEM((1, share), gain.dtype),
            pltpu.VMEM((2, tokens, HD), jnp.float32),
        ],
        scratch_shapes=[
            pltpu.VMEM(act_frames.shape, act_frames.dtype),
            pltpu.VMEM(fresh_frames.shape, fresh_frames.dtype),
            pltpu.SemaphoreType.DMA((6,)),
        ],
        cost_estimate=pl.CostEstimate(
            flops=0, bytes_accessed=2 * length * width, transcendentals=0
        ),
        compiler_params=pltpu.CompilerParams(vmem_limit_bytes=16 * MIB),
        name="load_values",
    )(*in_vmem(values), *in_hbm(act_frames, fresh_frames, batch, fresh, gain))


def begin_kernel(
    gain_ref, frames_ref, batch_ref, keys_ref, values_ref,
    queries_ref, sums_ref, stats_ref, share_ref,
):
    length = values_ref.shape[0]
    kv_here = values_ref.shape[1] // HD
    count, width = queries_ref.shape[0] // kv_here, gain_ref.shape[1] // kv_here
    bias = bias_of(keys_ref, frames_ref[0, :, :1])
    share_ref[...] = columns_of(outer_here(), batch_ref, share_ref.shape[1])[...]
    for g in range(kv_here):
        rows, columns = slice(g * count, (g + 1) * count), slice(g * width, (g + 1) * width)
        block = slice(g * HD, (g + 1) * HD)
        queries = queries_of(batch_ref[:, columns], gain_ref[:, columns])
        queries_ref[rows] = queries
        raw = scores(queries, keys_ref[:length, block], bias)
        top = top_of(raw)
        both = weigh(raw, top, values_ref[:, block])
        sums_ref[rows] = both[:, :HD]
        lane = lax.broadcasted_iota(jnp.int32, (count, HD), 1)
        stats_ref[rows] = jnp.where(lane < HD // 2, top, both[:, HD:])


def begin(gain, frames, batch, keys, values):
    length, width = values.shape
    tokens, half = batch.shape
    queries = HEADS // PAIR * tokens
    return pl.pallas_call(
        begin_kernel,
        in_specs=[WHOLE] * 5,
        out_specs=[WHOLE] * 4,
        out_shape=[
            jax.ShapeDtypeStruct((queries, HD), jnp.bfloat16),
            jax.ShapeDtypeStruct((queries, HD), jnp.float32),
            jax.ShapeDtypeStruct((queries, HD), jnp.float32),
            jax.ShapeDtypeStruct((tokens, half * HD // width), batch.dtype),
        ],
        cost_estimate=pl.CostEstimate(
            flops=2 * queries * length * 3 * HD,
            bytes_accessed=4 * length * width,
            transcendentals=queries * length,
        ),
        compiler_params=pltpu.CompilerParams(vmem_limit_bytes=16 * MIB),
        name="begin",
    )(*in_vmem(gain, frames, batch, keys, values))


def finish_kernel(
    d, kv_here, frames_ref, queries_ref, sums_ref, stats_ref, keys_ref, values_ref, out_ref
):
    length, count = values_ref.shape[0], queries_ref.shape[0] // kv_here
    g = outer_here() ^ d
    bias = bias_of(keys_ref, frames_ref[0, :, :1])
    rows = pl.ds(pl.multiple_of(g * count, count), count)
    raw = scores(queries_ref[rows], columns_of(g, keys_ref.at[:length], HD)[...], bias)
    stats = stats_ref[rows]
    before, totals = stats[:, :1], stats[:, HD // 2 : HD // 2 + 1]
    top = jnp.maximum(before, top_of(raw))
    factor = jnp.exp2(before - top)
    both = weigh(raw, top, columns_of(g, values_ref, HD)[...])
    weighted = both[:, :HD] + sums_ref[rows] * factor
    write_sums(out_ref, weighted, top, both[:, HD:] + totals * factor)


def chunk_call(kernel, name, d, kv_here, count, length, operands):
    return pl.pallas_call(
        functools.partial(kernel, d, kv_here),
        in_specs=[WHOLE] * len(operands),
        out_specs=WHOLE,
        out_shape=jax.ShapeDtypeStruct((count + STAT_ROWS, HD), jnp.bfloat16),
        cost_estimate=pl.CostEstimate(
            flops=2 * count * length * 3 * HD,
            bytes_accessed=4 * length * HD,
            transcendentals=count * length,
        ),
        compiler_params=pltpu.CompilerParams(vmem_limit_bytes=16 * MIB),
        name=name,
    )(*in_vmem(*operands))


def finish(d, frames, queries, sums, stats, keys, values):
    length, width = values.shape
    kv_here = width // HD
    operands = (frames, queries, sums, stats, keys, values)
    count = queries.shape[0] // kv_here
    return chunk_call(finish_kernel, "finish", d, kv_here, count, length, operands)


def partials_kernel(d, kv_here, frames_ref, *refs):
    kv_refs, (queries_ref, out_ref) = (refs[0:2], refs[2:4]), refs[4:]
    length = kv_refs[0][1].shape[0]
    g = outer_here() ^ d
    raws = [
        scores(
            queries_ref[...],
            columns_of(g, keys_ref.at[:length], HD)[...],
            bias_of(keys_ref, frames_ref[1, :, :1]),
        )
        for keys_ref, _ in kv_refs
    ]
    top = functools.reduce(jnp.maximum, [top_of(raw) for raw in raws])
    both = sum(
        weigh(raw, top, columns_of(g, values_ref, HD)[...])
        for raw, (_, values_ref) in zip(raws, kv_refs)
    )
    write_sums(out_ref, both[:, :HD], top, both[:, HD:])


def partials(d, frames, own, got, queries):
    length, width = own[1].shape
    operands = (frames, *own, *got, queries)
    return chunk_call(
        partials_kernel, "partials", d, width // HD, queries.shape[0], PAIR * length, operands
    )


def merge_kernel(*refs):
    *parts, out_ref = refs
    write_chunk(out_ref, *joined(parts, False))


def merge_first_kernel(*refs):
    *parts, share_ref, out_ref = refs
    x = head_rows(share_ref[...].astype(jnp.float32)).astype(jnp.bfloat16)
    write_chunk(out_ref, *joined(parts, False, x))


def merge(kernel, *parts):
    return pl.pallas_call(
        kernel,
        in_specs=[WHOLE] * len(parts),
        out_specs=WHOLE,
        out_shape=jax.ShapeDtypeStruct(parts[0].shape, parts[0].dtype),
        compiler_params=pltpu.CompilerParams(vmem_limit_bytes=8 * MIB),
        name="merge",
    )(*in_vmem(*parts))


def attended(one_ref, two_ref):
    one, two = one_ref[...].astype(jnp.float32), two_ref[...].astype(jnp.float32)
    here = inner_here() == 0
    parts = [jnp.where(here, one, two), jnp.where(here, two, one)]
    value, _, _ = joined([part.astype(jnp.bfloat16) for part in parts], True)
    return value


def columns_from(rows, tokens):
    pieces = [rows[at : at + tokens] for at in range(0, rows.shape[0], tokens)]
    return jnp.concatenate(pieces, axis=1)


def combine_kernel(gain_ref, fresh_ref, one_ref, two_ref, share_ref, queries_ref):
    tokens = fresh_ref.shape[0]
    handed = columns_from(attended(one_ref, two_ref), tokens).astype(jnp.bfloat16)
    fresh = fresh_ref[...].astype(jnp.float32)
    share = jnp.where(in_first_section(), fresh, handed.astype(jnp.float32))
    share = share.astype(jnp.bfloat16)
    share_ref[...] = share
    queries_ref[...] = queries_of(share, gain_ref[...])


def combine(gain, fresh, one, two):
    count = one.shape[0] - STAT_ROWS
    return pl.pallas_call(
        combine_kernel,
        in_specs=[WHOLE] * 4,
        out_specs=[WHOLE] * 2,
        out_shape=[
            jax.ShapeDtypeStruct(fresh.shape, fresh.dtype),
            jax.ShapeDtypeStruct((count, HD), jnp.bfloat16),
        ],
        compiler_params=pltpu.CompilerParams(vmem_limit_bytes=8 * MIB),
        name="combine",
    )(*in_vmem(gain, fresh, one, two))


def combine_last_kernel(share_ref, one_ref, two_ref, out_ref):
    tokens = out_ref.shape[0]
    total = head_rows(share_ref[...].astype(jnp.float32)) + attended(one_ref, two_ref)
    out_ref[...] = columns_from(total, tokens).astype(jnp.bfloat16)


def combine_last(share, one, two):
    return pl.pallas_call(
        combine_last_kernel,
        in_specs=[WHOLE] * 3,
        out_specs=WHOLE,
        out_shape=jax.ShapeDtypeStruct(share.shape, share.dtype),
        compiler_params=pltpu.CompilerParams(vmem_limit_bytes=8 * MIB),
        name="combine_last",
    )(*in_vmem(share, one, two))


def assemble_kernel(*refs):
    *pieces, out_ref = refs
    outers, width = len(pieces) // PAIR, pieces[0].shape[1]
    for n, refs in enumerate((pieces[:outers], pieces[outers:])):
        place = (place_here() + n) % PAIR
        for d, ref in enumerate(refs):
            columns_of(place * outers + (outer_here() ^ d), out_ref, width)[...] = ref[...]


def assemble(mine, others):
    tokens, width = mine[0].shape
    pieces = [*mine, *others]
    return pl.pallas_call(
        assemble_kernel,
        in_specs=[WHOLE] * len(pieces),
        out_specs=WHOLE,
        out_shape=jax.ShapeDtypeStruct((tokens, len(pieces) * width), jnp.bfloat16),
        compiler_params=pltpu.CompilerParams(vmem_limit_bytes=8 * MIB),
        name="assemble",
    )(*in_vmem(*pieces))


def body(
    activations,
    act_frames,
    fresh_batch,
    fresh_frames,
    norm_gain,
    cached_keys,
    cached_values,
    key_frames,
):
    own_keys, given_keys = load_keys(key_frames.reshape(-1, HD), cached_keys[0])
    got_keys = swapped(given_keys)
    own_values, given_values, batch, gain, fresh, fresh_gain, frames = load_values(
        act_frames, fresh_frames[None], cached_values[0], activations[0], fresh_batch, norm_gain
    )
    got_values = swapped(given_values)
    own, got = (own_keys, own_values), (got_keys, got_values)

    outers = lax.axis_size("ctx") // (INNER * PAIR)
    *terms, share = begin(gain, frames, batch, *own)
    chunk, *others = [finish(d, frames, *terms, *got) for d in range(outers)]
    chunk = merge(merge_first_kernel, *from_outer(others, 0)[::-1], chunk, share)
    one, two = [from_section_before(chunk, step) for step in range(INNER)]
    share, queries = combine(fresh_gain, fresh, one, two)
    queries = [swapped(queries), *from_outer([queries] * len(others))]

    chunk, *others = [partials(d, frames, own, got, piece) for d, piece in enumerate(queries)]
    chunk = merge(merge_kernel, *from_outer(others)[::-1], swapped(chunk))
    one, two = swapped(chunk), from_inner(chunk)
    share = combine_last(swapped(share), one, two)
    theirs = [swapped(share), *from_outer([share] * len(others))]
    return assemble([share, *(swapped(piece) for piece in theirs[1:])], theirs)[None]


def solution(mesh):
    placed = (
        P("section", None, None),
        P(),
        P(),
        P(),
        P("section", None),
        P("section", "ctx", None),
        P("section", "ctx", None),
        P("ctx"),
    )
    return jax.shard_map(
        body, mesh=mesh, in_specs=placed, out_specs=P("section", None, None), check_vma=False
    )
```

```python
import functools
import math

import jax
import jax.numpy as jnp
from jax import lax
from jax.experimental import pallas as pl
from jax.experimental.pallas import tpu as pltpu
from jax.sharding import PartitionSpec as P

HEADS = 64
HD = 128
PAIR = 2
INNER = 2
BLOCKS = 4
STAT_ROWS = 16
HIDDEN = -(2.0**100)
SCALE = HD**-0.5 * math.log2(math.e)
MIB = 1 << 20

epsilon = 1e-05

WHOLE = pl.BlockSpec(memory_space=pltpu.VMEM)
IN_HBM = pl.BlockSpec(memory_space=pltpu.HBM)


def in_hbm(*arrays):
    return [pltpu.with_memory_space_constraint(a, pltpu.HBM) for a in arrays]


def in_vmem(*arrays):
    return [pltpu.with_memory_space_constraint(a, pltpu.VMEM) for a in arrays]


def place_here():
    return lax.axis_index("ctx") % PAIR


def inner_here():
    return lax.axis_index("ctx") // PAIR % INNER


def outer_here():
    return lax.axis_index("ctx") // (PAIR * INNER)


def in_first_section():
    return lax.axis_index("section") == 0


def swapped(block):
    return lax.ppermute(block, "ctx", [(i, i ^ 1) for i in range(lax.axis_size("ctx"))])


def from_inner(block):
    size = lax.axis_size("ctx")
    return lax.ppermute(block, "ctx", [(i, i ^ PAIR ^ 1) for i in range(size)])


def from_outer(blocks, other_place=1):
    size = lax.axis_size("ctx")
    got = [
        lax.ppermute(
            block, "ctx", [(i, i ^ (INNER * PAIR * d) ^ other_place) for i in range(size)]
        )
        for d, block in reversed(list(enumerate(blocks, 1)))
    ]
    return got[::-1]


def from_section_before(block, outers):
    sections, size = lax.axis_size("section"), lax.axis_size("ctx")
    got = []
    for d in reversed(range(outers)):
        route = [
            (s * size + i, (s + 1) * size + (i ^ (INNER * PAIR * d) ^ 1))
            for s in range(sections - 1)
            for i in range(size)
        ]
        got.append(lax.ppermute(block, ("section", "ctx"), route))
    return got[::-1]


def head_rows(block):
    return jnp.concatenate(
        [block[:, at : at + HD] for at in range(0, block.shape[1], HD)], axis=0
    )


def row_of(ref):
    return jnp.concatenate([ref[i : i + 1] for i in range(ref.shape[0])], axis=1)


def columns_of(index, ref, width):
    return ref.at[:, pl.ds(pl.multiple_of(index * width, HD), width)]


def on_diagonal(rows):
    shape = (rows, HD)
    return lax.broadcasted_iota(jnp.int32, shape, 0) == lax.broadcasted_iota(jnp.int32, shape, 1)


def queries_of(x, gain):
    rows = head_rows(x.astype(jnp.float32))
    gain = head_rows(jnp.broadcast_to(gain, x.shape))
    norm = lax.rsqrt(jnp.mean(rows * rows, axis=-1, keepdims=True) + epsilon)
    return (rows * norm * gain).astype(jnp.bfloat16)


def bias_of(keys_ref, frames):
    length = keys_ref.shape[0] - STAT_ROWS
    width = keys_ref.shape[1]
    rows = -(-length // width)
    tail = keys_ref[length:].astype(jnp.float32)
    key_frames = jnp.concatenate([tail[i : i + 1] for i in range(rows)], axis=1)[:, :length]
    return jnp.where(key_frames <= frames, 0.0, HIDDEN)[None]


def scores(queries, key_block, bias):
    count, keys, tokens = queries.shape[0], key_block.shape[0], bias.shape[1]
    raw = lax.dot_general(
        queries, key_block, (((1,), (1,)), ((), ())), preferred_element_type=jnp.float32
    )
    raw = raw.reshape(count // tokens, tokens, keys) * SCALE + bias
    return raw.reshape(count, keys)


def top_of(raw):
    top = jnp.max(raw, axis=-1, keepdims=True)
    return top.astype(jnp.bfloat16).astype(jnp.float32)


def weigh(raw, top, value_block):
    probs = jnp.exp2(raw - top).astype(jnp.bfloat16)
    ones = jnp.ones((value_block.shape[0], HD), jnp.bfloat16)
    return jnp.dot(
        probs, jnp.concatenate([value_block, ones], axis=1), preferred_element_type=jnp.float32
    )


def groups_of(count):
    groups = -(-count // HD)
    held = count // groups
    return [slice(c * held, (c + 1) * held) for c in range(groups)]


def write_chunk(out_ref, weighted, tops, totals):
    count = weighted.shape[0]
    line = lax.broadcasted_iota(jnp.int32, (STAT_ROWS, HD), 0)
    stats = jnp.zeros((STAT_ROWS, HD), jnp.float32)
    for c, (top, total) in enumerate(zip(tops, totals)):
        high = total.astype(jnp.bfloat16).astype(jnp.float32)
        for n, row in enumerate((top, high, total - high)):
            stats = jnp.where(line == 3 * c + n, row, stats)
    out_ref[:count] = weighted.astype(jnp.bfloat16)
    out_ref[count:] = stats.astype(jnp.bfloat16)


def write_sums(out_ref, weighted, top, total):
    groups = groups_of(weighted.shape[0])
    diagonal = on_diagonal(groups[0].stop)

    def rows(column):
        column = jnp.broadcast_to(column, weighted.shape)
        return [
            jnp.sum(jnp.where(diagonal, column[group], 0.0), axis=0, keepdims=True)
            for group in groups
        ]

    write_chunk(out_ref, weighted, rows(top), rows(total))


def joined(parts, normed, x=None):
    count = parts[0].shape[0] - STAT_ROWS
    groups = groups_of(count)
    diagonal = on_diagonal(groups[0].stop)
    stats = [part[count:].astype(jnp.float32) for part in parts]
    values, tops, totals = [], [], []
    for c, group in enumerate(groups):
        points = [s[3 * c : 3 * c + 1] for s in stats]
        top = functools.reduce(jnp.maximum, points)
        factors = [jnp.exp2(point - top) for point in points]
        total = sum(
            f * (s[3 * c + 1 : 3 * c + 2] + s[3 * c + 2 : 3 * c + 3])
            for f, s in zip(factors, stats)
        )
        if normed:
            inverse = 1.0 / total
            factors = [f * inverse for f in factors]
        terms = list(zip(factors, parts)) + ([] if x is None else [(total, x)])
        value = 0.0
        for factor, part in terms:
            weight = jnp.where(diagonal, factor, 0.0)[:, : group.stop - group.start]
            high = weight.astype(jnp.bfloat16)
            low = (weight - high.astype(jnp.float32)).astype(jnp.bfloat16)
            for term in (high, low):
                value = value + jnp.dot(term, part[group], preferred_element_type=jnp.float32)
        values.append(value)
        tops.append(top)
        totals.append(total)
    return jnp.concatenate(values, axis=0), tops, totals


def halve(staged_ref, copies, own_ref, given_ref, tail):
    length, width = staged_ref.shape
    half, step = width // PAIR, length // BLOCKS
    if tail is not None:
        given_ref[length:] = tail()
        own_ref[length:] = tail()
    place = place_here()
    for b in range(BLOCKS):
        if copies:
            copies[b].wait()
        rows = pl.ds(b * step, step)
        given_ref[rows] = columns_of(1 - place, staged_ref.at[rows], half)[...]
        own_ref[rows] = columns_of(place, staged_ref.at[rows], half)[...]


def load_keys_kernel(
    key_frames_in, keys_in, own_ref, given_ref,
    key_frames_ref, staged_ref, sems, small_sem,
):
    length, half = staged_ref.shape[0], own_ref.shape[1]
    small = pltpu.make_async_copy(key_frames_in, key_frames_ref, small_sem)
    small.start()

    def tail():
        row = row_of(key_frames_ref).astype(jnp.float32)
        lines = -(-length // half)
        row = jnp.concatenate([row, jnp.zeros((1, lines * half - length), jnp.float32)], axis=1)
        line = lax.broadcasted_iota(jnp.int32, (STAT_ROWS, half), 0)
        lower = jnp.zeros((STAT_ROWS, half), jnp.float32)
        for n in range(lines):
            lower = jnp.where(line == n, row[:, n * half : (n + 1) * half], lower)
        return lower.astype(jnp.bfloat16)

    copies, step = [], length // BLOCKS
    for b in range(BLOCKS):
        rows = pl.ds(b * step, step)
        copies.append(pltpu.make_async_copy(keys_in.at[rows], staged_ref.at[rows], sems.at[b]))
        copies[-1].start()
    small.wait()
    halve(staged_ref, copies, own_ref, given_ref, tail)


def load_keys(key_frames, keys):
    length, width = keys.shape
    shape = (length + STAT_ROWS, width // PAIR)
    return pl.pallas_call(
        load_keys_kernel,
        in_specs=[IN_HBM] * 2,
        out_specs=[WHOLE] * 2,
        out_shape=[pltpu.VMEM(shape, keys.dtype)] * 2,
        scratch_shapes=[
            pltpu.VMEM(key_frames.shape, key_frames.dtype),
            pltpu.VMEM((length, width), keys.dtype),
            pltpu.SemaphoreType.DMA((BLOCKS,)),
            pltpu.SemaphoreType.DMA,
        ],
        cost_estimate=pl.CostEstimate(
            flops=0, bytes_accessed=2 * length * width, transcendentals=0
        ),
        compiler_params=pltpu.CompilerParams(vmem_limit_bytes=16 * MIB),
        name="load_keys",
    )(*in_hbm(key_frames, keys))


def load_values_kernel(
    values_ref, act_frames_in, fresh_frames_in, batch_in, fresh_in, gain_in,
    own_ref, given_ref, batch_ref, gain_ref, fresh_ref, frames_ref,
    act_frames_ref, fresh_frames_ref, small_sems,
):
    place, half = place_here(), gain_ref.shape[1]
    small = [
        (act_frames_in, act_frames_ref),
        (fresh_frames_in, fresh_frames_ref),
        (columns_of(place, batch_in, half), batch_ref),
        (columns_of(place, gain_in, half), gain_ref),
        (columns_of(place, fresh_in, half), fresh_ref),
    ]
    small = [pltpu.make_async_copy(a, b, small_sems.at[n]) for n, (a, b) in enumerate(small)]
    for copy in small:
        copy.start()
    halve(values_ref, [], own_ref, given_ref, None)
    for copy in small[:2]:
        copy.wait()

    tokens = frames_ref.shape[1]
    section = lax.axis_index("section")
    own_row = act_frames_ref[pl.ds(section, 1), :].astype(jnp.float32)
    prior_row = act_frames_ref[pl.ds(jnp.maximum(section - 1, 0), 1), :].astype(jnp.float32)
    fresh_row = fresh_frames_ref[...].astype(jnp.float32)
    next_row = jnp.where(in_first_section(), fresh_row, prior_row)
    shape = (tokens, tokens)
    diagonal = lax.broadcasted_iota(jnp.int32, shape, 0) == lax.broadcasted_iota(jnp.int32, shape, 1)
    for tick, row in enumerate((own_row, next_row)):
        column = jnp.sum(jnp.where(diagonal, row, 0.0), axis=1, keepdims=True)
        frames_ref[tick] = jnp.broadcast_to(column, (tokens, HD))

    for copy in small[2:]:
        copy.wait()


def load_values(act_frames, fresh_frames, values, batch, fresh, gain):
    length, width = values.shape
    tokens, model = batch.shape
    half = model // PAIR
    shape = (length, width // PAIR)
    return pl.pallas_call(
        load_values_kernel,
        in_specs=[WHOLE] + [IN_HBM] * 5,
        out_specs=[WHOLE] * 6,
        out_shape=[
            pltpu.VMEM(shape, values.dtype),
            pltpu.VMEM(shape, values.dtype),
            pltpu.VMEM((tokens, half), batch.dtype),
            pltpu.VMEM((1, half), gain.dtype),
            pltpu.VMEM((tokens, half), fresh.dtype),
            pltpu.VMEM((2, tokens, HD), jnp.float32),
        ],
        scratch_shapes=[
            pltpu.VMEM(act_frames.shape, act_frames.dtype),
            pltpu.VMEM(fresh_frames.shape, fresh_frames.dtype),
            pltpu.SemaphoreType.DMA((5,)),
        ],
        cost_estimate=pl.CostEstimate(
            flops=0, bytes_accessed=2 * length * width, transcendentals=0
        ),
        compiler_params=pltpu.CompilerParams(vmem_limit_bytes=16 * MIB),
        name="load_values",
    )(*in_vmem(values), *in_hbm(act_frames, fresh_frames, batch, fresh, gain))


def begin_kernel(
    gain_ref, frames_ref, batch_ref, keys_ref, values_ref,
    queries_ref, sums_ref, stats_ref, share_ref,
):
    length = values_ref.shape[0]
    kv_here = values_ref.shape[1] // HD
    count, width = queries_ref.shape[0] // kv_here, gain_ref.shape[1] // kv_here
    bias = bias_of(keys_ref, frames_ref[0, :, :1])
    share_ref[...] = columns_of(outer_here(), batch_ref, share_ref.shape[1])[...]
    for g in range(kv_here):
        rows, columns = slice(g * count, (g + 1) * count), slice(g * width, (g + 1) * width)
        block = slice(g * HD, (g + 1) * HD)
        queries = queries_of(batch_ref[:, columns], gain_ref[:, columns])
        queries_ref[rows] = queries
        raw = scores(queries, keys_ref[:length, block], bias)
        top = top_of(raw)
        both = weigh(raw, top, values_ref[:, block])
        sums_ref[rows] = both[:, :HD]
        lane = lax.broadcasted_iota(jnp.int32, (count, HD), 1)
        stats_ref[rows] = jnp.where(lane < HD // 2, top, both[:, HD:])


def begin(gain, frames, batch, keys, values):
    length, width = values.shape
    tokens, half = batch.shape
    queries = HEADS // PAIR * tokens
    return pl.pallas_call(
        begin_kernel,
        in_specs=[WHOLE] * 5,
        out_specs=[WHOLE] * 4,
        out_shape=[
            jax.ShapeDtypeStruct((queries, HD), jnp.bfloat16),
            jax.ShapeDtypeStruct((queries, HD), jnp.float32),
            jax.ShapeDtypeStruct((queries, HD), jnp.float32),
            jax.ShapeDtypeStruct((tokens, half * HD // width), batch.dtype),
        ],
        cost_estimate=pl.CostEstimate(
            flops=2 * queries * length * 3 * HD,
            bytes_accessed=4 * length * width,
            transcendentals=queries * length,
        ),
        compiler_params=pltpu.CompilerParams(vmem_limit_bytes=16 * MIB),
        name="begin",
    )(*in_vmem(gain, frames, batch, keys, values))


def finish_kernel(
    d, kv_here, frames_ref, queries_ref, sums_ref, stats_ref, keys_ref, values_ref, out_ref
):
    length, count = values_ref.shape[0], queries_ref.shape[0] // kv_here
    g = outer_here() ^ d
    bias = bias_of(keys_ref, frames_ref[0, :, :1])
    rows = pl.ds(pl.multiple_of(g * count, count), count)
    raw = scores(queries_ref[rows], columns_of(g, keys_ref.at[:length], HD)[...], bias)
    stats = stats_ref[rows]
    before, totals = stats[:, :1], stats[:, HD // 2 : HD // 2 + 1]
    top = jnp.maximum(before, top_of(raw))
    factor = jnp.exp2(before - top)
    both = weigh(raw, top, columns_of(g, values_ref, HD)[...])
    weighted = both[:, :HD] + sums_ref[rows] * factor
    write_sums(out_ref, weighted, top, both[:, HD:] + totals * factor)


def chunk_call(kernel, name, d, kv_here, count, length, operands):
    return pl.pallas_call(
        functools.partial(kernel, d, kv_here),
        in_specs=[WHOLE] * len(operands),
        out_specs=WHOLE,
        out_shape=jax.ShapeDtypeStruct((count + STAT_ROWS, HD), jnp.bfloat16),
        cost_estimate=pl.CostEstimate(
            flops=2 * count * length * 3 * HD,
            bytes_accessed=4 * length * HD,
            transcendentals=count * length,
        ),
        compiler_params=pltpu.CompilerParams(vmem_limit_bytes=16 * MIB),
        name=name,
    )(*in_vmem(*operands))


def finish(d, frames, queries, sums, stats, keys, values):
    length, width = values.shape
    kv_here = width // HD
    operands = (frames, queries, sums, stats, keys, values)
    count = queries.shape[0] // kv_here
    return chunk_call(finish_kernel, "finish", d, kv_here, count, length, operands)


def partials_kernel(d, kv_here, gain_ref, frames_ref, fresh_ref, *refs):
    kv_refs, (handed_ref, out_ref) = (refs[0:2], refs[2:4]), refs[4:]
    length, width = kv_refs[0][1].shape[0], handed_ref.shape[1]
    g = outer_here() ^ d
    fresh = columns_of(g, fresh_ref, width)[...].astype(jnp.float32)
    x = jnp.where(in_first_section(), fresh, handed_ref[...].astype(jnp.float32))
    queries = queries_of(x, columns_of(g, gain_ref, width)[...])
    raws = [
        scores(
            queries,
            columns_of(g, keys_ref.at[:length], HD)[...],
            bias_of(keys_ref, frames_ref[1, :, :1]),
        )
        for keys_ref, _ in kv_refs
    ]
    top = functools.reduce(jnp.maximum, [top_of(raw) for raw in raws])
    both = sum(
        weigh(raw, top, columns_of(g, values_ref, HD)[...])
        for raw, (_, values_ref) in zip(raws, kv_refs)
    )
    write_sums(out_ref, both[:, :HD], top, both[:, HD:])


def partials(d, gain, frames, fresh, own, got, handed):
    length, width = own[1].shape
    count = handed.shape[1] // HD * handed.shape[0]
    operands = (gain, frames, fresh, *own, *got, handed)
    return chunk_call(
        partials_kernel, "partials", d, width // HD, count, PAIR * length, operands
    )


def merge_kernel(*refs):
    *parts, out_ref = refs
    write_chunk(out_ref, *joined(parts, False))


def merge_first_kernel(*refs):
    *parts, share_ref, out_ref = refs
    x = head_rows(share_ref[...].astype(jnp.float32)).astype(jnp.bfloat16)
    write_chunk(out_ref, *joined(parts, False, x))


def merge(kernel, *parts):
    return pl.pallas_call(
        kernel,
        in_specs=[WHOLE] * len(parts),
        out_specs=WHOLE,
        out_shape=jax.ShapeDtypeStruct(parts[0].shape, parts[0].dtype),
        compiler_params=pltpu.CompilerParams(vmem_limit_bytes=8 * MIB),
        name="merge",
    )(*in_vmem(*parts))


def attended(one_ref, two_ref):
    one, two = one_ref[...].astype(jnp.float32), two_ref[...].astype(jnp.float32)
    here = inner_here() == 0
    parts = [jnp.where(here, one, two), jnp.where(here, two, one)]
    value, _, _ = joined([part.astype(jnp.bfloat16) for part in parts], True)
    return value


def columns_from(rows, tokens):
    pieces = [rows[at : at + tokens] for at in range(0, rows.shape[0], tokens)]
    return jnp.concatenate(pieces, axis=1)


def combine_kernel(one_ref, two_ref, out_ref):
    out_ref[...] = columns_from(attended(one_ref, two_ref), out_ref.shape[0]).astype(jnp.bfloat16)


def combine_last_kernel(one_ref, two_ref, fresh_ref, handed_ref, out_ref):
    fresh = columns_of(outer_here(), fresh_ref, out_ref.shape[1])[...].astype(jnp.float32)
    x = jnp.where(in_first_section(), fresh, handed_ref[...].astype(jnp.float32))
    total = head_rows(x) + attended(one_ref, two_ref)
    out_ref[...] = columns_from(total, out_ref.shape[0]).astype(jnp.bfloat16)


def combine(kernel, name, tokens, one, two, *rest):
    width = (one.shape[0] - STAT_ROWS) // tokens * HD
    return pl.pallas_call(
        kernel,
        in_specs=[WHOLE] * (2 + len(rest)),
        out_specs=WHOLE,
        out_shape=jax.ShapeDtypeStruct((tokens, width), jnp.bfloat16),
        compiler_params=pltpu.CompilerParams(vmem_limit_bytes=8 * MIB),
        name=name,
    )(*in_vmem(one, two, *rest))


def assemble_kernel(*refs):
    *pieces, out_ref = refs
    outers, width = len(pieces) // PAIR, pieces[0].shape[1]
    for n, refs in enumerate((pieces[:outers], pieces[outers:])):
        place = (place_here() + n) % PAIR
        for d, ref in enumerate(refs):
            columns_of(place * outers + (outer_here() ^ d), out_ref, width)[...] = ref[...]


def assemble(mine, others):
    tokens, width = mine[0].shape
    pieces = [*mine, *others]
    return pl.pallas_call(
        assemble_kernel,
        in_specs=[WHOLE] * len(pieces),
        out_specs=WHOLE,
        out_shape=jax.ShapeDtypeStruct((tokens, len(pieces) * width), jnp.bfloat16),
        compiler_params=pltpu.CompilerParams(vmem_limit_bytes=8 * MIB),
        name="assemble",
    )(*in_vmem(*pieces))


def body(
    activations,
    act_frames,
    fresh_batch,
    fresh_frames,
    norm_gain,
    cached_keys,
    cached_values,
    key_frames,
):
    own_keys, given_keys = load_keys(key_frames.reshape(-1, HD), cached_keys[0])
    got_keys = swapped(given_keys)
    own_values, given_values, batch, gain, fresh, frames = load_values(
        act_frames, fresh_frames[None], cached_values[0], activations[0], fresh_batch, norm_gain
    )
    got_values = swapped(given_values)
    own, got = (own_keys, own_values), (got_keys, got_values)
    tokens = fresh_batch.shape[0]
    outers = lax.axis_size("ctx") // (INNER * PAIR)

    *terms, share = begin(gain, frames, batch, *own)
    chunk, *others = [finish(d, frames, *terms, *got) for d in range(outers)]
    chunk = merge(merge_first_kernel, *from_outer(others, 0)[::-1], chunk, share)
    one, two = swapped(chunk), from_inner(chunk)
    share = combine(combine_kernel, "combine", tokens, one, two)
    handed = from_section_before(share, outers)

    chunk, *others = [
        partials(d, gain, frames, fresh, own, got, piece) for d, piece in enumerate(handed)
    ]
    chunk = merge(merge_kernel, *from_outer(others)[::-1], swapped(chunk))
    one, two = swapped(chunk), from_inner(chunk)
    share = combine(combine_last_kernel, "combine_last", tokens, one, two, fresh, handed[0])
    theirs = [swapped(share), *from_outer([share] * len(others))]
    return assemble([share, *(swapped(piece) for piece in theirs[1:])], theirs)[None]


def solution(mesh):
    placed = (
        P("section", None, None),
        P(),
        P(),
        P(),
        P("section", None),
        P("section", "ctx", None),
        P("section", "ctx", None),
        P("ctx"),
    )
    return jax.shard_map(
        body, mesh=mesh, in_specs=placed, out_specs=P("section", None, None), check_vma=False
    )
```

```python
import functools
import math

import jax
import jax.numpy as jnp
from jax import lax
from jax.experimental import pallas as pl
from jax.experimental.pallas import tpu as pltpu
from jax.sharding import PartitionSpec as P

HEADS = 64
HD = 128
PAIR = 2
INNER = 2
BLOCKS = 4
STAT_ROWS = 16
HIDDEN = -(2.0**100)
SCALE = HD**-0.5 * math.log2(math.e)
MIB = 1 << 20

epsilon = 1e-05

WHOLE = pl.BlockSpec(memory_space=pltpu.VMEM)
IN_HBM = pl.BlockSpec(memory_space=pltpu.HBM)


def in_hbm(*arrays):
    return [pltpu.with_memory_space_constraint(a, pltpu.HBM) for a in arrays]


def in_vmem(*arrays):
    return [pltpu.with_memory_space_constraint(a, pltpu.VMEM) for a in arrays]


def place_here():
    return lax.axis_index("ctx") % PAIR


def inner_here():
    return lax.axis_index("ctx") // PAIR % INNER


def outer_here():
    return lax.axis_index("ctx") // (PAIR * INNER)


def in_first_section():
    return lax.axis_index("section") == 0


def swapped(block):
    return lax.ppermute(block, "ctx", [(i, i ^ 1) for i in range(lax.axis_size("ctx"))])


def from_inner(block):
    size = lax.axis_size("ctx")
    return lax.ppermute(block, "ctx", [(i, i ^ PAIR ^ 1) for i in range(size)])


def from_outer(blocks, other_place=1):
    size = lax.axis_size("ctx")
    got = [
        lax.ppermute(
            block, "ctx", [(i, i ^ (INNER * PAIR * d) ^ other_place) for i in range(size)]
        )
        for d, block in reversed(list(enumerate(blocks, 1)))
    ]
    return got[::-1]


def from_section_before(block, step):
    sections, size = lax.axis_size("section"), lax.axis_size("ctx")
    route = [
        (s * size + i, (s + 1) * size + (i ^ (PAIR * step) ^ 1))
        for s in range(sections - 1)
        for i in range(size)
    ]
    return lax.ppermute(block, ("section", "ctx"), route)


def head_rows(block):
    return jnp.concatenate(
        [block[:, at : at + HD] for at in range(0, block.shape[1], HD)], axis=0
    )


def row_of(ref):
    return jnp.concatenate([ref[i : i + 1] for i in range(ref.shape[0])], axis=1)


def columns_of(index, ref, width):
    return ref.at[:, pl.ds(pl.multiple_of(index * width, HD), width)]


def on_diagonal(rows):
    shape = (rows, HD)
    return lax.broadcasted_iota(jnp.int32, shape, 0) == lax.broadcasted_iota(jnp.int32, shape, 1)


def queries_of(x, gain):
    rows = head_rows(x.astype(jnp.float32))
    gain = head_rows(jnp.broadcast_to(gain, x.shape))
    norm = lax.rsqrt(jnp.mean(rows * rows, axis=-1, keepdims=True) + epsilon)
    return (rows * norm * gain).astype(jnp.bfloat16)


def bias_of(keys_ref, frames):
    length = keys_ref.shape[0] - STAT_ROWS
    width = keys_ref.shape[1]
    rows = -(-length // width)
    tail = keys_ref[length:].astype(jnp.float32)
    key_frames = jnp.concatenate([tail[i : i + 1] for i in range(rows)], axis=1)[:, :length]
    return jnp.where(key_frames <= frames, 0.0, HIDDEN)[None]


def scores(queries, key_block, bias):
    count, keys, tokens = queries.shape[0], key_block.shape[0], bias.shape[1]
    raw = lax.dot_general(
        queries, key_block, (((1,), (1,)), ((), ())), preferred_element_type=jnp.float32
    )
    raw = raw.reshape(count // tokens, tokens, keys) * SCALE + bias
    return raw.reshape(count, keys)


def top_of(raw):
    top = jnp.max(raw, axis=-1, keepdims=True)
    return top.astype(jnp.bfloat16).astype(jnp.float32)


def weigh(raw, top, value_block):
    probs = jnp.exp2(raw - top).astype(jnp.bfloat16)
    ones = jnp.ones((value_block.shape[0], HD), jnp.bfloat16)
    return jnp.dot(
        probs, jnp.concatenate([value_block, ones], axis=1), preferred_element_type=jnp.float32
    )


def groups_of(count):
    groups = -(-count // HD)
    held = count // groups
    return [slice(c * held, (c + 1) * held) for c in range(groups)]


def write_chunk(out_ref, weighted, tops, totals):
    count = weighted.shape[0]
    line = lax.broadcasted_iota(jnp.int32, (STAT_ROWS, HD), 0)
    stats = jnp.zeros((STAT_ROWS, HD), jnp.float32)
    for c, (top, total) in enumerate(zip(tops, totals)):
        high = total.astype(jnp.bfloat16).astype(jnp.float32)
        for n, row in enumerate((top, high, total - high)):
            stats = jnp.where(line == 3 * c + n, row, stats)
    out_ref[:count] = weighted.astype(jnp.bfloat16)
    out_ref[count:] = stats.astype(jnp.bfloat16)


def write_sums(out_ref, weighted, top, total):
    groups = groups_of(weighted.shape[0])
    diagonal = on_diagonal(groups[0].stop)

    def rows(column):
        column = jnp.broadcast_to(column, weighted.shape)
        return [
            jnp.sum(jnp.where(diagonal, column[group], 0.0), axis=0, keepdims=True)
            for group in groups
        ]

    write_chunk(out_ref, weighted, rows(top), rows(total))


def joined(parts, normed, x=None):
    count = parts[0].shape[0] - STAT_ROWS
    groups = groups_of(count)
    diagonal = on_diagonal(groups[0].stop)
    stats = [part[count:].astype(jnp.float32) for part in parts]
    values, tops, totals = [], [], []
    for c, group in enumerate(groups):
        points = [s[3 * c : 3 * c + 1] for s in stats]
        top = functools.reduce(jnp.maximum, points)
        factors = [jnp.exp2(point - top) for point in points]
        total = sum(
            f * (s[3 * c + 1 : 3 * c + 2] + s[3 * c + 2 : 3 * c + 3])
            for f, s in zip(factors, stats)
        )
        if normed:
            inverse = 1.0 / total
            factors = [f * inverse for f in factors]
        terms = list(zip(factors, parts)) + ([] if x is None else [(total, x)])
        value = 0.0
        for factor, part in terms:
            weight = jnp.where(diagonal, factor, 0.0)[:, : group.stop - group.start]
            high = weight.astype(jnp.bfloat16)
            low = (weight - high.astype(jnp.float32)).astype(jnp.bfloat16)
            for term in (high, low):
                value = value + jnp.dot(term, part[group], preferred_element_type=jnp.float32)
        values.append(value)
        tops.append(top)
        totals.append(total)
    return jnp.concatenate(values, axis=0), tops, totals


def halve(staged_ref, copies, own_ref, given_ref, tail):
    length, width = staged_ref.shape
    half, step = width // PAIR, length // BLOCKS
    if tail is not None:
        given_ref[length:] = tail()
        own_ref[length:] = tail()
    place = place_here()
    for b in range(BLOCKS):
        if copies:
            copies[b].wait()
        rows = pl.ds(b * step, step)
        given_ref[rows] = columns_of(1 - place, staged_ref.at[rows], half)[...]
        own_ref[rows] = columns_of(place, staged_ref.at[rows], half)[...]


def load_keys_kernel(
    key_frames_in, keys_in, own_ref, given_ref,
    key_frames_ref, staged_ref, sems, small_sem,
):
    length, half = staged_ref.shape[0], own_ref.shape[1]
    small = pltpu.make_async_copy(key_frames_in, key_frames_ref, small_sem)
    small.start()

    def tail():
        row = row_of(key_frames_ref).astype(jnp.float32)
        lines = -(-length // half)
        row = jnp.concatenate([row, jnp.zeros((1, lines * half - length), jnp.float32)], axis=1)
        line = lax.broadcasted_iota(jnp.int32, (STAT_ROWS, half), 0)
        lower = jnp.zeros((STAT_ROWS, half), jnp.float32)
        for n in range(lines):
            lower = jnp.where(line == n, row[:, n * half : (n + 1) * half], lower)
        return lower.astype(jnp.bfloat16)

    copies, step = [], length // BLOCKS
    for b in range(BLOCKS):
        rows = pl.ds(b * step, step)
        copies.append(pltpu.make_async_copy(keys_in.at[rows], staged_ref.at[rows], sems.at[b]))
        copies[-1].start()
    small.wait()
    halve(staged_ref, copies, own_ref, given_ref, tail)


def load_keys(key_frames, keys):
    length, width = keys.shape
    shape = (length + STAT_ROWS, width // PAIR)
    return pl.pallas_call(
        load_keys_kernel,
        in_specs=[IN_HBM] * 2,
        out_specs=[WHOLE] * 2,
        out_shape=[pltpu.VMEM(shape, keys.dtype)] * 2,
        scratch_shapes=[
            pltpu.VMEM(key_frames.shape, key_frames.dtype),
            pltpu.VMEM((length, width), keys.dtype),
            pltpu.SemaphoreType.DMA((BLOCKS,)),
            pltpu.SemaphoreType.DMA,
        ],
        cost_estimate=pl.CostEstimate(
            flops=0, bytes_accessed=2 * length * width, transcendentals=0
        ),
        compiler_params=pltpu.CompilerParams(vmem_limit_bytes=16 * MIB),
        name="load_keys",
    )(*in_hbm(key_frames, keys))


def load_values_kernel(
    values_ref, act_frames_in, fresh_frames_in, batch_in, fresh_in, gain_in,
    own_ref, given_ref, batch_ref, gain_ref, fresh_ref, fresh_gain_ref, frames_ref,
    act_frames_ref, fresh_frames_ref, small_sems,
):
    place, half, width = place_here(), gain_ref.shape[1], fresh_ref.shape[1]
    share = (1 - place) * (half // width) + outer_here()
    small = [
        (act_frames_in, act_frames_ref),
        (fresh_frames_in, fresh_frames_ref),
        (columns_of(place, batch_in, half), batch_ref),
        (columns_of(place, gain_in, half), gain_ref),
        (columns_of(share, fresh_in, width), fresh_ref),
        (columns_of(share, gain_in, width), fresh_gain_ref),
    ]
    small = [pltpu.make_async_copy(a, b, small_sems.at[n]) for n, (a, b) in enumerate(small)]
    for copy in small:
        copy.start()
    halve(values_ref, [], own_ref, given_ref, None)
    for copy in small[:2]:
        copy.wait()

    tokens = frames_ref.shape[1]
    section = lax.axis_index("section")
    own_row = act_frames_ref[pl.ds(section, 1), :].astype(jnp.float32)
    prior_row = act_frames_ref[pl.ds(jnp.maximum(section - 1, 0), 1), :].astype(jnp.float32)
    fresh_row = fresh_frames_ref[...].astype(jnp.float32)
    next_row = jnp.where(in_first_section(), fresh_row, prior_row)
    shape = (tokens, tokens)
    diagonal = lax.broadcasted_iota(jnp.int32, shape, 0) == lax.broadcasted_iota(jnp.int32, shape, 1)
    for tick, row in enumerate((own_row, next_row)):
        column = jnp.sum(jnp.where(diagonal, row, 0.0), axis=1, keepdims=True)
        frames_ref[tick] = jnp.broadcast_to(column, (tokens, HD))

    for copy in small[2:]:
        copy.wait()


def load_values(act_frames, fresh_frames, values, batch, fresh, gain):
    length, width = values.shape
    tokens, model = batch.shape
    half = model // PAIR
    share = half * INNER * PAIR // lax.axis_size("ctx")
    shape = (length, width // PAIR)
    return pl.pallas_call(
        load_values_kernel,
        in_specs=[WHOLE] + [IN_HBM] * 5,
        out_specs=[WHOLE] * 7,
        out_shape=[
            pltpu.VMEM(shape, values.dtype),
            pltpu.VMEM(shape, values.dtype),
            pltpu.VMEM((tokens, half), batch.dtype),
            pltpu.VMEM((1, half), gain.dtype),
            pltpu.VMEM((tokens, share), fresh.dtype),
            pltpu.VMEM((1, share), gain.dtype),
            pltpu.VMEM((2, tokens, HD), jnp.float32),
        ],
        scratch_shapes=[
            pltpu.VMEM(act_frames.shape, act_frames.dtype),
            pltpu.VMEM(fresh_frames.shape, fresh_frames.dtype),
            pltpu.SemaphoreType.DMA((6,)),
        ],
        cost_estimate=pl.CostEstimate(
            flops=0, bytes_accessed=2 * length * width, transcendentals=0
        ),
        compiler_params=pltpu.CompilerParams(vmem_limit_bytes=16 * MIB),
        name="load_values",
    )(*in_vmem(values), *in_hbm(act_frames, fresh_frames, batch, fresh, gain))


def begin_kernel(
    gain_ref, frames_ref, batch_ref, keys_ref, values_ref,
    queries_ref, sums_ref, stats_ref, share_ref,
):
    length = values_ref.shape[0]
    kv_here = values_ref.shape[1] // HD
    count, width = queries_ref.shape[0] // kv_here, gain_ref.shape[1] // kv_here
    bias = bias_of(keys_ref, frames_ref[0, :, :1])
    share_ref[...] = columns_of(outer_here(), batch_ref, share_ref.shape[1])[...]
    for g in range(kv_here):
        rows, columns = slice(g * count, (g + 1) * count), slice(g * width, (g + 1) * width)
        block = slice(g * HD, (g + 1) * HD)
        queries = queries_of(batch_ref[:, columns], gain_ref[:, columns])
        queries_ref[rows] = queries
        raw = scores(queries, keys_ref[:length, block], bias)
        top = top_of(raw)
        both = weigh(raw, top, values_ref[:, block])
        sums_ref[rows] = both[:, :HD]
        lane = lax.broadcasted_iota(jnp.int32, (count, HD), 1)
        stats_ref[rows] = jnp.where(lane < HD // 2, top, both[:, HD:])


def begin(gain, frames, batch, keys, values):
    length, width = values.shape
    tokens, half = batch.shape
    queries = HEADS // PAIR * tokens
    return pl.pallas_call(
        begin_kernel,
        in_specs=[WHOLE] * 5,
        out_specs=[WHOLE] * 4,
        out_shape=[
            jax.ShapeDtypeStruct((queries, HD), jnp.bfloat16),
            jax.ShapeDtypeStruct((queries, HD), jnp.float32),
            jax.ShapeDtypeStruct((queries, HD), jnp.float32),
            jax.ShapeDtypeStruct((tokens, half * HD // width), batch.dtype),
        ],
        cost_estimate=pl.CostEstimate(
            flops=2 * queries * length * 3 * HD,
            bytes_accessed=4 * length * width,
            transcendentals=queries * length,
        ),
        compiler_params=pltpu.CompilerParams(vmem_limit_bytes=16 * MIB),
        name="begin",
    )(*in_vmem(gain, frames, batch, keys, values))


def finish_kernel(
    steps, kv_here, frames_ref, queries_ref, sums_ref, stats_ref, keys_ref, values_ref, *out_refs
):
    length, count = values_ref.shape[0], queries_ref.shape[0] // kv_here
    bias = bias_of(keys_ref, frames_ref[0, :, :1])
    for d, out_ref in zip(steps, out_refs):
        g = outer_here() ^ d
        rows = pl.ds(pl.multiple_of(g * count, count), count)
        raw = scores(queries_ref[rows], columns_of(g, keys_ref.at[:length], HD)[...], bias)
        stats = stats_ref[rows]
        before, totals = stats[:, :1], stats[:, HD // 2 : HD // 2 + 1]
        top = jnp.maximum(before, top_of(raw))
        factor = jnp.exp2(before - top)
        both = weigh(raw, top, columns_of(g, values_ref, HD)[...])
        weighted = both[:, :HD] + sums_ref[rows] * factor
        write_sums(out_ref, weighted, top, both[:, HD:] + totals * factor)


def in_calls(call, outers):
    chunks = {}
    for steps in [(outers - 1, outers - 2)] + [(d,) for d in reversed(range(outers - 2))]:
        chunks.update(zip(steps, call(steps)))
    return [chunks[d] for d in range(outers)]


def chunk_call(kernel, name, steps, kv_here, count, length, operands):
    chunk = jax.ShapeDtypeStruct((count + STAT_ROWS, HD), jnp.bfloat16)
    return pl.pallas_call(
        functools.partial(kernel, steps, kv_here),
        in_specs=[WHOLE] * len(operands),
        out_specs=[WHOLE] * len(steps),
        out_shape=[chunk] * len(steps),
        cost_estimate=pl.CostEstimate(
            flops=2 * len(steps) * count * length * 3 * HD,
            bytes_accessed=4 * len(steps) * length * HD,
            transcendentals=len(steps) * count * length,
        ),
        compiler_params=pltpu.CompilerParams(vmem_limit_bytes=16 * MIB),
        name=name,
    )(*in_vmem(*operands))


def finish(steps, frames, queries, sums, stats, keys, values):
    length, width = values.shape
    kv_here = width // HD
    operands = (frames, queries, sums, stats, keys, values)
    count = queries.shape[0] // kv_here
    return chunk_call(finish_kernel, "finish", steps, kv_here, count, length, operands)


def partials_kernel(steps, kv_here, frames_ref, *refs):
    kv_refs, refs = (refs[0:2], refs[2:4]), refs[4:]
    length = kv_refs[0][1].shape[0]
    biases = [bias_of(keys_ref, frames_ref[1, :, :1]) for keys_ref, _ in kv_refs]
    for d, queries_ref, out_ref in zip(steps, refs, refs[len(steps) :]):
        g = outer_here() ^ d
        queries = queries_ref[...]
        raws = [
            scores(queries, columns_of(g, keys_ref.at[:length], HD)[...], bias)
            for (keys_ref, _), bias in zip(kv_refs, biases)
        ]
        top = functools.reduce(jnp.maximum, [top_of(raw) for raw in raws])
        both = sum(
            weigh(raw, top, columns_of(g, values_ref, HD)[...])
            for raw, (_, values_ref) in zip(raws, kv_refs)
        )
        write_sums(out_ref, both[:, :HD], top, both[:, HD:])


def partials(steps, frames, own, got, queries):
    length, width = own[1].shape
    count = queries[0].shape[0]
    operands = (frames, *own, *got, *(queries[d] for d in steps))
    return chunk_call(
        partials_kernel, "partials", steps, width // HD, count, PAIR * length, operands
    )


def merge_kernel(*refs):
    *parts, out_ref = refs
    write_chunk(out_ref, *joined(parts, False))


def merge_first_kernel(*refs):
    *parts, share_ref, out_ref = refs
    x = head_rows(share_ref[...].astype(jnp.float32)).astype(jnp.bfloat16)
    write_chunk(out_ref, *joined(parts, False, x))


def merge(kernel, *parts):
    return pl.pallas_call(
        kernel,
        in_specs=[WHOLE] * len(parts),
        out_specs=WHOLE,
        out_shape=jax.ShapeDtypeStruct(parts[0].shape, parts[0].dtype),
        compiler_params=pltpu.CompilerParams(vmem_limit_bytes=8 * MIB),
        name="merge",
    )(*in_vmem(*parts))


def attended(one_ref, two_ref):
    one, two = one_ref[...].astype(jnp.float32), two_ref[...].astype(jnp.float32)
    here = inner_here() == 0
    parts = [jnp.where(here, one, two), jnp.where(here, two, one)]
    value, _, _ = joined([part.astype(jnp.bfloat16) for part in parts], True)
    return value


def columns_from(rows, tokens):
    pieces = [rows[at : at + tokens] for at in range(0, rows.shape[0], tokens)]
    return jnp.concatenate(pieces, axis=1)


def combine_kernel(gain_ref, fresh_ref, one_ref, two_ref, share_ref, queries_ref):
    tokens = fresh_ref.shape[0]
    handed = columns_from(attended(one_ref, two_ref), tokens).astype(jnp.bfloat16)
    fresh = fresh_ref[...].astype(jnp.float32)
    share = jnp.where(in_first_section(), fresh, handed.astype(jnp.float32))
    share = share.astype(jnp.bfloat16)
    share_ref[...] = share
    queries_ref[...] = queries_of(share, gain_ref[...])


def combine(gain, fresh, one, two):
    count = one.shape[0] - STAT_ROWS
    return pl.pallas_call(
        combine_kernel,
        in_specs=[WHOLE] * 4,
        out_specs=[WHOLE] * 2,
        out_shape=[
            jax.ShapeDtypeStruct(fresh.shape, fresh.dtype),
            jax.ShapeDtypeStruct((count, HD), jnp.bfloat16),
        ],
        compiler_params=pltpu.CompilerParams(vmem_limit_bytes=8 * MIB),
        name="combine",
    )(*in_vmem(gain, fresh, one, two))


def combine_last_kernel(share_ref, one_ref, two_ref, out_ref):
    tokens = out_ref.shape[0]
    total = head_rows(share_ref[...].astype(jnp.float32)) + attended(one_ref, two_ref)
    out_ref[...] = columns_from(total, tokens).astype(jnp.bfloat16)


def combine_last(share, one, two):
    return pl.pallas_call(
        combine_last_kernel,
        in_specs=[WHOLE] * 3,
        out_specs=WHOLE,
        out_shape=jax.ShapeDtypeStruct(share.shape, share.dtype),
        compiler_params=pltpu.CompilerParams(vmem_limit_bytes=8 * MIB),
        name="combine_last",
    )(*in_vmem(share, one, two))


def assemble_kernel(*refs):
    *pieces, out_ref, sems = refs
    outers, width = len(pieces) // PAIR, pieces[0].shape[1]
    copies = []
    for n in range(PAIR):
        place = (place_here() + n) % PAIR
        for d in range(outers):
            target = columns_of(place * outers + (outer_here() ^ d), out_ref, width)
            copy = pltpu.make_async_copy(pieces[n * outers + d], target, sems.at[n, d])
            copy.start()
            copies.append(copy)
    for copy in copies:
        copy.wait()


def assemble(mine, others):
    tokens, width = mine[0].shape
    pieces = [*mine, *others]
    return pl.pallas_call(
        assemble_kernel,
        in_specs=[WHOLE] * len(pieces),
        out_specs=IN_HBM,
        out_shape=jax.ShapeDtypeStruct((tokens, len(pieces) * width), jnp.bfloat16),
        scratch_shapes=[pltpu.SemaphoreType.DMA((PAIR, len(mine)))],
        compiler_params=pltpu.CompilerParams(vmem_limit_bytes=8 * MIB),
        name="assemble",
    )(*in_vmem(*pieces))


def body(
    activations,
    act_frames,
    fresh_batch,
    fresh_frames,
    norm_gain,
    cached_keys,
    cached_values,
    key_frames,
):
    own_keys, given_keys = load_keys(key_frames.reshape(-1, HD), cached_keys[0])
    got_keys = swapped(given_keys)
    own_values, given_values, batch, gain, fresh, fresh_gain, frames = load_values(
        act_frames, fresh_frames[None], cached_values[0], activations[0], fresh_batch, norm_gain
    )
    got_values = swapped(given_values)
    own, got = (own_keys, own_values), (got_keys, got_values)

    outers = lax.axis_size("ctx") // (INNER * PAIR)
    *terms, share = begin(gain, frames, batch, *own)
    chunk, *others = in_calls(lambda steps: finish(steps, frames, *terms, *got), outers)
    chunk = merge(merge_first_kernel, *from_outer(others, 0)[::-1], chunk, share)
    one, two = [from_section_before(chunk, step) for step in range(INNER)]
    share, queries = combine(fresh_gain, fresh, one, two)
    queries = [swapped(queries), *from_outer([queries] * len(others))]

    chunk, *others = in_calls(lambda steps: partials(steps, frames, own, got, queries), outers)
    chunk = merge(merge_kernel, *from_outer(others)[::-1], swapped(chunk))
    one, two = swapped(chunk), from_inner(chunk)
    share = combine_last(swapped(share), one, two)
    theirs = [swapped(share), *from_outer([share] * len(others))]
    return assemble([share, *(swapped(piece) for piece in theirs[1:])], theirs)[None]


def solution(mesh):
    placed = (
        P("section", None, None),
        P(),
        P(),
        P(),
        P("section", None),
        P("section", "ctx", None),
        P("section", "ctx", None),
        P("ctx"),
    )
    return jax.shard_map(
        body, mesh=mesh, in_specs=placed, out_specs=P("section", None, None), check_vma=False
    )
```

```python
import functools
import math

import jax
import jax.numpy as jnp
from jax import lax
from jax.experimental import pallas as pl
from jax.experimental.pallas import tpu as pltpu
from jax.sharding import PartitionSpec as P

HEADS = 64
HD = 128
PAIR = 2
INNER = 2
BLOCKS = 4
STAT_ROWS = 16
HIDDEN = -(2.0**100)
SCALE = HD**-0.5 * math.log2(math.e)
MIB = 1 << 20

epsilon = 1e-05

WHOLE = pl.BlockSpec(memory_space=pltpu.VMEM)
IN_HBM = pl.BlockSpec(memory_space=pltpu.HBM)


def in_hbm(*arrays):
    return [pltpu.with_memory_space_constraint(a, pltpu.HBM) for a in arrays]


def in_vmem(*arrays):
    return [pltpu.with_memory_space_constraint(a, pltpu.VMEM) for a in arrays]


def place_here():
    return lax.axis_index("ctx") % PAIR


def inner_here():
    return lax.axis_index("ctx") // PAIR % INNER


def outer_here():
    return lax.axis_index("ctx") // (PAIR * INNER)


def in_first_section():
    return lax.axis_index("section") == 0


def swapped(block):
    return lax.ppermute(block, "ctx", [(i, i ^ 1) for i in range(lax.axis_size("ctx"))])


def from_inner(block):
    size = lax.axis_size("ctx")
    return lax.ppermute(block, "ctx", [(i, i ^ PAIR ^ 1) for i in range(size)])


def from_outer(blocks, other_place=1):
    size = lax.axis_size("ctx")
    got = [
        lax.ppermute(
            block, "ctx", [(i, i ^ (INNER * PAIR * d) ^ other_place) for i in range(size)]
        )
        for d, block in reversed(list(enumerate(blocks, 1)))
    ]
    return got[::-1]


def from_section_before(block, step):
    sections, size = lax.axis_size("section"), lax.axis_size("ctx")
    route = [
        (s * size + i, (s + 1) * size + (i ^ (PAIR * step) ^ 1))
        for s in range(sections - 1)
        for i in range(size)
    ]
    return lax.ppermute(block, ("section", "ctx"), route)


def head_rows(block):
    return jnp.concatenate(
        [block[:, at : at + HD] for at in range(0, block.shape[1], HD)], axis=0
    )


def row_of(ref):
    return jnp.concatenate([ref[i : i + 1] for i in range(ref.shape[0])], axis=1)


def columns_of(index, ref, width):
    return ref.at[:, pl.ds(pl.multiple_of(index * width, HD), width)]


def on_diagonal(rows):
    shape = (rows, HD)
    return lax.broadcasted_iota(jnp.int32, shape, 0) == lax.broadcasted_iota(jnp.int32, shape, 1)


def queries_of(x, gain):
    rows = head_rows(x.astype(jnp.float32))
    gain = head_rows(jnp.broadcast_to(gain, x.shape))
    norm = lax.rsqrt(jnp.mean(rows * rows, axis=-1, keepdims=True) + epsilon)
    return (rows * norm * gain).astype(jnp.bfloat16)


def bias_of(keys_ref, frames):
    length = keys_ref.shape[0] - STAT_ROWS
    width = keys_ref.shape[1]
    rows = -(-length // width)
    tail = keys_ref[length:].astype(jnp.float32)
    key_frames = jnp.concatenate([tail[i : i + 1] for i in range(rows)], axis=1)[:, :length]
    return jnp.where(key_frames <= frames, 0.0, HIDDEN)[None]


def scores(queries, key_block, bias):
    count, keys, tokens = queries.shape[0], key_block.shape[0], bias.shape[1]
    raw = lax.dot_general(
        queries, key_block, (((1,), (1,)), ((), ())), preferred_element_type=jnp.float32
    )
    raw = raw.reshape(count // tokens, tokens, keys) * SCALE + bias
    return raw.reshape(count, keys)


def top_of(raw):
    top = jnp.max(raw, axis=-1, keepdims=True)
    return top.astype(jnp.bfloat16).astype(jnp.float32)


def weigh(raw, top, value_block):
    probs = jnp.exp2(raw - top).astype(jnp.bfloat16)
    ones = jnp.ones((value_block.shape[0], HD), jnp.bfloat16)
    return jnp.dot(
        probs, jnp.concatenate([value_block, ones], axis=1), preferred_element_type=jnp.float32
    )


def groups_of(count):
    groups = -(-count // HD)
    held = count // groups
    return [slice(c * held, (c + 1) * held) for c in range(groups)]


def write_chunk(out_ref, weighted, tops, totals):
    count = weighted.shape[0]
    line = lax.broadcasted_iota(jnp.int32, (STAT_ROWS, HD), 0)
    stats = jnp.zeros((STAT_ROWS, HD), jnp.float32)
    for c, (top, total) in enumerate(zip(tops, totals)):
        high = total.astype(jnp.bfloat16).astype(jnp.float32)
        for n, row in enumerate((top, high, total - high)):
            stats = jnp.where(line == 3 * c + n, row, stats)
    out_ref[:count] = weighted.astype(jnp.bfloat16)
    out_ref[count:] = stats.astype(jnp.bfloat16)


def write_sums(out_ref, weighted, top, total):
    groups = groups_of(weighted.shape[0])
    diagonal = on_diagonal(groups[0].stop)

    def rows(column):
        column = jnp.broadcast_to(column, weighted.shape)
        return [
            jnp.sum(jnp.where(diagonal, column[group], 0.0), axis=0, keepdims=True)
            for group in groups
        ]

    write_chunk(out_ref, weighted, rows(top), rows(total))


def joined(parts, normed, x=None):
    count = parts[0].shape[0] - STAT_ROWS
    groups = groups_of(count)
    diagonal = on_diagonal(groups[0].stop)
    stats = [part[count:].astype(jnp.float32) for part in parts]
    values, tops, totals = [], [], []
    for c, group in enumerate(groups):
        points = [s[3 * c : 3 * c + 1] for s in stats]
        top = functools.reduce(jnp.maximum, points)
        factors = [jnp.exp2(point - top) for point in points]
        total = sum(
            f * (s[3 * c + 1 : 3 * c + 2] + s[3 * c + 2 : 3 * c + 3])
            for f, s in zip(factors, stats)
        )
        if normed:
            inverse = 1.0 / total
            factors = [f * inverse for f in factors]
        terms = list(zip(factors, parts)) + ([] if x is None else [(total, x)])
        value = 0.0
        for factor, part in terms:
            weight = jnp.where(diagonal, factor, 0.0)[:, : group.stop - group.start]
            high = weight.astype(jnp.bfloat16)
            low = (weight - high.astype(jnp.float32)).astype(jnp.bfloat16)
            for term in (high, low):
                value = value + jnp.dot(term, part[group], preferred_element_type=jnp.float32)
        values.append(value)
        tops.append(top)
        totals.append(total)
    return jnp.concatenate(values, axis=0), tops, totals


def halve(staged_ref, copies, own_ref, given_ref):
    length, width = staged_ref.shape
    half, step = width // PAIR, length // BLOCKS
    place = place_here()
    for b in range(BLOCKS):
        if copies:
            copies[b].wait()
        rows = pl.ds(b * step, step)
        given_ref[rows] = columns_of(1 - place, staged_ref.at[rows], half)[...]
        own_ref[rows] = columns_of(place, staged_ref.at[rows], half)[...]


def column_of(row):
    shape = (row.shape[1], row.shape[1])
    diagonal = lax.broadcasted_iota(jnp.int32, shape, 0) == lax.broadcasted_iota(jnp.int32, shape, 1)
    return jnp.sum(jnp.where(diagonal, row, 0.0), axis=1, keepdims=True)


def load_keys_kernel(
    act_frames_in, fresh_frames_in, key_frames_in, batch_in, fresh_in, gain_in, keys_in,
    own_ref, given_ref, batch_ref, gain_ref, fresh_ref, fresh_gain_ref, frames_ref,
    act_frames_ref, fresh_frames_ref, key_frames_ref, staged_ref, sems, small_sems,
):
    place, length, width = place_here(), staged_ref.shape[0], own_ref.shape[1]
    half, share = gain_ref.shape[1], fresh_ref.shape[1]
    index = (1 - place) * (half // share) + outer_here()
    small = [
        (act_frames_in, act_frames_ref),
        (fresh_frames_in, fresh_frames_ref),
        (key_frames_in, key_frames_ref),
        (columns_of(place, batch_in, half), batch_ref),
        (columns_of(place, gain_in, half), gain_ref),
        (columns_of(index, fresh_in, share), fresh_ref),
        (columns_of(index, gain_in, share), fresh_gain_ref),
    ]
    small = [pltpu.make_async_copy(a, b, small_sems.at[n]) for n, (a, b) in enumerate(small)]
    copies, step = [], length // BLOCKS
    for b in range(BLOCKS):
        rows = pl.ds(b * step, step)
        copies.append(pltpu.make_async_copy(keys_in.at[rows], staged_ref.at[rows], sems.at[b]))
    for copy in small[:3] + copies + small[3:]:
        copy.start()
    for copy in small[:3]:
        copy.wait()

    tokens = frames_ref.shape[1]
    section = lax.axis_index("section")
    own_row = act_frames_ref[pl.ds(section, 1), :].astype(jnp.float32)
    prior_row = act_frames_ref[pl.ds(jnp.maximum(section - 1, 0), 1), :].astype(jnp.float32)
    fresh_row = fresh_frames_ref[...].astype(jnp.float32)
    next_row = jnp.where(in_first_section(), fresh_row, prior_row)
    for tick, row in enumerate((own_row, next_row)):
        frames_ref[tick] = jnp.broadcast_to(column_of(row), (tokens, HD))

    row = row_of(key_frames_ref).astype(jnp.float32)
    lines = -(-length // width)
    row = jnp.concatenate([row, jnp.zeros((1, lines * width - length), jnp.float32)], axis=1)
    line = lax.broadcasted_iota(jnp.int32, (STAT_ROWS, width), 0)
    tail = jnp.zeros((STAT_ROWS, width), jnp.float32)
    for n in range(lines):
        tail = jnp.where(line == n, row[:, n * width : (n + 1) * width], tail)
    for ref in (own_ref, given_ref):
        ref[length:] = tail.astype(jnp.bfloat16)
    halve(staged_ref, copies, own_ref, given_ref)
    for copy in small[3:]:
        copy.wait()


def load_keys(act_frames, fresh_frames, key_frames, batch, fresh, gain, keys):
    length, width = keys.shape
    tokens, model = batch.shape
    half = model // PAIR
    share = half * INNER * PAIR // lax.axis_size("ctx")
    shape = (length + STAT_ROWS, width // PAIR)
    frames = (act_frames, fresh_frames, key_frames)
    return pl.pallas_call(
        load_keys_kernel,
        in_specs=[IN_HBM] * 7,
        out_specs=[WHOLE] * 7,
        out_shape=[
            pltpu.VMEM(shape, keys.dtype),
            pltpu.VMEM(shape, keys.dtype),
            pltpu.VMEM((tokens, half), batch.dtype),
            pltpu.VMEM((1, half), gain.dtype),
            pltpu.VMEM((tokens, share), fresh.dtype),
            pltpu.VMEM((1, share), gain.dtype),
            pltpu.VMEM((2, tokens, HD), jnp.float32),
        ],
        scratch_shapes=[
            *(pltpu.VMEM(a.shape, a.dtype) for a in frames),
            pltpu.VMEM((length, width), keys.dtype),
            pltpu.SemaphoreType.DMA((BLOCKS,)),
            pltpu.SemaphoreType.DMA((7,)),
        ],
        cost_estimate=pl.CostEstimate(
            flops=0, bytes_accessed=2 * length * width, transcendentals=0
        ),
        compiler_params=pltpu.CompilerParams(vmem_limit_bytes=16 * MIB),
        name="load_keys",
    )(*in_hbm(*frames, batch, fresh, gain, keys))


def halve_values_kernel(values_ref, own_ref, given_ref):
    halve(values_ref, [], own_ref, given_ref)


def halve_values(values):
    length, width = values.shape
    half = pltpu.VMEM((length, width // PAIR), values.dtype)
    return pl.pallas_call(
        halve_values_kernel,
        in_specs=[WHOLE],
        out_specs=[WHOLE] * 2,
        out_shape=[half, half],
        cost_estimate=pl.CostEstimate(
            flops=0, bytes_accessed=2 * length * width, transcendentals=0
        ),
        compiler_params=pltpu.CompilerParams(vmem_limit_bytes=16 * MIB),
        name="halve_values",
    )(*in_vmem(values))


def begin_kernel(
    gain_ref, frames_ref, batch_ref, keys_ref, values_ref,
    queries_ref, sums_ref, stats_ref, share_ref,
):
    length = values_ref.shape[0]
    kv_here = values_ref.shape[1] // HD
    count, width = queries_ref.shape[0] // kv_here, gain_ref.shape[1] // kv_here
    bias = bias_of(keys_ref, frames_ref[0, :, :1])
    share_ref[...] = columns_of(outer_here(), batch_ref, share_ref.shape[1])[...]
    for g in range(kv_here):
        rows, columns = slice(g * count, (g + 1) * count), slice(g * width, (g + 1) * width)
        block = slice(g * HD, (g + 1) * HD)
        queries = queries_of(batch_ref[:, columns], gain_ref[:, columns])
        queries_ref[rows] = queries
        raw = scores(queries, keys_ref[:length, block], bias)
        top = top_of(raw)
        both = weigh(raw, top, values_ref[:, block])
        sums_ref[rows] = both[:, :HD]
        lane = lax.broadcasted_iota(jnp.int32, (count, HD), 1)
        stats_ref[rows] = jnp.where(lane < HD // 2, top, both[:, HD:])


def begin(gain, frames, batch, keys, values):
    length, width = values.shape
    tokens, half = batch.shape
    queries = HEADS // PAIR * tokens
    return pl.pallas_call(
        begin_kernel,
        in_specs=[WHOLE] * 5,
        out_specs=[WHOLE] * 4,
        out_shape=[
            jax.ShapeDtypeStruct((queries, HD), jnp.bfloat16),
            jax.ShapeDtypeStruct((queries, HD), jnp.float32),
            jax.ShapeDtypeStruct((queries, HD), jnp.float32),
            jax.ShapeDtypeStruct((tokens, half * HD // width), batch.dtype),
        ],
        cost_estimate=pl.CostEstimate(
            flops=2 * queries * length * 3 * HD,
            bytes_accessed=4 * length * width,
            transcendentals=queries * length,
        ),
        compiler_params=pltpu.CompilerParams(vmem_limit_bytes=16 * MIB),
        name="begin",
    )(*in_vmem(gain, frames, batch, keys, values))


def finish_kernel(
    steps, kv_here, frames_ref, queries_ref, sums_ref, stats_ref, keys_ref, values_ref, *out_refs
):
    length, count = values_ref.shape[0], queries_ref.shape[0] // kv_here
    bias = bias_of(keys_ref, frames_ref[0, :, :1])
    for d, out_ref in zip(steps, out_refs):
        g = outer_here() ^ d
        rows = pl.ds(pl.multiple_of(g * count, count), count)
        raw = scores(queries_ref[rows], columns_of(g, keys_ref.at[:length], HD)[...], bias)
        stats = stats_ref[rows]
        before, totals = stats[:, :1], stats[:, HD // 2 : HD // 2 + 1]
        top = jnp.maximum(before, top_of(raw))
        factor = jnp.exp2(before - top)
        both = weigh(raw, top, columns_of(g, values_ref, HD)[...])
        weighted = both[:, :HD] + sums_ref[rows] * factor
        write_sums(out_ref, weighted, top, both[:, HD:] + totals * factor)


def in_calls(call, outers, together):
    chunks, far = {}, outers - together
    for steps in [tuple(range(far, outers))[::-1]] + [(d,) for d in reversed(range(far))]:
        chunks.update(zip(steps, call(steps)))
    return [chunks[d] for d in range(outers)]


def chunk_call(kernel, name, steps, kv_here, count, length, operands):
    chunk = jax.ShapeDtypeStruct((count + STAT_ROWS, HD), jnp.bfloat16)
    return pl.pallas_call(
        functools.partial(kernel, steps, kv_here),
        in_specs=[WHOLE] * len(operands),
        out_specs=[WHOLE] * len(steps),
        out_shape=[chunk] * len(steps),
        cost_estimate=pl.CostEstimate(
            flops=2 * len(steps) * count * length * 3 * HD,
            bytes_accessed=4 * len(steps) * length * HD,
            transcendentals=len(steps) * count * length,
        ),
        compiler_params=pltpu.CompilerParams(vmem_limit_bytes=16 * MIB),
        name=name,
    )(*in_vmem(*operands))


def finish(steps, frames, queries, sums, stats, keys, values):
    length, width = values.shape
    kv_here = width // HD
    operands = (frames, queries, sums, stats, keys, values)
    count = queries.shape[0] // kv_here
    return chunk_call(finish_kernel, "finish", steps, kv_here, count, length, operands)


def partials_kernel(steps, kv_here, frames_ref, *refs):
    kv_refs, refs = (refs[0:2], refs[2:4]), refs[4:]
    length = kv_refs[0][1].shape[0]
    biases = [bias_of(keys_ref, frames_ref[1, :, :1]) for keys_ref, _ in kv_refs]
    for d, queries_ref, out_ref in zip(steps, refs, refs[len(steps) :]):
        g = outer_here() ^ d
        tops, sums = [], []
        for group in groups_of(queries_ref.shape[0]):
            raws = [
                scores(queries_ref[group], columns_of(g, keys_ref.at[:length], HD)[...], bias)
                for (keys_ref, _), bias in zip(kv_refs, biases)
            ]
            top = functools.reduce(jnp.maximum, [top_of(raw) for raw in raws])
            tops.append(top)
            sums.append(
                sum(
                    weigh(raw, top, columns_of(g, values_ref, HD)[...])
                    for raw, (_, values_ref) in zip(raws, kv_refs)
                )
            )
        both = jnp.concatenate(sums, axis=0)
        write_sums(out_ref, both[:, :HD], jnp.concatenate(tops, axis=0), both[:, HD:])


def partials(steps, frames, own, got, queries):
    length, width = own[1].shape
    count = queries[0].shape[0]
    operands = (frames, *own, *got, *(queries[d] for d in steps))
    return chunk_call(
        partials_kernel, "partials", steps, width // HD, count, PAIR * length, operands
    )


def merge_kernel(*refs):
    *parts, out_ref = refs
    write_chunk(out_ref, *joined(parts, False))


def merge_first_kernel(*refs):
    *parts, share_ref, out_ref = refs
    x = head_rows(share_ref[...].astype(jnp.float32)).astype(jnp.bfloat16)
    write_chunk(out_ref, *joined(parts, False, x))


def merge(kernel, *parts):
    return pl.pallas_call(
        kernel,
        in_specs=[WHOLE] * len(parts),
        out_specs=WHOLE,
        out_shape=jax.ShapeDtypeStruct(parts[0].shape, parts[0].dtype),
        compiler_params=pltpu.CompilerParams(vmem_limit_bytes=8 * MIB),
        name="merge",
    )(*in_vmem(*parts))


def attended(one_ref, two_ref):
    one, two = one_ref[...].astype(jnp.float32), two_ref[...].astype(jnp.float32)
    here = inner_here() == 0
    parts = [jnp.where(here, one, two), jnp.where(here, two, one)]
    value, _, _ = joined([part.astype(jnp.bfloat16) for part in parts], True)
    return value


def columns_from(rows, tokens):
    pieces = [rows[at : at + tokens] for at in range(0, rows.shape[0], tokens)]
    return jnp.concatenate(pieces, axis=1)


def combine_kernel(gain_ref, fresh_ref, one_ref, two_ref, share_ref, queries_ref):
    tokens = fresh_ref.shape[0]
    handed = columns_from(attended(one_ref, two_ref), tokens).astype(jnp.bfloat16)
    fresh = fresh_ref[...].astype(jnp.float32)
    share = jnp.where(in_first_section(), fresh, handed.astype(jnp.float32))
    share = share.astype(jnp.bfloat16)
    share_ref[...] = share
    queries_ref[...] = queries_of(share, gain_ref[...])


def combine(gain, fresh, one, two):
    count = one.shape[0] - STAT_ROWS
    return pl.pallas_call(
        combine_kernel,
        in_specs=[WHOLE] * 4,
        out_specs=[WHOLE] * 2,
        out_shape=[
            jax.ShapeDtypeStruct(fresh.shape, fresh.dtype),
            jax.ShapeDtypeStruct((count, HD), jnp.bfloat16),
        ],
        compiler_params=pltpu.CompilerParams(vmem_limit_bytes=8 * MIB),
        name="combine",
    )(*in_vmem(gain, fresh, one, two))


def combine_last_kernel(share_ref, one_ref, two_ref, out_ref):
    tokens = out_ref.shape[0]
    total = head_rows(share_ref[...].astype(jnp.float32)) + attended(one_ref, two_ref)
    out_ref[...] = columns_from(total, tokens).astype(jnp.bfloat16)


def combine_last(share, one, two):
    return pl.pallas_call(
        combine_last_kernel,
        in_specs=[WHOLE] * 3,
        out_specs=WHOLE,
        out_shape=jax.ShapeDtypeStruct(share.shape, share.dtype),
        compiler_params=pltpu.CompilerParams(vmem_limit_bytes=8 * MIB),
        name="combine_last",
    )(*in_vmem(share, one, two))


def assemble_kernel(*refs):
    *pieces, out_ref = refs
    outers, width = len(pieces) // PAIR, pieces[0].shape[1]
    for n, refs in enumerate((pieces[:outers], pieces[outers:])):
        place = (place_here() + n) % PAIR
        for d, ref in enumerate(refs):
            columns_of(place * outers + (outer_here() ^ d), out_ref, width)[...] = ref[...]


def assemble(mine, others):
    tokens, width = mine[0].shape
    pieces = [*mine, *others]
    return pl.pallas_call(
        assemble_kernel,
        in_specs=[WHOLE] * len(pieces),
        out_specs=WHOLE,
        out_shape=jax.ShapeDtypeStruct((tokens, len(pieces) * width), jnp.bfloat16),
        compiler_params=pltpu.CompilerParams(vmem_limit_bytes=8 * MIB),
        name="assemble",
    )(*in_vmem(*pieces))


def body(
    activations,
    act_frames,
    fresh_batch,
    fresh_frames,
    norm_gain,
    cached_keys,
    cached_values,
    key_frames,
):
    own_keys, given_keys, batch, gain, fresh, fresh_gain, frames = load_keys(
        act_frames, fresh_frames[None], key_frames.reshape(-1, HD), activations[0], fresh_batch,
        norm_gain, cached_keys[0],
    )
    got_keys = swapped(given_keys)
    own_values, given_values = halve_values(cached_values[0])
    got_values = swapped(given_values)
    own, got = (own_keys, own_values), (got_keys, got_values)

    outers = lax.axis_size("ctx") // (INNER * PAIR)
    *terms, share = begin(gain, frames, batch, *own)
    chunk, *others = in_calls(lambda steps: finish(steps, frames, *terms, *got), outers, 2)
    chunk = merge(merge_first_kernel, *from_outer(others, 0)[::-1], chunk, share)
    one, two = [from_section_before(chunk, step) for step in range(INNER)]
    share, queries = combine(fresh_gain, fresh, one, two)
    queries = [swapped(queries), *from_outer([queries] * len(others))]

    chunk, *others = in_calls(lambda steps: partials(steps, frames, own, got, queries), outers, 1)
    chunk = merge(merge_kernel, *from_outer(others)[::-1], swapped(chunk))
    one, two = swapped(chunk), from_inner(chunk)
    share = combine_last(swapped(share), one, two)
    theirs = [swapped(share), *from_outer([share] * len(others))]
    return assemble([share, *(swapped(piece) for piece in theirs[1:])], theirs)[None]


def solution(mesh):
    placed = (
        P("section", None, None),
        P(),
        P(),
        P(),
        P("section", None),
        P("section", "ctx", None),
        P("section", "ctx", None),
        P("ctx"),
    )
    return jax.shard_map(
        body, mesh=mesh, in_specs=placed, out_specs=P("section", None, None), check_vma=False
    )
```

```python
import functools
import math

import jax
import jax.numpy as jnp
from jax import lax
from jax.experimental import pallas as pl
from jax.experimental.pallas import tpu as pltpu
from jax.sharding import PartitionSpec as P

HEADS = 64
HD = 128
PAIR = 2
INNER = 2
BLOCKS = 4
STAT_ROWS = 16
HIDDEN = -(2.0**100)
SCALE = HD**-0.5 * math.log2(math.e)
MIB = 1 << 20

epsilon = 1e-05

WHOLE = pl.BlockSpec(memory_space=pltpu.VMEM)
IN_HBM = pl.BlockSpec(memory_space=pltpu.HBM)


def in_hbm(*arrays):
    return [pltpu.with_memory_space_constraint(a, pltpu.HBM) for a in arrays]


def in_vmem(*arrays):
    return [pltpu.with_memory_space_constraint(a, pltpu.VMEM) for a in arrays]


def place_here():
    return lax.axis_index("ctx") % PAIR


def inner_here():
    return lax.axis_index("ctx") // PAIR % INNER


def outer_here():
    return lax.axis_index("ctx") // (PAIR * INNER)


def in_first_section():
    return lax.axis_index("section") == 0


def swapped(block):
    return lax.ppermute(block, "ctx", [(i, i ^ 1) for i in range(lax.axis_size("ctx"))])


def from_inner(block):
    size = lax.axis_size("ctx")
    return lax.ppermute(block, "ctx", [(i, i ^ PAIR ^ 1) for i in range(size)])


def from_outer(blocks, other_place=1):
    size = lax.axis_size("ctx")
    got = [
        lax.ppermute(
            block, "ctx", [(i, i ^ (INNER * PAIR * d) ^ other_place) for i in range(size)]
        )
        for d, block in reversed(list(enumerate(blocks, 1)))
    ]
    return got[::-1]


def from_section_before(block, step):
    sections, size = lax.axis_size("section"), lax.axis_size("ctx")
    route = [
        (s * size + i, (s + 1) * size + (i ^ (PAIR * step) ^ 1))
        for s in range(sections - 1)
        for i in range(size)
    ]
    return lax.ppermute(block, ("section", "ctx"), route)


def head_rows(block):
    return jnp.concatenate(
        [block[:, at : at + HD] for at in range(0, block.shape[1], HD)], axis=0
    )


def row_of(ref):
    return jnp.concatenate([ref[i : i + 1] for i in range(ref.shape[0])], axis=1)


def columns_of(index, ref, width):
    return ref.at[:, pl.ds(pl.multiple_of(index * width, HD), width)]


def on_diagonal(rows):
    shape = (rows, HD)
    return lax.broadcasted_iota(jnp.int32, shape, 0) == lax.broadcasted_iota(jnp.int32, shape, 1)


def queries_of(x, gain):
    rows = head_rows(x.astype(jnp.float32))
    gain = head_rows(jnp.broadcast_to(gain, x.shape))
    norm = lax.rsqrt(jnp.mean(rows * rows, axis=-1, keepdims=True) + epsilon)
    return (rows * norm * gain).astype(jnp.bfloat16)


def bias_of(keys_ref, frames):
    length = keys_ref.shape[0] - STAT_ROWS
    width = keys_ref.shape[1]
    rows = -(-length // width)
    tail = keys_ref[length:].astype(jnp.float32)
    key_frames = jnp.concatenate([tail[i : i + 1] for i in range(rows)], axis=1)[:, :length]
    return jnp.where(key_frames <= frames, 0.0, HIDDEN)[None]


def scores(queries, key_block, bias):
    count, keys, tokens = queries.shape[0], key_block.shape[0], bias.shape[1]
    raw = lax.dot_general(
        queries, key_block, (((1,), (1,)), ((), ())), preferred_element_type=jnp.float32
    )
    raw = raw.reshape(count // tokens, tokens, keys) * SCALE + bias
    return raw.reshape(count, keys)


def top_of(raw):
    top = jnp.max(raw, axis=-1, keepdims=True)
    return top.astype(jnp.bfloat16).astype(jnp.float32)


def weigh(raw, top, value_block):
    probs = jnp.exp2(raw - top).astype(jnp.bfloat16)
    ones = jnp.ones((value_block.shape[0], HD), jnp.bfloat16)
    return jnp.dot(
        probs, jnp.concatenate([value_block, ones], axis=1), preferred_element_type=jnp.float32
    )


def groups_of(count):
    groups = -(-count // HD)
    held = count // groups
    return [slice(c * held, (c + 1) * held) for c in range(groups)]


def write_chunk(out_ref, weighted, tops, totals):
    count = weighted.shape[0]
    line = lax.broadcasted_iota(jnp.int32, (STAT_ROWS, HD), 0)
    stats = jnp.zeros((STAT_ROWS, HD), jnp.float32)
    for c, (top, total) in enumerate(zip(tops, totals)):
        high = total.astype(jnp.bfloat16).astype(jnp.float32)
        for n, row in enumerate((top, high, total - high)):
            stats = jnp.where(line == 3 * c + n, row, stats)
    out_ref[:count] = weighted.astype(jnp.bfloat16)
    out_ref[count:] = stats.astype(jnp.bfloat16)


def write_sums(out_ref, weighted, top, total):
    groups = groups_of(weighted.shape[0])
    diagonal = on_diagonal(groups[0].stop)

    def rows(column):
        column = jnp.broadcast_to(column, weighted.shape)
        return [
            jnp.sum(jnp.where(diagonal, column[group], 0.0), axis=0, keepdims=True)
            for group in groups
        ]

    write_chunk(out_ref, weighted, rows(top), rows(total))


def joined(parts, normed, x=None):
    count = parts[0].shape[0] - STAT_ROWS
    groups = groups_of(count)
    diagonal = on_diagonal(groups[0].stop)
    stats = [part[count:].astype(jnp.float32) for part in parts]
    values, tops, totals = [], [], []
    for c, group in enumerate(groups):
        points = [s[3 * c : 3 * c + 1] for s in stats]
        top = functools.reduce(jnp.maximum, points)
        factors = [jnp.exp2(point - top) for point in points]
        total = sum(
            f * (s[3 * c + 1 : 3 * c + 2] + s[3 * c + 2 : 3 * c + 3])
            for f, s in zip(factors, stats)
        )
        if normed:
            inverse = 1.0 / total
            factors = [f * inverse for f in factors]
        terms = list(zip(factors, parts)) + ([] if x is None else [(total, x)])
        value = 0.0
        for factor, part in terms:
            weight = jnp.where(diagonal, factor, 0.0)[:, : group.stop - group.start]
            high = weight.astype(jnp.bfloat16)
            low = (weight - high.astype(jnp.float32)).astype(jnp.bfloat16)
            for term in (high, low):
                value = value + jnp.dot(term, part[group], preferred_element_type=jnp.float32)
        values.append(value)
        tops.append(top)
        totals.append(total)
    return jnp.concatenate(values, axis=0), tops, totals


def halve(staged_ref, copies, own_ref, given_ref):
    length, width = staged_ref.shape
    half, step = width // PAIR, length // BLOCKS
    place = place_here()
    for b in range(BLOCKS):
        if copies:
            copies[b].wait()
        rows = pl.ds(b * step, step)
        given_ref[rows] = columns_of(1 - place, staged_ref.at[rows], half)[...]
        own_ref[rows] = columns_of(place, staged_ref.at[rows], half)[...]


def column_of(row):
    shape = (row.shape[1], row.shape[1])
    diagonal = lax.broadcasted_iota(jnp.int32, shape, 0) == lax.broadcasted_iota(jnp.int32, shape, 1)
    return jnp.sum(jnp.where(diagonal, row, 0.0), axis=1, keepdims=True)


def load_keys_kernel(
    act_frames_in, fresh_frames_in, key_frames_in, batch_in, fresh_in, gain_in, keys_in,
    own_ref, given_ref, batch_ref, gain_ref, share_ref, fresh_ref, fresh_gain_ref, frames_ref,
    act_frames_ref, fresh_frames_ref, key_frames_ref, staged_ref, sems, small_sems,
):
    place, length, width = place_here(), staged_ref.shape[0], own_ref.shape[1]
    share = fresh_ref.shape[1]
    outers = gain_ref.shape[1] // PAIR // share
    own_share = place * outers + outer_here()
    index = (1 - place) * outers + outer_here()
    small = [
        (act_frames_in, act_frames_ref),
        (fresh_frames_in, fresh_frames_ref),
        (key_frames_in, key_frames_ref),
        (batch_in, batch_ref),
        (gain_in, gain_ref),
        (columns_of(own_share, batch_in, share), share_ref),
        (columns_of(index, fresh_in, share), fresh_ref),
        (columns_of(index, gain_in, share), fresh_gain_ref),
    ]
    small = [pltpu.make_async_copy(a, b, small_sems.at[n]) for n, (a, b) in enumerate(small)]
    copies, step = [], length // BLOCKS
    for b in range(BLOCKS):
        rows = pl.ds(b * step, step)
        copies.append(pltpu.make_async_copy(keys_in.at[rows], staged_ref.at[rows], sems.at[b]))
    for copy in small[:3] + copies + small[3:]:
        copy.start()
    for copy in small[:3]:
        copy.wait()

    tokens = frames_ref.shape[1]
    section = lax.axis_index("section")
    own_row = act_frames_ref[pl.ds(section, 1), :].astype(jnp.float32)
    prior_row = act_frames_ref[pl.ds(jnp.maximum(section - 1, 0), 1), :].astype(jnp.float32)
    fresh_row = fresh_frames_ref[...].astype(jnp.float32)
    next_row = jnp.where(in_first_section(), fresh_row, prior_row)
    for tick, row in enumerate((own_row, next_row)):
        frames_ref[tick] = jnp.broadcast_to(column_of(row), (tokens, HD))

    row = row_of(key_frames_ref).astype(jnp.float32)
    lines = -(-length // width)
    row = jnp.concatenate([row, jnp.zeros((1, lines * width - length), jnp.float32)], axis=1)
    line = lax.broadcasted_iota(jnp.int32, (STAT_ROWS, width), 0)
    tail = jnp.zeros((STAT_ROWS, width), jnp.float32)
    for n in range(lines):
        tail = jnp.where(line == n, row[:, n * width : (n + 1) * width], tail)
    for ref in (own_ref, given_ref):
        ref[length:] = tail.astype(jnp.bfloat16)
    halve(staged_ref, copies, own_ref, given_ref)
    for copy in small[3:]:
        copy.wait()


def load_keys(act_frames, fresh_frames, key_frames, batch, fresh, gain, keys):
    length, width = keys.shape
    tokens, model = batch.shape
    share = model * INNER // lax.axis_size("ctx")
    shape = (length + STAT_ROWS, width // PAIR)
    frames = (act_frames, fresh_frames, key_frames)
    return pl.pallas_call(
        load_keys_kernel,
        in_specs=[IN_HBM] * 7,
        out_specs=[WHOLE] * 8,
        out_shape=[
            pltpu.VMEM(shape, keys.dtype),
            pltpu.VMEM(shape, keys.dtype),
            pltpu.VMEM(batch.shape, batch.dtype),
            pltpu.VMEM(gain.shape, gain.dtype),
            pltpu.VMEM((tokens, share), batch.dtype),
            pltpu.VMEM((tokens, share), fresh.dtype),
            pltpu.VMEM((1, share), gain.dtype),
            pltpu.VMEM((2, tokens, HD), jnp.float32),
        ],
        scratch_shapes=[
            *(pltpu.VMEM(a.shape, a.dtype) for a in frames),
            pltpu.VMEM((length, width), keys.dtype),
            pltpu.SemaphoreType.DMA((BLOCKS,)),
            pltpu.SemaphoreType.DMA((8,)),
        ],
        cost_estimate=pl.CostEstimate(
            flops=0, bytes_accessed=2 * length * width, transcendentals=0
        ),
        compiler_params=pltpu.CompilerParams(vmem_limit_bytes=16 * MIB),
        name="load_keys",
    )(*in_hbm(*frames, batch, fresh, gain, keys))


def halve_values_kernel(values_ref, own_ref, given_ref):
    halve(values_ref, [], own_ref, given_ref)


def halve_values(values):
    length, width = values.shape
    half = pltpu.VMEM((length, width // PAIR), values.dtype)
    return pl.pallas_call(
        halve_values_kernel,
        in_specs=[WHOLE],
        out_specs=[WHOLE] * 2,
        out_shape=[half, half],
        cost_estimate=pl.CostEstimate(
            flops=0, bytes_accessed=2 * length * width, transcendentals=0
        ),
        compiler_params=pltpu.CompilerParams(vmem_limit_bytes=16 * MIB),
        name="halve_values",
    )(*in_vmem(values))


def first_kernel(other, gain_ref, frames_ref, batch_ref, keys_ref, values_ref, out_ref):
    length, kv_here = values_ref.shape[0], out_ref.shape[0]
    width = gain_ref.shape[1] // (PAIR * kv_here)
    place = (place_here() + other) % PAIR
    bias = bias_of(keys_ref, frames_ref[0, :, :1])
    for g in range(kv_here):
        index, block = place * kv_here + g, slice(g * HD, (g + 1) * HD)
        x, gain = columns_of(index, batch_ref, width)[...], columns_of(index, gain_ref, width)[...]
        raw = scores(queries_of(x, gain), keys_ref[:length, block], bias)
        top = top_of(raw)
        both = weigh(raw, top, values_ref[:, block])
        write_sums(out_ref.at[g], both[:, :HD], top, both[:, HD:])


def first(other, gain, frames, batch, keys, values):
    length, width = values.shape
    tokens = batch.shape[0]
    kv_here = width // HD
    queries = HEADS // PAIR * tokens
    return pl.pallas_call(
        functools.partial(first_kernel, other),
        in_specs=[WHOLE] * 5,
        out_specs=WHOLE,
        out_shape=jax.ShapeDtypeStruct((kv_here, queries // kv_here + STAT_ROWS, HD), jnp.bfloat16),
        cost_estimate=pl.CostEstimate(
            flops=2 * queries * length * 3 * HD,
            bytes_accessed=4 * length * width,
            transcendentals=queries * length,
        ),
        compiler_params=pltpu.CompilerParams(vmem_limit_bytes=16 * MIB),
        name="first",
    )(*in_vmem(gain, frames, batch, keys, values))


def finish_kernel(steps, mine_ref, got_ref, *out_refs):
    for d, out_ref in zip(steps, out_refs):
        g = outer_here() ^ d
        write_chunk(out_ref, *joined([mine_ref.at[g], got_ref.at[g]], False))


def finish(steps, mine, got):
    chunk = jax.ShapeDtypeStruct(mine.shape[1:], mine.dtype)
    return pl.pallas_call(
        functools.partial(finish_kernel, steps),
        in_specs=[WHOLE] * 2,
        out_specs=[WHOLE] * len(steps),
        out_shape=[chunk] * len(steps),
        compiler_params=pltpu.CompilerParams(vmem_limit_bytes=8 * MIB),
        name="finish",
    )(*in_vmem(mine, got))


def in_calls(call, outers, together):
    chunks, far = {}, outers - together
    for steps in [tuple(range(far, outers))[::-1]] + [(d,) for d in reversed(range(far))]:
        chunks.update(zip(steps, call(steps)))
    return [chunks[d] for d in range(outers)]


def chunk_call(kernel, name, steps, kv_here, count, length, operands):
    chunk = jax.ShapeDtypeStruct((count + STAT_ROWS, HD), jnp.bfloat16)
    return pl.pallas_call(
        functools.partial(kernel, steps, kv_here),
        in_specs=[WHOLE] * len(operands),
        out_specs=[WHOLE] * len(steps),
        out_shape=[chunk] * len(steps),
        cost_estimate=pl.CostEstimate(
            flops=2 * len(steps) * count * length * 3 * HD,
            bytes_accessed=4 * len(steps) * length * HD,
            transcendentals=len(steps) * count * length,
        ),
        compiler_params=pltpu.CompilerParams(vmem_limit_bytes=16 * MIB),
        name=name,
    )(*in_vmem(*operands))


def partials_kernel(steps, kv_here, frames_ref, *refs):
    kv_refs, refs = (refs[0:2], refs[2:4]), refs[4:]
    length = kv_refs[0][1].shape[0]
    biases = [bias_of(keys_ref, frames_ref[1, :, :1]) for keys_ref, _ in kv_refs]
    for d, queries_ref, out_ref in zip(steps, refs, refs[len(steps) :]):
        g = outer_here() ^ d
        raws = [
            scores(queries_ref[...], columns_of(g, keys_ref.at[:length], HD)[...], bias)
            for (keys_ref, _), bias in zip(kv_refs, biases)
        ]
        top = functools.reduce(jnp.maximum, [top_of(raw) for raw in raws])
        both = sum(
            weigh(raw, top, columns_of(g, values_ref, HD)[...])
            for raw, (_, values_ref) in zip(raws, kv_refs)
        )
        write_sums(out_ref, both[:, :HD], top, both[:, HD:])


def partials(steps, frames, own, got, queries):
    length, width = own[1].shape
    count = queries[0].shape[0]
    operands = (frames, *own, *got, *(queries[d] for d in steps))
    return chunk_call(
        partials_kernel, "partials", steps, width // HD, count, PAIR * length, operands
    )


def merge_kernel(*refs):
    *parts, out_ref = refs
    write_chunk(out_ref, *joined(parts, False))


def merge_first_kernel(*refs):
    *parts, share_ref, out_ref = refs
    x = head_rows(share_ref[...].astype(jnp.float32)).astype(jnp.bfloat16)
    write_chunk(out_ref, *joined(parts, False, x))


def merge(kernel, *parts):
    return pl.pallas_call(
        kernel,
        in_specs=[WHOLE] * len(parts),
        out_specs=WHOLE,
        out_shape=jax.ShapeDtypeStruct(parts[0].shape, parts[0].dtype),
        compiler_params=pltpu.CompilerParams(vmem_limit_bytes=8 * MIB),
        name="merge",
    )(*in_vmem(*parts))


def attended(one_ref, two_ref):
    one, two = one_ref[...].astype(jnp.float32), two_ref[...].astype(jnp.float32)
    here = inner_here() == 0
    parts = [jnp.where(here, one, two), jnp.where(here, two, one)]
    value, _, _ = joined([part.astype(jnp.bfloat16) for part in parts], True)
    return value


def columns_from(rows, tokens):
    pieces = [rows[at : at + tokens] for at in range(0, rows.shape[0], tokens)]
    return jnp.concatenate(pieces, axis=1)


def combine_kernel(gain_ref, fresh_ref, one_ref, two_ref, share_ref, queries_ref):
    tokens = fresh_ref.shape[0]
    handed = columns_from(attended(one_ref, two_ref), tokens).astype(jnp.bfloat16)
    fresh = fresh_ref[...].astype(jnp.float32)
    share = jnp.where(in_first_section(), fresh, handed.astype(jnp.float32))
    share = share.astype(jnp.bfloat16)
    share_ref[...] = share
    queries_ref[...] = queries_of(share, gain_ref[...])


def combine(gain, fresh, one, two):
    count = one.shape[0] - STAT_ROWS
    return pl.pallas_call(
        combine_kernel,
        in_specs=[WHOLE] * 4,
        out_specs=[WHOLE] * 2,
        out_shape=[
            jax.ShapeDtypeStruct(fresh.shape, fresh.dtype),
            jax.ShapeDtypeStruct((count, HD), jnp.bfloat16),
        ],
        compiler_params=pltpu.CompilerParams(vmem_limit_bytes=8 * MIB),
        name="combine",
    )(*in_vmem(gain, fresh, one, two))


def combine_last_kernel(share_ref, one_ref, two_ref, out_ref):
    tokens = out_ref.shape[0]
    total = head_rows(share_ref[...].astype(jnp.float32)) + attended(one_ref, two_ref)
    out_ref[...] = columns_from(total, tokens).astype(jnp.bfloat16)


def combine_last(share, one, two):
    return pl.pallas_call(
        combine_last_kernel,
        in_specs=[WHOLE] * 3,
        out_specs=WHOLE,
        out_shape=jax.ShapeDtypeStruct(share.shape, share.dtype),
        compiler_params=pltpu.CompilerParams(vmem_limit_bytes=8 * MIB),
        name="combine_last",
    )(*in_vmem(share, one, two))


def assemble_kernel(*refs):
    *pieces, out_ref = refs
    outers, width = len(pieces) // PAIR, pieces[0].shape[1]
    for n, refs in enumerate((pieces[:outers], pieces[outers:])):
        place = (place_here() + n) % PAIR
        for d, ref in enumerate(refs):
            columns_of(place * outers + (outer_here() ^ d), out_ref, width)[...] = ref[...]


def assemble(mine, others):
    tokens, width = mine[0].shape
    pieces = [*mine, *others]
    return pl.pallas_call(
        assemble_kernel,
        in_specs=[WHOLE] * len(pieces),
        out_specs=WHOLE,
        out_shape=jax.ShapeDtypeStruct((tokens, len(pieces) * width), jnp.bfloat16),
        compiler_params=pltpu.CompilerParams(vmem_limit_bytes=8 * MIB),
        name="assemble",
    )(*in_vmem(*pieces))


def body(
    activations,
    act_frames,
    fresh_batch,
    fresh_frames,
    norm_gain,
    cached_keys,
    cached_values,
    key_frames,
):
    own_keys, given_keys, batch, gain, share, fresh, fresh_gain, frames = load_keys(
        act_frames, fresh_frames[None], key_frames.reshape(-1, HD), activations[0], fresh_batch,
        norm_gain, cached_keys[0],
    )
    own_values, given_values = halve_values(cached_values[0])

    outers = lax.axis_size("ctx") // (INNER * PAIR)
    theirs = swapped(first(1, gain, frames, batch, given_keys, given_values))
    mine = first(0, gain, frames, batch, own_keys, own_values)
    chunk, *others = in_calls(lambda steps: finish(steps, mine, theirs), outers, 2)
    own, got = (own_keys, own_values), (swapped(given_keys), swapped(given_values))
    chunk = merge(merge_first_kernel, *from_outer(others, 0)[::-1], chunk, share)
    one, two = [from_section_before(chunk, step) for step in range(INNER)]
    share, queries = combine(fresh_gain, fresh, one, two)
    queries = [swapped(queries), *from_outer([queries] * len(others))]

    chunk, *others = in_calls(lambda steps: partials(steps, frames, own, got, queries), outers, 1)
    chunk = merge(merge_kernel, *from_outer(others)[::-1], swapped(chunk))
    one, two = swapped(chunk), from_inner(chunk)
    share = combine_last(swapped(share), one, two)
    theirs = [swapped(share), *from_outer([share] * len(others))]
    return assemble([share, *(swapped(piece) for piece in theirs[1:])], theirs)[None]


def solution(mesh):
    placed = (
        P("section", None, None),
        P(),
        P(),
        P(),
        P("section", None),
        P("section", "ctx", None),
        P("section", "ctx", None),
        P("ctx"),
    )
    return jax.shard_map(
        body, mesh=mesh, in_specs=placed, out_specs=P("section", None, None), check_vma=False
    )
```

```python
import functools
import math

import jax
import jax.numpy as jnp
from jax import lax
from jax.experimental import pallas as pl
from jax.experimental.pallas import tpu as pltpu
from jax.sharding import PartitionSpec as P

HEADS = 64
HD = 128
PAIR = 2
INNER = 2
BLOCKS = 8
STAT_ROWS = 16
HIDDEN = -(2.0**100)
SCALE = HD**-0.5 * math.log2(math.e)
MIB = 1 << 20

epsilon = 1e-05

WHOLE = pl.BlockSpec(memory_space=pltpu.VMEM)
IN_HBM = pl.BlockSpec(memory_space=pltpu.HBM)


def in_hbm(*arrays):
    return [pltpu.with_memory_space_constraint(a, pltpu.HBM) for a in arrays]


def in_vmem(*arrays):
    return [pltpu.with_memory_space_constraint(a, pltpu.VMEM) for a in arrays]


def place_here():
    return lax.axis_index("ctx") % PAIR


def inner_here():
    return lax.axis_index("ctx") // PAIR % INNER


def outer_here():
    return lax.axis_index("ctx") // (PAIR * INNER)


def in_first_section():
    return lax.axis_index("section") == 0


def swapped(block):
    return lax.ppermute(block, "ctx", [(i, i ^ 1) for i in range(lax.axis_size("ctx"))])


def from_inner(block):
    size = lax.axis_size("ctx")
    return lax.ppermute(block, "ctx", [(i, i ^ PAIR ^ 1) for i in range(size)])


def from_outer(blocks):
    size = lax.axis_size("ctx")
    got = [
        lax.ppermute(block, "ctx", [(i, i ^ (INNER * PAIR * d) ^ 1) for i in range(size)])
        for d, block in reversed(list(enumerate(blocks, 1)))
    ]
    return got[::-1]


def from_section_before(block, step):
    sections, size = lax.axis_size("section"), lax.axis_size("ctx")
    route = [
        (s * size + i, (s + 1) * size + (i ^ (PAIR * step) ^ 1))
        for s in range(sections - 1)
        for i in range(size)
    ]
    return lax.ppermute(block, ("section", "ctx"), route)


def head_rows(block):
    return jnp.concatenate(
        [block[:, at : at + HD] for at in range(0, block.shape[1], HD)], axis=0
    )


def row_of(ref):
    return jnp.concatenate([ref[i : i + 1] for i in range(ref.shape[0])], axis=1)


def columns_of(index, ref, width):
    return ref.at[:, pl.ds(pl.multiple_of(index * width, HD), width)]


def on_diagonal(rows):
    shape = (rows, HD)
    return lax.broadcasted_iota(jnp.int32, shape, 0) == lax.broadcasted_iota(jnp.int32, shape, 1)


def queries_of(x, gain):
    rows = head_rows(x.astype(jnp.float32))
    gain = head_rows(jnp.broadcast_to(gain, x.shape))
    norm = lax.rsqrt(jnp.mean(rows * rows, axis=-1, keepdims=True) + epsilon)
    return (rows * norm * gain).astype(jnp.bfloat16)


def bias_of(keys_ref, frames):
    length = keys_ref.shape[0] - STAT_ROWS
    width = keys_ref.shape[1]
    rows = -(-length // width)
    tail = keys_ref[length:].astype(jnp.float32)
    key_frames = jnp.concatenate([tail[i : i + 1] for i in range(rows)], axis=1)[:, :length]
    return jnp.where(key_frames <= frames, 0.0, HIDDEN)[None]


def scores(queries, key_block, bias):
    count, keys, tokens = queries.shape[0], key_block.shape[0], bias.shape[1]
    raw = lax.dot_general(
        queries, key_block, (((1,), (1,)), ((), ())), preferred_element_type=jnp.float32
    )
    raw = raw.reshape(count // tokens, tokens, keys) * SCALE + bias
    return raw.reshape(count, keys)


def top_of(raw):
    top = jnp.max(raw, axis=-1, keepdims=True)
    return top.astype(jnp.bfloat16).astype(jnp.float32)


def weigh(raw, top, value_block):
    probs = jnp.exp2(raw - top).astype(jnp.bfloat16)
    ones = jnp.ones((value_block.shape[0], HD), jnp.bfloat16)
    return jnp.dot(
        probs, jnp.concatenate([value_block, ones], axis=1), preferred_element_type=jnp.float32
    )


def groups_of(count):
    groups = -(-count // HD)
    held = count // groups
    return [slice(c * held, (c + 1) * held) for c in range(groups)]


def write_chunk(out_ref, weighted, tops, totals):
    count = weighted.shape[0]
    line = lax.broadcasted_iota(jnp.int32, (STAT_ROWS, HD), 0)
    stats = jnp.zeros((STAT_ROWS, HD), jnp.float32)
    for c, (top, total) in enumerate(zip(tops, totals)):
        high = total.astype(jnp.bfloat16).astype(jnp.float32)
        for n, row in enumerate((top, high, total - high)):
            stats = jnp.where(line == 3 * c + n, row, stats)
    out_ref[:count] = weighted.astype(jnp.bfloat16)
    out_ref[count:] = stats.astype(jnp.bfloat16)


def write_sums(out_ref, weighted, top, total):
    groups = groups_of(weighted.shape[0])
    diagonal = on_diagonal(groups[0].stop)

    def rows(column):
        column = jnp.broadcast_to(column, weighted.shape)
        return [
            jnp.sum(jnp.where(diagonal, column[group], 0.0), axis=0, keepdims=True)
            for group in groups
        ]

    write_chunk(out_ref, weighted, rows(top), rows(total))


def joined(parts, normed, x=None):
    count = parts[0].shape[0] - STAT_ROWS
    groups = groups_of(count)
    diagonal = on_diagonal(groups[0].stop)
    stats = [part[count:].astype(jnp.float32) for part in parts]
    values, tops, totals = [], [], []
    for c, group in enumerate(groups):
        points = [s[3 * c : 3 * c + 1] for s in stats]
        top = functools.reduce(jnp.maximum, points)
        factors = [jnp.exp2(point - top) for point in points]
        total = sum(
            f * (s[3 * c + 1 : 3 * c + 2] + s[3 * c + 2 : 3 * c + 3])
            for f, s in zip(factors, stats)
        )
        if normed:
            inverse = 1.0 / total
            factors = [f * inverse for f in factors]
        terms = list(zip(factors, parts)) + ([] if x is None else [(total, x)])
        value = 0.0
        for factor, part in terms:
            weight = jnp.where(diagonal, factor, 0.0)[:, : group.stop - group.start]
            high = weight.astype(jnp.bfloat16)
            low = (weight - high.astype(jnp.float32)).astype(jnp.bfloat16)
            for term in (high, low):
                value = value + jnp.dot(term, part[group], preferred_element_type=jnp.float32)
        values.append(value)
        tops.append(top)
        totals.append(total)
    return jnp.concatenate(values, axis=0), tops, totals


def halve(staged_ref, copies, own_ref, given_ref):
    length, width = staged_ref.shape
    half, step = width // PAIR, length // BLOCKS
    place = place_here()
    for b in range(BLOCKS):
        if copies:
            copies[b].wait()
        rows = pl.ds(b * step, step)
        given_ref[rows] = columns_of(1 - place, staged_ref.at[rows], half)[...]
        own_ref[rows] = columns_of(place, staged_ref.at[rows], half)[...]


def column_of(row):
    shape = (row.shape[1], row.shape[1])
    diagonal = lax.broadcasted_iota(jnp.int32, shape, 0) == lax.broadcasted_iota(jnp.int32, shape, 1)
    return jnp.sum(jnp.where(diagonal, row, 0.0), axis=1, keepdims=True)


def load_keys_kernel(
    act_frames_in, fresh_frames_in, key_frames_in, batch_in, fresh_in, gain_in, keys_in,
    own_ref, given_ref, batch_ref, gain_ref, share_ref, fresh_ref, fresh_gain_ref, frames_ref,
    act_frames_ref, fresh_frames_ref, key_frames_ref, staged_ref, sems, small_sems,
):
    place, length, width = place_here(), staged_ref.shape[0], own_ref.shape[1]
    share = fresh_ref.shape[1]
    outers = gain_ref.shape[1] // PAIR // share
    own, other = (at * outers + outer_here() for at in (place, 1 - place))
    small = [
        (act_frames_in, act_frames_ref),
        (fresh_frames_in, fresh_frames_ref),
        (key_frames_in, key_frames_ref),
        (batch_in, batch_ref),
        (gain_in, gain_ref),
        (columns_of(other, batch_in, share), share_ref),
        (columns_of(own, fresh_in, share), fresh_ref),
        (columns_of(own, gain_in, share), fresh_gain_ref),
    ]
    small = [pltpu.make_async_copy(a, b, small_sems.at[n]) for n, (a, b) in enumerate(small)]
    copies, step = [], length // BLOCKS
    for b in range(BLOCKS):
        rows = pl.ds(b * step, step)
        copies.append(pltpu.make_async_copy(keys_in.at[rows], staged_ref.at[rows], sems.at[b]))
    for copy in small[:3] + copies + small[3:]:
        copy.start()
    for copy in small[:3]:
        copy.wait()

    tokens = frames_ref.shape[1]
    section = lax.axis_index("section")
    own_row = act_frames_ref[pl.ds(section, 1), :].astype(jnp.float32)
    prior_row = act_frames_ref[pl.ds(jnp.maximum(section - 1, 0), 1), :].astype(jnp.float32)
    fresh_row = fresh_frames_ref[...].astype(jnp.float32)
    next_row = jnp.where(in_first_section(), fresh_row, prior_row)
    for tick, row in enumerate((own_row, next_row)):
        frames_ref[tick] = jnp.broadcast_to(column_of(row), (tokens, HD))

    row = row_of(key_frames_ref).astype(jnp.float32)
    lines = -(-length // width)
    row = jnp.concatenate([row, jnp.zeros((1, lines * width - length), jnp.float32)], axis=1)
    line = lax.broadcasted_iota(jnp.int32, (STAT_ROWS, width), 0)
    tail = jnp.zeros((STAT_ROWS, width), jnp.float32)
    for n in range(lines):
        tail = jnp.where(line == n, row[:, n * width : (n + 1) * width], tail)
    for ref in (own_ref, given_ref):
        ref[length:] = tail.astype(jnp.bfloat16)
    halve(staged_ref, copies, own_ref, given_ref)
    for copy in small[3:]:
        copy.wait()


def load_keys(act_frames, fresh_frames, key_frames, batch, fresh, gain, keys):
    length, width = keys.shape
    tokens, model = batch.shape
    share = model * INNER // lax.axis_size("ctx")
    shape = (length + STAT_ROWS, width // PAIR)
    frames = (act_frames, fresh_frames, key_frames)
    return pl.pallas_call(
        load_keys_kernel,
        in_specs=[IN_HBM] * 7,
        out_specs=[WHOLE] * 8,
        out_shape=[
            pltpu.VMEM(shape, keys.dtype),
            pltpu.VMEM(shape, keys.dtype),
            pltpu.VMEM(batch.shape, batch.dtype),
            pltpu.VMEM(gain.shape, gain.dtype),
            pltpu.VMEM((tokens, share), batch.dtype),
            pltpu.VMEM((tokens, share), fresh.dtype),
            pltpu.VMEM((1, share), gain.dtype),
            pltpu.VMEM((2, tokens, HD), jnp.float32),
        ],
        scratch_shapes=[
            *(pltpu.VMEM(a.shape, a.dtype) for a in frames),
            pltpu.VMEM((length, width), keys.dtype),
            pltpu.SemaphoreType.DMA((BLOCKS,)),
            pltpu.SemaphoreType.DMA((8,)),
        ],
        cost_estimate=pl.CostEstimate(
            flops=0, bytes_accessed=2 * length * width, transcendentals=0
        ),
        compiler_params=pltpu.CompilerParams(vmem_limit_bytes=16 * MIB),
        name="load_keys",
    )(*in_hbm(*frames, batch, fresh, gain, keys))


def halve_values_kernel(values_ref, own_ref, given_ref):
    halve(values_ref, [], own_ref, given_ref)


def halve_values(values):
    length, width = values.shape
    half = pltpu.VMEM((length, width // PAIR), values.dtype)
    return pl.pallas_call(
        halve_values_kernel,
        in_specs=[WHOLE],
        out_specs=[WHOLE] * 2,
        out_shape=[half, half],
        cost_estimate=pl.CostEstimate(
            flops=0, bytes_accessed=2 * length * width, transcendentals=0
        ),
        compiler_params=pltpu.CompilerParams(vmem_limit_bytes=16 * MIB),
        name="halve_values",
    )(*in_vmem(values))


def first_kernel(other, gain_ref, frames_ref, batch_ref, keys_ref, values_ref, out_ref):
    length, kv_here = values_ref.shape[0], out_ref.shape[0]
    width = gain_ref.shape[1] // (PAIR * kv_here)
    place = (place_here() + other) % PAIR
    bias = bias_of(keys_ref, frames_ref[0, :, :1])
    for g in range(kv_here):
        index, block = place * kv_here + g, slice(g * HD, (g + 1) * HD)
        x, gain = columns_of(index, batch_ref, width)[...], columns_of(index, gain_ref, width)[...]
        raw = scores(queries_of(x, gain), keys_ref[:length, block], bias)
        top = top_of(raw)
        both = weigh(raw, top, values_ref[:, block])
        write_sums(out_ref.at[g], both[:, :HD], top, both[:, HD:])


def first(other, gain, frames, batch, keys, values):
    length, width = values.shape
    tokens = batch.shape[0]
    kv_here = width // HD
    queries = HEADS // PAIR * tokens
    return pl.pallas_call(
        functools.partial(first_kernel, other),
        in_specs=[WHOLE] * 5,
        out_specs=WHOLE,
        out_shape=jax.ShapeDtypeStruct((kv_here, queries // kv_here + STAT_ROWS, HD), jnp.bfloat16),
        cost_estimate=pl.CostEstimate(
            flops=2 * queries * length * 3 * HD,
            bytes_accessed=4 * length * width,
            transcendentals=queries * length,
        ),
        compiler_params=pltpu.CompilerParams(vmem_limit_bytes=16 * MIB),
        name="first",
    )(*in_vmem(gain, frames, batch, keys, values))


def finish_kernel(steps, mine_ref, got_ref, *out_refs):
    for d, out_ref in zip(steps, out_refs):
        g = outer_here() ^ d
        write_chunk(out_ref, *joined([mine_ref.at[g], got_ref.at[g]], False))


def finish(steps, mine, got):
    chunk = jax.ShapeDtypeStruct(mine.shape[1:], mine.dtype)
    return pl.pallas_call(
        functools.partial(finish_kernel, steps),
        in_specs=[WHOLE] * 2,
        out_specs=[WHOLE] * len(steps),
        out_shape=[chunk] * len(steps),
        compiler_params=pltpu.CompilerParams(vmem_limit_bytes=8 * MIB),
        name="finish",
    )(*in_vmem(mine, got))


def in_calls(call, outers, together):
    chunks, far = {}, outers - together
    for steps in [tuple(range(far, outers))[::-1]] + [(d,) for d in reversed(range(far))]:
        chunks.update(zip(steps, call(steps)))
    return [chunks[d] for d in range(outers)]


def chunk_call(kernel, name, steps, kv_here, count, length, operands):
    chunk = jax.ShapeDtypeStruct((count + STAT_ROWS, HD), jnp.bfloat16)
    return pl.pallas_call(
        functools.partial(kernel, steps, kv_here),
        in_specs=[WHOLE] * len(operands),
        out_specs=[WHOLE] * len(steps),
        out_shape=[chunk] * len(steps),
        cost_estimate=pl.CostEstimate(
            flops=2 * len(steps) * count * length * 3 * HD,
            bytes_accessed=4 * len(steps) * length * HD,
            transcendentals=len(steps) * count * length,
        ),
        compiler_params=pltpu.CompilerParams(vmem_limit_bytes=16 * MIB),
        name=name,
    )(*in_vmem(*operands))


def partials_kernel(steps, kv_here, frames_ref, *refs):
    kv_refs, refs = (refs[0:2], refs[2:4]), refs[4:]
    length = kv_refs[0][1].shape[0]
    biases = [bias_of(keys_ref, frames_ref[1, :, :1]) for keys_ref, _ in kv_refs]
    for d, queries_ref, out_ref in zip(steps, refs, refs[len(steps) :]):
        g = outer_here() ^ d
        raws = [
            scores(queries_ref[...], columns_of(g, keys_ref.at[:length], HD)[...], bias)
            for (keys_ref, _), bias in zip(kv_refs, biases)
        ]
        top = functools.reduce(jnp.maximum, [top_of(raw) for raw in raws])
        both = sum(
            weigh(raw, top, columns_of(g, values_ref, HD)[...])
            for raw, (_, values_ref) in zip(raws, kv_refs)
        )
        write_sums(out_ref, both[:, :HD], top, both[:, HD:])


def partials(steps, frames, own, got, queries):
    length, width = own[1].shape
    count = queries[0].shape[0]
    operands = (frames, *own, *got, *(queries[d] for d in steps))
    return chunk_call(
        partials_kernel, "partials", steps, width // HD, count, PAIR * length, operands
    )


def merge_kernel(*refs):
    *parts, out_ref = refs
    write_chunk(out_ref, *joined(parts, False))


def merge_first_kernel(*refs):
    *parts, share_ref, out_ref = refs
    x = head_rows(share_ref[...].astype(jnp.float32)).astype(jnp.bfloat16)
    write_chunk(out_ref, *joined(parts, False, x))


def merge(kernel, *parts):
    return pl.pallas_call(
        kernel,
        in_specs=[WHOLE] * len(parts),
        out_specs=WHOLE,
        out_shape=jax.ShapeDtypeStruct(parts[0].shape, parts[0].dtype),
        compiler_params=pltpu.CompilerParams(vmem_limit_bytes=8 * MIB),
        name="merge",
    )(*in_vmem(*parts))


def attended(one_ref, two_ref):
    one, two = one_ref[...].astype(jnp.float32), two_ref[...].astype(jnp.float32)
    here = inner_here() == 0
    parts = [jnp.where(here, one, two), jnp.where(here, two, one)]
    value, _, _ = joined([part.astype(jnp.bfloat16) for part in parts], True)
    return value


def columns_from(rows, tokens):
    pieces = [rows[at : at + tokens] for at in range(0, rows.shape[0], tokens)]
    return jnp.concatenate(pieces, axis=1)


def combine_kernel(gain_ref, fresh_ref, one_ref, two_ref, share_ref, queries_ref):
    tokens = fresh_ref.shape[0]
    handed = columns_from(attended(one_ref, two_ref), tokens).astype(jnp.bfloat16)
    fresh = fresh_ref[...].astype(jnp.float32)
    share = jnp.where(in_first_section(), fresh, handed.astype(jnp.float32))
    share = share.astype(jnp.bfloat16)
    share_ref[...] = share
    queries_ref[...] = queries_of(share, gain_ref[...])


def combine(gain, fresh, one, two):
    count = one.shape[0] - STAT_ROWS
    return pl.pallas_call(
        combine_kernel,
        in_specs=[WHOLE] * 4,
        out_specs=[WHOLE] * 2,
        out_shape=[
            jax.ShapeDtypeStruct(fresh.shape, fresh.dtype),
            jax.ShapeDtypeStruct((count, HD), jnp.bfloat16),
        ],
        compiler_params=pltpu.CompilerParams(vmem_limit_bytes=8 * MIB),
        name="combine",
    )(*in_vmem(gain, fresh, one, two))


def combine_last_kernel(share_ref, one_ref, two_ref, out_ref):
    tokens = out_ref.shape[0]
    total = head_rows(share_ref[...].astype(jnp.float32)) + attended(one_ref, two_ref)
    out_ref[...] = columns_from(total, tokens).astype(jnp.bfloat16)


def combine_last(share, one, two):
    return pl.pallas_call(
        combine_last_kernel,
        in_specs=[WHOLE] * 3,
        out_specs=WHOLE,
        out_shape=jax.ShapeDtypeStruct(share.shape, share.dtype),
        compiler_params=pltpu.CompilerParams(vmem_limit_bytes=8 * MIB),
        name="combine_last",
    )(*in_vmem(share, one, two))


def assemble_kernel(*refs):
    *pieces, out_ref = refs
    outers, width = len(pieces) // PAIR, pieces[0].shape[1]
    for n, refs in enumerate((pieces[:outers], pieces[outers:])):
        place = (place_here() + n) % PAIR
        for d, ref in enumerate(refs):
            columns_of(place * outers + (outer_here() ^ d), out_ref, width)[...] = ref[...]


def assemble(mine, others):
    tokens, width = mine[0].shape
    pieces = [*mine, *others]
    return pl.pallas_call(
        assemble_kernel,
        in_specs=[WHOLE] * len(pieces),
        out_specs=WHOLE,
        out_shape=jax.ShapeDtypeStruct((tokens, len(pieces) * width), jnp.bfloat16),
        compiler_params=pltpu.CompilerParams(vmem_limit_bytes=8 * MIB),
        name="assemble",
    )(*in_vmem(*pieces))


def body(
    activations,
    act_frames,
    fresh_batch,
    fresh_frames,
    norm_gain,
    cached_keys,
    cached_values,
    key_frames,
):
    own_keys, given_keys, batch, gain, share, fresh, fresh_gain, frames = load_keys(
        act_frames, fresh_frames[None], key_frames.reshape(-1, HD), activations[0], fresh_batch,
        norm_gain, cached_keys[0],
    )
    own_values, given_values = halve_values(cached_values[0])

    outers = lax.axis_size("ctx") // (INNER * PAIR)
    theirs = swapped(first(1, gain, frames, batch, given_keys, given_values))
    mine = first(0, gain, frames, batch, own_keys, own_values)
    chunk, *others = in_calls(lambda steps: finish(steps, mine, theirs), outers, 2)
    chunk = merge(merge_first_kernel, *from_outer(others)[::-1], swapped(chunk), share)
    one, two = [from_section_before(chunk, step) for step in range(INNER)]
    share, queries = combine(fresh_gain, fresh, one, two)
    queries = [swapped(queries), *from_outer([queries] * len(others))]

    own, got = (given_keys, given_values), (swapped(own_keys), swapped(own_values))
    chunk, *others = in_calls(lambda steps: partials(steps, frames, own, got, queries), outers, 1)
    chunk = merge(merge_kernel, *from_outer(others)[::-1], swapped(chunk))
    one, two = swapped(chunk), from_inner(chunk)
    share = combine_last(swapped(share), one, two)
    mine = [swapped(share), *from_outer([share] * len(others))]
    return assemble(mine, [share, *(swapped(piece) for piece in mine[1:])])[None]


def solution(mesh):
    placed = (
        P("section", None, None),
        P(),
        P(),
        P(),
        P("section", None),
        P("section", "ctx", None),
        P("section", "ctx", None),
        P("ctx"),
    )
    return jax.shard_map(
        body, mesh=mesh, in_specs=placed, out_specs=P("section", None, None), check_vma=False
    )
```

```python
import functools
import math

import jax
import jax.numpy as jnp
from jax import lax
from jax.experimental import pallas as pl
from jax.experimental.pallas import tpu as pltpu
from jax.sharding import PartitionSpec as P

HEADS = 64
HD = 128
PAIR = 2
INNER = 2
BLOCKS = 4
STAT_ROWS = 16
HIDDEN = -(2.0**100)
SCALE = HD**-0.5 * math.log2(math.e)
MIB = 1 << 20

epsilon = 1e-05

WHOLE = pl.BlockSpec(memory_space=pltpu.VMEM)
IN_HBM = pl.BlockSpec(memory_space=pltpu.HBM)


def in_hbm(*arrays):
    return [pltpu.with_memory_space_constraint(a, pltpu.HBM) for a in arrays]


def in_vmem(*arrays):
    return [pltpu.with_memory_space_constraint(a, pltpu.VMEM) for a in arrays]


def place_here():
    return lax.axis_index("ctx") % PAIR


def inner_here():
    return lax.axis_index("ctx") // PAIR % INNER


def outer_here():
    return lax.axis_index("ctx") // (PAIR * INNER)


def in_first_section():
    return lax.axis_index("section") == 0


def swapped(block):
    return lax.ppermute(block, "ctx", [(i, i ^ 1) for i in range(lax.axis_size("ctx"))])


def from_inner(block):
    size = lax.axis_size("ctx")
    return lax.ppermute(block, "ctx", [(i, i ^ PAIR ^ 1) for i in range(size)])


def from_outer(blocks, other_place=1):
    size = lax.axis_size("ctx")
    got = [
        lax.ppermute(
            block, "ctx", [(i, i ^ (INNER * PAIR * d) ^ other_place) for i in range(size)]
        )
        for d, block in reversed(list(enumerate(blocks, 1)))
    ]
    return got[::-1]


def from_section_before(block, step):
    sections, size = lax.axis_size("section"), lax.axis_size("ctx")
    route = [
        (s * size + i, (s + 1) % sections * size + (i ^ (PAIR * step) ^ 1))
        for s in range(sections)
        for i in range(size)
    ]
    return lax.ppermute(block, ("section", "ctx"), route)


def head_rows(block):
    return jnp.concatenate(
        [block[:, at : at + HD] for at in range(0, block.shape[1], HD)], axis=0
    )


def row_of(ref):
    return jnp.concatenate([ref[i : i + 1] for i in range(ref.shape[0])], axis=1)


def columns_of(index, ref, width):
    return ref.at[:, pl.ds(pl.multiple_of(index * width, HD), width)]


def on_diagonal(rows):
    shape = (rows, HD)
    return lax.broadcasted_iota(jnp.int32, shape, 0) == lax.broadcasted_iota(jnp.int32, shape, 1)


def queries_of(x, gain):
    rows = head_rows(x.astype(jnp.float32))
    gain = head_rows(jnp.broadcast_to(gain, x.shape))
    norm = lax.rsqrt(jnp.mean(rows * rows, axis=-1, keepdims=True) + epsilon)
    return (rows * norm * gain).astype(jnp.bfloat16)


def bias_of(keys_ref, frames):
    length = keys_ref.shape[0] - STAT_ROWS
    width = keys_ref.shape[1]
    rows = -(-length // width)
    tail = keys_ref[length:].astype(jnp.float32)
    key_frames = jnp.concatenate([tail[i : i + 1] for i in range(rows)], axis=1)[:, :length]
    return jnp.where(key_frames <= frames, 0.0, HIDDEN)[None]


def scores(queries, key_block, bias):
    count, keys, tokens = queries.shape[0], key_block.shape[0], bias.shape[1]
    raw = lax.dot_general(
        queries, key_block, (((1,), (1,)), ((), ())), preferred_element_type=jnp.float32
    )
    raw = raw.reshape(count // tokens, tokens, keys) * SCALE + bias
    return raw.reshape(count, keys)


def top_of(raw):
    top = jnp.max(raw, axis=-1, keepdims=True)
    return top.astype(jnp.bfloat16).astype(jnp.float32)


def weigh(raw, top, value_block):
    probs = jnp.exp2(raw - top).astype(jnp.bfloat16)
    ones = jnp.ones((value_block.shape[0], HD), jnp.bfloat16)
    return jnp.dot(
        probs, jnp.concatenate([value_block, ones], axis=1), preferred_element_type=jnp.float32
    )


def groups_of(count):
    groups = -(-count // HD)
    held = count // groups
    return [slice(c * held, (c + 1) * held) for c in range(groups)]


def write_chunk(out_ref, weighted, tops, totals):
    count = weighted.shape[0]
    line = lax.broadcasted_iota(jnp.int32, (STAT_ROWS, HD), 0)
    stats = jnp.zeros((STAT_ROWS, HD), jnp.float32)
    for c, (top, total) in enumerate(zip(tops, totals)):
        high = total.astype(jnp.bfloat16).astype(jnp.float32)
        for n, row in enumerate((top, high, total - high)):
            stats = jnp.where(line == 3 * c + n, row, stats)
    out_ref[:count] = weighted.astype(jnp.bfloat16)
    out_ref[count:] = stats.astype(jnp.bfloat16)


def write_sums(out_ref, weighted, top, total):
    groups = groups_of(weighted.shape[0])
    diagonal = on_diagonal(groups[0].stop)

    def rows(column):
        column = jnp.broadcast_to(column, weighted.shape)
        return [
            jnp.sum(jnp.where(diagonal, column[group], 0.0), axis=0, keepdims=True)
            for group in groups
        ]

    write_chunk(out_ref, weighted, rows(top), rows(total))


def joined(parts, normed, x=None):
    count = parts[0].shape[0] - STAT_ROWS
    groups = groups_of(count)
    diagonal = on_diagonal(groups[0].stop)
    stats = [part[count:].astype(jnp.float32) for part in parts]
    values, tops, totals = [], [], []
    for c, group in enumerate(groups):
        points = [s[3 * c : 3 * c + 1] for s in stats]
        top = functools.reduce(jnp.maximum, points)
        factors = [jnp.exp2(point - top) for point in points]
        total = sum(
            f * (s[3 * c + 1 : 3 * c + 2] + s[3 * c + 2 : 3 * c + 3])
            for f, s in zip(factors, stats)
        )
        if normed:
            inverse = 1.0 / total
            factors = [f * inverse for f in factors]
        terms = list(zip(factors, parts)) + ([] if x is None else [(total, x)])
        value = 0.0
        for factor, part in terms:
            weight = jnp.where(diagonal, factor, 0.0)[:, : group.stop - group.start]
            high = weight.astype(jnp.bfloat16)
            low = (weight - high.astype(jnp.float32)).astype(jnp.bfloat16)
            for term in (high, low):
                value = value + jnp.dot(term, part[group], preferred_element_type=jnp.float32)
        values.append(value)
        tops.append(top)
        totals.append(total)
    return jnp.concatenate(values, axis=0), tops, totals


def halve(staged_ref, copies, own_ref, given_ref):
    length, width = staged_ref.shape
    half, step = width // PAIR, length // BLOCKS
    place = place_here()
    for b in range(BLOCKS):
        if copies:
            copies[b].wait()
        rows = pl.ds(b * step, step)
        given_ref[rows] = columns_of(1 - place, staged_ref.at[rows], half)[...]
        own_ref[rows] = columns_of(place, staged_ref.at[rows], half)[...]


def column_of(row):
    shape = (row.shape[1], row.shape[1])
    diagonal = lax.broadcasted_iota(jnp.int32, shape, 0) == lax.broadcasted_iota(jnp.int32, shape, 1)
    return jnp.sum(jnp.where(diagonal, row, 0.0), axis=1, keepdims=True)


def load_keys_kernel(
    act_frames_in, fresh_frames_in, key_frames_in, batch_in, fresh_in, gain_in, keys_in,
    own_ref, given_ref, batch_ref, gain_ref, share_ref, fresh_ref, fresh_gain_ref, frames_ref,
    act_frames_ref, fresh_frames_ref, key_frames_ref, staged_ref, sems, small_sems,
):
    place, length, width = place_here(), staged_ref.shape[0], own_ref.shape[1]
    share = fresh_ref.shape[1]
    outers = gain_ref.shape[1] // PAIR // share
    own_share = place * outers + outer_here()
    index = (1 - place) * outers + outer_here()
    small = [
        (act_frames_in, act_frames_ref),
        (fresh_frames_in, fresh_frames_ref),
        (key_frames_in, key_frames_ref),
        (batch_in, batch_ref),
        (gain_in, gain_ref),
        (columns_of(own_share, batch_in, share), share_ref),
        (columns_of(index, fresh_in, share), fresh_ref),
        (columns_of(index, gain_in, share), fresh_gain_ref),
    ]
    small = [pltpu.make_async_copy(a, b, small_sems.at[n]) for n, (a, b) in enumerate(small)]
    copies, step = [], length // BLOCKS
    for b in range(BLOCKS):
        rows = pl.ds(b * step, step)
        copies.append(pltpu.make_async_copy(keys_in.at[rows], staged_ref.at[rows], sems.at[b]))
    for copy in small[:3] + copies + small[3:]:
        copy.start()
    for copy in small[:3]:
        copy.wait()

    tokens = frames_ref.shape[1]
    section = lax.axis_index("section")
    own_row = act_frames_ref[pl.ds(section, 1), :].astype(jnp.float32)
    prior_row = act_frames_ref[pl.ds(jnp.maximum(section - 1, 0), 1), :].astype(jnp.float32)
    fresh_row = fresh_frames_ref[...].astype(jnp.float32)
    next_row = jnp.where(in_first_section(), fresh_row, prior_row)
    for tick, row in enumerate((own_row, next_row)):
        frames_ref[tick] = jnp.broadcast_to(column_of(row), (tokens, HD))

    row = row_of(key_frames_ref).astype(jnp.float32)
    lines = -(-length // width)
    row = jnp.concatenate([row, jnp.zeros((1, lines * width - length), jnp.float32)], axis=1)
    line = lax.broadcasted_iota(jnp.int32, (STAT_ROWS, width), 0)
    tail = jnp.zeros((STAT_ROWS, width), jnp.float32)
    for n in range(lines):
        tail = jnp.where(line == n, row[:, n * width : (n + 1) * width], tail)
    for ref in (own_ref, given_ref):
        ref[length:] = tail.astype(jnp.bfloat16)
    halve(staged_ref, copies, own_ref, given_ref)
    for copy in small[3:]:
        copy.wait()


def load_keys(act_frames, fresh_frames, key_frames, batch, fresh, gain, keys):
    length, width = keys.shape
    tokens, model = batch.shape
    share = model * INNER // lax.axis_size("ctx")
    shape = (length + STAT_ROWS, width // PAIR)
    frames = (act_frames, fresh_frames, key_frames)
    return pl.pallas_call(
        load_keys_kernel,
        in_specs=[IN_HBM] * 7,
        out_specs=[WHOLE] * 8,
        out_shape=[
            pltpu.VMEM(shape, keys.dtype),
            pltpu.VMEM(shape, keys.dtype),
            pltpu.VMEM(batch.shape, batch.dtype),
            pltpu.VMEM(gain.shape, gain.dtype),
            pltpu.VMEM((tokens, share), batch.dtype),
            pltpu.VMEM((tokens, share), fresh.dtype),
            pltpu.VMEM((1, share), gain.dtype),
            pltpu.VMEM((2, tokens, HD), jnp.float32),
        ],
        scratch_shapes=[
            *(pltpu.VMEM(a.shape, a.dtype) for a in frames),
            pltpu.VMEM((length, width), keys.dtype),
            pltpu.SemaphoreType.DMA((BLOCKS,)),
            pltpu.SemaphoreType.DMA((8,)),
        ],
        cost_estimate=pl.CostEstimate(
            flops=0, bytes_accessed=2 * length * width, transcendentals=0
        ),
        compiler_params=pltpu.CompilerParams(vmem_limit_bytes=16 * MIB),
        name="load_keys",
    )(*in_hbm(*frames, batch, fresh, gain, keys))


def halve_values_kernel(values_ref, own_ref, given_ref):
    halve(values_ref, [], own_ref, given_ref)


def halve_values(values):
    length, width = values.shape
    half = pltpu.VMEM((length, width // PAIR), values.dtype)
    return pl.pallas_call(
        halve_values_kernel,
        in_specs=[WHOLE],
        out_specs=[WHOLE] * 2,
        out_shape=[half, half],
        cost_estimate=pl.CostEstimate(
            flops=0, bytes_accessed=2 * length * width, transcendentals=0
        ),
        compiler_params=pltpu.CompilerParams(vmem_limit_bytes=16 * MIB),
        name="halve_values",
    )(*in_vmem(values))


def first_kernel(other, gain_ref, frames_ref, batch_ref, keys_ref, values_ref, out_ref):
    length, kv_here = values_ref.shape[0], out_ref.shape[0]
    width = gain_ref.shape[1] // (PAIR * kv_here)
    place = (place_here() + other) % PAIR
    bias = bias_of(keys_ref, frames_ref[0, :, :1])
    for g in range(kv_here):
        index, block = place * kv_here + g, slice(g * HD, (g + 1) * HD)
        x, gain = columns_of(index, batch_ref, width)[...], columns_of(index, gain_ref, width)[...]
        raw = scores(queries_of(x, gain), keys_ref[:length, block], bias)
        top = top_of(raw)
        both = weigh(raw, top, values_ref[:, block])
        write_sums(out_ref.at[g], both[:, :HD], top, both[:, HD:])


def first(other, gain, frames, batch, keys, values):
    length, width = values.shape
    tokens = batch.shape[0]
    kv_here = width // HD
    queries = HEADS // PAIR * tokens
    return pl.pallas_call(
        functools.partial(first_kernel, other),
        in_specs=[WHOLE] * 5,
        out_specs=WHOLE,
        out_shape=jax.ShapeDtypeStruct((kv_here, queries // kv_here + STAT_ROWS, HD), jnp.bfloat16),
        cost_estimate=pl.CostEstimate(
            flops=2 * queries * length * 3 * HD,
            bytes_accessed=4 * length * width,
            transcendentals=queries * length,
        ),
        compiler_params=pltpu.CompilerParams(vmem_limit_bytes=16 * MIB),
        name="first",
    )(*in_vmem(gain, frames, batch, keys, values))


def finish_kernel(steps, mine_ref, got_ref, *out_refs):
    for d, out_ref in zip(steps, out_refs):
        g = outer_here() ^ d
        write_chunk(out_ref, *joined([mine_ref.at[g], got_ref.at[g]], False))


def finish(steps, mine, got):
    chunk = jax.ShapeDtypeStruct(mine.shape[1:], mine.dtype)
    return pl.pallas_call(
        functools.partial(finish_kernel, steps),
        in_specs=[WHOLE] * 2,
        out_specs=[WHOLE] * len(steps),
        out_shape=[chunk] * len(steps),
        compiler_params=pltpu.CompilerParams(vmem_limit_bytes=8 * MIB),
        name="finish",
    )(*in_vmem(mine, got))


def in_calls(call, outers, together):
    chunks, far = {}, outers - together
    for steps in [tuple(range(far, outers))[::-1]] + [(d,) for d in reversed(range(far))]:
        chunks.update(zip(steps, call(steps)))
    return [chunks[d] for d in range(outers)]


def chunk_call(kernel, name, steps, kv_here, count, length, operands):
    chunk = jax.ShapeDtypeStruct((count + STAT_ROWS, HD), jnp.bfloat16)
    return pl.pallas_call(
        functools.partial(kernel, steps, kv_here),
        in_specs=[WHOLE] * len(operands),
        out_specs=[WHOLE] * len(steps),
        out_shape=[chunk] * len(steps),
        cost_estimate=pl.CostEstimate(
            flops=2 * len(steps) * count * length * 3 * HD,
            bytes_accessed=4 * len(steps) * length * HD,
            transcendentals=len(steps) * count * length,
        ),
        compiler_params=pltpu.CompilerParams(vmem_limit_bytes=16 * MIB),
        name=name,
    )(*in_vmem(*operands))


def partials_kernel(steps, kv_here, frames_ref, *refs):
    kv_refs, refs = (refs[0:2], refs[2:4]), refs[4:]
    length = kv_refs[0][1].shape[0]
    biases = [bias_of(keys_ref, frames_ref[1, :, :1]) for keys_ref, _ in kv_refs]
    for d, queries_ref, out_ref in zip(steps, refs, refs[len(steps) :]):
        g = outer_here() ^ d
        raws = [
            scores(queries_ref[...], columns_of(g, keys_ref.at[:length], HD)[...], bias)
            for (keys_ref, _), bias in zip(kv_refs, biases)
        ]
        top = functools.reduce(jnp.maximum, [top_of(raw) for raw in raws])
        both = sum(
            weigh(raw, top, columns_of(g, values_ref, HD)[...])
            for raw, (_, values_ref) in zip(raws, kv_refs)
        )
        write_sums(out_ref, both[:, :HD], top, both[:, HD:])


def partials(steps, frames, own, got, queries):
    length, width = own[1].shape
    count = queries[0].shape[0]
    operands = (frames, *own, *got, *(queries[d] for d in steps))
    return chunk_call(
        partials_kernel, "partials", steps, width // HD, count, PAIR * length, operands
    )


def merge_kernel(*refs):
    *parts, out_ref = refs
    write_chunk(out_ref, *joined(parts, False))


def merge_first_kernel(*refs):
    *parts, share_ref, out_ref = refs
    x = head_rows(share_ref[...].astype(jnp.float32)).astype(jnp.bfloat16)
    write_chunk(out_ref, *joined(parts, False, x))


def merge(kernel, *parts):
    return pl.pallas_call(
        kernel,
        in_specs=[WHOLE] * len(parts),
        out_specs=WHOLE,
        out_shape=jax.ShapeDtypeStruct(parts[0].shape, parts[0].dtype),
        compiler_params=pltpu.CompilerParams(vmem_limit_bytes=8 * MIB),
        name="merge",
    )(*in_vmem(*parts))


def attended(one_ref, two_ref):
    one, two = one_ref[...].astype(jnp.float32), two_ref[...].astype(jnp.float32)
    here = inner_here() == 0
    parts = [jnp.where(here, one, two), jnp.where(here, two, one)]
    value, _, _ = joined([part.astype(jnp.bfloat16) for part in parts], True)
    return value


def columns_from(rows, tokens):
    pieces = [rows[at : at + tokens] for at in range(0, rows.shape[0], tokens)]
    return jnp.concatenate(pieces, axis=1)


def combine_kernel(gain_ref, fresh_ref, one_ref, two_ref, share_ref, queries_ref):
    tokens = fresh_ref.shape[0]
    handed = columns_from(attended(one_ref, two_ref), tokens).astype(jnp.bfloat16)
    fresh = fresh_ref[...].astype(jnp.float32)
    share = jnp.where(in_first_section(), fresh, handed.astype(jnp.float32))
    share = share.astype(jnp.bfloat16)
    share_ref[...] = share
    queries_ref[...] = queries_of(share, gain_ref[...])


def combine(gain, fresh, one, two):
    count = one.shape[0] - STAT_ROWS
    return pl.pallas_call(
        combine_kernel,
        in_specs=[WHOLE] * 4,
        out_specs=[WHOLE] * 2,
        out_shape=[
            jax.ShapeDtypeStruct(fresh.shape, fresh.dtype),
            jax.ShapeDtypeStruct((count, HD), jnp.bfloat16),
        ],
        compiler_params=pltpu.CompilerParams(vmem_limit_bytes=8 * MIB),
        name="combine",
    )(*in_vmem(gain, fresh, one, two))


def combine_last_kernel(share_ref, one_ref, two_ref, out_ref):
    tokens = out_ref.shape[0]
    total = head_rows(share_ref[...].astype(jnp.float32)) + attended(one_ref, two_ref)
    out_ref[...] = columns_from(total, tokens).astype(jnp.bfloat16)


def combine_last(share, one, two):
    return pl.pallas_call(
        combine_last_kernel,
        in_specs=[WHOLE] * 3,
        out_specs=WHOLE,
        out_shape=jax.ShapeDtypeStruct(share.shape, share.dtype),
        compiler_params=pltpu.CompilerParams(vmem_limit_bytes=8 * MIB),
        name="combine_last",
    )(*in_vmem(share, one, two))


def assemble_kernel(*refs):
    *pieces, out_ref = refs
    outers, width = len(pieces) // PAIR, pieces[0].shape[1]
    for n, refs in enumerate((pieces[:outers], pieces[outers:])):
        place = (place_here() + n) % PAIR
        for d, ref in enumerate(refs):
            columns_of(place * outers + (outer_here() ^ d), out_ref, width)[...] = ref[...]


def assemble(mine, others):
    tokens, width = mine[0].shape
    pieces = [*mine, *others]
    return pl.pallas_call(
        assemble_kernel,
        in_specs=[WHOLE] * len(pieces),
        out_specs=WHOLE,
        out_shape=jax.ShapeDtypeStruct((tokens, len(pieces) * width), jnp.bfloat16),
        compiler_params=pltpu.CompilerParams(vmem_limit_bytes=8 * MIB),
        name="assemble",
    )(*in_vmem(*pieces))


def body(
    activations,
    act_frames,
    fresh_batch,
    fresh_frames,
    norm_gain,
    cached_keys,
    cached_values,
    key_frames,
):
    own_keys, given_keys, batch, gain, share, fresh, fresh_gain, frames = load_keys(
        act_frames, fresh_frames[None], key_frames.reshape(-1, HD), activations[0], fresh_batch,
        norm_gain, cached_keys[0],
    )
    own_values, given_values = halve_values(cached_values[0])

    outers = lax.axis_size("ctx") // (INNER * PAIR)
    theirs = swapped(first(1, gain, frames, batch, given_keys, given_values))
    mine = first(0, gain, frames, batch, own_keys, own_values)
    chunk, *others = in_calls(lambda steps: finish(steps, mine, theirs), outers, 2)
    own, got = (own_keys, own_values), (swapped(given_keys), swapped(given_values))
    chunk = merge(merge_first_kernel, *from_outer(others, 0)[::-1], chunk, share)
    one, two = [from_section_before(chunk, step) for step in range(INNER)]
    share, queries = combine(fresh_gain, fresh, one, two)
    queries = [swapped(queries), *from_outer([queries] * len(others))]

    chunk, *others = in_calls(lambda steps: partials(steps, frames, own, got, queries), outers, 1)
    chunk = merge(merge_kernel, *from_outer(others)[::-1], swapped(chunk))
    one, two = swapped(chunk), from_inner(chunk)
    share = combine_last(swapped(share), one, two)
    theirs = [swapped(share), *from_outer([share] * len(others))]
    return assemble([share, *(swapped(piece) for piece in theirs[1:])], theirs)[None]


def solution(mesh):
    placed = (
        P("section", None, None),
        P(),
        P(),
        P(),
        P("section", None),
        P("section", "ctx", None),
        P("section", "ctx", None),
        P("ctx"),
    )
    return jax.shard_map(
        body, mesh=mesh, in_specs=placed, out_specs=P("section", None, None), check_vma=False
    )
```

```python
import functools
import math

import jax
import jax.numpy as jnp
from jax import lax
from jax.experimental import pallas as pl
from jax.experimental.pallas import tpu as pltpu
from jax.sharding import PartitionSpec as P

HEADS = 64
HD = 128
PAIR = 2
INNER = 2
BLOCKS = 4
STAT_ROWS = 16
HIDDEN = -(2.0**100)
SCALE = HD**-0.5 * math.log2(math.e)
MIB = 1 << 20

epsilon = 1e-05

WHOLE = pl.BlockSpec(memory_space=pltpu.VMEM)
IN_HBM = pl.BlockSpec(memory_space=pltpu.HBM)


def in_hbm(*arrays):
    return [pltpu.with_memory_space_constraint(a, pltpu.HBM) for a in arrays]


def in_vmem(*arrays):
    return [pltpu.with_memory_space_constraint(a, pltpu.VMEM) for a in arrays]


def place_here():
    return lax.axis_index("ctx") % PAIR


def inner_here():
    return lax.axis_index("ctx") // PAIR % INNER


def outer_here():
    return lax.axis_index("ctx") // (PAIR * INNER)


def in_first_section():
    return lax.axis_index("section") == 0


def swapped(block):
    return lax.ppermute(block, "ctx", [(i, i ^ 1) for i in range(lax.axis_size("ctx"))])


def from_inner(block):
    size = lax.axis_size("ctx")
    return lax.ppermute(block, "ctx", [(i, i ^ PAIR ^ 1) for i in range(size)])


def from_outer(blocks, other_place=1):
    size = lax.axis_size("ctx")
    got = [
        lax.ppermute(
            block, "ctx", [(i, i ^ (INNER * PAIR * d) ^ other_place) for i in range(size)]
        )
        for d, block in reversed(list(enumerate(blocks, 1)))
    ]
    return got[::-1]


def from_section_before(block, outers):
    sections, size = lax.axis_size("section"), lax.axis_size("ctx")
    got = []
    for d in reversed(range(outers)):
        route = [
            (s * size + i, (s + 1) % sections * size + (i ^ (INNER * PAIR * d) ^ 1))
            for s in range(sections)
            for i in range(size)
        ]
        got.append(lax.ppermute(block, ("section", "ctx"), route))
    return got[::-1]


def head_rows(block):
    return jnp.concatenate(
        [block[:, at : at + HD] for at in range(0, block.shape[1], HD)], axis=0
    )


def row_of(ref):
    return jnp.concatenate([ref[i : i + 1] for i in range(ref.shape[0])], axis=1)


def columns_of(index, ref, width):
    return ref.at[:, pl.ds(pl.multiple_of(index * width, HD), width)]


def on_diagonal(rows):
    shape = (rows, HD)
    return lax.broadcasted_iota(jnp.int32, shape, 0) == lax.broadcasted_iota(jnp.int32, shape, 1)


def queries_of(x, gain):
    rows = head_rows(x.astype(jnp.float32))
    gain = head_rows(jnp.broadcast_to(gain, x.shape))
    norm = lax.rsqrt(jnp.mean(rows * rows, axis=-1, keepdims=True) + epsilon)
    return (rows * norm * gain).astype(jnp.bfloat16)


def bias_of(keys_ref, frames):
    length = keys_ref.shape[0] - STAT_ROWS
    width = keys_ref.shape[1]
    rows = -(-length // width)
    tail = keys_ref[length:].astype(jnp.float32)
    key_frames = jnp.concatenate([tail[i : i + 1] for i in range(rows)], axis=1)[:, :length]
    return jnp.where(key_frames <= frames, 0.0, HIDDEN)[None]


def scores(queries, key_block, bias):
    count, keys, tokens = queries.shape[0], key_block.shape[0], bias.shape[1]
    raw = lax.dot_general(
        queries, key_block, (((1,), (1,)), ((), ())), preferred_element_type=jnp.float32
    )
    raw = raw.reshape(count // tokens, tokens, keys) * SCALE + bias
    return raw.reshape(count, keys)


def top_of(raw):
    top = jnp.max(raw, axis=-1, keepdims=True)
    return top.astype(jnp.bfloat16).astype(jnp.float32)


def weigh(raw, top, value_block):
    probs = jnp.exp2(raw - top).astype(jnp.bfloat16)
    ones = jnp.ones((value_block.shape[0], HD), jnp.bfloat16)
    return jnp.dot(
        probs, jnp.concatenate([value_block, ones], axis=1), preferred_element_type=jnp.float32
    )


def groups_of(count):
    groups = -(-count // HD)
    held = count // groups
    return [slice(c * held, (c + 1) * held) for c in range(groups)]


def write_chunk(out_ref, weighted, tops, totals):
    count = weighted.shape[0]
    line = lax.broadcasted_iota(jnp.int32, (STAT_ROWS, HD), 0)
    stats = jnp.zeros((STAT_ROWS, HD), jnp.float32)
    for c, (top, total) in enumerate(zip(tops, totals)):
        high = total.astype(jnp.bfloat16).astype(jnp.float32)
        for n, row in enumerate((top, high, total - high)):
            stats = jnp.where(line == 3 * c + n, row, stats)
    out_ref[:count] = weighted.astype(jnp.bfloat16)
    out_ref[count:] = stats.astype(jnp.bfloat16)


def write_sums(out_ref, weighted, top, total):
    groups = groups_of(weighted.shape[0])
    diagonal = on_diagonal(groups[0].stop)

    def rows(column):
        column = jnp.broadcast_to(column, weighted.shape)
        return [
            jnp.sum(jnp.where(diagonal, column[group], 0.0), axis=0, keepdims=True)
            for group in groups
        ]

    write_chunk(out_ref, weighted, rows(top), rows(total))


def joined(parts, normed, x=None):
    count = parts[0].shape[0] - STAT_ROWS
    groups = groups_of(count)
    diagonal = on_diagonal(groups[0].stop)
    stats = [part[count:].astype(jnp.float32) for part in parts]
    values, tops, totals = [], [], []
    for c, group in enumerate(groups):
        points = [s[3 * c : 3 * c + 1] for s in stats]
        top = functools.reduce(jnp.maximum, points)
        factors = [jnp.exp2(point - top) for point in points]
        total = sum(
            f * (s[3 * c + 1 : 3 * c + 2] + s[3 * c + 2 : 3 * c + 3])
            for f, s in zip(factors, stats)
        )
        if normed:
            inverse = 1.0 / total
            factors = [f * inverse for f in factors]
        terms = list(zip(factors, parts)) + ([] if x is None else [(total, x)])
        value = 0.0
        for factor, part in terms:
            weight = jnp.where(diagonal, factor, 0.0)[:, : group.stop - group.start]
            high = weight.astype(jnp.bfloat16)
            low = (weight - high.astype(jnp.float32)).astype(jnp.bfloat16)
            for term in (high, low):
                value = value + jnp.dot(term, part[group], preferred_element_type=jnp.float32)
        values.append(value)
        tops.append(top)
        totals.append(total)
    return jnp.concatenate(values, axis=0), tops, totals


def halve(staged_ref, copies, own_ref, given_ref):
    length, width = staged_ref.shape
    half, step = width // PAIR, length // BLOCKS
    place = place_here()
    for b in range(BLOCKS):
        if copies:
            copies[b].wait()
        rows = pl.ds(b * step, step)
        given_ref[rows] = columns_of(1 - place, staged_ref.at[rows], half)[...]
        own_ref[rows] = columns_of(place, staged_ref.at[rows], half)[...]


def column_of(row):
    shape = (row.shape[1], row.shape[1])
    diagonal = lax.broadcasted_iota(jnp.int32, shape, 0) == lax.broadcasted_iota(jnp.int32, shape, 1)
    return jnp.sum(jnp.where(diagonal, row, 0.0), axis=1, keepdims=True)


def load_keys_kernel(
    act_frames_in, fresh_frames_in, key_frames_in, batch_in, fresh_in, gain_in, keys_in,
    own_ref, given_ref, batch_ref, gain_ref, share_ref, fresh_ref, frames_ref,
    act_frames_ref, fresh_frames_ref, key_frames_ref, staged_ref, sems, small_sems,
):
    place, length, width = place_here(), staged_ref.shape[0], own_ref.shape[1]
    half, share = fresh_ref.shape[1], share_ref.shape[1]
    own_share = place * (half // share) + outer_here()
    small = [
        (act_frames_in, act_frames_ref),
        (fresh_frames_in, fresh_frames_ref),
        (key_frames_in, key_frames_ref),
        (batch_in, batch_ref),
        (gain_in, gain_ref),
        (columns_of(own_share, batch_in, share), share_ref),
        (columns_of(place, fresh_in, half), fresh_ref),
    ]
    small = [pltpu.make_async_copy(a, b, small_sems.at[n]) for n, (a, b) in enumerate(small)]
    copies, step = [], length // BLOCKS
    for b in range(BLOCKS):
        rows = pl.ds(b * step, step)
        copies.append(pltpu.make_async_copy(keys_in.at[rows], staged_ref.at[rows], sems.at[b]))
    for copy in small[:3] + copies + small[3:]:
        copy.start()
    for copy in small[:3]:
        copy.wait()

    tokens = frames_ref.shape[1]
    section = lax.axis_index("section")
    own_row = act_frames_ref[pl.ds(section, 1), :].astype(jnp.float32)
    prior_row = act_frames_ref[pl.ds(jnp.maximum(section - 1, 0), 1), :].astype(jnp.float32)
    fresh_row = fresh_frames_ref[...].astype(jnp.float32)
    next_row = jnp.where(in_first_section(), fresh_row, prior_row)
    for tick, row in enumerate((own_row, next_row)):
        frames_ref[tick] = jnp.broadcast_to(column_of(row), (tokens, HD))

    row = row_of(key_frames_ref).astype(jnp.float32)
    lines = -(-length // width)
    row = jnp.concatenate([row, jnp.zeros((1, lines * width - length), jnp.float32)], axis=1)
    line = lax.broadcasted_iota(jnp.int32, (STAT_ROWS, width), 0)
    tail = jnp.zeros((STAT_ROWS, width), jnp.float32)
    for n in range(lines):
        tail = jnp.where(line == n, row[:, n * width : (n + 1) * width], tail)
    for ref in (own_ref, given_ref):
        ref[length:] = tail.astype(jnp.bfloat16)
    halve(staged_ref, copies, own_ref, given_ref)
    for copy in small[3:]:
        copy.wait()


def load_keys(act_frames, fresh_frames, key_frames, batch, fresh, gain, keys):
    length, width = keys.shape
    tokens, model = batch.shape
    share = model * INNER // lax.axis_size("ctx")
    shape = (length + STAT_ROWS, width // PAIR)
    frames = (act_frames, fresh_frames, key_frames)
    return pl.pallas_call(
        load_keys_kernel,
        in_specs=[IN_HBM] * 7,
        out_specs=[WHOLE] * 7,
        out_shape=[
            pltpu.VMEM(shape, keys.dtype),
            pltpu.VMEM(shape, keys.dtype),
            pltpu.VMEM(batch.shape, batch.dtype),
            pltpu.VMEM(gain.shape, gain.dtype),
            pltpu.VMEM((tokens, share), batch.dtype),
            pltpu.VMEM((tokens, model // PAIR), fresh.dtype),
            pltpu.VMEM((2, tokens, HD), jnp.float32),
        ],
        scratch_shapes=[
            *(pltpu.VMEM(a.shape, a.dtype) for a in frames),
            pltpu.VMEM((length, width), keys.dtype),
            pltpu.SemaphoreType.DMA((BLOCKS,)),
            pltpu.SemaphoreType.DMA((7,)),
        ],
        cost_estimate=pl.CostEstimate(
            flops=0, bytes_accessed=2 * length * width, transcendentals=0
        ),
        compiler_params=pltpu.CompilerParams(vmem_limit_bytes=16 * MIB),
        name="load_keys",
    )(*in_hbm(*frames, batch, fresh, gain, keys))


def halve_values_kernel(values_ref, own_ref, given_ref):
    halve(values_ref, [], own_ref, given_ref)


def halve_values(values):
    length, width = values.shape
    half = pltpu.VMEM((length, width // PAIR), values.dtype)
    return pl.pallas_call(
        halve_values_kernel,
        in_specs=[WHOLE],
        out_specs=[WHOLE] * 2,
        out_shape=[half, half],
        cost_estimate=pl.CostEstimate(
            flops=0, bytes_accessed=2 * length * width, transcendentals=0
        ),
        compiler_params=pltpu.CompilerParams(vmem_limit_bytes=16 * MIB),
        name="halve_values",
    )(*in_vmem(values))


def first_kernel(other, gain_ref, frames_ref, batch_ref, keys_ref, values_ref, out_ref):
    length, kv_here = values_ref.shape[0], out_ref.shape[0]
    width = gain_ref.shape[1] // (PAIR * kv_here)
    place = (place_here() + other) % PAIR
    bias = bias_of(keys_ref, frames_ref[0, :, :1])
    for g in range(kv_here):
        index, block = place * kv_here + g, slice(g * HD, (g + 1) * HD)
        x, gain = columns_of(index, batch_ref, width)[...], columns_of(index, gain_ref, width)[...]
        raw = scores(queries_of(x, gain), keys_ref[:length, block], bias)
        top = top_of(raw)
        both = weigh(raw, top, values_ref[:, block])
        write_sums(out_ref.at[g], both[:, :HD], top, both[:, HD:])


def first(other, gain, frames, batch, keys, values):
    length, width = values.shape
    tokens = batch.shape[0]
    kv_here = width // HD
    queries = HEADS // PAIR * tokens
    return pl.pallas_call(
        functools.partial(first_kernel, other),
        in_specs=[WHOLE] * 5,
        out_specs=WHOLE,
        out_shape=jax.ShapeDtypeStruct((kv_here, queries // kv_here + STAT_ROWS, HD), jnp.bfloat16),
        cost_estimate=pl.CostEstimate(
            flops=2 * queries * length * 3 * HD,
            bytes_accessed=4 * length * width,
            transcendentals=queries * length,
        ),
        compiler_params=pltpu.CompilerParams(vmem_limit_bytes=16 * MIB),
        name="first",
    )(*in_vmem(gain, frames, batch, keys, values))


def finish_kernel(steps, mine_ref, got_ref, *out_refs):
    for d, out_ref in zip(steps, out_refs):
        g = outer_here() ^ d
        write_chunk(out_ref, *joined([mine_ref.at[g], got_ref.at[g]], False))


def finish(steps, mine, got):
    chunk = jax.ShapeDtypeStruct(mine.shape[1:], mine.dtype)
    return pl.pallas_call(
        functools.partial(finish_kernel, steps),
        in_specs=[WHOLE] * 2,
        out_specs=[WHOLE] * len(steps),
        out_shape=[chunk] * len(steps),
        compiler_params=pltpu.CompilerParams(vmem_limit_bytes=8 * MIB),
        name="finish",
    )(*in_vmem(mine, got))


def in_calls(call, outers, together):
    chunks, far = {}, outers - together
    for steps in [tuple(range(far, outers))[::-1]] + [(d,) for d in reversed(range(far))]:
        chunks.update(zip(steps, call(steps)))
    return [chunks[d] for d in range(outers)]


def chunk_call(kernel, name, steps, kv_here, count, length, operands):
    chunk = jax.ShapeDtypeStruct((count + STAT_ROWS, HD), jnp.bfloat16)
    return pl.pallas_call(
        functools.partial(kernel, steps, kv_here),
        in_specs=[WHOLE] * len(operands),
        out_specs=[WHOLE] * len(steps),
        out_shape=[chunk] * len(steps),
        cost_estimate=pl.CostEstimate(
            flops=2 * len(steps) * count * length * 3 * HD,
            bytes_accessed=4 * len(steps) * length * HD,
            transcendentals=len(steps) * count * length,
        ),
        compiler_params=pltpu.CompilerParams(vmem_limit_bytes=16 * MIB),
        name=name,
    )(*in_vmem(*operands))


def partials_kernel(steps, kv_here, gain_ref, frames_ref, fresh_ref, *refs):
    kv_refs, refs = (refs[0:2], refs[2:4]), refs[4:]
    length, width = kv_refs[0][1].shape[0], refs[0].shape[1]
    biases = [bias_of(keys_ref, frames_ref[1, :, :1]) for keys_ref, _ in kv_refs]
    for d, handed_ref, out_ref in zip(steps, refs, refs[len(steps) :]):
        g = outer_here() ^ d
        fresh = columns_of(g, fresh_ref, width)[...].astype(jnp.float32)
        x = jnp.where(in_first_section(), fresh, handed_ref[...].astype(jnp.float32))
        queries = queries_of(x, columns_of(place_here() * kv_here + g, gain_ref, width)[...])
        raws = [
            scores(queries, columns_of(g, keys_ref.at[:length], HD)[...], bias)
            for (keys_ref, _), bias in zip(kv_refs, biases)
        ]
        top = functools.reduce(jnp.maximum, [top_of(raw) for raw in raws])
        both = sum(
            weigh(raw, top, columns_of(g, values_ref, HD)[...])
            for raw, (_, values_ref) in zip(raws, kv_refs)
        )
        write_sums(out_ref, both[:, :HD], top, both[:, HD:])


def partials(steps, gain, frames, fresh, own, got, handed):
    length, width = own[1].shape
    tokens, columns = handed[0].shape
    count = columns // HD * tokens
    operands = (gain, frames, fresh, *own, *got, *(handed[d] for d in steps))
    return chunk_call(
        partials_kernel, "partials", steps, width // HD, count, PAIR * length, operands
    )


def merge_kernel(*refs):
    *parts, out_ref = refs
    write_chunk(out_ref, *joined(parts, False))


def merge_first_kernel(*refs):
    *parts, share_ref, out_ref = refs
    x = head_rows(share_ref[...].astype(jnp.float32)).astype(jnp.bfloat16)
    write_chunk(out_ref, *joined(parts, False, x))


def merge(kernel, *parts):
    return pl.pallas_call(
        kernel,
        in_specs=[WHOLE] * len(parts),
        out_specs=WHOLE,
        out_shape=jax.ShapeDtypeStruct(parts[0].shape, parts[0].dtype),
        compiler_params=pltpu.CompilerParams(vmem_limit_bytes=8 * MIB),
        name="merge",
    )(*in_vmem(*parts))


def attended(one_ref, two_ref):
    one, two = one_ref[...].astype(jnp.float32), two_ref[...].astype(jnp.float32)
    here = inner_here() == 0
    parts = [jnp.where(here, one, two), jnp.where(here, two, one)]
    value, _, _ = joined([part.astype(jnp.bfloat16) for part in parts], True)
    return value


def columns_from(rows, tokens):
    pieces = [rows[at : at + tokens] for at in range(0, rows.shape[0], tokens)]
    return jnp.concatenate(pieces, axis=1)


def combine_kernel(one_ref, two_ref, out_ref):
    out_ref[...] = columns_from(attended(one_ref, two_ref), out_ref.shape[0]).astype(jnp.bfloat16)


def combine_last_kernel(one_ref, two_ref, fresh_ref, handed_ref, out_ref):
    fresh = columns_of(outer_here(), fresh_ref, out_ref.shape[1])[...].astype(jnp.float32)
    x = jnp.where(in_first_section(), fresh, handed_ref[...].astype(jnp.float32))
    total = head_rows(x) + attended(one_ref, two_ref)
    out_ref[...] = columns_from(total, out_ref.shape[0]).astype(jnp.bfloat16)


def combine(kernel, name, tokens, one, two, *rest):
    width = (one.shape[0] - STAT_ROWS) // tokens * HD
    return pl.pallas_call(
        kernel,
        in_specs=[WHOLE] * (2 + len(rest)),
        out_specs=WHOLE,
        out_shape=jax.ShapeDtypeStruct((tokens, width), jnp.bfloat16),
        compiler_params=pltpu.CompilerParams(vmem_limit_bytes=8 * MIB),
        name=name,
    )(*in_vmem(one, two, *rest))


def assemble_kernel(*refs):
    *pieces, out_ref = refs
    outers, width = len(pieces) // PAIR, pieces[0].shape[1]
    for n, refs in enumerate((pieces[:outers], pieces[outers:])):
        place = (place_here() + n) % PAIR
        for d, ref in enumerate(refs):
            columns_of(place * outers + (outer_here() ^ d), out_ref, width)[...] = ref[...]


def assemble(mine, others):
    tokens, width = mine[0].shape
    pieces = [*mine, *others]
    return pl.pallas_call(
        assemble_kernel,
        in_specs=[WHOLE] * len(pieces),
        out_specs=WHOLE,
        out_shape=jax.ShapeDtypeStruct((tokens, len(pieces) * width), jnp.bfloat16),
        compiler_params=pltpu.CompilerParams(vmem_limit_bytes=8 * MIB),
        name="assemble",
    )(*in_vmem(*pieces))


def body(
    activations,
    act_frames,
    fresh_batch,
    fresh_frames,
    norm_gain,
    cached_keys,
    cached_values,
    key_frames,
):
    own_keys, given_keys, batch, gain, share, fresh, frames = load_keys(
        act_frames, fresh_frames[None], key_frames.reshape(-1, HD), activations[0], fresh_batch,
        norm_gain, cached_keys[0],
    )
    own_values, given_values = halve_values(cached_values[0])

    tokens = fresh_batch.shape[0]
    outers = lax.axis_size("ctx") // (INNER * PAIR)
    theirs = swapped(first(1, gain, frames, batch, given_keys, given_values))
    mine = first(0, gain, frames, batch, own_keys, own_values)
    chunk, *others = in_calls(lambda steps: finish(steps, mine, theirs), outers, 2)
    own, got = (own_keys, own_values), (swapped(given_keys), swapped(given_values))
    chunk = merge(merge_first_kernel, *from_outer(others, 0)[::-1], chunk, share)
    one, two = swapped(chunk), from_inner(chunk)
    share = combine(combine_kernel, "combine", tokens, one, two)
    handed = from_section_before(share, outers)

    chunk, *others = in_calls(
        lambda steps: partials(steps, gain, frames, fresh, own, got, handed), outers, 1
    )
    chunk = merge(merge_kernel, *from_outer(others)[::-1], swapped(chunk))
    one, two = swapped(chunk), from_inner(chunk)
    share = combine(combine_last_kernel, "combine_last", tokens, one, two, fresh, handed[0])
    theirs = [swapped(share), *from_outer([share] * len(others))]
    return assemble([share, *(swapped(piece) for piece in theirs[1:])], theirs)[None]


def solution(mesh):
    placed = (
        P("section", None, None),
        P(),
        P(),
        P(),
        P("section", None),
        P("section", "ctx", None),
        P("section", "ctx", None),
        P("ctx"),
    )
    return jax.shard_map(
        body, mesh=mesh, in_specs=placed, out_specs=P("section", None, None), check_vma=False
    )
```

```python
import functools
import math

import jax
import jax.numpy as jnp
from jax import lax
from jax.experimental import pallas as pl
from jax.experimental.pallas import tpu as pltpu
from jax.sharding import PartitionSpec as P

HEADS = 64
HD = 128
PAIR = 2
INNER = 2
BLOCKS = 4
STAT_ROWS = 16
HIDDEN = -(2.0**100)
SCALE = HD**-0.5 * math.log2(math.e)
MIB = 1 << 20

epsilon = 1e-05

WHOLE = pl.BlockSpec(memory_space=pltpu.VMEM)
IN_HBM = pl.BlockSpec(memory_space=pltpu.HBM)


def in_hbm(*arrays):
    return [pltpu.with_memory_space_constraint(a, pltpu.HBM) for a in arrays]


def in_vmem(*arrays):
    return [pltpu.with_memory_space_constraint(a, pltpu.VMEM) for a in arrays]


def place_here():
    return lax.axis_index("ctx") % PAIR


def inner_here():
    return lax.axis_index("ctx") // PAIR % INNER


def outer_here():
    return lax.axis_index("ctx") // (PAIR * INNER)


def in_first_section():
    return lax.axis_index("section") == 0


def swapped(block):
    return lax.ppermute(block, "ctx", [(i, i ^ 1) for i in range(lax.axis_size("ctx"))])


def from_inner(block):
    size = lax.axis_size("ctx")
    return lax.ppermute(block, "ctx", [(i, i ^ PAIR ^ 1) for i in range(size)])


def from_outer(blocks, other_place=1):
    size = lax.axis_size("ctx")
    got = [
        lax.ppermute(
            block, "ctx", [(i, i ^ (INNER * PAIR * d) ^ other_place) for i in range(size)]
        )
        for d, block in reversed(list(enumerate(blocks, 1)))
    ]
    return got[::-1]


def from_section_before(block, outers):
    sections, size = lax.axis_size("section"), lax.axis_size("ctx")
    got = []
    for d in reversed(range(outers)):
        route = [
            (s * size + i, (s + 1) % sections * size + (i ^ (INNER * PAIR * d) ^ 1))
            for s in range(sections)
            for i in range(size)
        ]
        got.append(lax.ppermute(block, ("section", "ctx"), route))
    return got[::-1]


def head_rows(block):
    return jnp.concatenate(
        [block[:, at : at + HD] for at in range(0, block.shape[1], HD)], axis=0
    )


def row_of(ref):
    return jnp.concatenate([ref[i : i + 1] for i in range(ref.shape[0])], axis=1)


def columns_of(index, ref, width):
    return ref.at[:, pl.ds(pl.multiple_of(index * width, HD), width)]


def on_diagonal(rows):
    shape = (rows, HD)
    return lax.broadcasted_iota(jnp.int32, shape, 0) == lax.broadcasted_iota(jnp.int32, shape, 1)


def queries_of(x, gain):
    rows = head_rows(x.astype(jnp.float32))
    gain = head_rows(jnp.broadcast_to(gain, x.shape))
    norm = lax.rsqrt(jnp.mean(rows * rows, axis=-1, keepdims=True) + epsilon)
    return (rows * norm * gain).astype(jnp.bfloat16)


def bias_of(keys_ref, frames):
    length = keys_ref.shape[0] - STAT_ROWS
    width = keys_ref.shape[1]
    rows = -(-length // width)
    tail = keys_ref[length:].astype(jnp.float32)
    key_frames = jnp.concatenate([tail[i : i + 1] for i in range(rows)], axis=1)[:, :length]
    return jnp.where(key_frames <= frames, 0.0, HIDDEN)[None]


def scores(queries, key_block, bias):
    count, keys, tokens = queries.shape[0], key_block.shape[0], bias.shape[1]
    raw = lax.dot_general(
        queries, key_block, (((1,), (1,)), ((), ())), preferred_element_type=jnp.float32
    )
    raw = raw.reshape(count // tokens, tokens, keys) * SCALE + bias
    return raw.reshape(count, keys)


def top_of(raw):
    top = jnp.max(raw, axis=-1, keepdims=True)
    return top.astype(jnp.bfloat16).astype(jnp.float32)


def weigh(raw, top, value_block):
    probs = jnp.exp2(raw - top).astype(jnp.bfloat16)
    ones = jnp.ones((value_block.shape[0], HD), jnp.bfloat16)
    return jnp.dot(
        probs, jnp.concatenate([value_block, ones], axis=1), preferred_element_type=jnp.float32
    )


def groups_of(count):
    groups = -(-count // HD)
    held = count // groups
    return [slice(c * held, (c + 1) * held) for c in range(groups)]


def write_chunk(out_ref, weighted, tops, totals):
    count = weighted.shape[0]
    line = lax.broadcasted_iota(jnp.int32, (STAT_ROWS, HD), 0)
    stats = jnp.zeros((STAT_ROWS, HD), jnp.float32)
    for c, (top, total) in enumerate(zip(tops, totals)):
        high = total.astype(jnp.bfloat16).astype(jnp.float32)
        for n, row in enumerate((top, high, total - high)):
            stats = jnp.where(line == 3 * c + n, row, stats)
    out_ref[:count] = weighted.astype(jnp.bfloat16)
    out_ref[count:] = stats.astype(jnp.bfloat16)


def write_sums(out_ref, weighted, top, total):
    groups = groups_of(weighted.shape[0])
    diagonal = on_diagonal(groups[0].stop)

    def rows(column):
        column = jnp.broadcast_to(column, weighted.shape)
        return [
            jnp.sum(jnp.where(diagonal, column[group], 0.0), axis=0, keepdims=True)
            for group in groups
        ]

    write_chunk(out_ref, weighted, rows(top), rows(total))


def joined(parts, normed, x=None):
    count = parts[0].shape[0] - STAT_ROWS
    groups = groups_of(count)
    diagonal = on_diagonal(groups[0].stop)
    stats = [part[count:].astype(jnp.float32) for part in parts]
    values, tops, totals = [], [], []
    for c, group in enumerate(groups):
        points = [s[3 * c : 3 * c + 1] for s in stats]
        top = functools.reduce(jnp.maximum, points)
        factors = [jnp.exp2(point - top) for point in points]
        total = sum(
            f * (s[3 * c + 1 : 3 * c + 2] + s[3 * c + 2 : 3 * c + 3])
            for f, s in zip(factors, stats)
        )
        if normed:
            inverse = 1.0 / total
            factors = [f * inverse for f in factors]
        terms = list(zip(factors, parts)) + ([] if x is None else [(total, x)])
        value = 0.0
        for factor, part in terms:
            weight = jnp.where(diagonal, factor, 0.0)[:, : group.stop - group.start]
            high = weight.astype(jnp.bfloat16)
            low = (weight - high.astype(jnp.float32)).astype(jnp.bfloat16)
            for term in (high, low):
                value = value + jnp.dot(term, part[group], preferred_element_type=jnp.float32)
        values.append(value)
        tops.append(top)
        totals.append(total)
    return jnp.concatenate(values, axis=0), tops, totals


def halve(staged_ref, copies, own_ref, given_ref):
    length, width = staged_ref.shape
    half, step = width // PAIR, length // BLOCKS
    place = place_here()
    for b in range(BLOCKS):
        if copies:
            copies[b].wait()
        rows = pl.ds(b * step, step)
        given_ref[rows] = columns_of(1 - place, staged_ref.at[rows], half)[...]
        own_ref[rows] = columns_of(place, staged_ref.at[rows], half)[...]


def column_of(row):
    shape = (row.shape[1], row.shape[1])
    diagonal = lax.broadcasted_iota(jnp.int32, shape, 0) == lax.broadcasted_iota(jnp.int32, shape, 1)
    return jnp.sum(jnp.where(diagonal, row, 0.0), axis=1, keepdims=True)


def load_keys_kernel(
    act_frames_in, fresh_frames_in, key_frames_in, batch_in, fresh_in, gain_in, keys_in,
    own_ref, given_ref, batch_ref, gain_ref, share_ref, fresh_ref, frames_ref,
    act_frames_ref, fresh_frames_ref, key_frames_ref, staged_ref, sems, small_sems,
):
    place, length, width = place_here(), staged_ref.shape[0], own_ref.shape[1]
    half, share = fresh_ref.shape[1], share_ref.shape[1]
    own_share = place * (half // share) + outer_here()
    small = [
        (act_frames_in, act_frames_ref),
        (fresh_frames_in, fresh_frames_ref),
        (key_frames_in, key_frames_ref),
        (batch_in, batch_ref),
        (gain_in, gain_ref),
        (columns_of(own_share, batch_in, share), share_ref),
        (columns_of(place, fresh_in, half), fresh_ref),
    ]
    small = [pltpu.make_async_copy(a, b, small_sems.at[n]) for n, (a, b) in enumerate(small)]
    copies, step = [], length // BLOCKS
    for b in range(BLOCKS):
        rows = pl.ds(b * step, step)
        copies.append(pltpu.make_async_copy(keys_in.at[rows], staged_ref.at[rows], sems.at[b]))
    for copy in small[:3] + copies + small[3:]:
        copy.start()
    for copy in small[:3]:
        copy.wait()

    tokens = frames_ref.shape[1]
    section = lax.axis_index("section")
    own_row = act_frames_ref[pl.ds(section, 1), :].astype(jnp.float32)
    prior_row = act_frames_ref[pl.ds(jnp.maximum(section - 1, 0), 1), :].astype(jnp.float32)
    fresh_row = fresh_frames_ref[...].astype(jnp.float32)
    next_row = jnp.where(in_first_section(), fresh_row, prior_row)
    for tick, row in enumerate((own_row, next_row)):
        frames_ref[tick] = jnp.broadcast_to(column_of(row), (tokens, HD))

    row = row_of(key_frames_ref).astype(jnp.float32)
    lines = -(-length // width)
    row = jnp.concatenate([row, jnp.zeros((1, lines * width - length), jnp.float32)], axis=1)
    line = lax.broadcasted_iota(jnp.int32, (STAT_ROWS, width), 0)
    tail = jnp.zeros((STAT_ROWS, width), jnp.float32)
    for n in range(lines):
        tail = jnp.where(line == n, row[:, n * width : (n + 1) * width], tail)
    for ref in (own_ref, given_ref):
        ref[length:] = tail.astype(jnp.bfloat16)
    halve(staged_ref, copies, own_ref, given_ref)
    for copy in small[3:]:
        copy.wait()


def load_keys(act_frames, fresh_frames, key_frames, batch, fresh, gain, keys):
    length, width = keys.shape
    tokens, model = batch.shape
    share = model * INNER // lax.axis_size("ctx")
    shape = (length + STAT_ROWS, width // PAIR)
    frames = (act_frames, fresh_frames, key_frames)
    return pl.pallas_call(
        load_keys_kernel,
        in_specs=[IN_HBM] * 7,
        out_specs=[WHOLE] * 7,
        out_shape=[
            pltpu.VMEM(shape, keys.dtype),
            pltpu.VMEM(shape, keys.dtype),
            pltpu.VMEM(batch.shape, batch.dtype),
            pltpu.VMEM(gain.shape, gain.dtype),
            pltpu.VMEM((tokens, share), batch.dtype),
            pltpu.VMEM((tokens, model // PAIR), fresh.dtype),
            pltpu.VMEM((2, tokens, HD), jnp.float32),
        ],
        scratch_shapes=[
            *(pltpu.VMEM(a.shape, a.dtype) for a in frames),
            pltpu.VMEM((length, width), keys.dtype),
            pltpu.SemaphoreType.DMA((BLOCKS,)),
            pltpu.SemaphoreType.DMA((7,)),
        ],
        cost_estimate=pl.CostEstimate(
            flops=0, bytes_accessed=2 * length * width, transcendentals=0
        ),
        compiler_params=pltpu.CompilerParams(vmem_limit_bytes=16 * MIB),
        name="load_keys",
    )(*in_hbm(*frames, batch, fresh, gain, keys))


def halve_values_kernel(values_ref, own_ref, given_ref):
    halve(values_ref, [], own_ref, given_ref)


def halve_values(values):
    length, width = values.shape
    half = pltpu.VMEM((length, width // PAIR), values.dtype)
    return pl.pallas_call(
        halve_values_kernel,
        in_specs=[WHOLE],
        out_specs=[WHOLE] * 2,
        out_shape=[half, half],
        cost_estimate=pl.CostEstimate(
            flops=0, bytes_accessed=2 * length * width, transcendentals=0
        ),
        compiler_params=pltpu.CompilerParams(vmem_limit_bytes=16 * MIB),
        name="halve_values",
    )(*in_vmem(values))


def first_kernel(other, gain_ref, frames_ref, batch_ref, keys_ref, values_ref, out_ref):
    length, kv_here = values_ref.shape[0], out_ref.shape[0]
    width = gain_ref.shape[1] // (PAIR * kv_here)
    place = (place_here() + other) % PAIR
    bias = bias_of(keys_ref, frames_ref[0, :, :1])
    for g in range(kv_here):
        index, block = place * kv_here + g, slice(g * HD, (g + 1) * HD)
        x, gain = columns_of(index, batch_ref, width)[...], columns_of(index, gain_ref, width)[...]
        raw = scores(queries_of(x, gain), keys_ref[:length, block], bias)
        top = top_of(raw)
        both = weigh(raw, top, values_ref[:, block])
        write_sums(out_ref.at[g], both[:, :HD], top, both[:, HD:])


def first(other, gain, frames, batch, keys, values):
    length, width = values.shape
    tokens = batch.shape[0]
    kv_here = width // HD
    queries = HEADS // PAIR * tokens
    return pl.pallas_call(
        functools.partial(first_kernel, other),
        in_specs=[WHOLE] * 5,
        out_specs=WHOLE,
        out_shape=jax.ShapeDtypeStruct((kv_here, queries // kv_here + STAT_ROWS, HD), jnp.bfloat16),
        cost_estimate=pl.CostEstimate(
            flops=2 * queries * length * 3 * HD,
            bytes_accessed=4 * length * width,
            transcendentals=queries * length,
        ),
        compiler_params=pltpu.CompilerParams(vmem_limit_bytes=16 * MIB),
        name="first",
    )(*in_vmem(gain, frames, batch, keys, values))


def finish_kernel(steps, mine_ref, got_ref, *out_refs):
    for d, out_ref in zip(steps, out_refs):
        g = outer_here() ^ d
        write_chunk(out_ref, *joined([mine_ref.at[g], got_ref.at[g]], False))


def finish(steps, mine, got):
    chunk = jax.ShapeDtypeStruct(mine.shape[1:], mine.dtype)
    return pl.pallas_call(
        functools.partial(finish_kernel, steps),
        in_specs=[WHOLE] * 2,
        out_specs=[WHOLE] * len(steps),
        out_shape=[chunk] * len(steps),
        compiler_params=pltpu.CompilerParams(vmem_limit_bytes=8 * MIB),
        name="finish",
    )(*in_vmem(mine, got))


def in_calls(call, outers, together):
    chunks, far = {}, outers - together
    for steps in [tuple(range(far, outers))[::-1]] + [(d,) for d in reversed(range(far))]:
        chunks.update(zip(steps, call(steps)))
    return [chunks[d] for d in range(outers)]


def chunk_call(kernel, name, steps, kv_here, count, length, operands):
    chunk = jax.ShapeDtypeStruct((count + STAT_ROWS, HD), jnp.bfloat16)
    return pl.pallas_call(
        functools.partial(kernel, steps, kv_here),
        in_specs=[WHOLE] * len(operands),
        out_specs=[WHOLE] * len(steps),
        out_shape=[chunk] * len(steps),
        cost_estimate=pl.CostEstimate(
            flops=2 * len(steps) * count * length * 3 * HD,
            bytes_accessed=4 * len(steps) * length * HD,
            transcendentals=len(steps) * count * length,
        ),
        compiler_params=pltpu.CompilerParams(vmem_limit_bytes=16 * MIB),
        name=name,
    )(*in_vmem(*operands))


def partials_kernel(steps, kv_here, gain_ref, frames_ref, fresh_ref, *refs):
    kv_refs, refs = (refs[0:2], refs[2:4]), refs[4:]
    length, width = kv_refs[0][1].shape[0], refs[0].shape[1]
    biases = [bias_of(keys_ref, frames_ref[1, :, :1]) for keys_ref, _ in kv_refs]
    for d, handed_ref, out_ref in zip(steps, refs, refs[len(steps) :]):
        g = outer_here() ^ d
        fresh = columns_of(g, fresh_ref, width)[...].astype(jnp.float32)
        x = jnp.where(in_first_section(), fresh, handed_ref[...].astype(jnp.float32))
        queries = queries_of(x, columns_of(place_here() * kv_here + g, gain_ref, width)[...])
        raws = [
            scores(queries, columns_of(g, keys_ref.at[:length], HD)[...], bias)
            for (keys_ref, _), bias in zip(kv_refs, biases)
        ]
        top = functools.reduce(jnp.maximum, [top_of(raw) for raw in raws])
        both = sum(
            weigh(raw, top, columns_of(g, values_ref, HD)[...])
            for raw, (_, values_ref) in zip(raws, kv_refs)
        )
        write_sums(out_ref, both[:, :HD], top, both[:, HD:])


def partials(steps, gain, frames, fresh, own, got, handed):
    length, width = own[1].shape
    tokens, columns = handed[0].shape
    count = columns // HD * tokens
    operands = (gain, frames, fresh, *own, *got, *(handed[d] for d in steps))
    return chunk_call(
        partials_kernel, "partials", steps, width // HD, count, PAIR * length, operands
    )


def merge_kernel(*refs):
    *parts, out_ref = refs
    write_chunk(out_ref, *joined(parts, False))


def merge_first_kernel(*refs):
    *parts, share_ref, out_ref = refs
    x = head_rows(share_ref[...].astype(jnp.float32)).astype(jnp.bfloat16)
    write_chunk(out_ref, *joined(parts, False, x))


def merge(kernel, *parts):
    return pl.pallas_call(
        kernel,
        in_specs=[WHOLE] * len(parts),
        out_specs=WHOLE,
        out_shape=jax.ShapeDtypeStruct(parts[0].shape, parts[0].dtype),
        compiler_params=pltpu.CompilerParams(vmem_limit_bytes=8 * MIB),
        name="merge",
    )(*in_vmem(*parts))


def attended(one_ref, two_ref):
    one, two = one_ref[...].astype(jnp.float32), two_ref[...].astype(jnp.float32)
    here = inner_here() == 0
    parts = [jnp.where(here, one, two), jnp.where(here, two, one)]
    value, _, _ = joined([part.astype(jnp.bfloat16) for part in parts], True)
    return value


def columns_from(rows, tokens):
    pieces = [rows[at : at + tokens] for at in range(0, rows.shape[0], tokens)]
    return jnp.concatenate(pieces, axis=1)


def combine_kernel(two_ref, one_ref, out_ref):
    out_ref[...] = columns_from(attended(one_ref, two_ref), out_ref.shape[0]).astype(jnp.bfloat16)


def combine_last_kernel(two_ref, one_ref, fresh_ref, handed_ref, out_ref):
    fresh = columns_of(outer_here(), fresh_ref, out_ref.shape[1])[...].astype(jnp.float32)
    x = jnp.where(in_first_section(), fresh, handed_ref[...].astype(jnp.float32))
    total = head_rows(x) + attended(one_ref, two_ref)
    out_ref[...] = columns_from(total, out_ref.shape[0]).astype(jnp.bfloat16)


def combine(kernel, name, tokens, one, two, *rest):
    width = (one.shape[0] - STAT_ROWS) // tokens * HD
    return pl.pallas_call(
        kernel,
        in_specs=[WHOLE] * (2 + len(rest)),
        out_specs=WHOLE,
        out_shape=jax.ShapeDtypeStruct((tokens, width), jnp.bfloat16),
        compiler_params=pltpu.CompilerParams(vmem_limit_bytes=8 * MIB),
        name=name,
    )(*in_vmem(two, one, *rest))


def assemble_kernel(*refs):
    *pieces, out_ref = refs
    outers, width = len(pieces) // PAIR, pieces[0].shape[1]
    for n, refs in enumerate((pieces[:outers], pieces[outers:])):
        place = (place_here() + n) % PAIR
        for d, ref in zip(reversed(range(outers)), refs):
            columns_of(place * outers + (outer_here() ^ d), out_ref, width)[...] = ref[...]


def assemble(mine, others):
    tokens, width = mine[0].shape
    pieces = [*mine[::-1], *others[::-1]]
    return pl.pallas_call(
        assemble_kernel,
        in_specs=[WHOLE] * len(pieces),
        out_specs=WHOLE,
        out_shape=jax.ShapeDtypeStruct((tokens, len(pieces) * width), jnp.bfloat16),
        compiler_params=pltpu.CompilerParams(vmem_limit_bytes=8 * MIB),
        name="assemble",
    )(*in_vmem(*pieces))


def body(
    activations,
    act_frames,
    fresh_batch,
    fresh_frames,
    norm_gain,
    cached_keys,
    cached_values,
    key_frames,
):
    own_keys, given_keys, batch, gain, share, fresh, frames = load_keys(
        act_frames, fresh_frames[None], key_frames.reshape(-1, HD), activations[0], fresh_batch,
        norm_gain, cached_keys[0],
    )
    own_values, given_values = halve_values(cached_values[0])

    tokens = fresh_batch.shape[0]
    outers = lax.axis_size("ctx") // (INNER * PAIR)
    theirs = swapped(first(1, gain, frames, batch, given_keys, given_values))
    mine = first(0, gain, frames, batch, own_keys, own_values)
    chunk, *others = in_calls(lambda steps: finish(steps, mine, theirs), outers, 2)
    own, got = (own_keys, own_values), (swapped(given_keys), swapped(given_values))
    chunk = merge(merge_first_kernel, *from_outer(others, 0)[::-1], chunk, share)
    one, two = swapped(chunk), from_inner(chunk)
    share = combine(combine_kernel, "combine", tokens, one, two)
    handed = from_section_before(share, outers)

    chunk, *others = in_calls(
        lambda steps: partials(steps, gain, frames, fresh, own, got, handed), outers, 1
    )
    chunk = merge(merge_kernel, swapped(chunk), *from_outer(others))
    one, two = swapped(chunk), from_inner(chunk)
    share = combine(combine_last_kernel, "combine_last", tokens, one, two, fresh, handed[0])
    theirs = [swapped(share), *from_outer([share] * len(others))]
    return assemble([share, *(swapped(piece) for piece in theirs[1:])], theirs)[None]


def solution(mesh):
    placed = (
        P("section", None, None),
        P(),
        P(),
        P(),
        P("section", None),
        P("section", "ctx", None),
        P("section", "ctx", None),
        P("ctx"),
    )
    return jax.shard_map(
        body, mesh=mesh, in_specs=placed, out_specs=P("section", None, None), check_vma=False
    )
```

```python
import functools
import math

import jax
import jax.numpy as jnp
from jax import lax
from jax.experimental import pallas as pl
from jax.experimental.pallas import tpu as pltpu
from jax.sharding import PartitionSpec as P

HEADS = 64
HD = 128
PAIR = 2
INNER = 2
BLOCKS = 4
STAT_ROWS = 16
HIDDEN = -(2.0**100)
SCALE = HD**-0.5 * math.log2(math.e)
MIB = 1 << 20

epsilon = 1e-05

WHOLE = pl.BlockSpec(memory_space=pltpu.VMEM)
IN_HBM = pl.BlockSpec(memory_space=pltpu.HBM)


def in_hbm(*arrays):
    return [pltpu.with_memory_space_constraint(a, pltpu.HBM) for a in arrays]


def in_vmem(*arrays):
    return [pltpu.with_memory_space_constraint(a, pltpu.VMEM) for a in arrays]


def place_here():
    return lax.axis_index("ctx") % PAIR


def inner_here():
    return lax.axis_index("ctx") // PAIR % INNER


def outer_here():
    return lax.axis_index("ctx") // (PAIR * INNER)


def in_first_section():
    return lax.axis_index("section") == 0


def swapped(block):
    return lax.ppermute(block, "ctx", [(i, i ^ 1) for i in range(lax.axis_size("ctx"))])


def from_inner(block):
    size = lax.axis_size("ctx")
    return lax.ppermute(block, "ctx", [(i, i ^ PAIR ^ 1) for i in range(size)])


def from_outer(blocks, other_place=1):
    size = lax.axis_size("ctx")
    got = [
        lax.ppermute(
            block, "ctx", [(i, i ^ (INNER * PAIR * d) ^ other_place) for i in range(size)]
        )
        for d, block in reversed(list(enumerate(blocks, 1)))
    ]
    return got[::-1]


def from_section_before(block, outers):
    sections, size = lax.axis_size("section"), lax.axis_size("ctx")
    got = []
    for d in reversed(range(outers)):
        route = [
            (s * size + i, (s + 1) % sections * size + (i ^ (INNER * PAIR * d) ^ 1))
            for s in range(sections)
            for i in range(size)
        ]
        got.append(lax.ppermute(block, ("section", "ctx"), route))
    return got[::-1]


def head_rows(block):
    return jnp.concatenate(
        [block[:, at : at + HD] for at in range(0, block.shape[1], HD)], axis=0
    )


def row_of(ref):
    return jnp.concatenate([ref[i : i + 1] for i in range(ref.shape[0])], axis=1)


def columns_of(index, ref, width):
    return ref.at[:, pl.ds(pl.multiple_of(index * width, HD), width)]


def on_diagonal(rows):
    shape = (rows, HD)
    return lax.broadcasted_iota(jnp.int32, shape, 0) == lax.broadcasted_iota(jnp.int32, shape, 1)


def queries_of(x, gain):
    rows = head_rows(x.astype(jnp.float32))
    gain = head_rows(jnp.broadcast_to(gain, x.shape))
    norm = lax.rsqrt(jnp.mean(rows * rows, axis=-1, keepdims=True) + epsilon)
    return (rows * norm * gain).astype(jnp.bfloat16)


def bias_of(keys_ref, frames):
    length = keys_ref.shape[0] - STAT_ROWS
    width = keys_ref.shape[1]
    rows = -(-length // width)
    tail = keys_ref[length:].astype(jnp.float32)
    key_frames = jnp.concatenate([tail[i : i + 1] for i in range(rows)], axis=1)[:, :length]
    return jnp.where(key_frames <= frames, 0.0, HIDDEN)[None]


def scores(queries, key_block, bias):
    count, keys, tokens = queries.shape[0], key_block.shape[0], bias.shape[1]
    raw = lax.dot_general(
        queries, key_block, (((1,), (1,)), ((), ())), preferred_element_type=jnp.float32
    )
    raw = raw.reshape(count // tokens, tokens, keys) * SCALE + bias
    return raw.reshape(count, keys)


def top_of(raw):
    top = jnp.max(raw, axis=-1, keepdims=True)
    return top.astype(jnp.bfloat16).astype(jnp.float32)


def weigh(raw, top, value_block):
    probs = jnp.exp2(raw - top).astype(jnp.bfloat16)
    ones = jnp.ones((value_block.shape[0], HD), jnp.bfloat16)
    return jnp.dot(
        probs, jnp.concatenate([value_block, ones], axis=1), preferred_element_type=jnp.float32
    )


def groups_of(count):
    groups = -(-count // HD)
    held = count // groups
    return [slice(c * held, (c + 1) * held) for c in range(groups)]


def write_chunk(out_ref, weighted, tops, totals):
    count = weighted.shape[0]
    line = lax.broadcasted_iota(jnp.int32, (STAT_ROWS, HD), 0)
    stats = jnp.zeros((STAT_ROWS, HD), jnp.float32)
    for c, (top, total) in enumerate(zip(tops, totals)):
        high = total.astype(jnp.bfloat16).astype(jnp.float32)
        for n, row in enumerate((top, high, total - high)):
            stats = jnp.where(line == 3 * c + n, row, stats)
    out_ref[:count] = weighted.astype(jnp.bfloat16)
    out_ref[count:] = stats.astype(jnp.bfloat16)


def write_sums(out_ref, weighted, top, total):
    groups = groups_of(weighted.shape[0])
    diagonal = on_diagonal(groups[0].stop)

    def rows(column):
        column = jnp.broadcast_to(column, weighted.shape)
        return [
            jnp.sum(jnp.where(diagonal, column[group], 0.0), axis=0, keepdims=True)
            for group in groups
        ]

    write_chunk(out_ref, weighted, rows(top), rows(total))


def joined(parts, normed, x=None):
    count = parts[0].shape[0] - STAT_ROWS
    groups = groups_of(count)
    diagonal = on_diagonal(groups[0].stop)
    stats = [part[count:].astype(jnp.float32) for part in parts]
    values, tops, totals = [], [], []
    for c, group in enumerate(groups):
        points = [s[3 * c : 3 * c + 1] for s in stats]
        top = functools.reduce(jnp.maximum, points)
        factors = [jnp.exp2(point - top) for point in points]
        total = sum(
            f * (s[3 * c + 1 : 3 * c + 2] + s[3 * c + 2 : 3 * c + 3])
            for f, s in zip(factors, stats)
        )
        if normed:
            inverse = 1.0 / total
            factors = [f * inverse for f in factors]
        terms = list(zip(factors, parts)) + ([] if x is None else [(total, x)])
        value = 0.0
        for factor, part in terms:
            weight = jnp.where(diagonal, factor, 0.0)[:, : group.stop - group.start]
            high = weight.astype(jnp.bfloat16)
            low = (weight - high.astype(jnp.float32)).astype(jnp.bfloat16)
            for term in (high, low):
                value = value + jnp.dot(term, part[group], preferred_element_type=jnp.float32)
        values.append(value)
        tops.append(top)
        totals.append(total)
    return jnp.concatenate(values, axis=0), tops, totals


def halve(staged_ref, copies, own_ref, given_ref):
    length, width = staged_ref.shape
    half, step = width // PAIR, length // BLOCKS
    place = place_here()
    for b in range(BLOCKS):
        if copies:
            copies[b].wait()
        rows = pl.ds(b * step, step)
        given_ref[rows] = columns_of(1 - place, staged_ref.at[rows], half)[...]
        own_ref[rows] = columns_of(place, staged_ref.at[rows], half)[...]


def column_of(row):
    shape = (row.shape[1], row.shape[1])
    diagonal = lax.broadcasted_iota(jnp.int32, shape, 0) == lax.broadcasted_iota(jnp.int32, shape, 1)
    return jnp.sum(jnp.where(diagonal, row, 0.0), axis=1, keepdims=True)


def load_keys_kernel(
    act_frames_in, fresh_frames_in, key_frames_in, batch_in, fresh_in, gain_in, keys_in,
    own_ref, given_ref, batch_ref, gain_ref, share_ref, fresh_ref, frames_ref,
    act_frames_ref, fresh_frames_ref, key_frames_ref, staged_ref, sems, small_sems,
):
    place, length, width = place_here(), staged_ref.shape[0], own_ref.shape[1]
    half, share = fresh_ref.shape[1], share_ref.shape[1]
    own_share = place * (half // share) + outer_here()
    small = [
        (act_frames_in, act_frames_ref),
        (fresh_frames_in, fresh_frames_ref),
        (key_frames_in, key_frames_ref),
        (batch_in, batch_ref),
        (gain_in, gain_ref),
        (columns_of(own_share, batch_in, share), share_ref),
        (columns_of(place, fresh_in, half), fresh_ref),
    ]
    small = [pltpu.make_async_copy(a, b, small_sems.at[n]) for n, (a, b) in enumerate(small)]
    copies, step = [], length // BLOCKS
    for b in range(BLOCKS):
        rows = pl.ds(b * step, step)
        copies.append(pltpu.make_async_copy(keys_in.at[rows], staged_ref.at[rows], sems.at[b]))
    for copy in small[:3] + copies + small[3:]:
        copy.start()
    for copy in small[:3]:
        copy.wait()

    tokens = frames_ref.shape[1]
    section = lax.axis_index("section")
    own_row = act_frames_ref[pl.ds(section, 1), :].astype(jnp.float32)
    prior_row = act_frames_ref[pl.ds(jnp.maximum(section - 1, 0), 1), :].astype(jnp.float32)
    fresh_row = fresh_frames_ref[...].astype(jnp.float32)
    next_row = jnp.where(in_first_section(), fresh_row, prior_row)
    for tick, row in enumerate((own_row, next_row)):
        frames_ref[tick] = jnp.broadcast_to(column_of(row), (tokens, HD))

    row = row_of(key_frames_ref).astype(jnp.float32)
    lines = -(-length // width)
    row = jnp.concatenate([row, jnp.zeros((1, lines * width - length), jnp.float32)], axis=1)
    line = lax.broadcasted_iota(jnp.int32, (STAT_ROWS, width), 0)
    tail = jnp.zeros((STAT_ROWS, width), jnp.float32)
    for n in range(lines):
        tail = jnp.where(line == n, row[:, n * width : (n + 1) * width], tail)
    for ref in (own_ref, given_ref):
        ref[length:] = tail.astype(jnp.bfloat16)
    halve(staged_ref, copies, own_ref, given_ref)
    for copy in small[3:]:
        copy.wait()


def load_keys(act_frames, fresh_frames, key_frames, batch, fresh, gain, keys):
    length, width = keys.shape
    tokens, model = batch.shape
    share = model * INNER // lax.axis_size("ctx")
    shape = (length + STAT_ROWS, width // PAIR)
    frames = (act_frames, fresh_frames, key_frames)
    return pl.pallas_call(
        load_keys_kernel,
        in_specs=[IN_HBM] * 7,
        out_specs=[WHOLE] * 7,
        out_shape=[
            pltpu.VMEM(shape, keys.dtype),
            pltpu.VMEM(shape, keys.dtype),
            pltpu.VMEM(batch.shape, batch.dtype),
            pltpu.VMEM(gain.shape, gain.dtype),
            pltpu.VMEM((tokens, share), batch.dtype),
            pltpu.VMEM((tokens, model // PAIR), fresh.dtype),
            pltpu.VMEM((2, tokens, HD), jnp.float32),
        ],
        scratch_shapes=[
            *(pltpu.VMEM(a.shape, a.dtype) for a in frames),
            pltpu.VMEM((length, width), keys.dtype),
            pltpu.SemaphoreType.DMA((BLOCKS,)),
            pltpu.SemaphoreType.DMA((7,)),
        ],
        cost_estimate=pl.CostEstimate(
            flops=0, bytes_accessed=2 * length * width, transcendentals=0
        ),
        compiler_params=pltpu.CompilerParams(vmem_limit_bytes=16 * MIB),
        name="load_keys",
    )(*in_hbm(*frames, batch, fresh, gain, keys))


def both_of(ref):
    rows = (ref.shape[0] + STAT_ROWS) // 2
    return ref.at[:rows], ref.at[rows:]


def halve_values_kernel(values_ref, keys_ref, own_ref, given_ref):
    given_keys, given_values = both_of(given_ref)
    given_keys[...] = keys_ref[...]
    halve(values_ref, [], own_ref, given_values)


def halve_values(values, given_keys):
    length, width = values.shape
    rows, half = given_keys.shape
    return pl.pallas_call(
        halve_values_kernel,
        in_specs=[WHOLE] * 2,
        out_specs=[WHOLE] * 2,
        out_shape=[
            pltpu.VMEM((length, half), values.dtype),
            pltpu.VMEM((rows + length, half), values.dtype),
        ],
        cost_estimate=pl.CostEstimate(
            flops=0, bytes_accessed=2 * length * width, transcendentals=0
        ),
        compiler_params=pltpu.CompilerParams(vmem_limit_bytes=16 * MIB),
        name="halve_values",
    )(*in_vmem(values, given_keys))


def first_kernel(other, gain_ref, frames_ref, batch_ref, *refs):
    *kv_refs, out_ref = refs
    keys_ref, values_ref = kv_refs if len(kv_refs) == 2 else both_of(*kv_refs)
    length, kv_here = values_ref.shape[0], out_ref.shape[0]
    width = gain_ref.shape[1] // (PAIR * kv_here)
    place = (place_here() + other) % PAIR
    bias = bias_of(keys_ref, frames_ref[0, :, :1])
    for g in range(kv_here):
        index, block = place * kv_here + g, slice(g * HD, (g + 1) * HD)
        x, gain = columns_of(index, batch_ref, width)[...], columns_of(index, gain_ref, width)[...]
        raw = scores(queries_of(x, gain), keys_ref[:length, block], bias)
        top = top_of(raw)
        both = weigh(raw, top, values_ref[:, block])
        write_sums(out_ref.at[g], both[:, :HD], top, both[:, HD:])


def first(other, length, gain, frames, batch, *kv):
    width = kv[0].shape[1]
    tokens = batch.shape[0]
    kv_here = width // HD
    queries = HEADS // PAIR * tokens
    return pl.pallas_call(
        functools.partial(first_kernel, other),
        in_specs=[WHOLE] * (3 + len(kv)),
        out_specs=WHOLE,
        out_shape=jax.ShapeDtypeStruct((kv_here, queries // kv_here + STAT_ROWS, HD), jnp.bfloat16),
        cost_estimate=pl.CostEstimate(
            flops=2 * queries * length * 3 * HD,
            bytes_accessed=4 * length * width,
            transcendentals=queries * length,
        ),
        compiler_params=pltpu.CompilerParams(vmem_limit_bytes=16 * MIB),
        name="first",
    )(*in_vmem(gain, frames, batch, *kv))


def finish_kernel(steps, mine_ref, got_ref, *out_refs):
    for d, out_ref in zip(steps, out_refs):
        g = outer_here() ^ d
        write_chunk(out_ref, *joined([mine_ref.at[g], got_ref.at[g]], False))


def finish(steps, mine, got):
    chunk = jax.ShapeDtypeStruct(mine.shape[1:], mine.dtype)
    return pl.pallas_call(
        functools.partial(finish_kernel, steps),
        in_specs=[WHOLE] * 2,
        out_specs=[WHOLE] * len(steps),
        out_shape=[chunk] * len(steps),
        compiler_params=pltpu.CompilerParams(vmem_limit_bytes=8 * MIB),
        name="finish",
    )(*in_vmem(mine, got))


def in_calls(call, outers, together):
    chunks, far = {}, outers - together
    for steps in [tuple(range(far, outers))[::-1]] + [(d,) for d in reversed(range(far))]:
        chunks.update(zip(steps, call(steps)))
    return [chunks[d] for d in range(outers)]


def chunk_call(kernel, name, steps, kv_here, count, length, operands):
    chunk = jax.ShapeDtypeStruct((count + STAT_ROWS, HD), jnp.bfloat16)
    return pl.pallas_call(
        functools.partial(kernel, steps, kv_here),
        in_specs=[WHOLE] * len(operands),
        out_specs=[WHOLE] * len(steps),
        out_shape=[chunk] * len(steps),
        cost_estimate=pl.CostEstimate(
            flops=2 * len(steps) * count * length * 3 * HD,
            bytes_accessed=4 * len(steps) * length * HD,
            transcendentals=len(steps) * count * length,
        ),
        compiler_params=pltpu.CompilerParams(vmem_limit_bytes=16 * MIB),
        name=name,
    )(*in_vmem(*operands))


def partials_kernel(steps, kv_here, gain_ref, frames_ref, fresh_ref, *refs):
    kv_refs, refs = (refs[0:2], both_of(refs[2])), refs[3:]
    length, width = kv_refs[0][1].shape[0], refs[0].shape[1]
    biases = [bias_of(keys_ref, frames_ref[1, :, :1]) for keys_ref, _ in kv_refs]
    for d, handed_ref, out_ref in zip(steps, refs, refs[len(steps) :]):
        g = outer_here() ^ d
        fresh = columns_of(g, fresh_ref, width)[...].astype(jnp.float32)
        x = jnp.where(in_first_section(), fresh, handed_ref[...].astype(jnp.float32))
        queries = queries_of(x, columns_of(place_here() * kv_here + g, gain_ref, width)[...])
        raws = [
            scores(queries, columns_of(g, keys_ref.at[:length], HD)[...], bias)
            for (keys_ref, _), bias in zip(kv_refs, biases)
        ]
        top = functools.reduce(jnp.maximum, [top_of(raw) for raw in raws])
        both = sum(
            weigh(raw, top, columns_of(g, values_ref, HD)[...])
            for raw, (_, values_ref) in zip(raws, kv_refs)
        )
        write_sums(out_ref, both[:, :HD], top, both[:, HD:])


def partials(steps, gain, frames, fresh, own, got, handed):
    length, width = own[1].shape
    tokens, columns = handed[0].shape
    count = columns // HD * tokens
    operands = (gain, frames, fresh, *own, got, *(handed[d] for d in steps))
    return chunk_call(
        partials_kernel, "partials", steps, width // HD, count, PAIR * length, operands
    )


def merge_kernel(*refs):
    *parts, out_ref = refs
    write_chunk(out_ref, *joined(parts, False))


def merge_first_kernel(*refs):
    *parts, share_ref, out_ref = refs
    x = head_rows(share_ref[...].astype(jnp.float32)).astype(jnp.bfloat16)
    write_chunk(out_ref, *joined(parts, False, x))


def merge(kernel, *parts):
    return pl.pallas_call(
        kernel,
        in_specs=[WHOLE] * len(parts),
        out_specs=WHOLE,
        out_shape=jax.ShapeDtypeStruct(parts[0].shape, parts[0].dtype),
        compiler_params=pltpu.CompilerParams(vmem_limit_bytes=8 * MIB),
        name="merge",
    )(*in_vmem(*parts))


def attended(one_ref, two_ref):
    one, two = one_ref[...].astype(jnp.float32), two_ref[...].astype(jnp.float32)
    here = inner_here() == 0
    parts = [jnp.where(here, one, two), jnp.where(here, two, one)]
    value, _, _ = joined([part.astype(jnp.bfloat16) for part in parts], True)
    return value


def columns_from(rows, tokens):
    pieces = [rows[at : at + tokens] for at in range(0, rows.shape[0], tokens)]
    return jnp.concatenate(pieces, axis=1)


def combine_kernel(two_ref, one_ref, out_ref):
    out_ref[...] = columns_from(attended(one_ref, two_ref), out_ref.shape[0]).astype(jnp.bfloat16)


def combine_last_kernel(two_ref, one_ref, fresh_ref, handed_ref, out_ref):
    fresh = columns_of(outer_here(), fresh_ref, out_ref.shape[1])[...].astype(jnp.float32)
    x = jnp.where(in_first_section(), fresh, handed_ref[...].astype(jnp.float32))
    total = head_rows(x) + attended(one_ref, two_ref)
    out_ref[...] = columns_from(total, out_ref.shape[0]).astype(jnp.bfloat16)


def combine(kernel, name, tokens, one, two, *rest):
    width = (one.shape[0] - STAT_ROWS) // tokens * HD
    return pl.pallas_call(
        kernel,
        in_specs=[WHOLE] * (2 + len(rest)),
        out_specs=WHOLE,
        out_shape=jax.ShapeDtypeStruct((tokens, width), jnp.bfloat16),
        compiler_params=pltpu.CompilerParams(vmem_limit_bytes=8 * MIB),
        name=name,
    )(*in_vmem(two, one, *rest))


def assemble_kernel(*refs):
    *pieces, out_ref = refs
    outers, width = len(pieces) // PAIR, pieces[0].shape[1]
    for n, refs in enumerate((pieces[:outers], pieces[outers:])):
        place = (place_here() + n) % PAIR
        for d, ref in zip(reversed(range(outers)), refs):
            columns_of(place * outers + (outer_here() ^ d), out_ref, width)[...] = ref[...]


def assemble(mine, others):
    tokens, width = mine[0].shape
    pieces = [*mine[::-1], *others[::-1]]
    return pl.pallas_call(
        assemble_kernel,
        in_specs=[WHOLE] * len(pieces),
        out_specs=WHOLE,
        out_shape=jax.ShapeDtypeStruct((tokens, len(pieces) * width), jnp.bfloat16),
        compiler_params=pltpu.CompilerParams(vmem_limit_bytes=8 * MIB),
        name="assemble",
    )(*in_vmem(*pieces))


def body(
    activations,
    act_frames,
    fresh_batch,
    fresh_frames,
    norm_gain,
    cached_keys,
    cached_values,
    key_frames,
):
    own_keys, given_keys, batch, gain, share, fresh, frames = load_keys(
        act_frames, fresh_frames[None], key_frames.reshape(-1, HD), activations[0], fresh_batch,
        norm_gain, cached_keys[0],
    )
    own_values, given = halve_values(cached_values[0], given_keys)

    tokens = fresh_batch.shape[0]
    outers = lax.axis_size("ctx") // (INNER * PAIR)
    length = own_values.shape[0]
    theirs = swapped(first(1, length, gain, frames, batch, given))
    mine = first(0, length, gain, frames, batch, own_keys, own_values)
    chunk, *others = in_calls(lambda steps: finish(steps, mine, theirs), outers, 2)
    own, got = (own_keys, own_values), swapped(given)
    chunk = merge(merge_first_kernel, chunk, *from_outer(others, 0), share)
    one, two = swapped(chunk), from_inner(chunk)
    share = combine(combine_kernel, "combine", tokens, one, two)
    handed = from_section_before(share, outers)

    chunk, *others = in_calls(
        lambda steps: partials(steps, gain, frames, fresh, own, got, handed), outers, 1
    )
    chunk = merge(merge_kernel, swapped(chunk), *from_outer(others))
    one, two = swapped(chunk), from_inner(chunk)
    share = combine(combine_last_kernel, "combine_last", tokens, one, two, fresh, handed[0])
    theirs = [swapped(share), *from_outer([share] * len(others))]
    return assemble([share, *(swapped(piece) for piece in theirs[1:])], theirs)[None]


def solution(mesh):
    placed = (
        P("section", None, None),
        P(),
        P(),
        P(),
        P("section", None),
        P("section", "ctx", None),
        P("section", "ctx", None),
        P("ctx"),
    )
    return jax.shard_map(
        body, mesh=mesh, in_specs=placed, out_specs=P("section", None, None), check_vma=False
    )
```

```python
import functools
import math

import jax
import jax.numpy as jnp
from jax import lax
from jax.experimental import pallas as pl
from jax.experimental.pallas import tpu as pltpu
from jax.sharding import PartitionSpec as P

HEADS = 64
HD = 128
PAIR = 2
INNER = 2
BLOCKS = 4
STAT_ROWS = 16
HIDDEN = -(2.0**100)
SCALE = HD**-0.5 * math.log2(math.e)
MIB = 1 << 20

epsilon = 1e-05

WHOLE = pl.BlockSpec(memory_space=pltpu.VMEM)
IN_HBM = pl.BlockSpec(memory_space=pltpu.HBM)


def in_hbm(*arrays):
    return [pltpu.with_memory_space_constraint(a, pltpu.HBM) for a in arrays]


def in_vmem(*arrays):
    return [pltpu.with_memory_space_constraint(a, pltpu.VMEM) for a in arrays]


def place_here():
    return lax.axis_index("ctx") % PAIR


def inner_here():
    return lax.axis_index("ctx") // PAIR % INNER


def outer_here():
    return lax.axis_index("ctx") // (PAIR * INNER)


def in_first_section():
    return lax.axis_index("section") == 0


def swapped(block):
    return lax.ppermute(block, "ctx", [(i, i ^ 1) for i in range(lax.axis_size("ctx"))])


def from_inner(block):
    size = lax.axis_size("ctx")
    return lax.ppermute(block, "ctx", [(i, i ^ PAIR ^ 1) for i in range(size)])


def from_outer(blocks, other_place=1):
    size = lax.axis_size("ctx")
    got = [
        lax.ppermute(
            block, "ctx", [(i, i ^ (INNER * PAIR * d) ^ other_place) for i in range(size)]
        )
        for d, block in reversed(list(enumerate(blocks, 1)))
    ]
    return got[::-1]


def from_section_before(block, steps):
    sections, size = lax.axis_size("section"), lax.axis_size("ctx")
    got = {}
    for d in steps:
        route = [
            (s * size + i, (s + 1) % sections * size + (i ^ (INNER * PAIR * d) ^ 1))
            for s in range(sections)
            for i in range(size)
        ]
        got[d] = lax.ppermute(block, ("section", "ctx"), route)
    return got


def head_rows(block):
    return jnp.concatenate(
        [block[:, at : at + HD] for at in range(0, block.shape[1], HD)], axis=0
    )


def row_of(ref):
    return jnp.concatenate([ref[i : i + 1] for i in range(ref.shape[0])], axis=1)


def columns_of(index, ref, width):
    return ref.at[:, pl.ds(pl.multiple_of(index * width, HD), width)]


def on_diagonal(rows):
    shape = (rows, HD)
    return lax.broadcasted_iota(jnp.int32, shape, 0) == lax.broadcasted_iota(jnp.int32, shape, 1)


def queries_of(x, gain):
    rows = head_rows(x.astype(jnp.float32))
    gain = head_rows(jnp.broadcast_to(gain, x.shape))
    norm = lax.rsqrt(jnp.mean(rows * rows, axis=-1, keepdims=True) + epsilon)
    return (rows * norm * gain).astype(jnp.bfloat16)


def bias_of(keys_ref, frames):
    length = keys_ref.shape[0] - STAT_ROWS
    width = keys_ref.shape[1]
    rows = -(-length // width)
    tail = keys_ref[length:].astype(jnp.float32)
    key_frames = jnp.concatenate([tail[i : i + 1] for i in range(rows)], axis=1)[:, :length]
    return jnp.where(key_frames <= frames, 0.0, HIDDEN)[None]


def scores(queries, key_block, bias):
    count, keys, tokens = queries.shape[0], key_block.shape[0], bias.shape[1]
    raw = lax.dot_general(
        queries, key_block, (((1,), (1,)), ((), ())), preferred_element_type=jnp.float32
    )
    raw = raw.reshape(count // tokens, tokens, keys) * SCALE + bias
    return raw.reshape(count, keys)


def top_of(raw):
    top = jnp.max(raw, axis=-1, keepdims=True)
    return top.astype(jnp.bfloat16).astype(jnp.float32)


def weigh(raw, top, value_block):
    probs = jnp.exp2(raw - top).astype(jnp.bfloat16)
    ones = jnp.ones((value_block.shape[0], HD), jnp.bfloat16)
    return jnp.dot(
        probs, jnp.concatenate([value_block, ones], axis=1), preferred_element_type=jnp.float32
    )


def groups_of(count):
    groups = -(-count // HD)
    held = count // groups
    return [slice(c * held, (c + 1) * held) for c in range(groups)]


def write_chunk(out_ref, weighted, tops, totals):
    count = weighted.shape[0]
    line = lax.broadcasted_iota(jnp.int32, (STAT_ROWS, HD), 0)
    stats = jnp.zeros((STAT_ROWS, HD), jnp.float32)
    for c, (top, total) in enumerate(zip(tops, totals)):
        high = total.astype(jnp.bfloat16).astype(jnp.float32)
        for n, row in enumerate((top, high, total - high)):
            stats = jnp.where(line == 3 * c + n, row, stats)
    out_ref[:count] = weighted.astype(jnp.bfloat16)
    out_ref[count:] = stats.astype(jnp.bfloat16)


def write_sums(out_ref, weighted, top, total):
    groups = groups_of(weighted.shape[0])
    diagonal = on_diagonal(groups[0].stop)

    def rows(column):
        column = jnp.broadcast_to(column, weighted.shape)
        return [
            jnp.sum(jnp.where(diagonal, column[group], 0.0), axis=0, keepdims=True)
            for group in groups
        ]

    write_chunk(out_ref, weighted, rows(top), rows(total))


def joined(parts, normed, x=None):
    count = parts[0].shape[0] - STAT_ROWS
    groups = groups_of(count)
    diagonal = on_diagonal(groups[0].stop)
    stats = [part[count:].astype(jnp.float32) for part in parts]
    values, tops, totals = [], [], []
    for c, group in enumerate(groups):
        points = [s[3 * c : 3 * c + 1] for s in stats]
        top = functools.reduce(jnp.maximum, points)
        factors = [jnp.exp2(point - top) for point in points]
        total = sum(
            f * (s[3 * c + 1 : 3 * c + 2] + s[3 * c + 2 : 3 * c + 3])
            for f, s in zip(factors, stats)
        )
        if normed:
            inverse = 1.0 / total
            factors = [f * inverse for f in factors]
        terms = list(zip(factors, parts)) + ([] if x is None else [(total, x)])
        value = 0.0
        for factor, part in terms:
            weight = jnp.where(diagonal, factor, 0.0)[:, : group.stop - group.start]
            high = weight.astype(jnp.bfloat16)
            low = (weight - high.astype(jnp.float32)).astype(jnp.bfloat16)
            for term in (high, low):
                value = value + jnp.dot(term, part[group], preferred_element_type=jnp.float32)
        values.append(value)
        tops.append(top)
        totals.append(total)
    return jnp.concatenate(values, axis=0), tops, totals


def halve(staged_ref, copies, own_ref, given_ref):
    length, width = staged_ref.shape
    half, step = width // PAIR, length // BLOCKS
    place = place_here()
    for b in range(BLOCKS):
        if copies:
            copies[b].wait()
        rows = pl.ds(b * step, step)
        given_ref[rows] = columns_of(1 - place, staged_ref.at[rows], half)[...]
        own_ref[rows] = columns_of(place, staged_ref.at[rows], half)[...]


def column_of(row):
    shape = (row.shape[1], row.shape[1])
    diagonal = lax.broadcasted_iota(jnp.int32, shape, 0) == lax.broadcasted_iota(jnp.int32, shape, 1)
    return jnp.sum(jnp.where(diagonal, row, 0.0), axis=1, keepdims=True)


def load_keys_kernel(
    act_frames_in, fresh_frames_in, key_frames_in, batch_in, fresh_in, gain_in, keys_in,
    own_ref, given_ref, batch_ref, gain_ref, share_ref, fresh_ref, frames_ref,
    act_frames_ref, fresh_frames_ref, key_frames_ref, staged_ref, sems, small_sems,
):
    place, length, width = place_here(), staged_ref.shape[0], own_ref.shape[1]
    half, share = fresh_ref.shape[1], share_ref.shape[1]
    own_share = place * (half // share) + outer_here()
    small = [
        (act_frames_in, act_frames_ref),
        (fresh_frames_in, fresh_frames_ref),
        (key_frames_in, key_frames_ref),
        (batch_in, batch_ref),
        (gain_in, gain_ref),
        (columns_of(own_share, batch_in, share), share_ref),
        (columns_of(place, fresh_in, half), fresh_ref),
    ]
    small = [pltpu.make_async_copy(a, b, small_sems.at[n]) for n, (a, b) in enumerate(small)]
    copies, step = [], length // BLOCKS
    for b in range(BLOCKS):
        rows = pl.ds(b * step, step)
        copies.append(pltpu.make_async_copy(keys_in.at[rows], staged_ref.at[rows], sems.at[b]))
    for copy in small[:3] + copies + small[3:]:
        copy.start()
    for copy in small[:3]:
        copy.wait()

    tokens = frames_ref.shape[1]
    section = lax.axis_index("section")
    own_row = act_frames_ref[pl.ds(section, 1), :].astype(jnp.float32)
    prior_row = act_frames_ref[pl.ds(jnp.maximum(section - 1, 0), 1), :].astype(jnp.float32)
    fresh_row = fresh_frames_ref[...].astype(jnp.float32)
    next_row = jnp.where(in_first_section(), fresh_row, prior_row)
    for tick, row in enumerate((own_row, next_row)):
        frames_ref[tick] = jnp.broadcast_to(column_of(row), (tokens, HD))

    row = row_of(key_frames_ref).astype(jnp.float32)
    lines = -(-length // width)
    row = jnp.concatenate([row, jnp.zeros((1, lines * width - length), jnp.float32)], axis=1)
    line = lax.broadcasted_iota(jnp.int32, (STAT_ROWS, width), 0)
    tail = jnp.zeros((STAT_ROWS, width), jnp.float32)
    for n in range(lines):
        tail = jnp.where(line == n, row[:, n * width : (n + 1) * width], tail)
    for ref in (own_ref, given_ref):
        ref[length:] = tail.astype(jnp.bfloat16)
    halve(staged_ref, copies, own_ref, given_ref)
    for copy in small[3:]:
        copy.wait()


def load_keys(act_frames, fresh_frames, key_frames, batch, fresh, gain, keys):
    length, width = keys.shape
    tokens, model = batch.shape
    share = model * INNER // lax.axis_size("ctx")
    shape = (length + STAT_ROWS, width // PAIR)
    frames = (act_frames, fresh_frames, key_frames)
    return pl.pallas_call(
        load_keys_kernel,
        in_specs=[IN_HBM] * 7,
        out_specs=[WHOLE] * 7,
        out_shape=[
            pltpu.VMEM(shape, keys.dtype),
            pltpu.VMEM(shape, keys.dtype),
            pltpu.VMEM(batch.shape, batch.dtype),
            pltpu.VMEM(gain.shape, gain.dtype),
            pltpu.VMEM((tokens, share), batch.dtype),
            pltpu.VMEM((tokens, model // PAIR), fresh.dtype),
            pltpu.VMEM((2, tokens, HD), jnp.float32),
        ],
        scratch_shapes=[
            *(pltpu.VMEM(a.shape, a.dtype) for a in frames),
            pltpu.VMEM((length, width), keys.dtype),
            pltpu.SemaphoreType.DMA((BLOCKS,)),
            pltpu.SemaphoreType.DMA((7,)),
        ],
        cost_estimate=pl.CostEstimate(
            flops=0, bytes_accessed=2 * length * width, transcendentals=0
        ),
        compiler_params=pltpu.CompilerParams(vmem_limit_bytes=16 * MIB),
        name="load_keys",
    )(*in_hbm(*frames, batch, fresh, gain, keys))


def halve_values_kernel(values_ref, own_ref, given_ref):
    halve(values_ref, [], own_ref, given_ref)


def halve_values(values):
    length, width = values.shape
    half = pltpu.VMEM((length, width // PAIR), values.dtype)
    return pl.pallas_call(
        halve_values_kernel,
        in_specs=[WHOLE],
        out_specs=[WHOLE] * 2,
        out_shape=[half, half],
        cost_estimate=pl.CostEstimate(
            flops=0, bytes_accessed=2 * length * width, transcendentals=0
        ),
        compiler_params=pltpu.CompilerParams(vmem_limit_bytes=16 * MIB),
        name="halve_values",
    )(*in_vmem(values))


def first_kernel(other, gain_ref, frames_ref, batch_ref, keys_ref, values_ref, out_ref):
    length, kv_here = values_ref.shape[0], out_ref.shape[0]
    width = gain_ref.shape[1] // (PAIR * kv_here)
    place = (place_here() + other) % PAIR
    bias = bias_of(keys_ref, frames_ref[0, :, :1])
    for g in range(kv_here):
        index, block = place * kv_here + g, slice(g * HD, (g + 1) * HD)
        x, gain = columns_of(index, batch_ref, width)[...], columns_of(index, gain_ref, width)[...]
        raw = scores(queries_of(x, gain), keys_ref[:length, block], bias)
        top = top_of(raw)
        both = weigh(raw, top, values_ref[:, block])
        write_sums(out_ref.at[g], both[:, :HD], top, both[:, HD:])


def first(other, gain, frames, batch, keys, values):
    length, width = values.shape
    tokens = batch.shape[0]
    kv_here = width // HD
    queries = HEADS // PAIR * tokens
    return pl.pallas_call(
        functools.partial(first_kernel, other),
        in_specs=[WHOLE] * 5,
        out_specs=WHOLE,
        out_shape=jax.ShapeDtypeStruct((kv_here, queries // kv_here + STAT_ROWS, HD), jnp.bfloat16),
        cost_estimate=pl.CostEstimate(
            flops=2 * queries * length * 3 * HD,
            bytes_accessed=4 * length * width,
            transcendentals=queries * length,
        ),
        compiler_params=pltpu.CompilerParams(vmem_limit_bytes=16 * MIB),
        name="first",
    )(*in_vmem(gain, frames, batch, keys, values))


def finish_kernel(steps, mine_ref, got_ref, *out_refs):
    for d, out_ref in zip(steps, out_refs):
        g = outer_here() ^ d
        write_chunk(out_ref, *joined([mine_ref.at[g], got_ref.at[g]], False))


def finish(steps, mine, got):
    chunk = jax.ShapeDtypeStruct(mine.shape[1:], mine.dtype)
    return pl.pallas_call(
        functools.partial(finish_kernel, steps),
        in_specs=[WHOLE] * 2,
        out_specs=[WHOLE] * len(steps),
        out_shape=[chunk] * len(steps),
        compiler_params=pltpu.CompilerParams(vmem_limit_bytes=8 * MIB),
        name="finish",
    )(*in_vmem(mine, got))


def in_calls(call, outers, together):
    chunks, far = {}, outers - together
    for steps in [tuple(range(far, outers))[::-1]] + [(d,) for d in reversed(range(far))]:
        chunks.update(zip(steps, call(steps)))
    return [chunks[d] for d in range(outers)]


def chunk_call(kernel, name, steps, kv_here, count, length, operands):
    chunk = jax.ShapeDtypeStruct((count + STAT_ROWS, HD), jnp.bfloat16)
    return pl.pallas_call(
        functools.partial(kernel, steps, kv_here),
        in_specs=[WHOLE] * len(operands),
        out_specs=[WHOLE] * len(steps),
        out_shape=[chunk] * len(steps),
        cost_estimate=pl.CostEstimate(
            flops=2 * len(steps) * count * length * 3 * HD,
            bytes_accessed=4 * len(steps) * length * HD,
            transcendentals=len(steps) * count * length,
        ),
        compiler_params=pltpu.CompilerParams(vmem_limit_bytes=16 * MIB),
        name=name,
    )(*in_vmem(*operands))


def partials_kernel(steps, kv_here, gain_ref, frames_ref, fresh_ref, *refs):
    kv_refs, refs = (refs[0:2], refs[2:4]), refs[4:]
    length, width = kv_refs[0][1].shape[0], refs[0].shape[1]
    biases = [bias_of(keys_ref, frames_ref[1, :, :1]) for keys_ref, _ in kv_refs]
    for d, handed_ref, out_ref in zip(steps, refs, refs[len(steps) :]):
        g = outer_here() ^ d
        fresh = columns_of(g, fresh_ref, width)[...].astype(jnp.float32)
        x = jnp.where(in_first_section(), fresh, handed_ref[...].astype(jnp.float32))
        queries = queries_of(x, columns_of(place_here() * kv_here + g, gain_ref, width)[...])
        raws = [
            scores(queries, columns_of(g, keys_ref.at[:length], HD)[...], bias)
            for (keys_ref, _), bias in zip(kv_refs, biases)
        ]
        top = functools.reduce(jnp.maximum, [top_of(raw) for raw in raws])
        both = sum(
            weigh(raw, top, columns_of(g, values_ref, HD)[...])
            for raw, (_, values_ref) in zip(raws, kv_refs)
        )
        write_sums(out_ref, both[:, :HD], top, both[:, HD:])


def partials(steps, gain, frames, fresh, own, got, handed):
    length, width = own[1].shape
    tokens, columns = handed[steps[0]].shape
    count = columns // HD * tokens
    operands = (gain, frames, fresh, *own, *got, *(handed[d] for d in steps))
    return chunk_call(
        partials_kernel, "partials", steps, width // HD, count, PAIR * length, operands
    )


def merge_kernel(*refs):
    *parts, out_ref = refs
    write_chunk(out_ref, *joined(parts, False))


def merge_first_kernel(*refs):
    *parts, share_ref, out_ref = refs
    x = head_rows(share_ref[...].astype(jnp.float32)).astype(jnp.bfloat16)
    write_chunk(out_ref, *joined(parts, False, x))


def merge(kernel, *parts):
    return pl.pallas_call(
        kernel,
        in_specs=[WHOLE] * len(parts),
        out_specs=WHOLE,
        out_shape=jax.ShapeDtypeStruct(parts[0].shape, parts[0].dtype),
        compiler_params=pltpu.CompilerParams(vmem_limit_bytes=8 * MIB),
        name="merge",
    )(*in_vmem(*parts))


def attended(one_ref, two_ref):
    one, two = one_ref[...].astype(jnp.float32), two_ref[...].astype(jnp.float32)
    here = inner_here() == 0
    parts = [jnp.where(here, one, two), jnp.where(here, two, one)]
    value, _, _ = joined([part.astype(jnp.bfloat16) for part in parts], True)
    return value


def columns_from(rows, tokens):
    pieces = [rows[at : at + tokens] for at in range(0, rows.shape[0], tokens)]
    return jnp.concatenate(pieces, axis=1)


def combine_kernel(two_ref, one_ref, out_ref):
    out_ref[...] = columns_from(attended(one_ref, two_ref), out_ref.shape[0]).astype(jnp.bfloat16)


def combine_last_kernel(two_ref, one_ref, fresh_ref, handed_ref, out_ref):
    fresh = columns_of(outer_here(), fresh_ref, out_ref.shape[1])[...].astype(jnp.float32)
    x = jnp.where(in_first_section(), fresh, handed_ref[...].astype(jnp.float32))
    total = head_rows(x) + attended(one_ref, two_ref)
    out_ref[...] = columns_from(total, out_ref.shape[0]).astype(jnp.bfloat16)


def combine(kernel, name, tokens, one, two, *rest):
    width = (one.shape[0] - STAT_ROWS) // tokens * HD
    return pl.pallas_call(
        kernel,
        in_specs=[WHOLE] * (2 + len(rest)),
        out_specs=WHOLE,
        out_shape=jax.ShapeDtypeStruct((tokens, width), jnp.bfloat16),
        compiler_params=pltpu.CompilerParams(vmem_limit_bytes=8 * MIB),
        name=name,
    )(*in_vmem(two, one, *rest))


def assemble_kernel(*refs):
    *pieces, out_ref = refs
    outers, width = len(pieces) // PAIR, pieces[0].shape[1]
    for n, refs in enumerate((pieces[:outers], pieces[outers:])):
        place = (place_here() + n) % PAIR
        for d, ref in zip(reversed(range(outers)), refs):
            columns_of(place * outers + (outer_here() ^ d), out_ref, width)[...] = ref[...]


def assemble(mine, others):
    tokens, width = mine[0].shape
    pieces = [*mine[::-1], *others[::-1]]
    return pl.pallas_call(
        assemble_kernel,
        in_specs=[WHOLE] * len(pieces),
        out_specs=WHOLE,
        out_shape=jax.ShapeDtypeStruct((tokens, len(pieces) * width), jnp.bfloat16),
        compiler_params=pltpu.CompilerParams(vmem_limit_bytes=8 * MIB),
        name="assemble",
    )(*in_vmem(*pieces))


def body(
    activations,
    act_frames,
    fresh_batch,
    fresh_frames,
    norm_gain,
    cached_keys,
    cached_values,
    key_frames,
):
    own_keys, given_keys, batch, gain, share, fresh, frames = load_keys(
        act_frames, fresh_frames[None], key_frames.reshape(-1, HD), activations[0], fresh_batch,
        norm_gain, cached_keys[0],
    )
    own_values, given_values = halve_values(cached_values[0])

    tokens = fresh_batch.shape[0]
    outers = lax.axis_size("ctx") // (INNER * PAIR)
    theirs = swapped(first(1, gain, frames, batch, given_keys, given_values))
    mine = first(0, gain, frames, batch, own_keys, own_values)
    chunk, *others = in_calls(lambda steps: finish(steps, mine, theirs), outers, outers - 1)
    own, got = (own_keys, own_values), (swapped(given_keys), swapped(given_values))
    chunk = merge(merge_first_kernel, *from_outer(others, 0)[::-1], chunk, share)
    one, two = swapped(chunk), from_inner(chunk)
    share = combine(combine_kernel, "combine", tokens, one, two)

    handed = from_section_before(share, range(outers - 1, 0, -1))

    def work(d):
        return partials((d,), gain, frames, fresh, own, got, handed)[0]

    far = work(outers - 1)
    share, _ = lax.optimization_barrier((share, far))
    handed.update(from_section_before(share, [0]))
    others = [work(d) for d in range(outers - 2, 0, -1)][::-1] + [far]
    chunk = work(0)
    chunk = merge(merge_kernel, swapped(chunk), *from_outer(others))
    one, two = swapped(chunk), from_inner(chunk)
    share = combine(combine_last_kernel, "combine_last", tokens, one, two, fresh, handed[0])
    theirs = [swapped(share), *from_outer([share] * len(others))]
    return assemble([share, *(swapped(piece) for piece in theirs[1:])], theirs)[None]


def solution(mesh):
    placed = (
        P("section", None, None),
        P(),
        P(),
        P(),
        P("section", None),
        P("section", "ctx", None),
        P("section", "ctx", None),
        P("ctx"),
    )
    return jax.shard_map(
        body, mesh=mesh, in_specs=placed, out_specs=P("section", None, None), check_vma=False
    )
```

```python
import functools
import math

import jax
import jax.numpy as jnp
from jax import lax
from jax.experimental import pallas as pl
from jax.experimental.pallas import tpu as pltpu
from jax.sharding import PartitionSpec as P

HEADS = 64
HD = 128
PAIR = 2
INNER = 2
BLOCKS = 4
STAT_ROWS = 16
HIDDEN = -(2.0**100)
SCALE = HD**-0.5 * math.log2(math.e)
MIB = 1 << 20

epsilon = 1e-05

WHOLE = pl.BlockSpec(memory_space=pltpu.VMEM)
IN_HBM = pl.BlockSpec(memory_space=pltpu.HBM)


def in_hbm(*arrays):
    return [pltpu.with_memory_space_constraint(a, pltpu.HBM) for a in arrays]


def in_vmem(*arrays):
    return [pltpu.with_memory_space_constraint(a, pltpu.VMEM) for a in arrays]


def place_here():
    return lax.axis_index("ctx") % PAIR


def inner_here():
    return lax.axis_index("ctx") // PAIR % INNER


def outer_here():
    return lax.axis_index("ctx") // (PAIR * INNER)


def in_first_section():
    return lax.axis_index("section") == 0


def swapped(block):
    return lax.ppermute(block, "ctx", [(i, i ^ 1) for i in range(lax.axis_size("ctx"))])


def from_inner(block):
    size = lax.axis_size("ctx")
    return lax.ppermute(block, "ctx", [(i, i ^ PAIR ^ 1) for i in range(size)])


def from_outer(blocks, other_place=1):
    size = lax.axis_size("ctx")
    got = [
        lax.ppermute(
            block, "ctx", [(i, i ^ (INNER * PAIR * d) ^ other_place) for i in range(size)]
        )
        for d, block in reversed(list(enumerate(blocks, 1)))
    ]
    return got[::-1]


def from_section_before(block, step):
    sections, size = lax.axis_size("section"), lax.axis_size("ctx")
    route = [
        (s * size + i, (s + 1) % sections * size + (i ^ (PAIR * step) ^ 1))
        for s in range(sections)
        for i in range(size)
    ]
    return lax.ppermute(block, ("section", "ctx"), route)


def head_rows(block):
    return jnp.concatenate(
        [block[:, at : at + HD] for at in range(0, block.shape[1], HD)], axis=0
    )


def row_of(ref):
    return jnp.concatenate([ref[i : i + 1] for i in range(ref.shape[0])], axis=1)


def columns_of(index, ref, width):
    return ref.at[:, pl.ds(pl.multiple_of(index * width, HD), width)]


def on_diagonal(rows):
    shape = (rows, HD)
    return lax.broadcasted_iota(jnp.int32, shape, 0) == lax.broadcasted_iota(jnp.int32, shape, 1)


def queries_of(x, gain):
    rows = head_rows(x.astype(jnp.float32))
    gain = head_rows(jnp.broadcast_to(gain, x.shape))
    norm = lax.rsqrt(jnp.mean(rows * rows, axis=-1, keepdims=True) + epsilon)
    return (rows * norm * gain).astype(jnp.bfloat16)


def bias_of(keys_ref, frames):
    length = keys_ref.shape[0] - STAT_ROWS
    width = keys_ref.shape[1]
    rows = -(-length // width)
    tail = keys_ref[length:].astype(jnp.float32)
    key_frames = jnp.concatenate([tail[i : i + 1] for i in range(rows)], axis=1)[:, :length]
    return jnp.where(key_frames <= frames, 0.0, HIDDEN)[None]


def scores(queries, key_block, bias):
    count, keys, tokens = queries.shape[0], key_block.shape[0], bias.shape[1]
    raw = lax.dot_general(
        queries, key_block, (((1,), (1,)), ((), ())), preferred_element_type=jnp.float32
    )
    raw = raw.reshape(count // tokens, tokens, keys) * SCALE + bias
    return raw.reshape(count, keys)


def top_of(raw):
    top = jnp.max(raw, axis=-1, keepdims=True)
    return top.astype(jnp.bfloat16).astype(jnp.float32)


def weigh(raw, top, value_block):
    probs = jnp.exp2(raw - top).astype(jnp.bfloat16)
    ones = jnp.ones((value_block.shape[0], HD), jnp.bfloat16)
    return jnp.dot(
        probs, jnp.concatenate([value_block, ones], axis=1), preferred_element_type=jnp.float32
    )


def groups_of(count):
    groups = -(-count // HD)
    held = count // groups
    return [slice(c * held, (c + 1) * held) for c in range(groups)]


def write_chunk(out_ref, weighted, tops, totals):
    count = weighted.shape[0]
    line = lax.broadcasted_iota(jnp.int32, (STAT_ROWS, HD), 0)
    stats = jnp.zeros((STAT_ROWS, HD), jnp.float32)
    for c, (top, total) in enumerate(zip(tops, totals)):
        high = total.astype(jnp.bfloat16).astype(jnp.float32)
        for n, row in enumerate((top, high, total - high)):
            stats = jnp.where(line == 3 * c + n, row, stats)
    out_ref[:count] = weighted.astype(jnp.bfloat16)
    out_ref[count:] = stats.astype(jnp.bfloat16)


def write_sums(out_ref, weighted, top, total):
    groups = groups_of(weighted.shape[0])
    diagonal = on_diagonal(groups[0].stop)

    def rows(column):
        column = jnp.broadcast_to(column, weighted.shape)
        return [
            jnp.sum(jnp.where(diagonal, column[group], 0.0), axis=0, keepdims=True)
            for group in groups
        ]

    write_chunk(out_ref, weighted, rows(top), rows(total))


def joined(parts, normed, x=None):
    count = parts[0].shape[0] - STAT_ROWS
    groups = groups_of(count)
    diagonal = on_diagonal(groups[0].stop)
    stats = [part[count:].astype(jnp.float32) for part in parts]
    values, tops, totals = [], [], []
    for c, group in enumerate(groups):
        points = [s[3 * c : 3 * c + 1] for s in stats]
        top = functools.reduce(jnp.maximum, points)
        factors = [jnp.exp2(point - top) for point in points]
        total = sum(
            f * (s[3 * c + 1 : 3 * c + 2] + s[3 * c + 2 : 3 * c + 3])
            for f, s in zip(factors, stats)
        )
        if normed:
            inverse = 1.0 / total
            factors = [f * inverse for f in factors]
        terms = list(zip(factors, parts)) + ([] if x is None else [(total, x)])
        value = 0.0
        for factor, part in terms:
            weight = jnp.where(diagonal, factor, 0.0)[:, : group.stop - group.start]
            high = weight.astype(jnp.bfloat16)
            low = (weight - high.astype(jnp.float32)).astype(jnp.bfloat16)
            for term in (high, low):
                value = value + jnp.dot(term, part[group], preferred_element_type=jnp.float32)
        values.append(value)
        tops.append(top)
        totals.append(total)
    return jnp.concatenate(values, axis=0), tops, totals


def halve(staged_ref, copies, own_ref, given_ref):
    length, width = staged_ref.shape
    half, step = width // PAIR, length // BLOCKS
    place = place_here()
    for b in range(BLOCKS):
        if copies:
            copies[b].wait()
        rows = pl.ds(b * step, step)
        given_ref[rows] = columns_of(1 - place, staged_ref.at[rows], half)[...]
        own_ref[rows] = columns_of(place, staged_ref.at[rows], half)[...]


def column_of(row):
    shape = (row.shape[1], row.shape[1])
    diagonal = lax.broadcasted_iota(jnp.int32, shape, 0) == lax.broadcasted_iota(jnp.int32, shape, 1)
    return jnp.sum(jnp.where(diagonal, row, 0.0), axis=1, keepdims=True)


def load_keys_kernel(
    act_frames_in, fresh_frames_in, key_frames_in, batch_in, fresh_in, gain_in, keys_in,
    own_ref, given_ref, batch_ref, gain_ref, share_ref, fresh_ref, fresh_gain_ref, frames_ref,
    act_frames_ref, fresh_frames_ref, key_frames_ref, staged_ref, sems, small_sems,
):
    place, length, width = place_here(), staged_ref.shape[0], own_ref.shape[1]
    share = fresh_ref.shape[1]
    outers = gain_ref.shape[1] // PAIR // share
    own_share = place * outers + outer_here()
    index = (1 - place) * outers + outer_here()
    small = [
        (act_frames_in, act_frames_ref),
        (fresh_frames_in, fresh_frames_ref),
        (key_frames_in, key_frames_ref),
        (batch_in, batch_ref),
        (gain_in, gain_ref),
        (columns_of(own_share, batch_in, share), share_ref),
        (columns_of(index, fresh_in, share), fresh_ref),
        (columns_of(index, gain_in, share), fresh_gain_ref),
    ]
    small = [pltpu.make_async_copy(a, b, small_sems.at[n]) for n, (a, b) in enumerate(small)]
    copies, step = [], length // BLOCKS
    for b in range(BLOCKS):
        rows = pl.ds(b * step, step)
        copies.append(pltpu.make_async_copy(keys_in.at[rows], staged_ref.at[rows], sems.at[b]))
    for copy in small[:3] + copies + small[3:]:
        copy.start()
    for copy in small[:3]:
        copy.wait()

    tokens = frames_ref.shape[1]
    section = lax.axis_index("section")
    own_row = act_frames_ref[pl.ds(section, 1), :].astype(jnp.float32)
    prior_row = act_frames_ref[pl.ds(jnp.maximum(section - 1, 0), 1), :].astype(jnp.float32)
    fresh_row = fresh_frames_ref[...].astype(jnp.float32)
    next_row = jnp.where(in_first_section(), fresh_row, prior_row)
    for tick, row in enumerate((own_row, next_row)):
        frames_ref[tick] = jnp.broadcast_to(column_of(row), (tokens, HD))

    row = row_of(key_frames_ref).astype(jnp.float32)
    lines = -(-length // width)
    row = jnp.concatenate([row, jnp.zeros((1, lines * width - length), jnp.float32)], axis=1)
    line = lax.broadcasted_iota(jnp.int32, (STAT_ROWS, width), 0)
    tail = jnp.zeros((STAT_ROWS, width), jnp.float32)
    for n in range(lines):
        tail = jnp.where(line == n, row[:, n * width : (n + 1) * width], tail)
    for ref in (own_ref, given_ref):
        ref[length:] = tail.astype(jnp.bfloat16)
    halve(staged_ref, copies, own_ref, given_ref)
    for copy in small[3:]:
        copy.wait()


def load_keys(act_frames, fresh_frames, key_frames, batch, fresh, gain, keys):
    length, width = keys.shape
    tokens, model = batch.shape
    share = model * INNER // lax.axis_size("ctx")
    shape = (length + STAT_ROWS, width // PAIR)
    frames = (act_frames, fresh_frames, key_frames)
    return pl.pallas_call(
        load_keys_kernel,
        in_specs=[IN_HBM] * 7,
        out_specs=[WHOLE] * 8,
        out_shape=[
            pltpu.VMEM(shape, keys.dtype),
            pltpu.VMEM(shape, keys.dtype),
            pltpu.VMEM(batch.shape, batch.dtype),
            pltpu.VMEM(gain.shape, gain.dtype),
            pltpu.VMEM((tokens, share), batch.dtype),
            pltpu.VMEM((tokens, share), fresh.dtype),
            pltpu.VMEM((1, share), gain.dtype),
            pltpu.VMEM((2, tokens, HD), jnp.float32),
        ],
        scratch_shapes=[
            *(pltpu.VMEM(a.shape, a.dtype) for a in frames),
            pltpu.VMEM((length, width), keys.dtype),
            pltpu.SemaphoreType.DMA((BLOCKS,)),
            pltpu.SemaphoreType.DMA((8,)),
        ],
        cost_estimate=pl.CostEstimate(
            flops=0, bytes_accessed=2 * length * width, transcendentals=0
        ),
        compiler_params=pltpu.CompilerParams(vmem_limit_bytes=16 * MIB),
        name="load_keys",
    )(*in_hbm(*frames, batch, fresh, gain, keys))


def halve_values_kernel(values_ref, own_ref, given_ref):
    halve(values_ref, [], own_ref, given_ref)


def halve_values(values):
    length, width = values.shape
    half = pltpu.VMEM((length, width // PAIR), values.dtype)
    return pl.pallas_call(
        halve_values_kernel,
        in_specs=[WHOLE],
        out_specs=[WHOLE] * 2,
        out_shape=[half, half],
        cost_estimate=pl.CostEstimate(
            flops=0, bytes_accessed=2 * length * width, transcendentals=0
        ),
        compiler_params=pltpu.CompilerParams(vmem_limit_bytes=16 * MIB),
        name="halve_values",
    )(*in_vmem(values))


def first_kernel(other, gain_ref, frames_ref, batch_ref, keys_ref, values_ref, out_ref):
    length, kv_here = values_ref.shape[0], out_ref.shape[0]
    width = gain_ref.shape[1] // (PAIR * kv_here)
    place = (place_here() + other) % PAIR
    bias = bias_of(keys_ref, frames_ref[0, :, :1])
    for g in range(kv_here):
        index, block = place * kv_here + g, slice(g * HD, (g + 1) * HD)
        x, gain = columns_of(index, batch_ref, width)[...], columns_of(index, gain_ref, width)[...]
        raw = scores(queries_of(x, gain), keys_ref[:length, block], bias)
        top = top_of(raw)
        both = weigh(raw, top, values_ref[:, block])
        write_sums(out_ref.at[g], both[:, :HD], top, both[:, HD:])


def first(other, gain, frames, batch, keys, values):
    length, width = values.shape
    tokens = batch.shape[0]
    kv_here = width // HD
    queries = HEADS // PAIR * tokens
    return pl.pallas_call(
        functools.partial(first_kernel, other),
        in_specs=[WHOLE] * 5,
        out_specs=WHOLE,
        out_shape=jax.ShapeDtypeStruct((kv_here, queries // kv_here + STAT_ROWS, HD), jnp.bfloat16),
        cost_estimate=pl.CostEstimate(
            flops=2 * queries * length * 3 * HD,
            bytes_accessed=4 * length * width,
            transcendentals=queries * length,
        ),
        compiler_params=pltpu.CompilerParams(vmem_limit_bytes=16 * MIB),
        name="first",
    )(*in_vmem(gain, frames, batch, keys, values))


def finish_kernel(steps, mine_ref, got_ref, *out_refs):
    for d, out_ref in zip(steps, out_refs):
        g = outer_here() ^ d
        write_chunk(out_ref, *joined([mine_ref.at[g], got_ref.at[g]], False))


def finish(steps, mine, got):
    chunk = jax.ShapeDtypeStruct(mine.shape[1:], mine.dtype)
    return pl.pallas_call(
        functools.partial(finish_kernel, steps),
        in_specs=[WHOLE] * 2,
        out_specs=[WHOLE] * len(steps),
        out_shape=[chunk] * len(steps),
        compiler_params=pltpu.CompilerParams(vmem_limit_bytes=8 * MIB),
        name="finish",
    )(*in_vmem(mine, got))


def in_calls(call, outers, together):
    chunks, far = {}, outers - together
    for steps in [tuple(range(far, outers))[::-1]] + [(d,) for d in reversed(range(far))]:
        chunks.update(zip(steps, call(steps)))
    return [chunks[d] for d in range(outers)]


def chunk_call(kernel, name, steps, kv_here, count, length, operands):
    chunk = jax.ShapeDtypeStruct((count + STAT_ROWS, HD), jnp.bfloat16)
    return pl.pallas_call(
        functools.partial(kernel, steps, kv_here),
        in_specs=[WHOLE] * len(operands),
        out_specs=[WHOLE] * len(steps),
        out_shape=[chunk] * len(steps),
        cost_estimate=pl.CostEstimate(
            flops=2 * len(steps) * count * length * 3 * HD,
            bytes_accessed=4 * len(steps) * length * HD,
            transcendentals=len(steps) * count * length,
        ),
        compiler_params=pltpu.CompilerParams(vmem_limit_bytes=16 * MIB),
        name=name,
    )(*in_vmem(*operands))


def partials_kernel(steps, kv_here, frames_ref, *refs):
    kv_refs, refs = (refs[0:2], refs[2:4]), refs[4:]
    length = kv_refs[0][1].shape[0]
    biases = [bias_of(keys_ref, frames_ref[1, :, :1]) for keys_ref, _ in kv_refs]
    for d, queries_ref, out_ref in zip(steps, refs, refs[len(steps) :]):
        g = outer_here() ^ d
        raws = [
            scores(queries_ref[...], columns_of(g, keys_ref.at[:length], HD)[...], bias)
            for (keys_ref, _), bias in zip(kv_refs, biases)
        ]
        top = functools.reduce(jnp.maximum, [top_of(raw) for raw in raws])
        both = sum(
            weigh(raw, top, columns_of(g, values_ref, HD)[...])
            for raw, (_, values_ref) in zip(raws, kv_refs)
        )
        write_sums(out_ref, both[:, :HD], top, both[:, HD:])


def partials(steps, frames, own, got, queries):
    length, width = own[1].shape
    count = queries[0].shape[0]
    operands = (frames, *own, *got, *(queries[d] for d in steps))
    return chunk_call(
        partials_kernel, "partials", steps, width // HD, count, PAIR * length, operands
    )


def merge_kernel(*refs):
    *parts, out_ref = refs
    write_chunk(out_ref, *joined(parts, False))


def merge_first_kernel(*refs):
    *parts, share_ref, out_ref = refs
    x = head_rows(share_ref[...].astype(jnp.float32)).astype(jnp.bfloat16)
    write_chunk(out_ref, *joined(parts, False, x))


def merge(kernel, *parts):
    return pl.pallas_call(
        kernel,
        in_specs=[WHOLE] * len(parts),
        out_specs=WHOLE,
        out_shape=jax.ShapeDtypeStruct(parts[0].shape, parts[0].dtype),
        compiler_params=pltpu.CompilerParams(vmem_limit_bytes=8 * MIB),
        name="merge",
    )(*in_vmem(*parts))


def attended(one_ref, two_ref):
    one, two = one_ref[...].astype(jnp.float32), two_ref[...].astype(jnp.float32)
    here = inner_here() == 0
    parts = [jnp.where(here, one, two), jnp.where(here, two, one)]
    value, _, _ = joined([part.astype(jnp.bfloat16) for part in parts], True)
    return value


def columns_from(rows, tokens):
    pieces = [rows[at : at + tokens] for at in range(0, rows.shape[0], tokens)]
    return jnp.concatenate(pieces, axis=1)


def combine_kernel(gain_ref, fresh_ref, one_ref, two_ref, share_ref, queries_ref):
    tokens = fresh_ref.shape[0]
    handed = columns_from(attended(one_ref, two_ref), tokens).astype(jnp.bfloat16)
    fresh = fresh_ref[...].astype(jnp.float32)
    share = jnp.where(in_first_section(), fresh, handed.astype(jnp.float32))
    share = share.astype(jnp.bfloat16)
    share_ref[...] = share
    queries_ref[...] = queries_of(share, gain_ref[...])


def combine(gain, fresh, one, two):
    count = one.shape[0] - STAT_ROWS
    return pl.pallas_call(
        combine_kernel,
        in_specs=[WHOLE] * 4,
        out_specs=[WHOLE] * 2,
        out_shape=[
            jax.ShapeDtypeStruct(fresh.shape, fresh.dtype),
            jax.ShapeDtypeStruct((count, HD), jnp.bfloat16),
        ],
        compiler_params=pltpu.CompilerParams(vmem_limit_bytes=8 * MIB),
        name="combine",
    )(*in_vmem(gain, fresh, one, two))


def combine_last_kernel(two_ref, one_ref, share_ref, out_ref):
    tokens = out_ref.shape[0]
    total = head_rows(share_ref[...].astype(jnp.float32)) + attended(one_ref, two_ref)
    out_ref[...] = columns_from(total, tokens).astype(jnp.bfloat16)


def combine_last(share, one, two):
    return pl.pallas_call(
        combine_last_kernel,
        in_specs=[WHOLE] * 3,
        out_specs=WHOLE,
        out_shape=jax.ShapeDtypeStruct(share.shape, share.dtype),
        compiler_params=pltpu.CompilerParams(vmem_limit_bytes=8 * MIB),
        name="combine_last",
    )(*in_vmem(two, one, share))


def assemble_kernel(*refs):
    *pieces, out_ref = refs
    outers, width = len(pieces) // PAIR, pieces[0].shape[1]
    for n, refs in enumerate((pieces[:outers], pieces[outers:])):
        place = (place_here() + n) % PAIR
        for d, ref in zip(reversed(range(outers)), refs):
            columns_of(place * outers + (outer_here() ^ d), out_ref, width)[...] = ref[...]


def assemble(mine, others):
    tokens, width = mine[0].shape
    pieces = [*mine[::-1], *others[::-1]]
    return pl.pallas_call(
        assemble_kernel,
        in_specs=[WHOLE] * len(pieces),
        out_specs=WHOLE,
        out_shape=jax.ShapeDtypeStruct((tokens, len(pieces) * width), jnp.bfloat16),
        compiler_params=pltpu.CompilerParams(vmem_limit_bytes=8 * MIB),
        name="assemble",
    )(*in_vmem(*pieces))


def body(
    activations,
    act_frames,
    fresh_batch,
    fresh_frames,
    norm_gain,
    cached_keys,
    cached_values,
    key_frames,
):
    own_keys, given_keys, batch, gain, share, fresh, fresh_gain, frames = load_keys(
        act_frames, fresh_frames[None], key_frames.reshape(-1, HD), activations[0], fresh_batch,
        norm_gain, cached_keys[0],
    )
    own_values, given_values = halve_values(cached_values[0])

    outers = lax.axis_size("ctx") // (INNER * PAIR)
    theirs = swapped(first(1, gain, frames, batch, given_keys, given_values))
    mine = first(0, gain, frames, batch, own_keys, own_values)
    chunk, *others = in_calls(lambda steps: finish(steps, mine, theirs), outers, 2)
    own, got = (own_keys, own_values), (swapped(given_keys), swapped(given_values))
    chunk = merge(merge_first_kernel, *from_outer(others, 0)[::-1], chunk, share)
    one, two = [from_section_before(chunk, step) for step in range(INNER)]
    share, queries = combine(fresh_gain, fresh, one, two)
    queries = [swapped(queries), *from_outer([queries] * len(others))]

    chunk, *others = in_calls(lambda steps: partials(steps, frames, own, got, queries), outers, 1)
    chunk = merge(merge_kernel, swapped(chunk), *from_outer(others))
    one, two = swapped(chunk), from_inner(chunk)
    share = combine_last(swapped(share), one, two)
    theirs = [swapped(share), *from_outer([share] * len(others))]
    return assemble([share, *(swapped(piece) for piece in theirs[1:])], theirs)[None]


def solution(mesh):
    placed = (
        P("section", None, None),
        P(),
        P(),
        P(),
        P("section", None),
        P("section", "ctx", None),
        P("section", "ctx", None),
        P("ctx"),
    )
    return jax.shard_map(
        body, mesh=mesh, in_specs=placed, out_specs=P("section", None, None), check_vma=False
    )
```

```python
import functools
import math

import jax
import jax.numpy as jnp
from jax import lax
from jax.experimental import pallas as pl
from jax.experimental.pallas import tpu as pltpu
from jax.sharding import PartitionSpec as P

HEADS = 64
HD = 128
PAIR = 2
INNER = 2
BLOCKS = 4
STAT_ROWS = 16
HIDDEN = -(2.0**100)
SCALE = HD**-0.5 * math.log2(math.e)
MIB = 1 << 20

epsilon = 1e-05

WHOLE = pl.BlockSpec(memory_space=pltpu.VMEM)
IN_HBM = pl.BlockSpec(memory_space=pltpu.HBM)


def in_hbm(*arrays):
    return [pltpu.with_memory_space_constraint(a, pltpu.HBM) for a in arrays]


def in_vmem(*arrays):
    return [pltpu.with_memory_space_constraint(a, pltpu.VMEM) for a in arrays]


def place_here():
    return lax.axis_index("ctx") % PAIR


def inner_here():
    return lax.axis_index("ctx") // PAIR % INNER


def outer_here():
    return lax.axis_index("ctx") // (PAIR * INNER)


def in_first_section():
    return lax.axis_index("section") == 0


def swapped(block):
    return lax.ppermute(block, "ctx", [(i, i ^ 1) for i in range(lax.axis_size("ctx"))])


def from_inner(block):
    size = lax.axis_size("ctx")
    return lax.ppermute(block, "ctx", [(i, i ^ PAIR ^ 1) for i in range(size)])


def from_outer(blocks, other_place=1):
    size = lax.axis_size("ctx")
    got = [
        lax.ppermute(
            block, "ctx", [(i, i ^ (INNER * PAIR * d) ^ other_place) for i in range(size)]
        )
        for d, block in reversed(list(enumerate(blocks, 1)))
    ]
    return got[::-1]


def from_section_before(block, step):
    sections, size = lax.axis_size("section"), lax.axis_size("ctx")
    route = [
        (s * size + i, (s + 1) % sections * size + (i ^ (PAIR * step) ^ 1))
        for s in range(sections)
        for i in range(size)
    ]
    return lax.ppermute(block, ("section", "ctx"), route)


def head_rows(block):
    return jnp.concatenate(
        [block[:, at : at + HD] for at in range(0, block.shape[1], HD)], axis=0
    )


def row_of(ref):
    return jnp.concatenate([ref[i : i + 1] for i in range(ref.shape[0])], axis=1)


def columns_of(index, ref, width):
    return ref.at[:, pl.ds(pl.multiple_of(index * width, HD), width)]


def on_diagonal(rows):
    shape = (rows, HD)
    return lax.broadcasted_iota(jnp.int32, shape, 0) == lax.broadcasted_iota(jnp.int32, shape, 1)


def queries_of(x, gain):
    rows = head_rows(x.astype(jnp.float32))
    gain = head_rows(jnp.broadcast_to(gain, x.shape))
    norm = lax.rsqrt(jnp.mean(rows * rows, axis=-1, keepdims=True) + epsilon)
    return (rows * norm * gain).astype(jnp.bfloat16)


def bias_of(keys_ref, frames):
    length = keys_ref.shape[0] - STAT_ROWS
    width = keys_ref.shape[1]
    rows = -(-length // width)
    tail = keys_ref[length:].astype(jnp.float32)
    key_frames = jnp.concatenate([tail[i : i + 1] for i in range(rows)], axis=1)[:, :length]
    return jnp.where(key_frames <= frames, 0.0, HIDDEN)[None]


def scores(queries, key_block, bias):
    count, keys, tokens = queries.shape[0], key_block.shape[0], bias.shape[1]
    raw = lax.dot_general(
        queries, key_block, (((1,), (1,)), ((), ())), preferred_element_type=jnp.float32
    )
    raw = raw.reshape(count // tokens, tokens, keys) * SCALE + bias
    return raw.reshape(count, keys)


def top_of(raw):
    top = jnp.max(raw, axis=-1, keepdims=True)
    return top.astype(jnp.bfloat16).astype(jnp.float32)


def weigh(raw, top, value_block):
    probs = jnp.exp2(raw - top).astype(jnp.bfloat16)
    ones = jnp.ones((value_block.shape[0], HD), jnp.bfloat16)
    return jnp.dot(
        probs, jnp.concatenate([value_block, ones], axis=1), preferred_element_type=jnp.float32
    )


def groups_of(count):
    groups = -(-count // HD)
    held = count // groups
    return [slice(c * held, (c + 1) * held) for c in range(groups)]


def write_chunk(out_ref, weighted, tops, totals):
    count = weighted.shape[0]
    line = lax.broadcasted_iota(jnp.int32, (STAT_ROWS, HD), 0)
    stats = jnp.zeros((STAT_ROWS, HD), jnp.float32)
    for c, (top, total) in enumerate(zip(tops, totals)):
        high = total.astype(jnp.bfloat16).astype(jnp.float32)
        for n, row in enumerate((top, high, total - high)):
            stats = jnp.where(line == 3 * c + n, row, stats)
    out_ref[:count] = weighted.astype(jnp.bfloat16)
    out_ref[count:] = stats.astype(jnp.bfloat16)


def write_sums(out_ref, weighted, top, total):
    groups = groups_of(weighted.shape[0])
    diagonal = on_diagonal(groups[0].stop)

    def rows(column):
        column = jnp.broadcast_to(column, weighted.shape)
        return [
            jnp.sum(jnp.where(diagonal, column[group], 0.0), axis=0, keepdims=True)
            for group in groups
        ]

    write_chunk(out_ref, weighted, rows(top), rows(total))


def joined(parts, normed, x=None):
    count = parts[0].shape[0] - STAT_ROWS
    groups = groups_of(count)
    diagonal = on_diagonal(groups[0].stop)
    stats = [part[count:].astype(jnp.float32) for part in parts]
    values, tops, totals = [], [], []
    for c, group in enumerate(groups):
        points = [s[3 * c : 3 * c + 1] for s in stats]
        top = functools.reduce(jnp.maximum, points)
        factors = [jnp.exp2(point - top) for point in points]
        total = sum(
            f * (s[3 * c + 1 : 3 * c + 2] + s[3 * c + 2 : 3 * c + 3])
            for f, s in zip(factors, stats)
        )
        if normed:
            inverse = 1.0 / total
            factors = [f * inverse for f in factors]
        terms = list(zip(factors, parts)) + ([] if x is None else [(total, x)])
        value = 0.0
        for factor, part in terms:
            weight = jnp.where(diagonal, factor, 0.0)[:, : group.stop - group.start]
            high = weight.astype(jnp.bfloat16)
            low = (weight - high.astype(jnp.float32)).astype(jnp.bfloat16)
            for term in (high, low):
                value = value + jnp.dot(term, part[group], preferred_element_type=jnp.float32)
        values.append(value)
        tops.append(top)
        totals.append(total)
    return jnp.concatenate(values, axis=0), tops, totals


def halve(staged_ref, copies, own_ref, given_ref):
    length, width = staged_ref.shape
    half, step = width // PAIR, length // BLOCKS
    place = place_here()
    for b in range(BLOCKS):
        if copies:
            copies[b].wait()
        rows = pl.ds(b * step, step)
        given_ref[rows] = columns_of(1 - place, staged_ref.at[rows], half)[...]
        own_ref[rows] = columns_of(place, staged_ref.at[rows], half)[...]


def column_of(row):
    shape = (row.shape[1], row.shape[1])
    diagonal = lax.broadcasted_iota(jnp.int32, shape, 0) == lax.broadcasted_iota(jnp.int32, shape, 1)
    return jnp.sum(jnp.where(diagonal, row, 0.0), axis=1, keepdims=True)


def load_keys_kernel(
    act_frames_in, fresh_frames_in, key_frames_in, batch_in, fresh_in, gain_in, keys_in,
    own_ref, given_ref, batch_ref, gain_ref, share_ref, fresh_ref, fresh_gain_ref, frames_ref,
    act_frames_ref, fresh_frames_ref, key_frames_ref, staged_ref, sems, small_sems,
):
    place, length, width = place_here(), staged_ref.shape[0], own_ref.shape[1]
    share = fresh_ref.shape[1]
    outers = gain_ref.shape[1] // PAIR // share
    own_share = place * outers + outer_here()
    index = (1 - place) * outers + outer_here()
    small = [
        (act_frames_in, act_frames_ref),
        (fresh_frames_in, fresh_frames_ref),
        (key_frames_in, key_frames_ref),
        (batch_in, batch_ref),
        (gain_in, gain_ref),
        (columns_of(own_share, batch_in, share), share_ref),
        (columns_of(index, fresh_in, share), fresh_ref),
        (columns_of(index, gain_in, share), fresh_gain_ref),
    ]
    small = [pltpu.make_async_copy(a, b, small_sems.at[n]) for n, (a, b) in enumerate(small)]
    copies, step = [], length // BLOCKS
    for b in range(BLOCKS):
        rows = pl.ds(b * step, step)
        copies.append(pltpu.make_async_copy(keys_in.at[rows], staged_ref.at[rows], sems.at[b]))
    for copy in small[:3] + copies + small[3:]:
        copy.start()
    for copy in small[:3]:
        copy.wait()

    tokens = frames_ref.shape[1]
    section = lax.axis_index("section")
    own_row = act_frames_ref[pl.ds(section, 1), :].astype(jnp.float32)
    prior_row = act_frames_ref[pl.ds(jnp.maximum(section - 1, 0), 1), :].astype(jnp.float32)
    fresh_row = fresh_frames_ref[...].astype(jnp.float32)
    next_row = jnp.where(in_first_section(), fresh_row, prior_row)
    for tick, row in enumerate((own_row, next_row)):
        frames_ref[tick] = jnp.broadcast_to(column_of(row), (tokens, HD))

    row = row_of(key_frames_ref).astype(jnp.float32)
    lines = -(-length // width)
    row = jnp.concatenate([row, jnp.zeros((1, lines * width - length), jnp.float32)], axis=1)
    line = lax.broadcasted_iota(jnp.int32, (STAT_ROWS, width), 0)
    tail = jnp.zeros((STAT_ROWS, width), jnp.float32)
    for n in range(lines):
        tail = jnp.where(line == n, row[:, n * width : (n + 1) * width], tail)
    for ref in (own_ref, given_ref):
        ref[length:] = tail.astype(jnp.bfloat16)
    halve(staged_ref, copies, own_ref, given_ref)
    for copy in small[3:]:
        copy.wait()


def load_keys(act_frames, fresh_frames, key_frames, batch, fresh, gain, keys):
    length, width = keys.shape
    tokens, model = batch.shape
    share = model * INNER // lax.axis_size("ctx")
    shape = (length + STAT_ROWS, width // PAIR)
    frames = (act_frames, fresh_frames, key_frames)
    return pl.pallas_call(
        load_keys_kernel,
        in_specs=[IN_HBM] * 7,
        out_specs=[WHOLE] * 8,
        out_shape=[
            pltpu.VMEM(shape, keys.dtype),
            pltpu.VMEM(shape, keys.dtype),
            pltpu.VMEM(batch.shape, batch.dtype),
            pltpu.VMEM(gain.shape, gain.dtype),
            pltpu.VMEM((tokens, share), batch.dtype),
            pltpu.VMEM((tokens, share), fresh.dtype),
            pltpu.VMEM((1, share), gain.dtype),
            pltpu.VMEM((2, tokens, HD), jnp.float32),
        ],
        scratch_shapes=[
            *(pltpu.VMEM(a.shape, a.dtype) for a in frames),
            pltpu.VMEM((length, width), keys.dtype),
            pltpu.SemaphoreType.DMA((BLOCKS,)),
            pltpu.SemaphoreType.DMA((8,)),
        ],
        cost_estimate=pl.CostEstimate(
            flops=0, bytes_accessed=2 * length * width, transcendentals=0
        ),
        compiler_params=pltpu.CompilerParams(vmem_limit_bytes=16 * MIB),
        name="load_keys",
    )(*in_hbm(*frames, batch, fresh, gain, keys))


def halve_values_kernel(values_ref, own_ref, given_ref):
    halve(values_ref, [], own_ref, given_ref)


def halve_values(values):
    length, width = values.shape
    half = pltpu.VMEM((length, width // PAIR), values.dtype)
    return pl.pallas_call(
        halve_values_kernel,
        in_specs=[WHOLE],
        out_specs=[WHOLE] * 2,
        out_shape=[half, half],
        cost_estimate=pl.CostEstimate(
            flops=0, bytes_accessed=2 * length * width, transcendentals=0
        ),
        compiler_params=pltpu.CompilerParams(vmem_limit_bytes=16 * MIB),
        name="halve_values",
    )(*in_vmem(values))


def first_kernel(other, gain_ref, frames_ref, batch_ref, keys_ref, values_ref, out_ref):
    length, kv_here = values_ref.shape[0], out_ref.shape[0]
    width = gain_ref.shape[1] // (PAIR * kv_here)
    place = (place_here() + other) % PAIR
    bias = bias_of(keys_ref, frames_ref[0, :, :1])
    for g in range(kv_here):
        index, block = place * kv_here + g, slice(g * HD, (g + 1) * HD)
        x, gain = columns_of(index, batch_ref, width)[...], columns_of(index, gain_ref, width)[...]
        raw = scores(queries_of(x, gain), keys_ref[:length, block], bias)
        top = top_of(raw)
        both = weigh(raw, top, values_ref[:, block])
        write_sums(out_ref.at[g], both[:, :HD], top, both[:, HD:])


def first(other, gain, frames, batch, keys, values):
    length, width = values.shape
    tokens = batch.shape[0]
    kv_here = width // HD
    queries = HEADS // PAIR * tokens
    return pl.pallas_call(
        functools.partial(first_kernel, other),
        in_specs=[WHOLE] * 5,
        out_specs=WHOLE,
        out_shape=jax.ShapeDtypeStruct((kv_here, queries // kv_here + STAT_ROWS, HD), jnp.bfloat16),
        cost_estimate=pl.CostEstimate(
            flops=2 * queries * length * 3 * HD,
            bytes_accessed=4 * length * width,
            transcendentals=queries * length,
        ),
        compiler_params=pltpu.CompilerParams(vmem_limit_bytes=16 * MIB),
        name="first",
    )(*in_vmem(gain, frames, batch, keys, values))


def finish_kernel(steps, mine_ref, got_ref, *out_refs):
    for d, out_ref in zip(steps, out_refs):
        g = outer_here() ^ d
        write_chunk(out_ref, *joined([mine_ref.at[g], got_ref.at[g]], False))


def finish(steps, mine, got):
    chunk = jax.ShapeDtypeStruct(mine.shape[1:], mine.dtype)
    return pl.pallas_call(
        functools.partial(finish_kernel, steps),
        in_specs=[WHOLE] * 2,
        out_specs=[WHOLE] * len(steps),
        out_shape=[chunk] * len(steps),
        compiler_params=pltpu.CompilerParams(vmem_limit_bytes=8 * MIB),
        name="finish",
    )(*in_vmem(mine, got))


def in_calls(call, outers, together):
    chunks, far = {}, outers - together
    for steps in [tuple(range(far, outers))[::-1]] + [(d,) for d in reversed(range(far))]:
        chunks.update(zip(steps, call(steps)))
    return [chunks[d] for d in range(outers)]


def chunk_call(kernel, name, steps, kv_here, count, length, operands):
    chunk = jax.ShapeDtypeStruct((count + STAT_ROWS, HD), jnp.bfloat16)
    return pl.pallas_call(
        functools.partial(kernel, steps, kv_here),
        in_specs=[WHOLE] * len(operands),
        out_specs=[WHOLE] * len(steps),
        out_shape=[chunk] * len(steps),
        cost_estimate=pl.CostEstimate(
            flops=2 * len(steps) * count * length * 3 * HD,
            bytes_accessed=4 * len(steps) * length * HD,
            transcendentals=len(steps) * count * length,
        ),
        compiler_params=pltpu.CompilerParams(vmem_limit_bytes=16 * MIB),
        name=name,
    )(*in_vmem(*operands))


def partials_kernel(steps, kv_here, frames_ref, *refs):
    kv_refs, refs = (refs[0:2], refs[2:4]), refs[4:]
    length = kv_refs[0][1].shape[0]
    biases = [bias_of(keys_ref, frames_ref[1, :, :1]) for keys_ref, _ in kv_refs]
    for d, queries_ref, out_ref in zip(steps, refs, refs[len(steps) :]):
        g = outer_here() ^ d
        raws = [
            scores(queries_ref[...], columns_of(g, keys_ref.at[:length], HD)[...], bias)
            for (keys_ref, _), bias in zip(kv_refs, biases)
        ]
        top = functools.reduce(jnp.maximum, [top_of(raw) for raw in raws])
        both = sum(
            weigh(raw, top, columns_of(g, values_ref, HD)[...])
            for raw, (_, values_ref) in zip(raws, kv_refs)
        )
        write_sums(out_ref, both[:, :HD], top, both[:, HD:])


def partials(steps, frames, own, got, queries):
    length, width = own[1].shape
    count = queries[0].shape[0]
    operands = (frames, *own, *got, *(queries[d] for d in steps))
    return chunk_call(
        partials_kernel, "partials", steps, width // HD, count, PAIR * length, operands
    )


def merge_kernel(*refs):
    *parts, out_ref = refs
    write_chunk(out_ref, *joined(parts, False))


def merge_first_kernel(*refs):
    *parts, share_ref, out_ref = refs
    x = head_rows(share_ref[...].astype(jnp.float32)).astype(jnp.bfloat16)
    write_chunk(out_ref, *joined(parts, False, x))


def merge(kernel, *parts):
    return pl.pallas_call(
        kernel,
        in_specs=[WHOLE] * len(parts),
        out_specs=WHOLE,
        out_shape=jax.ShapeDtypeStruct(parts[0].shape, parts[0].dtype),
        compiler_params=pltpu.CompilerParams(vmem_limit_bytes=8 * MIB),
        name="merge",
    )(*in_vmem(*parts))


def attended(one_ref, two_ref):
    one, two = one_ref[...].astype(jnp.float32), two_ref[...].astype(jnp.float32)
    here = inner_here() == 0
    parts = [jnp.where(here, one, two), jnp.where(here, two, one)]
    value, _, _ = joined([part.astype(jnp.bfloat16) for part in parts], True)
    return value


def columns_from(rows, tokens):
    pieces = [rows[at : at + tokens] for at in range(0, rows.shape[0], tokens)]
    return jnp.concatenate(pieces, axis=1)


def combine_kernel(gain_ref, fresh_ref, one_ref, two_ref, share_ref, queries_ref):
    tokens = fresh_ref.shape[0]
    handed = columns_from(attended(one_ref, two_ref), tokens).astype(jnp.bfloat16)
    fresh = fresh_ref[...].astype(jnp.float32)
    share = jnp.where(in_first_section(), fresh, handed.astype(jnp.float32))
    share = share.astype(jnp.bfloat16)
    share_ref[...] = share
    queries_ref[...] = queries_of(share, gain_ref[...])


def combine(gain, fresh, one, two):
    count = one.shape[0] - STAT_ROWS
    return pl.pallas_call(
        combine_kernel,
        in_specs=[WHOLE] * 4,
        out_specs=[WHOLE] * 2,
        out_shape=[
            jax.ShapeDtypeStruct(fresh.shape, fresh.dtype),
            jax.ShapeDtypeStruct((count, HD), jnp.bfloat16),
        ],
        compiler_params=pltpu.CompilerParams(vmem_limit_bytes=8 * MIB),
        name="combine",
    )(*in_vmem(gain, fresh, one, two))


def combine_last_kernel(two_ref, one_ref, share_ref, out_ref):
    tokens = out_ref.shape[0]
    total = head_rows(share_ref[...].astype(jnp.float32)) + attended(one_ref, two_ref)
    out_ref[...] = columns_from(total, tokens).astype(jnp.bfloat16)


def combine_last(share, one, two):
    return pl.pallas_call(
        combine_last_kernel,
        in_specs=[WHOLE] * 3,
        out_specs=WHOLE,
        out_shape=jax.ShapeDtypeStruct(share.shape, share.dtype),
        compiler_params=pltpu.CompilerParams(vmem_limit_bytes=8 * MIB),
        name="combine_last",
    )(*in_vmem(two, one, share))


def assemble_kernel(*refs):
    *pieces, out_ref = refs
    outers, width = len(pieces) // PAIR, pieces[0].shape[1]
    for n, refs in enumerate((pieces[:outers], pieces[outers:])):
        place = (place_here() + n) % PAIR
        for d, ref in zip(reversed(range(outers)), refs):
            columns_of(place * outers + (outer_here() ^ d), out_ref, width)[...] = ref[...]


def assemble(mine, others):
    tokens, width = mine[0].shape
    pieces = [*mine[::-1], *others[::-1]]
    return pl.pallas_call(
        assemble_kernel,
        in_specs=[WHOLE] * len(pieces),
        out_specs=WHOLE,
        out_shape=jax.ShapeDtypeStruct((tokens, len(pieces) * width), jnp.bfloat16),
        compiler_params=pltpu.CompilerParams(vmem_limit_bytes=8 * MIB),
        name="assemble",
    )(*in_vmem(*pieces))


def body(
    activations,
    act_frames,
    fresh_batch,
    fresh_frames,
    norm_gain,
    cached_keys,
    cached_values,
    key_frames,
):
    own_keys, given_keys, batch, gain, share, fresh, fresh_gain, frames = load_keys(
        act_frames, fresh_frames[None], key_frames.reshape(-1, HD), activations[0], fresh_batch,
        norm_gain, cached_keys[0],
    )
    own_values, given_values = halve_values(cached_values[0])

    outers = lax.axis_size("ctx") // (INNER * PAIR)
    theirs = swapped(first(1, gain, frames, batch, given_keys, given_values))
    mine = first(0, gain, frames, batch, own_keys, own_values)
    chunk, *others = in_calls(lambda steps: finish(steps, mine, theirs), outers, outers - 1)
    own, got = (own_keys, own_values), (swapped(given_keys), swapped(given_values))
    chunk = merge(merge_first_kernel, *from_outer(others, 0)[::-1], chunk, share)
    one, two = [from_section_before(chunk, step) for step in range(INNER)]
    share, queries = combine(fresh_gain, fresh, one, two)
    queries = [swapped(queries), *from_outer([queries] * len(others))]

    chunk, *others = in_calls(lambda steps: partials(steps, frames, own, got, queries), outers, 1)
    chunk = merge(merge_kernel, swapped(chunk), *from_outer(others))
    one, two = swapped(chunk), from_inner(chunk)
    share = combine_last(swapped(share), one, two)
    theirs = [swapped(share), *from_outer([share] * len(others))]
    return assemble([share, *(swapped(piece) for piece in theirs[1:])], theirs)[None]


def solution(mesh):
    placed = (
        P("section", None, None),
        P(),
        P(),
        P(),
        P("section", None),
        P("section", "ctx", None),
        P("section", "ctx", None),
        P("ctx"),
    )
    return jax.shard_map(
        body, mesh=mesh, in_specs=placed, out_specs=P("section", None, None), check_vma=False
    )
```
